32 devices in a mesh: dp: 8 (over z, y), mp: 4 (over x, core).
Axes of the slice: x: 2, y: 2, z: 4, core: 2. Of those that a mesh axis runs over, the one named last changes fastest.
Arguments:
- hidden_in: bfloat16 [16, 1024, 1024], P('dp', 'mp'), may hold values from -6 to 6
- pair_lengths: int32 [16, 8], P('dp'), may hold values from 2 to 1010, as said below
- prefix_keys: bfloat16 [64, 1024], replicated, may hold values from -6 to 6
- prefix_values: bfloat16 [64, 1024], replicated, may hold values from -6 to 6
- project_weight: bfloat16 [1024, 3072], replicated, may hold values from -0.1875 to 0.1875
- project_bias: bfloat16 [3072], replicated, may hold values from -0.4375 to 0.4375
- output_weight: bfloat16 [1024, 1024], replicated, may hold values from -1 to 1
- output_bias: bfloat16 [1024], replicated, may hold values from -6 to 6
- first_gain: bfloat16 [1024], replicated, may hold values from 0.5 to 1.5
- first_shift: bfloat16 [1024], replicated, may hold values from -6 to 6
- expand_weight: bfloat16 [1024, 4096], P(None, 'mp'), may hold values from -0.1875 to 0.1875
- expand_bias: bfloat16 [4096], P('mp'), may hold values from -6 to 6
- reduce_weight: bfloat16 [4096, 1024], P('mp'), may hold values from -0.09375 to 0.09375
- reduce_bias: bfloat16 [1024], replicated, may hold values from -6 to 6
- second_gain: bfloat16 [1024], replicated, may hold values from 0.5 to 1.5
- second_shift: bfloat16 [1024], replicated, may hold values from -6 to 6
- upstream: bfloat16 [16, 1024, 1024], P('dp', 'mp'), may hold values from -6 to 6
Outputs:
- hidden_out: bfloat16 [16, 1024, 1024], P('dp', 'mp')
- grad_in: bfloat16 [16, 1024, 1024], P('dp', 'mp')
- grad_prefix_keys: float32 [64, 1024], replicated
- grad_prefix_values: float32 [64, 1024], replicated
The draws below stay inside these ranges and needn't reach their ends.
Inputs may be any that keep to these rules, and one draw needn't show every extreme that they name: `pair_lengths`: the 8 pairs of a row lie end to end from its first position; their lengths add up to 1024 or less, and the positions after them are pad. A pair is at most 1024 - 2 * (7) long.
All inputs are finite; a program needn't handle non-finite values.
Results may differ from the reference program's by a relative error of at most 0.015.
Values may be sent and summed in bfloat16 or wider, within the bound.
No kernel may reach another device: no remote copies, remote signals or barrier semaphores. Data moves between devices by JAX's collectives and lax.ppermute only.
A program may use at most 192 MiB of HBM per device.

```python
import jax
import jax.numpy as jnp
from jax import lax

D = 1024
HEADS = 16
FF = 4096
PREFIX = 64
SEQ = 1024
PAIRS = 8
SHARD = 256
ROWS = 16


def draw_pair_lengths(key, part):
    key = jax.random.fold_in(key, 11)
    short_key, pad_key, slot_key = jax.random.split(key, 3)
    short_most = max(2, (SHARD - 1) // PAIRS)
    first_row = jnp.arange(ROWS, dtype=jnp.int32)[:, None] == 0
    shorts = jax.random.randint(short_key, (ROWS, PAIRS), 2, short_most + 1)
    shorts = jnp.where(first_row, 2, shorts)
    padding = jax.random.randint(pad_key, (ROWS, 1), 0, short_most + 1)
    padding = jnp.where(first_row, 0, padding)
    long_slot = jax.random.randint(slot_key, (ROWS, 1), 0, PAIRS)
    is_long = jnp.arange(PAIRS, dtype=jnp.int32)[None, :] == long_slot
    others = jnp.sum(jnp.where(is_long, 0, shorts), axis=1, keepdims=True)
    return jnp.where(is_long, SEQ - padding - others, shorts).astype(jnp.int32)


def block_levels(stream_key, dims, shards, least, largest):
    def one(dim, shards_of):
        draws = jax.random.uniform(jax.random.fold_in(jax.random.fold_in(stream_key, 6), dim), (shards_of,), jnp.float32, least / len(shards), largest / len(shards))
        return jnp.repeat(jnp.exp(draws), dims[dim] // shards_of).reshape((-1,) + (1,) * (len(dims) - dim - 1))

    loudness = one(*shards[0])
    for cut in shards[1:]:
        loudness = loudness * one(*cut)
    return loudness


def centred(own_key, dims, width, bound, cuts=(), held_as=jnp.bfloat16):
    result = jax.random.normal(own_key, dims, jnp.float32) * width
    if len(cuts) > 0:
        result = block_levels(own_key, dims, cuts, -0.22, 0.18) * result
    return jnp.clip(result, min=-bound, max=bound).astype(held_as)


def setup_inputs(seed: int = 0) -> dict:
    seeds = jax.random.split(jax.random.key(seed), 18)
    return {
        "hidden_in": centred(seeds[0], (ROWS, SEQ, D), 1.0, 6.0, ((0, 8), (1, 4))),
        "pair_lengths": draw_pair_lengths(jax.random.fold_in(seeds[17], 71), 0),
        "prefix_keys": centred(seeds[2], (PREFIX, D), 1.0, 6.0),
        "prefix_values": centred(seeds[3], (PREFIX, D), 1.0, 6.0),
        "project_weight": centred(seeds[4], (D, 3 * D), D ** -0.5, 0.1875),
        "project_bias": centred(seeds[5], (3 * D,), 0.03, 0.4375),
        "output_weight": centred(seeds[6], (D, D), (D // 32) ** -0.5, 1.0),
        "output_bias": centred(seeds[7], (D,), 0.5, 6.0),
        "first_gain": jnp.clip(1.0 + 0.1 * jax.random.normal(seeds[8], (D,), jnp.float32), 0.5, 1.5).astype(jnp.bfloat16),
        "first_shift": centred(seeds[9], (D,), 0.5, 6.0),
        "expand_weight": centred(seeds[10], (D, FF), D ** -0.5, 0.1875, ((1, 4),)),
        "expand_bias": centred(seeds[11], (FF,), 0.5, 6.0, ((0, 4),)),
        "reduce_weight": centred(seeds[12], (FF, D), FF ** -0.5, 0.09375, ((0, 4),)),
        "reduce_bias": centred(seeds[13], (D,), 0.5, 6.0),
        "second_gain": jnp.clip(1.0 + 0.1 * jax.random.normal(seeds[14], (D,), jnp.float32), 0.5, 1.5).astype(jnp.bfloat16),
        "second_shift": centred(seeds[15], (D,), 0.5, 6.0),
        "upstream": centred(seeds[16], (ROWS, SEQ, D), 1.0, 6.0, ((0, 8), (1, 4))),
    }


@jax.custom_vjp
def low(v):
    return lax.optimization_barrier(v.astype(jnp.bfloat16)).astype(jnp.float32)

@jax.custom_vjp
def low_back(v):
    return v

def low_keep(v):
    return (low(v), None)

def low_pass(kept, grad):
    return (grad,)

def back_keep(v):
    return (v, None)

def back_low(kept, grad):
    return (low(grad),)
low.defvjp(low_keep, low_pass)
low_back.defvjp(back_keep, back_low)
highest = lax.Precision.HIGHEST
epsilon = 1e-05
masked_score = -1e+30
root_half = 0.7071067811865476

def exact_gelu(inputs):
    return 0.5 * inputs * (1.0 + jax.scipy.special.erf(inputs * root_half))

def normalize(inputs, gain_row, shift_row):
    row_mean = lax.optimization_barrier(jnp.mean(inputs, axis=-1, keepdims=True))
    centered = inputs - row_mean
    variance = lax.optimization_barrier(jnp.mean(centered * centered, axis=-1, keepdims=True))
    return centered * lax.rsqrt(variance + epsilon) * gain_row + shift_row

def matmul(left_side, right_side):
    return jnp.dot(left_side, right_side, precision=highest, preferred_element_type=jnp.float32)

def segment_ids(lengths_row):
    boundary = jnp.cumsum(lengths_row)
    position = jnp.arange(SEQ, dtype=jnp.int32)
    return lax.optimization_barrier(jnp.sum((position[:, None] >= boundary[None, :]).astype(jnp.int32), axis=1))

def layer_row(tokens, keys_prefix, values_prefix, segment, weights):
    project_weight, project_bias, output_weight, output_bias, first_gain, first_shift, expand_weight, expand_bias, reduce_weight, reduce_bias, second_gain, second_shift = weights
    head_width = D // HEADS
    score_scale = head_width ** (-0.5)
    projected = matmul(tokens, project_weight) + project_bias
    queries = low(low_back(projected[:, :D]))
    keys = low(low_back(projected[:, D:2 * D]))
    values = low(low_back(projected[:, 2 * D:]))
    all_keys = jnp.concatenate([keys_prefix, keys], 0).reshape(PREFIX + SEQ, HEADS, head_width)
    all_values = jnp.concatenate([values_prefix, values], 0).reshape(PREFIX + SEQ, HEADS, head_width)
    query_heads = queries.reshape(SEQ, HEADS, head_width)
    live_rows = segment < PAIRS
    same_pair = (segment[:, None] == segment[None, :]) & live_rows[None, :]
    allowed = jnp.concatenate([jnp.ones((SEQ, PREFIX), dtype=bool), same_pair], 1)
    scores = jnp.einsum('qhd,khd->hqk', query_heads, all_keys, precision=highest) * score_scale
    scores = low_back(jnp.where(allowed[None], scores, masked_score))
    row_max = lax.optimization_barrier(jnp.max(scores, axis=-1, keepdims=True))
    exponent = jnp.exp(scores - row_max)
    probs_low = low(exponent / lax.optimization_barrier(jnp.sum(exponent, axis=-1, keepdims=True)))
    attended = jnp.einsum('hqk,khd->qhd', probs_low, all_values, precision=highest).reshape(SEQ, D)
    attended = low(low_back(attended))
    branch = low_back(matmul(attended, output_weight) + output_bias)
    first_norm = normalize(tokens + branch, first_gain, first_shift)
    hidden = low_back(matmul(low(first_norm), expand_weight) + expand_bias)
    active = low(exact_gelu(hidden))
    feed_out = low_back(matmul(active, reduce_weight) + reduce_bias)
    second_norm = normalize(first_norm + feed_out, second_gain, second_shift)
    return second_norm * live_rows[:, None].astype(jnp.float32)

def reference(hidden_in, pair_lengths, prefix_keys, prefix_values, project_weight, project_bias, output_weight, output_bias, first_gain, first_shift, expand_weight, expand_bias, reduce_weight, reduce_bias, second_gain, second_shift, upstream):
    weights = tuple((tensor.astype(jnp.float32) for tensor in (project_weight, project_bias, output_weight, output_bias, first_gain, first_shift, expand_weight, expand_bias, reduce_weight, reduce_bias, second_gain, second_shift)))
    keys_prefix = prefix_keys.astype(jnp.float32)
    values_prefix = prefix_values.astype(jnp.float32)

    def one_row(totals, inputs):
        tokens, lengths_row, cotangent = inputs
        segment = segment_ids(lengths_row)

        def forward(tokens_in, keys_in, values_in):
            return layer_row(tokens_in, keys_in, values_in, segment, weights)
        output, pullback = jax.vjp(forward, tokens.astype(jnp.float32), keys_prefix, values_prefix)
        grad_tokens, grad_keys, grad_values = pullback(cotangent.astype(jnp.float32))
        return ((totals[0] + grad_keys, totals[1] + grad_values), (output.astype(jnp.bfloat16), grad_tokens.astype(jnp.bfloat16)))
    initial = (jnp.zeros((PREFIX, D), jnp.float32), jnp.zeros((PREFIX, D), jnp.float32))
    prefix_sums, (outputs, gradients) = lax.scan(one_row, initial, (hidden_in, pair_lengths, upstream))
    return (outputs, gradients, prefix_sums[0], prefix_sums[1])
```

```python
import functools

import jax
import jax.numpy as jnp
from jax import lax
from jax.experimental import pallas as pl
from jax.experimental.pallas import tpu as pltpu
from jax.sharding import PartitionSpec as P

HEADS = 16
PAIRS = 8

epsilon = 1e-05
masked_score = -1e30
root_half = 0.7071067811865476
inverse_root = 0.3989422804014327
log2_e = 1.4426950408889634
ln_2 = 0.6931471805599453
VMEM_LIMIT = 56 * 2**20

bf16 = jnp.bfloat16
f32 = jnp.float32


def dot(left, right, left_dim=1, right_dim=0):
    return lax.dot_general(
        left, right, (((left_dim,), (right_dim,)), ((), ())), preferred_element_type=f32
    )


def params(**kwargs):
    return pltpu.CompilerParams(vmem_limit_bytes=VMEM_LIMIT, **kwargs)


def cost(flops, bytes_accessed, transcendentals=0):
    return pl.CostEstimate(
        flops=int(flops), bytes_accessed=int(bytes_accessed), transcendentals=int(transcendentals)
    )


ANY = pl.BlockSpec(memory_space=pl.ANY)


def swap(array, axis, bit, size):
    return lax.ppermute(array, axis, [(i, i ^ bit) for i in range(size)])


def project_kernel(core_ref, own, cross, own2, cross2, weight, bias, out):
    part = pl.program_id(0)
    scale = jnp.where(part == 0, log2_e * 0.125, 1.0).astype(f32)
    shift = bias[...].astype(f32)
    weights = weight[...]
    block = own.shape[0]
    for i, ref in enumerate((own, cross, own2, cross2)):
        out[0, i * block : (i + 1) * block, :] = (
            (dot(ref[...], weights) + shift) * scale
        ).astype(bf16)


def project(core, blocks, weight, bias):
    block, width = blocks[0].shape
    half = width // 2
    spec = pl.BlockSpec((block, width), lambda j, k: (0, 0))
    return pl.pallas_call(
        project_kernel,
        grid_spec=pltpu.PrefetchScalarGridSpec(
            num_scalar_prefetch=1,
            grid=(3,),
            in_specs=[spec] * 4
            + [
                pl.BlockSpec((width, half), lambda j, k: (0, 2 * j + k[0])),
                pl.BlockSpec((1, half), lambda j, k: (0, 2 * j + k[0])),
            ],
            out_specs=pl.BlockSpec((1, 4 * block, half), lambda j, k: (j, 0, 0)),
        ),
        out_shape=jax.ShapeDtypeStruct((3, 4 * block, half), bf16),
        compiler_params=params(),
        cost_estimate=cost(2 * 4 * block * width * 3 * half, 2 * (4 * block * width + 3 * width * half + 3 * 4 * block * half)),
        name="project",
    )(core, *blocks, weight, bias)


def head_mask(shape, head, axis):
    return (lax.broadcasted_iota(jnp.int32, shape, axis) // 64) == head


def attend_kernel(
    core_ref, qkv, prefix_k, prefix_v, seg_row, seg_col,
    out_mine, out_other, exps, recips, keys, values_t,
):
    prefix = prefix_k.shape[0]
    tokens = qkv.shape[1]
    count = prefix + tokens
    chunk = 256
    keys[:prefix, :] = prefix_k[...]
    keys[prefix:, :] = qkv[1]
    values_t[:128, :prefix] = prefix_v[...].astype(f32).T.astype(bf16)
    values_t[:128, prefix:] = qkv[2].astype(f32).T.astype(bf16)
    values_t[128:, :] = jnp.ones((values_t.shape[0] - 128, count), bf16)
    seg_keys = jnp.concatenate([seg_col[...]] * (chunk // 128), axis=1)
    for start in range(0, tokens, chunk):
        cols = slice(start, start + chunk)
        query = qkv[0, cols, :]
        allowed = seg_keys == seg_row[0:1, cols]
        parts = []
        for head in range(2):
            masked = jnp.where(head_mask((chunk, 128), head, 1), query, jnp.zeros_like(query))
            scores_p = dot(keys[:prefix, :], masked, 1, 1)
            scores_r = jnp.where(allowed, dot(keys[prefix:, :], masked, 1, 1), masked_score)
            top = jnp.maximum(
                jnp.max(scores_p, axis=0, keepdims=True), jnp.max(scores_r, axis=0, keepdims=True)
            )
            exps[0, head, :prefix, cols] = jnp.exp2(scores_p - top).astype(bf16)
            exps[0, head, prefix:, cols] = jnp.exp2(scores_r - top).astype(bf16)
            weights = exps[0, head, :, cols]
            summed = dot(
                jnp.concatenate([values_t[64 * head : 64 * head + 64, :], values_t[128:, :]], axis=0),
                weights,
            )
            recip = 1.0 / summed[64:65, :]
            recips[0, head, :, cols] = jnp.broadcast_to(recip, (8, chunk))
            parts.append(summed[:64, :] * recip)
        result = jnp.concatenate(parts, axis=0).T.astype(bf16)
        if start < tokens // 2:
            out_mine[cols, :] = result
        else:
            out_other[start - tokens // 2 : start - tokens // 2 + chunk, :] = result


def attend(core, qkv, prefix_keys, prefix_values, seg_row, seg_col):
    _, tokens, half = qkv.shape
    prefix = prefix_keys.shape[0]
    count = prefix + tokens
    pairs = half // 128
    prefix_spec = pl.BlockSpec((prefix, 128), lambda p, k: (0, k[0] * pairs + p))
    out_spec = pl.BlockSpec((tokens // 2, 128), lambda p, k: (0, p))
    out = jax.ShapeDtypeStruct((tokens // 2, half), bf16)
    return pl.pallas_call(
        attend_kernel,
        grid_spec=pltpu.PrefetchScalarGridSpec(
            num_scalar_prefetch=1,
            grid=(pairs,),
            in_specs=[
                pl.BlockSpec((3, tokens, 128), lambda p, k: (0, 0, p)),
                prefix_spec,
                prefix_spec,
                pl.BlockSpec((8, tokens), lambda p, k: (0, 0)),
                pl.BlockSpec((tokens, 128), lambda p, k: (0, 0)),
            ],
            out_specs=[
                out_spec,
                out_spec,
                pl.BlockSpec((1, 2, count, tokens), lambda p, k: (p, 0, 0, 0)),
                pl.BlockSpec((1, 2, 8, tokens), lambda p, k: (p, 0, 0, 0)),
            ],
            scratch_shapes=[pltpu.VMEM((count, 128), bf16), pltpu.VMEM((128 + 16, count), bf16)],
        ),
        out_shape=[
            out,
            out,
            jax.ShapeDtypeStruct((pairs, 2, count, tokens), bf16),
            jax.ShapeDtypeStruct((pairs, 2, 8, tokens), f32),
        ],
        compiler_params=params(),
        cost_estimate=cost(16 * pairs * 2 * count * tokens * 64, 2 * pairs * 2 * count * tokens, pairs * 2 * count * tokens),
        name="attend",
    )(core, qkv, prefix_keys, prefix_values, seg_row, seg_col)


def attend_back_kernel(
    core_ref, qkv, prefix_k, prefix_v, exps, recips, attended_mine, attended_other,
    grad_mine, grad_other, out_mine, out_other, out_prefix,
    keys, values, keys_t, slopes, queries_t,
):
    prefix = prefix_k.shape[0]
    tokens = qkv.shape[1]
    half = tokens // 2
    keys[:prefix, :] = prefix_k[...]
    keys[prefix:, :] = qkv[1]
    values[:prefix, :] = prefix_v[...]
    values[prefix:, :] = qkv[2]
    keys_t[...] = keys[...].astype(f32).T.astype(bf16)
    query = qkv[0]
    grad = jnp.concatenate([grad_mine[...], grad_other[...]], axis=0).astype(f32)
    attended = jnp.concatenate([attended_mine[...], attended_other[...]], axis=0).astype(f32)
    grad_t = grad.T
    product_t = (grad * attended).T
    zeros = jnp.zeros((64, tokens), f32)
    grad_keys = None
    grad_values = None
    for head in range(2):
        rows = slice(64 * head, 64 * head + 64)
        recip = recips[0, head, 0:1, :]
        spread = jnp.sum(product_t[rows, :], axis=0, keepdims=True) * recip
        scaled = grad_t[rows, :] * recip
        scaled_t = jnp.concatenate([scaled, zeros] if head == 0 else [zeros, scaled], axis=0)
        scaled_n = scaled_t.T.astype(bf16)
        scaled_t = scaled_t.astype(bf16)
        for start in range(0, tokens, 256):
            cols = slice(start, start + 256)
            grad_probs = dot(values[...], scaled_t[:, cols])
            slopes[head, :, cols] = (
                exps[0, head, :, cols].astype(f32) * (grad_probs - spread[:, cols])
            ).astype(bf16)
            queries_t[rows, cols] = dot(keys_t[rows, :], slopes[head, :, cols]) * 0.125
        masked = jnp.where(head_mask((tokens, 128), head, 1), query, jnp.zeros_like(query))
        value_part = dot(exps[0, head], scaled_n)
        key_part = dot(slopes[head], masked)
        grad_keys = key_part if head == 0 else grad_keys + key_part
        grad_values = value_part if head == 0 else grad_values + value_part
    grad_keys = grad_keys * ln_2
    grad_queries = queries_t[...].T.astype(bf16)
    out_prefix[0] = grad_keys[:prefix]
    out_prefix[1] = grad_values[:prefix]
    out_mine[0] = grad_queries[:half]
    out_other[0] = grad_queries[half:]
    out_mine[1] = grad_keys[prefix : prefix + half].astype(bf16)
    out_other[1] = grad_keys[prefix + half :].astype(bf16)
    out_mine[2] = grad_values[prefix : prefix + half].astype(bf16)
    out_other[2] = grad_values[prefix + half :].astype(bf16)


def attend_back(core, qkv, prefix_keys, prefix_values, exps, recips, attended, grads):
    _, tokens, half = qkv.shape
    prefix = prefix_keys.shape[0]
    count = prefix + tokens
    pairs = half // 128
    prefix_spec = pl.BlockSpec((prefix, 128), lambda p, k: (0, k[0] * pairs + p))
    token_spec = pl.BlockSpec((tokens // 2, 128), lambda p, k: (0, p))
    out_spec = pl.BlockSpec((3, tokens // 2, 128), lambda p, k: (0, 0, p))
    out = jax.ShapeDtypeStruct((3, tokens // 2, half), bf16)
    return pl.pallas_call(
        attend_back_kernel,
        grid_spec=pltpu.PrefetchScalarGridSpec(
            num_scalar_prefetch=1,
            grid=(pairs,),
            in_specs=[
                pl.BlockSpec((3, tokens, 128), lambda p, k: (0, 0, p)),
                prefix_spec,
                prefix_spec,
                pl.BlockSpec((1, 2, count, tokens), lambda p, k: (p, 0, 0, 0)),
                pl.BlockSpec((1, 2, 8, tokens), lambda p, k: (p, 0, 0, 0)),
                token_spec,
                token_spec,
                token_spec,
                token_spec,
            ],
            out_specs=[out_spec, out_spec, pl.BlockSpec((2, prefix, 128), lambda p, k: (0, 0, p))],
            scratch_shapes=[
                pltpu.VMEM((count, 128), bf16),
                pltpu.VMEM((count, 128), bf16),
                pltpu.VMEM((128, count), bf16),
                pltpu.VMEM((2, count, tokens), bf16),
                pltpu.VMEM((128, tokens), f32),
            ],
        ),
        out_shape=[out, out, jax.ShapeDtypeStruct((2, prefix, half), f32)],
        compiler_params=params(),
        cost_estimate=cost(32 * pairs * 2 * count * tokens * 64, 2 * pairs * 2 * count * tokens),
        name="attend_back",
    )(core, qkv, prefix_keys, prefix_values, exps, recips, *attended, *grads)


def mean_rows(array):
    return jnp.mean(array, axis=-1, keepdims=True)


def unit_norm(array):
    centered = array - mean_rows(array)
    inverse = lax.rsqrt(mean_rows(centered * centered) + epsilon)
    return centered * inverse, inverse


def norm_back(scaled, unit, inverse):
    return inverse * (scaled - mean_rows(scaled) - unit * mean_rows(scaled * unit))


def gelu_both(hidden):
    gate = 0.5 * (1.0 + lax.erf(hidden * root_half))
    slope = gate + hidden * inverse_root * jnp.exp(-0.5 * hidden * hidden)
    return (hidden * gate).astype(bf16), slope.astype(bf16)


def start_all(copies):
    for copy in copies:
        copy.start()


def forward_kernel(
    core_ref, mine, other, own, cross, output_weight, output_bias, gain, shift,
    expand_own, expand_sib, reduce_own, reduce_sib, bias_own, bias_sib,
    unit_out, inverse_out, total_out, slope_out,
    out_w, expand_w, reduce_w, low, sems,
):
    core = core_ref[0]
    copies = [
        pltpu.make_async_copy(output_weight, out_w, sems.at[0]),
        pltpu.make_async_copy(expand_own, expand_w.at[0], sems.at[1]),
        pltpu.make_async_copy(reduce_own, reduce_w.at[0], sems.at[2]),
        pltpu.make_async_copy(expand_sib, expand_w.at[1], sems.at[3]),
        pltpu.make_async_copy(reduce_sib, reduce_w.at[1], sems.at[4]),
    ]
    start_all(copies)
    copies[0].wait()
    half = mine.shape[1]
    block = own.shape[0]
    for i, ref in enumerate((own, cross)):
        rows = slice(i * block, (i + 1) * block)
        branch = dot(mine[rows, :], out_w[pl.ds(pl.multiple_of(core * half, half), half), :])
        branch += dot(other[rows, :], out_w[pl.ds(pl.multiple_of((1 - core) * half, half), half), :])
        unit, inverse = unit_norm(ref[...].astype(f32) + (branch + output_bias[...].astype(f32)))
        unit_out[rows, :] = unit
        inverse_out[rows, :] = jnp.broadcast_to(inverse, (block, 128))
        low[rows, :] = (unit * gain[...].astype(f32) + shift[...].astype(f32)).astype(bf16)
    chunk = 512
    hidden_here = expand_own.shape[1]
    first = True
    for i, bias in enumerate((bias_own, bias_sib)):
        copies[1 + 2 * i].wait()
        copies[2 + 2 * i].wait()
        for start in range(0, hidden_here, chunk):
            cols = slice(start, start + chunk)
            hidden = dot(low[...], expand_w[i, :, cols]) + bias[0:1, cols].astype(f32)
            active, slope = gelu_both(hidden)
            slope_out[:, i * hidden_here + start : i * hidden_here + start + chunk] = slope
            part = dot(active, reduce_w[i, cols, :])
            if first:
                total_out[...] = part
            else:
                total_out[...] += part
            first = False


VM = pl.BlockSpec(memory_space=pltpu.VMEM)
SM = pl.BlockSpec(memory_space=pltpu.SMEM)


def forward(core, mine, other, own, cross, output_weight, output_bias, gain, shift, weights):
    tokens = mine.shape[0]
    width = own.shape[1]
    hidden = weights[0].shape[1]
    return pl.pallas_call(
        forward_kernel,
        in_specs=[SM, VM, VM, VM, VM, ANY, VM, VM, VM, ANY, ANY, ANY, ANY, VM, VM],
        out_specs=[VM, VM, VM, VM],
        out_shape=[
            jax.ShapeDtypeStruct((tokens, width), f32),
            jax.ShapeDtypeStruct((tokens, 128), f32),
            jax.ShapeDtypeStruct((tokens, width), f32),
            jax.ShapeDtypeStruct((tokens, 2 * hidden), bf16),
        ],
        scratch_shapes=[
            pltpu.VMEM((width, width), bf16),
            pltpu.VMEM((2, width, hidden), bf16),
            pltpu.VMEM((2, hidden, width), bf16),
            pltpu.VMEM((tokens, width), bf16),
            pltpu.SemaphoreType.DMA((5,)),
        ],
        compiler_params=params(),
        cost_estimate=cost(2 * tokens * width * (width + 4 * hidden), 2 * width * (width + 4 * hidden) + 14 * tokens * width),
        name="forward",
    )(core, mine, other, own, cross, output_weight, output_bias, gain, shift, *weights)


def middle_kernel(
    core_ref, unit, inverse, total, slope_local, seg, upstream_own, upstream_cross,
    gain1, shift1, reduce_bias, gain2, shift2,
    output_weight, expand_own, expand_sib, reduce_own, reduce_sib,
    p0, p1, p2, p3, s0, s1, s2, s3,
    hidden_own, hidden_cross, grad_branch, grad_att_mine, grad_att_other,
    out_w, expand_w, reduce_w, pieces, low, slope, acc, acc2, sems,
):
    core = core_ref[0]
    remote = (p0, p1, p2, p3, s0, s1, s2, s3)
    count = len(remote)
    piece_copies = [
        pltpu.make_async_copy(ref, pieces.at[i], sems.at[i]) for i, ref in enumerate(remote)
    ]
    weight_copies = [
        pltpu.make_async_copy(reduce_own, reduce_w.at[0], sems.at[count]),
        pltpu.make_async_copy(expand_own, expand_w.at[0], sems.at[count + 1]),
        pltpu.make_async_copy(reduce_sib, reduce_w.at[1], sems.at[count + 2]),
        pltpu.make_async_copy(expand_sib, expand_w.at[1], sems.at[count + 3]),
        pltpu.make_async_copy(output_weight, out_w, sems.at[count + 4]),
    ]
    start_all(piece_copies)
    start_all(weight_copies)
    tokens, width = unit.shape
    block = upstream_own.shape[0]
    quarter = (p0.shape[0] - 16) // 2
    first_gain = gain1[...].astype(f32)
    first_shift = shift1[...].astype(f32)
    low[...] = (unit[...] * first_gain + first_shift).astype(bf16)
    acc[...] = total[...]
    for i in range(count):
        piece_copies[i].wait()
        hidden = dot(low[...], pieces[i, :quarter, :], 1, 1) + pieces[
            i, 2 * quarter : 2 * quarter + 1, :quarter
        ].astype(f32)
        active, slope_part = gelu_both(hidden)
        slope[i] = slope_part
        acc[...] += dot(active, pieces[i, quarter : 2 * quarter, :])
    second_gain = gain2[...].astype(f32)
    second_shift = shift2[...].astype(f32)
    for i, (up, out) in enumerate(((upstream_own, hidden_own), (upstream_cross, hidden_cross))):
        rows = slice(i * block, (i + 1) * block)
        live = jnp.where(seg[rows, 0:1] < PAIRS, 1.0, 0.0).astype(f32)
        first_norm = unit[rows, :] * first_gain + first_shift
        unit2, inverse2 = unit_norm(first_norm + (acc[rows, :] + reduce_bias[...].astype(f32)))
        out[...] = ((unit2 * second_gain + second_shift) * live).astype(bf16)
        grad_feed = norm_back(up[...].astype(f32) * live * second_gain, unit2, inverse2)
        acc2[rows, :] = grad_feed
        low[rows, :] = grad_feed.astype(bf16)
    for i in range(count):
        back = (
            dot(low[...], pieces[i, quarter : 2 * quarter, :], 1, 1) * slope[i].astype(f32)
        ).astype(bf16)
        acc2[...] += dot(back, pieces[i, :quarter, :])
    hidden_here = expand_own.shape[1]
    chunk = 512
    for i in range(2):
        weight_copies[2 * i].wait()
        weight_copies[2 * i + 1].wait()
        for start in range(0, hidden_here, chunk):
            cols = slice(start, start + chunk)
            back = (
                dot(low[...], reduce_w[i, cols, :], 1, 1)
                * slope_local[:, i * hidden_here + start : i * hidden_here + start + chunk].astype(f32)
            ).astype(bf16)
            acc2[...] += dot(back, expand_w[i, :, cols], 1, 1)
    for i in range(2):
        rows = slice(i * block, (i + 1) * block)
        grad = norm_back(acc2[rows, :] * first_gain, unit[rows, :], inverse[rows, 0:1])
        grad_branch[rows, :] = grad
        low[rows, :] = grad.astype(bf16)
    weight_copies[4].wait()
    half = width // 2
    grad_att_mine[...] = dot(
        low[...], out_w[pl.ds(pl.multiple_of(core * half, half), half), :], 1, 1
    ).astype(bf16)
    grad_att_other[...] = dot(
        low[...], out_w[pl.ds(pl.multiple_of((1 - core) * half, half), half), :], 1, 1
    ).astype(bf16)


def middle(core, saved, seg, upstream, vectors, output_weight, weights, pieces):
    tokens, width = saved[0].shape
    block = upstream[0].shape[0]
    hidden = weights[0].shape[1]
    piece_rows = pieces[0].shape[0]
    quarter = (piece_rows - 16) // 2
    count = len(pieces)
    return pl.pallas_call(
        middle_kernel,
        in_specs=[SM] + [VM] * 12 + [ANY] * 13,
        out_specs=[VM] * 5,
        out_shape=[
            jax.ShapeDtypeStruct((block, width), bf16),
            jax.ShapeDtypeStruct((block, width), bf16),
            jax.ShapeDtypeStruct((tokens, width), f32),
            jax.ShapeDtypeStruct((tokens, width // 2), bf16),
            jax.ShapeDtypeStruct((tokens, width // 2), bf16),
        ],
        scratch_shapes=[
            pltpu.VMEM((width, width), bf16),
            pltpu.VMEM((2, width, hidden), bf16),
            pltpu.VMEM((2, hidden, width), bf16),
            pltpu.VMEM((count, piece_rows, width), bf16),
            pltpu.VMEM((tokens, width), bf16),
            pltpu.VMEM((count, tokens, quarter), bf16),
            pltpu.VMEM((tokens, width), f32),
            pltpu.VMEM((tokens, width), f32),
            pltpu.SemaphoreType.DMA((count + 5,)),
        ],
        compiler_params=params(),
        cost_estimate=cost(2 * tokens * width * (width + 12 * hidden), 2 * width * (width + 8 * hidden) + 24 * tokens * width),
        name="middle",
    )(core, *saved, seg, *upstream, *vectors, output_weight, *weights, *pieces)


def project_back_kernel(core_ref, mine, other, grad_branch, weight, out_own, out_cross, weight_v, sems):
    core = core_ref[0]
    half = mine.shape[2]
    copies = [
        pltpu.make_async_copy(
            weight.at[:, pl.ds(j * half, half)], weight_v.at[:, pl.ds(j * half, half)], sems.at[j]
        )
        for j in range(6)
    ]
    start_all(copies)
    for copy in copies:
        copy.wait()
    block = out_own.shape[0]
    for i, out in ((1, out_cross), (0, out_own)):
        rows = slice(i * block, (i + 1) * block)
        total = grad_branch[rows, :]
        for j in range(3):
            total += dot(
                mine[j, rows, :],
                weight_v[:, pl.ds(pl.multiple_of((2 * j + core) * half, half), half)], 1, 1,
            )
            total += dot(
                other[j, rows, :],
                weight_v[:, pl.ds(pl.multiple_of((2 * j + 1 - core) * half, half), half)], 1, 1,
            )
        out[...] = total.astype(bf16)


def project_back(core, mine, other, grad_branch, weight):
    tokens, width = grad_branch.shape
    out = jax.ShapeDtypeStruct((tokens // 2, width), bf16)
    return pl.pallas_call(
        project_back_kernel,
        in_specs=[SM, VM, VM, VM, ANY],
        out_specs=[VM, VM],
        out_shape=[out, out],
        scratch_shapes=[pltpu.VMEM(weight.shape, bf16), pltpu.SemaphoreType.DMA((6,))],
        compiler_params=params(),
        cost_estimate=cost(6 * tokens * width * width, 16 * tokens * width + 6 * width * width),
        name="project_back",
    )(core, mine, other, grad_branch, weight)


def shards(
    sizes,
    hidden_in,
    pair_lengths,
    prefix_keys,
    prefix_values,
    project_weight,
    project_bias,
    output_weight,
    output_bias,
    first_gain,
    first_shift,
    expand_weight,
    expand_bias,
    reduce_weight,
    reduce_bias,
    second_gain,
    second_shift,
    upstream,
):
    dp_size, mp_size = sizes
    rows_here, shard_len, width = hidden_in.shape
    hidden_here = expand_weight.shape[1]
    prefix = prefix_keys.shape[0]
    half = width // 2
    place = lax.axis_index("mp")
    chip, core = place // 2, place % 2
    core_id = core.reshape(1).astype(jnp.int32)

    def across(array):
        return swap(array, "mp", 2, mp_size)

    def beside(array):
        return swap(array, "mp", 1, mp_size)

    def take(array, index):
        return lax.dynamic_index_in_dim(array, index, 0, keepdims=False)

    def row(vector):
        return vector.reshape(1, -1)

    own = take(hidden_in, chip)
    cross = across(take(hidden_in, 1 - chip))
    own2, cross2 = beside(own), beside(cross)

    quarter = hidden_here // 4
    part = lax.axis_index("dp") % 4

    def pack(index):
        start = index * quarter
        up = lax.dynamic_slice_in_dim(expand_weight, start, quarter, 1).T
        down = lax.dynamic_slice_in_dim(reduce_weight, start, quarter, 0)
        bias = lax.dynamic_slice_in_dim(expand_bias, start, quarter, 0)
        bias = jnp.pad(bias.reshape(1, quarter), ((0, 15), (0, width - quarter)))
        return jnp.concatenate([up, down, bias], 0)

    piece0 = across(pack(part))
    piece3 = across(pack(part ^ 3))
    piece1 = swap(piece0, "dp", 1, dp_size)
    piece2 = swap(piece0, "dp", 2, dp_size)
    pieces = [piece0, piece1, piece2, piece3]
    pieces = pieces + [beside(piece) for piece in pieces]
    expand_sib, reduce_sib = beside(expand_weight), beside(reduce_weight)
    bias_own = row(expand_bias)
    bias_sib = beside(bias_own)

    up_own = take(upstream, chip)
    up_cross = across(take(upstream, 1 - chip))

    boundary = jnp.cumsum(take(pair_lengths, chip))
    offsets = jnp.stack(
        [2 * chip + core, 2 * (1 - chip) + core, 2 * chip + 1 - core, 2 * (1 - chip) + 1 - core]
    )
    position = (
        offsets[:, None] * shard_len + jnp.arange(shard_len, dtype=jnp.int32)[None, :]
    ).reshape(-1)
    segment = jnp.sum((position[:, None] >= boundary[None, :]).astype(jnp.int32), axis=1)
    tokens = segment.shape[0]
    seg_row = jnp.broadcast_to(segment[None, :], (8, tokens))
    seg_query = jnp.broadcast_to(segment[:, None], (tokens, 128))
    seg_col = jnp.where(seg_query < PAIRS, seg_query, PAIRS + 1)

    qkv = project(core_id, (own, cross, own2, cross2), project_weight, row(project_bias))
    attended_mine, attended_other, exps, recips = attend(
        core_id, qkv, prefix_keys, prefix_values, seg_row, seg_col
    )
    attended_here = beside(attended_other)
    weights = (expand_weight, expand_sib, reduce_weight, reduce_sib)
    unit, inverse, total, slope = forward(
        core_id, attended_mine, attended_here, own, cross, output_weight, row(output_bias),
        row(first_gain), row(first_shift), weights + (bias_own, bias_sib),
    )
    hidden_own, hidden_cross, grad_branch, grad_mine, grad_theirs = middle(
        core_id, (unit, inverse, total, slope), seg_query[: tokens // 2], (up_own, up_cross),
        (row(first_gain), row(first_shift), row(reduce_bias), row(second_gain), row(second_shift)),
        output_weight, weights, pieces,
    )
    grad_here = beside(grad_theirs)

    def assemble(mine, theirs):
        return jnp.where(chip == 0, jnp.stack([mine, theirs]), jnp.stack([theirs, mine]))

    hidden_out = assemble(hidden_own, across(hidden_cross))
    back_mine, back_other, grad_prefix = attend_back(
        core_id, qkv, prefix_keys, prefix_values, exps, recips,
        (attended_mine, attended_other), (grad_mine, grad_here),
    )
    for axis, size, bits in (("mp", mp_size, (2,)), ("dp", dp_size, None)):
        if bits is None:
            bits = [1 << i for i in range((size - 1).bit_length())]
        for bit in bits:
            grad_prefix = grad_prefix + swap(grad_prefix, axis, bit, size)
    grad_prefix_sib = beside(grad_prefix)
    grad_prefix = jnp.where(
        core == 0,
        jnp.concatenate([grad_prefix, grad_prefix_sib], 2),
        jnp.concatenate([grad_prefix_sib, grad_prefix], 2),
    )
    back_here = beside(back_other)
    in_own, in_cross = project_back(core_id, back_mine, back_here, grad_branch, project_weight)
    grad_in = assemble(in_own, across(in_cross))
    return (hidden_out, grad_in, grad_prefix[0], grad_prefix[1])


def solution(mesh):
    placed = (
        P("dp", "mp", None),
        P("dp", None),
        P(),
        P(),
        P(),
        P(),
        P(),
        P(),
        P(),
        P(),
        P(None, "mp"),
        P("mp"),
        P("mp", None),
        P(),
        P(),
        P(),
        P("dp", "mp", None),
    )
    return jax.shard_map(
        functools.partial(shards, (mesh.shape["dp"], mesh.shape["mp"])),
        mesh=mesh,
        in_specs=placed,
        out_specs=(P("dp", "mp", None), P("dp", "mp", None), P(), P()),
        check_vma=False,
    )
```

```python
import functools

import jax
import jax.numpy as jnp
from jax import lax
from jax.experimental import pallas as pl
from jax.experimental.pallas import tpu as pltpu
from jax.sharding import PartitionSpec as P

HEADS = 16
PAIRS = 8

epsilon = 1e-05
masked_score = -1e30
root_half = 0.7071067811865476
inverse_root = 0.3989422804014327
log2_e = 1.4426950408889634
ln_2 = 0.6931471805599453

bf16 = jnp.bfloat16
f32 = jnp.float32


def dot(left, right, left_dim=1, right_dim=0):
    return lax.dot_general(
        left, right, (((left_dim,), (right_dim,)), ((), ())), preferred_element_type=f32
    )


def params(mebibytes):
    return pltpu.CompilerParams(vmem_limit_bytes=mebibytes * 2**20)


def cost(flops, bytes_accessed, transcendentals=0):
    return pl.CostEstimate(
        flops=int(flops), bytes_accessed=int(bytes_accessed), transcendentals=int(transcendentals)
    )


ANY = pl.BlockSpec(memory_space=pl.ANY)
VM = pl.BlockSpec(memory_space=pltpu.VMEM)
SM = pl.BlockSpec(memory_space=pltpu.SMEM)
BRIEF = (1e6, 1e5)


def swap(array, axis, bit, size):
    return lax.ppermute(array, axis, [(i, i ^ bit) for i in range(size)])


class Copies:
    def __init__(self, sems):
        self.sems, self.used = sems, 0

    def __call__(self, source, target):
        copy = pltpu.make_async_copy(source, target, self.sems.at[self.used])
        self.used += 1
        return copy


def start_all(copies):
    for copy in copies:
        copy.start()


def wait_all(copies):
    for copy in copies:
        copy.wait()


def columns_at(start, size):
    return pl.ds(pl.multiple_of(start, size), size)


def project_tokens(core, copies, parts, weight, bias, out, place, tokens_v, weight_v, out_v):
    block = parts[0].shape[-2]
    half = out.shape[2]
    token_copies = [
        copies(part, tokens_v.at[pl.ds(i * block, block)]) for i, part in enumerate(parts)
    ]
    weight_copies = [
        copies(weight.at[:, columns_at((2 * j + core) * half, half)], weight_v.at[j])
        for j in range(3)
    ]
    start_all(token_copies + weight_copies)
    wait_all(token_copies)
    out_copies = []
    for j in range(3):
        weight_copies[j].wait()
        shift = bias[:, columns_at((2 * j + core) * half, half)].astype(f32)
        result = dot(tokens_v[...], weight_v[j]) + shift
        if j == 0:
            result = result * (log2_e * 0.125)
        out_v[j] = result.astype(bf16)
        copy = copies(out_v.at[j], out.at[j, pl.ds(place * 2 * block, 2 * block)])
        copy.start()
        out_copies.append(copy)
    return out_copies


def project_first_kernel(
    scalars, hidden, hidden2, weight, bias, expand, reduce, bias_rows,
    out, pack0, pack3, tokens_v, weight_v, out_v, packs, sems,
):
    core, chip, part = scalars[0], scalars[1], scalars[2]
    copies = Copies(sems)
    width, hidden_here = expand.shape
    quarter = hidden_here // 4
    pack_copies = []
    for n, index in enumerate((part, 3 - part)):
        pack = packs.at[n]
        columns = columns_at(index * quarter, quarter)
        for i in range(width // quarter):
            rows = pl.ds(i * quarter, quarter)
            pack_copies.append(copies(expand.at[rows, columns], pack.at[pl.ds(0, quarter), rows]))
        pack_copies.append(copies(reduce.at[columns], pack.at[pl.ds(quarter, quarter)]))
        pack_copies.append(
            copies(bias_rows.at[:, columns], pack.at[pl.ds(2 * quarter, 16), pl.ds(0, quarter)])
        )
    start_all(pack_copies)
    out_copies = project_tokens(
        core, copies, (hidden.at[chip], hidden2.at[chip]), weight, bias, out, 0,
        tokens_v, weight_v, out_v,
    )
    wait_all(pack_copies)
    pack_copies = [copies(packs.at[n], pack) for n, pack in enumerate((pack0, pack3))]
    start_all(pack_copies)
    wait_all(pack_copies + out_copies)


def project_second_kernel(scalars, cross, cross2, weight, bias, _, out, tokens_v, weight_v, out_v, sems):
    copies = Copies(sems)
    wait_all(
        project_tokens(
            scalars[0], copies, (cross, cross2), weight, bias, out, 1, tokens_v, weight_v, out_v
        )
    )


def project_scratch(block, width, half, count, more=()):
    return [
        pltpu.VMEM((2 * block, width), bf16),
        pltpu.VMEM((3, width, half), bf16),
        pltpu.VMEM((3, 2 * block, half), bf16),
        *more,
        pltpu.SemaphoreType.DMA((count,)),
    ]


def project_first(scalars, hidden, hidden2, weight, bias, expand, reduce, bias_rows):
    _, block, width = hidden.shape
    half = width // 2
    quarter = expand.shape[1] // 4
    pack = jax.ShapeDtypeStruct((2 * quarter + 16, width), bf16)
    return pl.pallas_call(
        project_first_kernel,
        in_specs=[SM, ANY, ANY, ANY, VM, ANY, ANY, ANY],
        out_specs=[ANY] * 3,
        out_shape=[jax.ShapeDtypeStruct((3, 4 * block, half), bf16), pack, pack],
        scratch_shapes=project_scratch(
            block, width, half, 2 * (width // quarter + 3) + 8, [pltpu.VMEM((2, *pack.shape), bf16)]
        ),
        compiler_params=params(56),
        cost_estimate=cost(2 * 2 * block * width * 3 * half, 2 * (2 * block * width + 3 * width * half + 3 * 2 * block * half)),
        name="project_first",
    )(scalars, hidden, hidden2, weight, bias, expand, reduce, bias_rows)


def project_second(scalars, cross, cross2, weight, bias, qkv):
    block, width = cross.shape
    half = width // 2
    return pl.pallas_call(
        project_second_kernel,
        in_specs=[SM, ANY, ANY, ANY, VM, ANY],
        out_specs=ANY,
        out_shape=jax.ShapeDtypeStruct(qkv.shape, bf16),
        input_output_aliases={5: 0},
        scratch_shapes=project_scratch(block, width, half, 8),
        compiler_params=params(56),
        cost_estimate=cost(2 * 2 * block * width * 3 * half, 2 * (2 * block * width + 3 * width * half + 3 * 2 * block * half)),
        name="project_second",
    )(scalars, cross, cross2, weight, bias, qkv)


def head_mask(shape, head, axis):
    return (lax.broadcasted_iota(jnp.int32, shape, axis) // 64) == head


def keep_head(array, head, axis):
    return jnp.where(head_mask(array.shape, head, axis), array, jnp.zeros_like(array))


def attend_kernel(
    core_ref, query, key, value, prefix_k, prefix_v, key_mask, query_mask,
    out_mine, out_other, exps, recips, keys, values_t,
):
    prefix = prefix_k.shape[0]
    tokens = query.shape[1]
    count = prefix + tokens
    chunk = tokens // 4
    keys[:prefix, :128] = prefix_k[...]
    keys[prefix:, :128] = key[0]

    @pl.when(pl.program_id(0) == 0)
    def _():
        keys[:, 128:] = key_mask[...]
        values_t[:, 64:, :] = jnp.ones((2, values_t.shape[1] - 64, count), bf16)

    prefix_t = prefix_v[...].astype(f32).T.astype(bf16)
    value_t = value[0].astype(f32).T.astype(bf16)
    for head in range(2):
        values_t[head, :64, :prefix] = prefix_t[64 * head : 64 * head + 64]
        values_t[head, :64, prefix:] = value_t[64 * head : 64 * head + 64]
    units = [(i, head) for i in range(4) for head in range(2)]

    def score(unit):
        i, head = unit
        rows = slice(i * chunk, (i + 1) * chunk)
        masked = jnp.concatenate([keep_head(query[0, rows, :], head, 1), query_mask[rows, :]], axis=1)
        return dot(keys[...], masked, 1, 1)

    ahead = 2
    pending = [score(unit) for unit in units[:ahead]]
    for n, (i, head) in enumerate(units):
        scores = pending.pop(0)
        if n + ahead < len(units):
            pending.append(score(units[n + ahead]))
        cols = slice(i * chunk, (i + 1) * chunk)
        top = jnp.max(scores, axis=0, keepdims=True)
        weights = jnp.exp2(scores - top).astype(bf16)
        exps[0, head, :, cols] = weights
        summed = dot(values_t[head], weights)
        recip = 1.0 / summed[64:65, :]
        recips[0, head, :, cols] = jnp.broadcast_to(recip, (8, chunk))
        out = out_other if i % 2 else out_mine
        out[64 * head : 64 * head + 64, (i // 2) * chunk : (i // 2 + 1) * chunk] = (
            summed[:64, :] * recip
        ).astype(bf16)


def attend(core, qkv, prefix_keys, prefix_values, key_mask, query_mask):
    _, tokens, half = qkv.shape
    prefix = prefix_keys.shape[0]
    count = prefix + tokens
    pairs = half // 128
    prefix_spec = pl.BlockSpec((prefix, 128), lambda p, k: (0, k[0] * pairs + p))
    out_spec = pl.BlockSpec((128, tokens // 2), lambda p, k: (p, 0))
    out = jax.ShapeDtypeStruct((half, tokens // 2), bf16)
    return pl.pallas_call(
        attend_kernel,
        grid_spec=pltpu.PrefetchScalarGridSpec(
            num_scalar_prefetch=1,
            grid=(pairs,),
            in_specs=[
                pl.BlockSpec((1, tokens, 128), lambda p, k, j=j: (j, 0, p)) for j in range(3)
            ]
            + [
                prefix_spec,
                prefix_spec,
                pl.BlockSpec((count, 128), lambda p, k: (0, 0)),
                pl.BlockSpec((tokens, 128), lambda p, k: (0, 0)),
            ],
            out_specs=[
                out_spec,
                out_spec,
                pl.BlockSpec((1, 2, count, tokens), lambda p, k: (p, 0, 0, 0)),
                pl.BlockSpec((1, 2, 8, tokens), lambda p, k: (p, 0, 0, 0)),
            ],
            scratch_shapes=[pltpu.VMEM((count, 256), bf16), pltpu.VMEM((2, 64 + 16, count), bf16)],
        ),
        out_shape=[
            out,
            out,
            jax.ShapeDtypeStruct((pairs, 2, count, tokens), bf16),
            jax.ShapeDtypeStruct((pairs, 2, 8, tokens), f32),
        ],
        compiler_params=params(52),
        cost_estimate=cost(*BRIEF),
        name="attend",
    )(core, qkv, qkv, qkv, prefix_keys, prefix_values, key_mask, query_mask)


def prefix_back_kernel(
    core_ref, query, prefix_v, exps, recips, attended_mine, attended_other, grad_mine, grad_other,
    out_scaled, out_spread, out_prefix,
):
    tokens = query.shape[1]
    chunk = tokens // 4
    pairs = exps.shape[0]

    def ordered(mine, other, rows):
        return jnp.concatenate(
            [
                mine[rows, :chunk], other[rows, :chunk], mine[rows, chunk:], other[rows, chunk:],
            ],
            axis=1,
        ).astype(f32)

    for pair in range(pairs):
        columns = slice(128 * pair, 128 * pair + 128)
        parts, spreads = [], []
        for head in range(2):
            rows = slice(128 * pair + 64 * head, 128 * pair + 64 * head + 64)
            scaled = ordered(grad_mine, grad_other, rows) * recips[pair, head, 0:1, :]
            attended = ordered(attended_mine, attended_other, rows)
            parts.append(scaled.astype(bf16))
            spreads.append(jnp.sum(scaled * attended, axis=0, keepdims=True))
        zeros = jnp.zeros_like(parts[0])
        out_scaled[pair] = jnp.concatenate(parts, axis=0)
        out_spread[pair] = jnp.concatenate(spreads + [jnp.zeros((6, tokens), f32)], axis=0)
        grad_keys = grad_values = None
        for head in range(2):
            scaled = jnp.concatenate([parts[0], zeros] if head == 0 else [zeros, parts[1]], axis=0)
            grad_probs = dot(prefix_v[:, columns], scaled)
            weights = exps[pair, head]
            slopes = (weights.astype(f32) * (grad_probs - spreads[head])).astype(bf16)
            key_part = dot(slopes, keep_head(query[0, :, columns], head, 1))
            value_part = dot(weights, scaled, 1, 1)
            grad_keys = key_part if head == 0 else grad_keys + key_part
            grad_values = value_part if head == 0 else grad_values + value_part
        out_prefix[0, :, columns] = grad_keys * ln_2
        out_prefix[1, :, columns] = grad_values


def prefix_back(core, qkv, prefix_values, exps, recips, attended, grads):
    _, tokens, half = qkv.shape
    prefix = prefix_values.shape[0]
    pairs = half // 128
    heads_spec = pl.BlockSpec((half, tokens // 2), lambda i, k: (0, 0))
    return pl.pallas_call(
        prefix_back_kernel,
        grid_spec=pltpu.PrefetchScalarGridSpec(
            num_scalar_prefetch=1,
            grid=(1,),
            in_specs=[
                pl.BlockSpec((1, tokens, half), lambda i, k: (0, 0, 0)),
                pl.BlockSpec((prefix, half), lambda i, k: (0, k[0])),
                pl.BlockSpec((pairs, 2, prefix, tokens), lambda i, k: (0, 0, 0, 0)),
                pl.BlockSpec((pairs, 2, 8, tokens), lambda i, k: (0, 0, 0, 0)),
                heads_spec,
                heads_spec,
                heads_spec,
                heads_spec,
            ],
            out_specs=[
                pl.BlockSpec((pairs, 128, tokens), lambda i, k: (0, 0, 0)),
                pl.BlockSpec((pairs, 8, tokens), lambda i, k: (0, 0, 0)),
                pl.BlockSpec((2, prefix, half), lambda i, k: (0, 0, 0)),
            ],
        ),
        out_shape=[
            jax.ShapeDtypeStruct((pairs, 128, tokens), bf16),
            jax.ShapeDtypeStruct((pairs, 8, tokens), f32),
            jax.ShapeDtypeStruct((2, prefix, half), f32),
        ],
        compiler_params=params(52),
        cost_estimate=cost(*BRIEF),
        name="prefix_back",
    )(core, qkv, prefix_values, exps, recips, *attended, *grads)


def attend_back_kernel(
    core_ref, query, key, value, prefix_k, prefix_v, exps, scaled, spread,
    out_mine, out_own2, out_cross2, keys, values, keys_t, slopes, queries_t,
):
    prefix = prefix_k.shape[0]
    tokens = query.shape[1]
    chunk = tokens // 4
    keys[:prefix, :] = prefix_k[...]
    keys[prefix:, :] = key[0]
    values[:prefix, :] = prefix_v[...]
    values[prefix:, :] = value[0]
    keys_t[...] = keys[...].astype(f32).T.astype(bf16)
    units = [(head, i) for head in range(2) for i in range(4)]

    def head_rows(array, head):
        zeros = jnp.zeros_like(array[:64])
        return jnp.concatenate([array[:64], zeros] if head == 0 else [zeros, array[64:]], axis=0)

    def grad_probs(unit):
        head, i = unit
        return dot(values[...], head_rows(scaled[0, :, i * chunk : (i + 1) * chunk], head))

    def value_part(head):
        return dot(exps[0, head, prefix:, :], head_rows(scaled[0], head), 1, 1)

    def key_part(head):
        return dot(slopes[head, prefix:, :], keep_head(query[0], head, 1))

    ahead = 4
    pending = [grad_probs(unit) for unit in units[:ahead]]
    for n, (head, i) in enumerate(units):
        grads = pending.pop(0)
        if n + ahead < len(units):
            pending.append(grad_probs(units[n + ahead]))
        cols = slice(i * chunk, (i + 1) * chunk)
        slopes[head, :, cols] = (
            exps[0, head, :, cols].astype(f32) * (grads - spread[0, head : head + 1, cols])
        ).astype(bf16)
        if n == 0:
            value_first = value_part(0)
        rows = slice(64 * head, 64 * head + 64)
        queries_t[rows, cols] = dot(keys_t[rows, :], slopes[head, :, cols]) * 0.125
        if n == 4:
            key_first = key_part(0)
    value_grads = (value_first + value_part(1)).astype(bf16)
    key_grads = ((key_first + key_part(1)) * ln_2).astype(bf16)
    for j, array in enumerate((queries_t[...].T.astype(bf16), key_grads, value_grads)):
        out_mine[j, :chunk] = array[:chunk]
        out_own2[j] = array[chunk : 2 * chunk]
        out_mine[j, chunk:] = array[2 * chunk : 3 * chunk]
        out_cross2[j] = array[3 * chunk :]


def attend_back(core, qkv, prefix_keys, prefix_values, exps, scaled, spread):
    _, tokens, half = qkv.shape
    prefix = prefix_keys.shape[0]
    count = prefix + tokens
    pairs = half // 128
    prefix_spec = pl.BlockSpec((prefix, 128), lambda p, k: (0, k[0] * pairs + p))
    rows = (tokens // 2, tokens // 4, tokens // 4)
    return pl.pallas_call(
        attend_back_kernel,
        grid_spec=pltpu.PrefetchScalarGridSpec(
            num_scalar_prefetch=1,
            grid=(pairs,),
            in_specs=[
                pl.BlockSpec((1, tokens, 128), lambda p, k, j=j: (j, 0, p)) for j in range(3)
            ]
            + [
                prefix_spec,
                prefix_spec,
                pl.BlockSpec((1, 2, count, tokens), lambda p, k: (p, 0, 0, 0)),
                pl.BlockSpec((1, 128, tokens), lambda p, k: (p, 0, 0)),
                pl.BlockSpec((1, 8, tokens), lambda p, k: (p, 0, 0)),
            ],
            out_specs=[pl.BlockSpec((3, n, 128), lambda p, k: (0, 0, p)) for n in rows],
            scratch_shapes=[
                pltpu.VMEM((count, 128), bf16),
                pltpu.VMEM((count, 128), bf16),
                pltpu.VMEM((128, count), bf16),
                pltpu.VMEM((2, count, tokens), bf16),
                pltpu.VMEM((128, tokens), f32),
            ],
        ),
        out_shape=[jax.ShapeDtypeStruct((3, n, half), bf16) for n in rows],
        compiler_params=params(46),
        cost_estimate=cost(*BRIEF),
        name="attend_back",
    )(core, qkv, qkv, qkv, prefix_keys, prefix_values, exps, scaled, spread)


def mean_rows(array):
    return jnp.mean(array, axis=-1, keepdims=True)


def unit_norm(array):
    centered = array - mean_rows(array)
    inverse = lax.rsqrt(mean_rows(centered * centered) + epsilon)
    return centered * inverse, inverse


def norm_back(scaled, unit, inverse):
    return inverse * (scaled - mean_rows(scaled) - unit * mean_rows(scaled * unit))


def gelu_both(hidden):
    gate = 0.5 * (1.0 + lax.erf(hidden * root_half))
    slope = gate + hidden * inverse_root * jnp.exp(-0.5 * hidden * hidden)
    return (hidden * gate).astype(bf16), slope.astype(bf16)


def feed_forward(steps, total):
    hidden = None
    for i, step in enumerate(steps):
        if i == 0:
            wait_all(step[3])
            hidden = step[0]()
        following = None
        if i + 1 < len(steps):
            wait_all(steps[i + 1][3])
            following = steps[i + 1][0]()
        active, slope = gelu_both(hidden)
        step[1](slope)
        part = dot(active, step[2]())
        if total is None:
            total = part
        elif hasattr(total, "at"):
            total[...] += part
        hidden = following


def forward_kernel(
    core_ref, mine, other, own, cross, vectors, output_weight,
    expand_own, expand_sib, reduce_own, reduce_sib, bias_own, bias_sib,
    unit_out, inverse_out, total_out, slope_out, low,
    out_w, expand_w, reduce_w, own_v, sems,
):
    core, chip = core_ref[0], core_ref[1]
    copies = [
        pltpu.make_async_copy(output_weight, out_w, sems.at[0]),
        pltpu.make_async_copy(expand_own, expand_w.at[0], sems.at[1]),
        pltpu.make_async_copy(reduce_own, reduce_w.at[0], sems.at[2]),
        pltpu.make_async_copy(expand_sib, expand_w.at[1], sems.at[3]),
        pltpu.make_async_copy(reduce_sib, reduce_w.at[1], sems.at[4]),
        pltpu.make_async_copy(own.at[chip], own_v, sems.at[5]),
    ]
    start_all(copies[5:] + copies[:5])
    copies[5].wait()
    copies[0].wait()
    half = mine.shape[0]
    block = own_v.shape[0]
    output_bias, gain, shift = (vectors[i : i + 1, :].astype(f32) for i in range(3))
    for i, ref in enumerate((own_v, cross)):
        rows = slice(i * block, (i + 1) * block)
        branch = dot(mine[:, rows], out_w[pl.ds(pl.multiple_of(core * half, half), half), :], 0, 0)
        branch += dot(
            other[:, rows], out_w[pl.ds(pl.multiple_of((1 - core) * half, half), half), :], 0, 0
        )
        unit, inverse = unit_norm(ref[...].astype(f32) + (branch + output_bias))
        unit_out[rows, :] = unit
        inverse_out[rows, :] = jnp.broadcast_to(inverse, (block, 128))
        low[rows, :] = (unit * gain + shift).astype(bf16)
    chunk = 512
    hidden_here = expand_own.shape[1]

    def step(i, bias, start):
        cols = slice(start, start + chunk)

        def store(slope):
            slope_out[:, i * hidden_here + start : i * hidden_here + start + chunk] = slope

        return (
            lambda: dot(low[...], expand_w[i, :, cols]) + bias[0:1, cols].astype(f32),
            store,
            lambda: reduce_w[i, cols, :],
            copies[1 + 2 * i : 3 + 2 * i] if start == 0 else [],
        )

    total_out[...] = jnp.zeros(total_out.shape, f32)
    feed_forward(
        [
            step(i, bias, start)
            for i, bias in enumerate((bias_own, bias_sib))
            for start in range(0, hidden_here, chunk)
        ],
        total_out,
    )


def forward(core, mine, other, own, cross, vectors, output_weight, weights):
    tokens = mine.shape[1]
    _, block, width = own.shape
    hidden = weights[0].shape[1]
    return pl.pallas_call(
        forward_kernel,
        in_specs=[SM, VM, VM, ANY, VM, VM] + [ANY] * 5 + [VM] * 2,
        out_specs=[VM] * 5,
        out_shape=[
            jax.ShapeDtypeStruct((tokens, width), f32),
            jax.ShapeDtypeStruct((tokens, 128), f32),
            jax.ShapeDtypeStruct((tokens, width), f32),
            jax.ShapeDtypeStruct((tokens, 2 * hidden), bf16),
            jax.ShapeDtypeStruct((tokens, width), bf16),
        ],
        scratch_shapes=[
            pltpu.VMEM((width, width), bf16),
            pltpu.VMEM((2, width, hidden), bf16),
            pltpu.VMEM((2, hidden, width), bf16),
            pltpu.VMEM((block, width), bf16),
            pltpu.SemaphoreType.DMA((6,)),
        ],
        compiler_params=params(54),
        cost_estimate=cost(*BRIEF),
        name="forward",
    )(core, mine, other, own, cross, vectors, output_weight, *weights)


def piece_copies(copies, pieces, place, expand_r, reduce_r, bias_r):
    quarter = (pieces[0].shape[0] - 16) // 2
    result = []
    for i, ref in enumerate(pieces):
        here = pl.ds((place + i) * quarter, quarter)
        group = []
        for j in range(pieces[0].shape[1] // quarter):
            rows = pl.ds(j * quarter, quarter)
            group.append(copies(ref.at[pl.ds(0, quarter), rows], expand_r.at[rows, here]))
        group.append(copies(ref.at[pl.ds(quarter, quarter)], reduce_r.at[here]))
        if bias_r is not None:
            group.append(copies(ref.at[pl.ds(2 * quarter, 16)], bias_r.at[i]))
        result.append(group)
    return result


def piece_sems(pieces, with_bias):
    quarter = (pieces[0].shape[0] - 16) // 2
    return len(pieces) * (pieces[0].shape[1] // quarter + 1 + (1 if with_bias else 0))


def piece_steps(count, place, quarter, low, expand_r, reduce_r, bias_r, slope_out, waits):
    def step(first, n):
        rows = slice((place + first) * quarter, (place + first + n) * quarter)

        def hidden():
            bias = [bias_r[first + i, 0:1, :quarter] for i in range(n)]
            bias = bias[0] if n == 1 else jnp.concatenate(bias, axis=1)
            return dot(low[...], expand_r[:, rows]) + bias.astype(f32)

        def store(slope):
            slope_out[:, first * quarter : (first + n) * quarter] = slope

        return (
            hidden,
            store,
            lambda: reduce_r[rows, :],
            [copy for i in range(n) for copy in waits[first + i]],
        )

    return [step(first, min(2, count - first)) for first in range(0, count, 2)]


def remote_kernel(count, *refs):
    low_in, total_in = refs[:2]
    pieces = refs[2 : 2 + count]
    total_out, slope_out, low, expand_r, reduce_r, bias_r, sems = refs[2 + count :]
    copies = Copies(sems)
    first = [copies(low_in, low), copies(total_in, total_out)]
    waits = piece_copies(copies, pieces, 0, expand_r, reduce_r, bias_r)
    start_all(first[:1] + waits[0] + waits[1] + first[1:])
    for group in waits[2:]:
        start_all(group)
    quarter = (pieces[0].shape[0] - 16) // 2
    steps = piece_steps(count, 0, quarter, low, expand_r, reduce_r, bias_r, slope_out, waits)
    steps[0] = steps[0][:3] + (first + steps[0][3],)
    feed_forward(steps, total_out)


def remote(low, total, pieces):
    tokens, width = total.shape
    count = len(pieces)
    quarter = (pieces[0].shape[0] - 16) // 2
    return pl.pallas_call(
        functools.partial(remote_kernel, count),
        in_specs=[ANY] * (2 + count),
        out_specs=[VM] * 2,
        out_shape=[
            jax.ShapeDtypeStruct((tokens, width), f32),
            jax.ShapeDtypeStruct((tokens, count * quarter), bf16),
        ],
        scratch_shapes=[
            pltpu.VMEM((tokens, width), bf16),
            pltpu.VMEM((width, count * quarter), bf16),
            pltpu.VMEM((count * quarter, width), bf16),
            pltpu.VMEM((count, 16, width), bf16),
            pltpu.SemaphoreType.DMA((2 + piece_sems(pieces, True),)),
        ],
        compiler_params=params(52),
        cost_estimate=cost(*BRIEF),
        name="remote",
    )(low, total, *pieces)


def middle_kernel(early, late, *refs):
    scalars, query_mask, vectors = refs[:3]
    low_in, unit_in, inverse, total_in, slope_in, slope2_in, upstream, up_cross = refs[3:11]
    output_weight, expand_own, expand_sib, reduce_own, reduce_sib = refs[11:16]
    pieces = refs[16 : 16 + early + late]
    hidden_own, hidden_cross, grad_out, att_mine, att_other = refs[16 + early + late : 21 + early + late]
    (
        out_w, expand_w, reduce_w, expand_r, reduce_r, bias_r, low, unit, acc, back_acc,
        slope_l, slope_e, slope_s, up, hidden, sems,
    ) = refs[21 + early + late :]
    core, chip = scalars[0], scalars[1]
    copies = Copies(sems)
    tokens, width = unit.shape
    block = tokens // 2
    quarter = (pieces[0].shape[0] - 16) // 2
    chunk = 2 * quarter
    hidden_here = expand_own.shape[1]
    rows_of = [pl.ds(i * block, block) for i in range(2)]

    low_copy = copies(low_in, low)
    late_waits = piece_copies(copies, pieces[early:], early, expand_r, reduce_r, bias_r)
    norm_copies = [
        [
            copies(total_in.at[rows_of[i]], acc.at[rows_of[i]]),
            copies(unit_in.at[rows_of[i]], unit.at[rows_of[i]]),
            copies((upstream.at[chip], up_cross)[i], up.at[rows_of[i]]),
        ]
        for i in range(2)
    ]
    local_copies = [
        [copies((reduce_own, reduce_sib)[i], reduce_w.at[i]), copies((expand_own, expand_sib)[i], expand_w.at[i])]
        for i in range(2)
    ]
    slope_copy = copies(slope_in, slope_l)
    early_copies = piece_copies(copies, pieces[:early], 0, expand_r, reduce_r, None)
    slope2_copy = copies(slope2_in, slope_e)
    out_copy = copies(output_weight, out_w)
    start_all([low_copy] + [copy for group in late_waits + norm_copies for copy in group])
    start_all([local_copies[0][0], slope_copy, local_copies[0][1]] + local_copies[1])
    start_all([copy for group in early_copies for copy in group] + [slope2_copy, out_copy])

    steps = piece_steps(late, early, quarter, low, expand_r, reduce_r, bias_r, slope_s, late_waits)
    steps[0] = steps[0][:3] + ([low_copy] + steps[0][3],)
    for group in norm_copies:
        wait_all(group[:1])
    feed_forward(steps, acc)

    first_gain, first_shift, reduce_bias, second_gain, second_shift = (
        vectors[i : i + 1, :].astype(f32) for i in range(1, 6)
    )
    hidden_copies = []
    for i in range(2):
        wait_all(norm_copies[i][1:])
        for start in range(i * block, (i + 1) * block, block // 2):
            rows = slice(start, start + block // 2)
            masked = slice(2 * i * block + start - i * block, 2 * i * block + start - i * block + block // 2)
            live = 1.0 - query_mask[masked, PAIRS : PAIRS + 1].astype(f32)
            first_norm = unit[rows, :] * first_gain + first_shift
            unit2, inverse2 = unit_norm(first_norm + (acc[rows, :] + reduce_bias))
            hidden[rows, :] = ((unit2 * second_gain + second_shift) * live).astype(bf16)
            grad_feed = norm_back(up[rows, :].astype(f32) * live * second_gain, unit2, inverse2)
            back_acc[rows, :] = grad_feed
            low[rows, :] = grad_feed.astype(bf16)
        copy = copies(hidden.at[rows_of[i]], (hidden_own, hidden_cross)[i])
        copy.start()
        hidden_copies.append(copy)

    backs = []
    for i in range(2):
        for start in range(0, hidden_here, chunk):
            cols = slice(start, start + chunk)
            place = slice(i * hidden_here + start, i * hidden_here + start + chunk)
            backs.append(
                (
                    lambda i=i, cols=cols: reduce_w[i, cols, :],
                    lambda i=i, cols=cols: expand_w[i, :, cols],
                    1,
                    lambda place=place: slope_l[:, place],
                    ([slope_copy] if i + start == 0 else []) + (local_copies[i] if start == 0 else []),
                )
            )
    total_pieces = early + late
    for first in range(0, total_pieces, 2):
        rows = slice(first * quarter, (first + 2) * quarter)

        def slopes(first=first):
            parts = [
                slope_e[:, j * quarter : (j + 1) * quarter]
                if j < early
                else slope_s[:, (j - early) * quarter : (j - early + 1) * quarter]
                for j in (first, first + 1)
            ]
            return jnp.concatenate(parts, axis=1)

        waits = [copy for j in (first, first + 1) if j < early for copy in early_copies[j]]
        backs.append(
            (
                lambda rows=rows: reduce_r[rows, :],
                lambda rows=rows: expand_r[:, rows],
                1,
                slopes,
                ([slope2_copy] if first == 0 else []) + waits,
            )
        )

    def grads(step):
        wait_all(step[4])
        return dot(low[...], step[0](), 1, 1)

    grad = grads(backs[0])
    for i, step in enumerate(backs):
        following = grads(backs[i + 1]) if i + 1 < len(backs) else None
        back = (grad * step[3]().astype(f32)).astype(bf16)
        back_acc[...] += dot(back, step[1](), 1, step[2])
        grad = following

    grad_copies = []
    for i in range(2):
        for start in range(i * block, (i + 1) * block, block // 2):
            rows = slice(start, start + block // 2)
            grad = norm_back(back_acc[rows, :] * first_gain, unit[rows, :], inverse[rows, 0:1])
            acc[rows, :] = grad
            low[rows, :] = grad.astype(bf16)
        copy = copies(acc.at[rows_of[i]], grad_out.at[rows_of[i]])
        copy.start()
        grad_copies.append(copy)
    out_copy.wait()
    half = width // 2
    att_other[...] = dot(
        out_w[pl.ds(pl.multiple_of((1 - core) * half, half), half), :], low[...], 1, 1
    ).astype(bf16)
    att_mine[...] = dot(
        out_w[pl.ds(pl.multiple_of(core * half, half), half), :], low[...], 1, 1
    ).astype(bf16)
    wait_all(hidden_copies + grad_copies)


def middle(scalars, query_mask, vectors, saved, upstream, output_weight, weights, early, late):
    tokens, width = saved[1].shape
    block = tokens // 2
    hidden = weights[0].shape[1]
    piece_rows = early[0].shape[0]
    quarter = (piece_rows - 16) // 2
    count = len(early) + len(late)
    return pl.pallas_call(
        functools.partial(middle_kernel, len(early), len(late)),
        in_specs=[SM, VM, VM] + [ANY] * 2 + [VM] + [ANY] * (10 + count),
        out_specs=[ANY] * 3 + [VM] * 2,
        out_shape=[
            jax.ShapeDtypeStruct((block, width), bf16),
            jax.ShapeDtypeStruct((block, width), bf16),
            jax.ShapeDtypeStruct((tokens, width), f32),
            jax.ShapeDtypeStruct((width // 2, tokens), bf16),
            jax.ShapeDtypeStruct((width // 2, tokens), bf16),
        ],
        scratch_shapes=[
            pltpu.VMEM((width, width), bf16),
            pltpu.VMEM((2, width, hidden), bf16),
            pltpu.VMEM((2, hidden, width), bf16),
            pltpu.VMEM((width, count * quarter), bf16),
            pltpu.VMEM((count * quarter, width), bf16),
            pltpu.VMEM((len(late), 16, width), bf16),
            pltpu.VMEM((tokens, width), bf16),
            pltpu.VMEM((tokens, width), f32),
            pltpu.VMEM((tokens, width), f32),
            pltpu.VMEM((tokens, width), f32),
            pltpu.VMEM((tokens, 2 * hidden), bf16),
            pltpu.VMEM((tokens, len(early) * quarter), bf16),
            pltpu.VMEM((tokens, len(late) * quarter), bf16),
            pltpu.VMEM((tokens, width), bf16),
            pltpu.VMEM((tokens, width), bf16),
            pltpu.SemaphoreType.DMA((18 + piece_sems(late, True) + piece_sems(early, False),)),
        ],
        compiler_params=params(56),
        cost_estimate=cost(*BRIEF),
        name="middle",
    )(scalars, query_mask, vectors, *saved, *upstream, output_weight, *weights, *early, *late)


def project_back_kernel(place, core_ref, mine, other, grad_branch, weight, out, left, weight_v, grad, sems):
    core = core_ref[0]
    copies = Copies(sems)
    _, rows, half = other.shape
    width = weight.shape[0]
    parts = 4
    step = width // parts

    def columns(j):
        return pl.ds(pl.multiple_of(j * half, half), half)

    here = pl.ds(place * rows, rows)
    left_copies = [
        copy
        for j in range(3)
        for copy in (
            copies(mine.at[j, here], left.at[:, columns(2 * j + core)]),
            copies(other.at[j], left.at[:, columns(2 * j + 1 - core)]),
        )
    ]
    weight_copies = [
        copies(weight.at[pl.ds(i * step, step)], weight_v.at[pl.ds(i * step, step)])
        for i in range(parts)
    ]
    grad_copy = copies(grad_branch.at[here], grad)
    start_all(left_copies + weight_copies[:1] + [grad_copy] + weight_copies[1:])
    wait_all(left_copies)
    for i in range(parts):
        cols = slice(i * step, (i + 1) * step)
        weight_copies[i].wait()
        total = dot(left[...], weight_v[cols, :], 1, 1)
        if i == 0:
            grad_copy.wait()
        out[:, cols] = (grad[:, cols] + total).astype(bf16)


def project_back(core, mine, other, grad_branch, weight, place):
    _, rows, half = other.shape
    width = weight.shape[0]
    return pl.pallas_call(
        functools.partial(project_back_kernel, place),
        in_specs=[SM] + [ANY] * 4,
        out_specs=VM,
        out_shape=jax.ShapeDtypeStruct((rows, width), bf16),
        scratch_shapes=[
            pltpu.VMEM((rows, 6 * half), bf16),
            pltpu.VMEM(weight.shape, bf16),
            pltpu.VMEM((rows, width), f32),
            pltpu.SemaphoreType.DMA((11,)),
        ],
        compiler_params=params(56),
        cost_estimate=cost(*BRIEF),
        name="project_back",
    )(core, mine, other, grad_branch, weight)


def shards(
    sizes,
    hidden_in,
    pair_lengths,
    prefix_keys,
    prefix_values,
    project_weight,
    project_bias,
    output_weight,
    output_bias,
    first_gain,
    first_shift,
    expand_weight,
    expand_bias,
    reduce_weight,
    reduce_bias,
    second_gain,
    second_shift,
    upstream,
):
    dp_size, mp_size = sizes
    rows_here, shard_len, width = hidden_in.shape
    hidden_here = expand_weight.shape[1]
    prefix = prefix_keys.shape[0]
    half = width // 2
    place = lax.axis_index("mp")
    chip, core = place // 2, place % 2
    part = lax.axis_index("dp") % 4
    scalars = jnp.stack([core, chip, part]).astype(jnp.int32)

    def across(array):
        return swap(array, "mp", 2, mp_size)

    def beside(array):
        return swap(array, "mp", 1, mp_size)

    def take(array, index):
        return lax.dynamic_index_in_dim(array, index, 0, keepdims=False)

    def row(vector):
        return vector.reshape(1, -1)

    cross = across(take(hidden_in, 1 - chip))
    hidden2 = beside(hidden_in)

    boundary = jnp.cumsum(take(pair_lengths, chip))
    blocks = jnp.stack(
        [2 * chip + core, 2 * chip + 1 - core, 2 * (1 - chip) + core, 2 * (1 - chip) + 1 - core]
    )
    position = (
        blocks[:, None] * shard_len + jnp.arange(shard_len, dtype=jnp.int32)[None, :]
    ).reshape(-1)
    segment = jnp.sum((position[:, None] >= boundary[None, :]).astype(jnp.int32), axis=1)
    column = jnp.arange(128, dtype=jnp.int32)[None, :]
    query_mask = (segment[:, None] == column).astype(bf16)
    key_mask = jnp.where(
        (segment[:, None] == column) & (column < PAIRS), 0.0, masked_score
    ).astype(bf16)
    key_mask = jnp.concatenate([jnp.zeros((prefix, 128), bf16), key_mask], 0)
    vectors = jnp.stack(
        [output_bias, first_gain, first_shift, reduce_bias, second_gain, second_shift]
        + [jnp.zeros_like(output_bias)] * 2
    )
    bias_row = row(project_bias)
    bias_own = jnp.broadcast_to(row(expand_bias), (16, hidden_here))
    up_theirs = take(upstream, 1 - chip)

    qkv, pack0, pack3 = project_first(
        scalars, hidden_in, hidden2, project_weight, bias_row, expand_weight, reduce_weight, bias_own
    )
    cross, qkv, key_mask, query_mask, vectors, up_theirs = lax.optimization_barrier(
        (cross, qkv, key_mask, query_mask, vectors, up_theirs)
    )
    cross2 = beside(cross)
    piece0 = across(pack0)
    piece3 = across(pack3)
    expand_sib, reduce_sib, bias_sib = beside(expand_weight), beside(reduce_weight), beside(bias_own)
    up_cross = across(up_theirs)
    qkv = project_second(scalars, cross, cross2, project_weight, bias_row, qkv)
    attended_mine, attended_other, exps, recips = attend(
        scalars, qkv, prefix_keys, prefix_values, key_mask, query_mask
    )
    piece0, attended_other = lax.optimization_barrier((piece0, attended_other))
    piece1 = swap(piece0, "dp", 1, dp_size)
    piece2 = swap(piece0, "dp", 2, dp_size)
    attended_here = beside(attended_other)
    weights = (expand_weight, expand_sib, reduce_weight, reduce_sib)
    unit, inverse, total, slope, low = forward(
        scalars, attended_mine, attended_here, hidden_in, cross, vectors, output_weight,
        weights + (bias_own, bias_sib),
    )
    piece1, piece2, piece3, low = lax.optimization_barrier((piece1, piece2, piece3, low))
    early = [piece0, beside(piece0), piece1, piece2, piece3]
    late = [beside(piece) for piece in (piece1, piece2, piece3)]
    total, slope2 = remote(low, total, early)
    hidden_own, hidden_cross, grad_branch, grad_mine, grad_theirs = middle(
        scalars, query_mask, vectors, (low, unit, inverse, total, slope, slope2),
        (upstream, up_cross), output_weight, weights, early, late,
    )
    grad_here = beside(grad_theirs)

    def assemble(mine, theirs):
        return jnp.where(chip == 0, jnp.stack([mine, theirs]), jnp.stack([theirs, mine]))

    scaled, spread, grad_prefix = prefix_back(
        scalars, qkv, prefix_values, exps, recips,
        (attended_mine, attended_other), (grad_mine, grad_here),
    )

    def both(array, bit):
        return lax.ppermute(
            array, ("dp", "mp"),
            [(d * mp_size + m, (d ^ bit) * mp_size + (m ^ 2)) for d in range(dp_size) for m in range(mp_size)],
        )

    spread_parts = (across(grad_prefix), swap(grad_prefix, "dp", 2, dp_size), both(grad_prefix, 2))
    back_mine, back_own2, back_cross2 = attend_back(
        scalars, qkv, prefix_keys, prefix_values, exps, scaled, spread
    )
    spread_parts, back_mine, back_own2, back_cross2, hidden_cross = lax.optimization_barrier(
        (spread_parts, back_mine, back_own2, back_cross2, hidden_cross)
    )
    grad_prefix = (grad_prefix + spread_parts[0]) + (spread_parts[1] + spread_parts[2])
    hidden_theirs = across(hidden_cross)
    cross_there = beside(back_cross2)
    own_there = beside(back_own2)
    near = swap(grad_prefix, "dp", 1, dp_size)
    in_cross = project_back(scalars, back_mine, cross_there, grad_branch, project_weight, 1)
    in_cross, near = lax.optimization_barrier((in_cross, near))
    in_cross = across(in_cross)
    grad_prefix = grad_prefix + near
    bit = 8
    while bit < dp_size:
        grad_prefix = grad_prefix + swap(grad_prefix, "dp", bit, dp_size)
        bit *= 2
    far = swap(grad_prefix, "dp", 4, dp_size)
    in_own = project_back(scalars, back_mine, own_there, grad_branch, project_weight, 0)
    far, in_own = lax.optimization_barrier((far, in_own))
    grad_prefix = grad_prefix + far
    grad_prefix_sib = beside(grad_prefix)
    grad_prefix = jnp.where(
        core == 0,
        jnp.concatenate([grad_prefix, grad_prefix_sib], 2),
        jnp.concatenate([grad_prefix_sib, grad_prefix], 2),
    )
    hidden_out = assemble(hidden_own, hidden_theirs)
    grad_in = assemble(in_own, in_cross)
    return (hidden_out, grad_in, grad_prefix[0], grad_prefix[1])


def solution(mesh):
    placed = (
        P("dp", "mp", None),
        P("dp", None),
        P(),
        P(),
        P(),
        P(),
        P(),
        P(),
        P(),
        P(),
        P(None, "mp"),
        P("mp"),
        P("mp", None),
        P(),
        P(),
        P(),
        P("dp", "mp", None),
    )
    return jax.shard_map(
        functools.partial(shards, (mesh.shape["dp"], mesh.shape["mp"])),
        mesh=mesh,
        in_specs=placed,
        out_specs=(P("dp", "mp", None), P("dp", "mp", None), P(), P()),
        check_vma=False,
    )
```

```python
import functools

import jax
import jax.numpy as jnp
from jax import lax
from jax.experimental import pallas as pl
from jax.experimental.pallas import tpu as pltpu
from jax.sharding import PartitionSpec as P

HEADS = 16
PAIRS = 8

epsilon = 1e-05
masked_score = -1e30
root_half = 0.7071067811865476
inverse_root = 0.3989422804014327
log2_e = 1.4426950408889634
ln_2 = 0.6931471805599453

bf16 = jnp.bfloat16
f32 = jnp.float32


def dot(left, right, left_dim=1, right_dim=0):
    return lax.dot_general(
        left, right, (((left_dim,), (right_dim,)), ((), ())), preferred_element_type=f32
    )


def params(mebibytes):
    return pltpu.CompilerParams(vmem_limit_bytes=mebibytes * 2**20)


def cost(flops, bytes_accessed, transcendentals=0):
    return pl.CostEstimate(
        flops=int(flops), bytes_accessed=int(bytes_accessed), transcendentals=int(transcendentals)
    )


ANY = pl.BlockSpec(memory_space=pl.ANY)
VM = pl.BlockSpec(memory_space=pltpu.VMEM)
SM = pl.BlockSpec(memory_space=pltpu.SMEM)
BRIEF = (1e6, 1e5)


def swap(array, axis, bit, size):
    return lax.ppermute(array, axis, [(i, i ^ bit) for i in range(size)])


class Copies:
    def __init__(self, sems):
        self.sems, self.used = sems, 0

    def __call__(self, source, target):
        copy = pltpu.make_async_copy(source, target, self.sems.at[self.used])
        self.used += 1
        return copy


def start_all(copies):
    for copy in copies:
        copy.start()


def wait_all(copies):
    for copy in copies:
        copy.wait()


def columns_at(start, size):
    return pl.ds(pl.multiple_of(start, size), size)


def project_tokens(core, copies, parts, weight, bias, out, place, tokens_v, weight_v, out_v):
    block = parts[0].shape[-2]
    half = out.shape[2]
    token_copies = [
        copies(part, tokens_v.at[pl.ds(i * block, block)]) for i, part in enumerate(parts)
    ]
    weight_copies = [
        copies(weight.at[:, columns_at((2 * j + core) * half, half)], weight_v.at[j])
        for j in range(3)
    ]
    start_all(token_copies + weight_copies)
    wait_all(token_copies)
    out_copies = []
    for j in range(3):
        weight_copies[j].wait()
        shift = jnp.where(
            core == 0,
            bias[2 * j * half : (2 * j + 1) * half].astype(f32),
            bias[(2 * j + 1) * half : (2 * j + 2) * half].astype(f32),
        )
        result = dot(tokens_v[...], weight_v[j]) + shift.reshape(1, half)
        if j == 0:
            result = result * (log2_e * 0.125)
        out_v[j] = result.astype(bf16)
        copy = copies(out_v.at[j], out.at[j, pl.ds(place * 2 * block, 2 * block)])
        copy.start()
        out_copies.append(copy)
    return out_copies


def project_first_kernel(
    scalars, hidden, hidden2, weight, bias, expand, reduce, hidden_bias, upstream,
    out, pack0, pack3, tokens_v, weight_v, out_v, packs, bias_v, sems,
):
    core, chip, part = scalars[0], scalars[1], scalars[2]
    copies = Copies(sems)
    width, hidden_here = expand.shape
    quarter = hidden_here // 4
    bias_v[...] = jnp.broadcast_to(
        hidden_bias[...].astype(f32).reshape(1, hidden_here), (16, hidden_here)
    ).astype(bf16)
    pack_copies = []
    for n, index in enumerate((part, 3 - part)):
        pack = packs.at[n]
        columns = columns_at(index * quarter, quarter)
        for i in range(width // quarter):
            rows = pl.ds(i * quarter, quarter)
            pack_copies.append(copies(expand.at[rows, columns], pack.at[pl.ds(0, quarter), rows]))
        pack_copies.append(
            copies(bias_v.at[:, columns], pack.at[pl.ds(quarter, 16), pl.ds(0, quarter)])
        )
        pack_copies.append(copies(reduce.at[columns], pack.at[pl.ds(quarter + 16, quarter)]))
    pack_copies.append(
        copies(upstream.at[1 - chip], packs.at[1, pl.ds(2 * quarter + 16, upstream.shape[1])])
    )
    start_all(pack_copies)
    out_copies = project_tokens(
        core, copies, (hidden.at[chip], hidden2.at[chip]), weight, bias, out, 0,
        tokens_v, weight_v, out_v,
    )
    wait_all(pack_copies)
    pack_copies = [
        copies(packs.at[0, pl.ds(0, 2 * quarter + 16)], pack0),
        copies(packs.at[1], pack3),
    ]
    start_all(pack_copies)
    wait_all(pack_copies + out_copies)


def project_second_kernel(scalars, cross, cross2, weight, bias, _, out, tokens_v, weight_v, out_v, sems):
    copies = Copies(sems)
    wait_all(
        project_tokens(
            scalars[0], copies, (cross, cross2), weight, bias, out, 1, tokens_v, weight_v, out_v
        )
    )


def project_scratch(block, width, half, count, more=()):
    return [
        pltpu.VMEM((2 * block, width), bf16),
        pltpu.VMEM((3, width, half), bf16),
        pltpu.VMEM((3, 2 * block, half), bf16),
        *more,
        pltpu.SemaphoreType.DMA((count,)),
    ]


def project_first(scalars, hidden, hidden2, weight, bias, expand, reduce, hidden_bias, upstream):
    _, block, width = hidden.shape
    half = width // 2
    quarter = expand.shape[1] // 4
    packs = [
        jax.ShapeDtypeStruct((rows, width), bf16)
        for rows in (2 * quarter + 16, 2 * quarter + 16 + block)
    ]
    return pl.pallas_call(
        project_first_kernel,
        in_specs=[SM, ANY, ANY, ANY, VM, ANY, ANY, VM, ANY],
        out_specs=[ANY] * 3,
        out_shape=[jax.ShapeDtypeStruct((3, 4 * block, half), bf16), *packs],
        scratch_shapes=project_scratch(
            block, width, half, 2 * (width // quarter + 2) + 12,
            [pltpu.VMEM((2, *packs[1].shape), bf16), pltpu.VMEM((16, expand.shape[1]), bf16)],
        ),
        compiler_params=params(56),
        cost_estimate=cost(*BRIEF),
        name="project_first",
    )(scalars, hidden, hidden2, weight, bias, expand, reduce, hidden_bias, upstream)


def project_second(scalars, cross, cross2, weight, bias, qkv):
    block, width = cross.shape
    half = width // 2
    return pl.pallas_call(
        project_second_kernel,
        in_specs=[SM, ANY, ANY, ANY, VM, ANY],
        out_specs=ANY,
        out_shape=jax.ShapeDtypeStruct(qkv.shape, bf16),
        input_output_aliases={5: 0},
        scratch_shapes=project_scratch(block, width, half, 8),
        compiler_params=params(56),
        cost_estimate=cost(2 * 2 * block * width * 3 * half, 2 * (2 * block * width + 3 * width * half + 3 * 2 * block * half)),
        name="project_second",
    )(scalars, cross, cross2, weight, bias, qkv)


def head_mask(shape, head, axis):
    return (lax.broadcasted_iota(jnp.int32, shape, axis) // 64) == head


def keep_head(array, head, axis):
    return jnp.where(head_mask(array.shape, head, axis), array, jnp.zeros_like(array))


def attend_kernel(
    core_ref, query, key, value, prefix_k, prefix_v, key_mask, query_mask,
    out_mine, out_other, exps_mine, exps_other, recips_mine, recips_other, keys, values_t,
):
    prefix = prefix_k.shape[0]
    tokens = query.shape[1]
    count = prefix + tokens
    chunk = tokens // 4
    keys[:prefix, :128] = prefix_k[...]
    keys[prefix:, :128] = key[0]

    @pl.when(pl.program_id(0) == 0)
    def _():
        keys[:, 128:] = key_mask[...]
        values_t[:, 64:, :] = jnp.ones((2, values_t.shape[1] - 64, count), bf16)

    prefix_t = prefix_v[...].astype(f32).T.astype(bf16)
    value_t = value[0].astype(f32).T.astype(bf16)
    for head in range(2):
        values_t[head, :64, :prefix] = prefix_t[64 * head : 64 * head + 64]
        values_t[head, :64, prefix:] = value_t[64 * head : 64 * head + 64]
    units = [(i, head) for i in (1, 3, 0, 2) for head in range(2)]

    def score(unit):
        i, head = unit
        rows = slice(i * chunk, (i + 1) * chunk)
        masked = jnp.concatenate([keep_head(query[0, rows, :], head, 1), query_mask[rows, :]], axis=1)
        return dot(keys[...], masked, 1, 1)

    ahead = 2
    pending = [score(unit) for unit in units[:ahead]]
    for n, (i, head) in enumerate(units):
        scores = pending.pop(0)
        if n + ahead < len(units):
            pending.append(score(units[n + ahead]))
        out, exps, recips = (
            (out_mine, exps_mine, recips_mine), (out_other, exps_other, recips_other)
        )[i % 2]
        cols = slice(i // 2 * chunk, (i // 2 + 1) * chunk)
        top = jnp.max(scores, axis=0, keepdims=True)
        weights = jnp.exp2(scores - top).astype(bf16)
        exps[0, head, :, cols] = weights
        summed = dot(values_t[head], weights)
        recip = 1.0 / summed[64:65, :]
        recips[0, head, :, cols] = jnp.broadcast_to(recip, (8, chunk))
        out[64 * head : 64 * head + 64, cols] = (summed[:64, :] * recip).astype(bf16)


def attend(core, qkv, prefix_keys, prefix_values, key_mask, query_mask):
    _, tokens, half = qkv.shape
    prefix = prefix_keys.shape[0]
    count = prefix + tokens
    pairs = half // 128
    prefix_spec = pl.BlockSpec((prefix, 128), lambda p, k: (0, k[0] * pairs + p))
    out_spec = pl.BlockSpec((128, tokens // 2), lambda p, k: (p, 0))
    exps_spec = pl.BlockSpec((1, 2, count, tokens // 2), lambda p, k: (p, 0, 0, 0))
    recips_spec = pl.BlockSpec((1, 2, 8, tokens // 2), lambda p, k: (p, 0, 0, 0))
    return pl.pallas_call(
        attend_kernel,
        grid_spec=pltpu.PrefetchScalarGridSpec(
            num_scalar_prefetch=1,
            grid=(pairs,),
            in_specs=[
                pl.BlockSpec((1, tokens, 128), lambda p, k, j=j: (j, 0, p)) for j in range(3)
            ]
            + [
                prefix_spec,
                prefix_spec,
                pl.BlockSpec((count, 128), lambda p, k: (0, 0)),
                pl.BlockSpec((tokens, 128), lambda p, k: (0, 0)),
            ],
            out_specs=[out_spec] * 2 + [exps_spec] * 2 + [recips_spec] * 2,
            scratch_shapes=[pltpu.VMEM((count, 256), bf16), pltpu.VMEM((2, 64 + 16, count), bf16)],
        ),
        out_shape=[jax.ShapeDtypeStruct((half, tokens // 2), bf16)] * 2
        + [jax.ShapeDtypeStruct((pairs, 2, count, tokens // 2), bf16)] * 2
        + [jax.ShapeDtypeStruct((pairs, 2, 8, tokens // 2), f32)] * 2,
        compiler_params=params(56),
        cost_estimate=cost(*BRIEF),
        name="attend",
    )(core, qkv, qkv, qkv, prefix_keys, prefix_values, key_mask, query_mask)


def ordered_rows(array):
    block = array.shape[0] // 4
    return [array[i * block : (i + 1) * block] for i in (0, 2, 1, 3)]


def prefix_back_kernel(
    core_ref, query, prefix_v, exps_mine, exps_other, recips_mine, recips_other,
    attended_mine, attended_other, grad_mine, grad_other, out_scaled, out_spread, out_prefix,
):
    pairs = exps_mine.shape[0]
    half_tokens = exps_mine.shape[3]
    sides = (
        (exps_mine, recips_mine, attended_mine, grad_mine),
        (exps_other, recips_other, attended_other, grad_other),
    )
    for pair in range(pairs):
        columns = slice(128 * pair, 128 * pair + 128)
        queries = ordered_rows(query[0, :, columns])
        units = []
        for side, (exps, recips, attended, grad) in enumerate(sides):
            tokens = slice(side * half_tokens, (side + 1) * half_tokens)
            query_side = jnp.concatenate(queries[2 * side : 2 * side + 2], axis=0)
            parts, spreads = [], []
            for head in range(2):
                rows = slice(128 * pair + 64 * head, 128 * pair + 64 * head + 64)
                scaled = grad[rows, :].astype(f32) * recips[pair, head, 0:1, :]
                parts.append(scaled.astype(bf16))
                spreads.append(
                    jnp.sum(scaled * attended[rows, :].astype(f32), axis=0, keepdims=True)
                )
            zeros = jnp.zeros_like(parts[0])
            out_scaled[pair, :, tokens] = jnp.concatenate(parts, axis=0)
            out_spread[pair, :, tokens] = jnp.concatenate(
                spreads + [jnp.zeros((6, half_tokens), f32)], axis=0
            )
            for head in range(2):
                scaled = jnp.concatenate(
                    [parts[0], zeros] if head == 0 else [zeros, parts[1]], axis=0
                )
                grad_probs = dot(prefix_v[:, columns], scaled)
                units.append((exps[pair, head], head, scaled, spreads[head], query_side, grad_probs))
        slopes = [
            (weights.astype(f32) * (grad_probs - spread)).astype(bf16)
            for weights, _, _, spread, _, grad_probs in units
        ]
        grad_keys = grad_values = None
        for (weights, head, scaled, _, query_side, _), slope in zip(units, slopes):
            key_part = dot(slope, keep_head(query_side, head, 1))
            value_part = dot(weights, scaled, 1, 1)
            grad_keys = key_part if grad_keys is None else grad_keys + key_part
            grad_values = value_part if grad_values is None else grad_values + value_part
        out_prefix[0, :, columns] = grad_keys * ln_2
        out_prefix[1, :, columns] = grad_values


def prefix_back(core, qkv, prefix_values, exps, recips, attended, grads):
    _, tokens, half = qkv.shape
    prefix = prefix_values.shape[0]
    pairs = half // 128
    heads_spec = pl.BlockSpec((half, tokens // 2), lambda i, k: (0, 0))
    exps_spec = pl.BlockSpec((pairs, 2, prefix, tokens // 2), lambda i, k: (0, 0, 0, 0))
    recips_spec = pl.BlockSpec((pairs, 2, 8, tokens // 2), lambda i, k: (0, 0, 0, 0))
    return pl.pallas_call(
        prefix_back_kernel,
        grid_spec=pltpu.PrefetchScalarGridSpec(
            num_scalar_prefetch=1,
            grid=(1,),
            in_specs=[
                pl.BlockSpec((1, tokens, half), lambda i, k: (0, 0, 0)),
                pl.BlockSpec((prefix, half), lambda i, k: (0, k[0])),
            ]
            + [exps_spec] * 2
            + [recips_spec] * 2
            + [heads_spec] * 4,
            out_specs=[
                pl.BlockSpec((pairs, 128, tokens), lambda i, k: (0, 0, 0)),
                pl.BlockSpec((pairs, 8, tokens), lambda i, k: (0, 0, 0)),
                pl.BlockSpec((2, prefix, half), lambda i, k: (0, 0, 0)),
            ],
        ),
        out_shape=[
            jax.ShapeDtypeStruct((pairs, 128, tokens), bf16),
            jax.ShapeDtypeStruct((pairs, 8, tokens), f32),
            jax.ShapeDtypeStruct((2, prefix, half), f32),
        ],
        compiler_params=params(56),
        cost_estimate=cost(*BRIEF),
        name="prefix_back",
    )(core, qkv, prefix_values, *exps, *recips, *attended, *grads)


def attend_back_kernel(
    core_ref, query, key, value, prefix_k, prefix_v, exps_mine, exps_other, scaled, spread,
    out_mine, out_own2, out_cross2, keys, values, keys_t, slopes, queries, queries_t,
):
    prefix = prefix_k.shape[0]
    tokens = query.shape[1]
    chunk = tokens // 4
    keys[:prefix, :] = prefix_k[...]
    keys[prefix:, :] = key[0]
    values[:prefix, :] = prefix_v[...]
    values[prefix:, :] = value[0]
    keys_t[...] = keys[...].astype(f32).T.astype(bf16)
    queries[...] = jnp.concatenate(ordered_rows(query[0]), axis=0)
    units = [(head, i) for head in range(2) for i in range(4)]

    def head_rows(array, head):
        zeros = jnp.zeros_like(array[:64])
        return jnp.concatenate([array[:64], zeros] if head == 0 else [zeros, array[64:]], axis=0)

    def grad_probs(unit):
        head, i = unit
        return dot(values[...], head_rows(scaled[0, :, i * chunk : (i + 1) * chunk], head))

    def exps_of(head, i):
        return (exps_mine, exps_other)[i // 2][0, head, :, i % 2 * chunk : (i % 2 + 1) * chunk]

    def value_part(head):
        total = None
        for side, exps in enumerate((exps_mine, exps_other)):
            cols = slice(2 * side * chunk, 2 * (side + 1) * chunk)
            part = dot(exps[0, head, prefix:, :], head_rows(scaled[0, :, cols], head), 1, 1)
            total = part if total is None else total + part
        return total

    def key_part(head):
        return dot(slopes[head, prefix:, :], keep_head(queries[...], head, 1))

    ahead = 4
    pending = [grad_probs(unit) for unit in units[:ahead]]
    for n, (head, i) in enumerate(units):
        grads = pending.pop(0)
        if n + ahead < len(units):
            pending.append(grad_probs(units[n + ahead]))
        cols = slice(i * chunk, (i + 1) * chunk)
        slopes[head, :, cols] = (
            exps_of(head, i).astype(f32) * (grads - spread[0, head : head + 1, cols])
        ).astype(bf16)
        if n == 0:
            value_first = value_part(0)
        rows = slice(64 * head, 64 * head + 64)
        queries_t[rows, cols] = dot(keys_t[rows, :], slopes[head, :, cols]) * 0.125
        if n == 4:
            key_first = key_part(0)
    value_grads = (value_first + value_part(1)).astype(bf16)
    key_grads = ((key_first + key_part(1)) * ln_2).astype(bf16)
    query_grads = queries_t[...].T.astype(bf16)
    for j, parts in enumerate(
        ([query_grads[i * chunk : (i + 1) * chunk] for i in range(4)],)
        + tuple(ordered_rows(array) for array in (key_grads, value_grads))
    ):
        out_mine[j, :chunk] = parts[0]
        out_mine[j, chunk:] = parts[1]
        out_own2[j] = parts[2]
        out_cross2[j] = parts[3]


def attend_back(core, qkv, prefix_keys, prefix_values, exps, scaled, spread):
    _, tokens, half = qkv.shape
    prefix = prefix_keys.shape[0]
    count = prefix + tokens
    pairs = half // 128
    prefix_spec = pl.BlockSpec((prefix, 128), lambda p, k: (0, k[0] * pairs + p))
    exps_spec = pl.BlockSpec((1, 2, count, tokens // 2), lambda p, k: (p, 0, 0, 0))
    rows = (tokens // 2, tokens // 4, tokens // 4)
    return pl.pallas_call(
        attend_back_kernel,
        grid_spec=pltpu.PrefetchScalarGridSpec(
            num_scalar_prefetch=1,
            grid=(pairs,),
            in_specs=[
                pl.BlockSpec((1, tokens, 128), lambda p, k, j=j: (j, 0, p)) for j in range(3)
            ]
            + [
                prefix_spec,
                prefix_spec,
                exps_spec,
                exps_spec,
                pl.BlockSpec((1, 128, tokens), lambda p, k: (p, 0, 0)),
                pl.BlockSpec((1, 8, tokens), lambda p, k: (p, 0, 0)),
            ],
            out_specs=[pl.BlockSpec((3, n, 128), lambda p, k: (0, 0, p)) for n in rows],
            scratch_shapes=[
                pltpu.VMEM((count, 128), bf16),
                pltpu.VMEM((count, 128), bf16),
                pltpu.VMEM((128, count), bf16),
                pltpu.VMEM((2, count, tokens), bf16),
                pltpu.VMEM((tokens, 128), bf16),
                pltpu.VMEM((128, tokens), f32),
            ],
        ),
        out_shape=[jax.ShapeDtypeStruct((3, n, half), bf16) for n in rows],
        compiler_params=params(54),
        cost_estimate=cost(*BRIEF),
        name="attend_back",
    )(core, qkv, qkv, qkv, prefix_keys, prefix_values, *exps, scaled, spread)


def mean_rows(array):
    return jnp.mean(array, axis=-1, keepdims=True)


def unit_norm(array):
    centered = array - mean_rows(array)
    inverse = lax.rsqrt(mean_rows(centered * centered) + epsilon)
    return centered * inverse, inverse


def norm_back(scaled, unit, inverse):
    return inverse * (scaled - mean_rows(scaled) - unit * mean_rows(scaled * unit))


def gelu_both(hidden):
    gate = 0.5 * (1.0 + lax.erf(hidden * root_half))
    slope = gate + hidden * inverse_root * jnp.exp(-0.5 * hidden * hidden)
    return (hidden * gate).astype(bf16), slope.astype(bf16)


def feed_forward(steps, total):
    hidden = None
    for i, step in enumerate(steps):
        if i == 0:
            wait_all(step[3])
            hidden = step[0]()
        following = None
        if i + 1 < len(steps):
            wait_all(steps[i + 1][3])
            following = steps[i + 1][0]()
        active, slope = gelu_both(hidden)
        step[1](slope)
        part = dot(active, step[2]())
        if total is None:
            total = part
        elif hasattr(total, "at"):
            total[...] += part
        hidden = following


def forward_kernel(
    core_ref, mine, other, own, cross, output_bias, first_gain, first_shift, output_weight,
    expand_own, expand_sib, reduce_own, reduce_sib, bias_own, bias_sib,
    unit_out, inverse_out, total_out, slope_out, low,
    out_w, expand_w, reduce_w, own_v, sems,
):
    core, chip = core_ref[0], core_ref[1]
    copies = [
        pltpu.make_async_copy(output_weight, out_w, sems.at[0]),
        pltpu.make_async_copy(expand_own, expand_w.at[0], sems.at[1]),
        pltpu.make_async_copy(reduce_own, reduce_w.at[0], sems.at[2]),
        pltpu.make_async_copy(expand_sib, expand_w.at[1], sems.at[3]),
        pltpu.make_async_copy(reduce_sib, reduce_w.at[1], sems.at[4]),
        pltpu.make_async_copy(own.at[chip], own_v, sems.at[5]),
    ]
    start_all(copies[5:] + copies[:5])
    copies[5].wait()
    copies[0].wait()
    half = mine.shape[0]
    block = own_v.shape[0]
    output_row, gain, shift = (
        ref[...].astype(f32).reshape(1, -1) for ref in (output_bias, first_gain, first_shift)
    )
    for i, ref in enumerate((own_v, cross)):
        rows = slice(i * block, (i + 1) * block)
        branch = dot(mine[:, rows], out_w[pl.ds(pl.multiple_of(core * half, half), half), :], 0, 0)
        branch += dot(
            other[:, rows], out_w[pl.ds(pl.multiple_of((1 - core) * half, half), half), :], 0, 0
        )
        unit, inverse = unit_norm(ref[...].astype(f32) + (branch + output_row))
        unit_out[rows, :] = unit
        inverse_out[rows, :] = jnp.broadcast_to(inverse, (block, 128))
        low[rows, :] = (unit * gain + shift).astype(bf16)
    chunk = 512
    hidden_here = expand_own.shape[1]

    def step(i, bias, start):
        cols = slice(start, start + chunk)

        def store(slope):
            slope_out[:, i * hidden_here + start : i * hidden_here + start + chunk] = slope

        return (
            lambda: dot(low[...], expand_w[i, :, cols]) + bias[cols].astype(f32).reshape(1, chunk),
            store,
            lambda: reduce_w[i, cols, :],
            copies[1 + 2 * i : 3 + 2 * i] if start == 0 else [],
        )

    total_out[...] = jnp.zeros(total_out.shape, f32)
    feed_forward(
        [
            step(i, bias, start)
            for i, bias in enumerate((bias_own, bias_sib))
            for start in range(0, hidden_here, chunk)
        ],
        total_out,
    )


def forward(core, mine, other, own, cross, vectors, output_weight, weights):
    tokens = mine.shape[1]
    _, block, width = own.shape
    hidden = weights[0].shape[1]
    return pl.pallas_call(
        forward_kernel,
        in_specs=[SM, VM, VM, ANY] + [VM] * 4 + [ANY] * 5 + [VM] * 2,
        out_specs=[VM] * 5,
        out_shape=[
            jax.ShapeDtypeStruct((tokens, width), f32),
            jax.ShapeDtypeStruct((tokens, 128), f32),
            jax.ShapeDtypeStruct((tokens, width), f32),
            jax.ShapeDtypeStruct((tokens, 2 * hidden), bf16),
            jax.ShapeDtypeStruct((tokens, width), bf16),
        ],
        scratch_shapes=[
            pltpu.VMEM((width, width), bf16),
            pltpu.VMEM((2, width, hidden), bf16),
            pltpu.VMEM((2, hidden, width), bf16),
            pltpu.VMEM((block, width), bf16),
            pltpu.SemaphoreType.DMA((6,)),
        ],
        compiler_params=params(36),
        cost_estimate=cost(*BRIEF),
        name="forward",
    )(core, mine, other, own, cross, *vectors, output_weight, *weights)


def piece_copies(copies, pieces, place, quarter, expand_r, reduce_r, bias_r):
    width = expand_r.shape[0]
    result = []
    for i, piece in enumerate(pieces):
        here = pl.ds((place + i) * quarter, quarter)
        group = []
        for j in range(width // quarter):
            rows = pl.ds(j * quarter, quarter)
            group.append(copies(piece.at[pl.ds(0, quarter), rows], expand_r.at[rows, here]))
        group.append(copies(piece.at[pl.ds(quarter + 16, quarter)], reduce_r.at[here]))
        if bias_r is not None:
            group.append(copies(piece.at[pl.ds(quarter, 16)], bias_r.at[i]))
        result.append(group)
    return result


def piece_steps(count, place, quarter, low, expand_r, reduce_r, bias_r, slope_out, waits):
    def step(first, n):
        rows = slice((place + first) * quarter, (place + first + n) * quarter)

        def hidden():
            bias = [bias_r[first + i, 0:1, :quarter] for i in range(n)]
            bias = bias[0] if n == 1 else jnp.concatenate(bias, axis=1)
            return dot(low[...], expand_r[:, rows]) + bias.astype(f32)

        def store(slope):
            slope_out[:, first * quarter : (first + n) * quarter] = slope

        return (
            hidden,
            store,
            lambda: reduce_r[rows, :],
            [copy for i in range(n) for copy in waits[first + i]],
        )

    return [step(first, min(2, count - first)) for first in range(0, count, 2)]


def remote_kernel(count, *refs):
    low_in, total_in = refs[:2]
    pieces = refs[2 : 2 + count]
    total_out, slope_out, low, expand_r, reduce_r, bias_r, sems = refs[2 + count :]
    quarter = reduce_r.shape[0] // count
    copies = Copies(sems)
    first = [copies(low_in, low), copies(total_in, total_out)]
    waits = piece_copies(copies, pieces, 0, quarter, expand_r, reduce_r, bias_r)
    start_all(first[:1] + waits[0] + waits[1] + first[1:])
    for group in waits[2:]:
        start_all(group)
    steps = piece_steps(count, 0, quarter, low, expand_r, reduce_r, bias_r, slope_out, waits)
    steps[0] = steps[0][:3] + (first + steps[0][3],)
    feed_forward(steps, total_out)


def remote(low, total, pieces, quarter):
    tokens, width = total.shape
    count = len(pieces)
    return pl.pallas_call(
        functools.partial(remote_kernel, count),
        in_specs=[ANY] * (2 + count),
        out_specs=[VM] * 2,
        out_shape=[
            jax.ShapeDtypeStruct((tokens, width), f32),
            jax.ShapeDtypeStruct((tokens, count * quarter), bf16),
        ],
        scratch_shapes=[
            pltpu.VMEM((tokens, width), bf16),
            pltpu.VMEM((width, count * quarter), bf16),
            pltpu.VMEM((count * quarter, width), bf16),
            pltpu.VMEM((count, 16, width), bf16),
            pltpu.SemaphoreType.DMA((2 + count * (width // quarter + 2),)),
        ],
        compiler_params=params(26),
        cost_estimate=cost(*BRIEF),
        name="remote",
    )(low, total, *pieces)


def middle_kernel(early, late, *refs):
    count = early + late
    scalars, query_mask = refs[:2]
    vectors = refs[2:7]
    low_in, unit_in, inverse, total_in, slope_in, slope2_in, upstream = refs[7:14]
    output_weight, expand_own, expand_sib, reduce_own, reduce_sib = refs[14:19]
    pieces = refs[19 : 19 + count]
    hidden_own, hidden_cross, grad_out, att_mine, att_other = refs[19 + count : 24 + count]
    (
        out_w, expand_w, reduce_w, expand_r, reduce_r, bias_r, low, unit, acc, back_acc,
        slope_l, slope_e, slope_s, up, hidden, sems,
    ) = refs[24 + count :]
    core, chip = scalars[0], scalars[1]
    copies = Copies(sems)
    tokens, width = unit.shape
    block = tokens // 2
    quarter = reduce_r.shape[0] // count
    chunk = 2 * quarter
    hidden_here = expand_own.shape[1]
    rows_of = [pl.ds(i * block, block) for i in range(2)]

    up_cross = pieces[early + 2].at[pl.ds(2 * quarter + 16, block)]
    low_copy = copies(low_in, low)
    late_waits = piece_copies(copies, pieces[early:], early, quarter, expand_r, reduce_r, bias_r)
    norm_copies = [
        [
            copies(total_in.at[rows_of[i]], acc.at[rows_of[i]]),
            copies(unit_in.at[rows_of[i]], unit.at[rows_of[i]]),
            copies((upstream.at[chip], up_cross)[i], up.at[rows_of[i]]),
        ]
        for i in range(2)
    ]
    local_copies = [
        [copies((reduce_own, reduce_sib)[i], reduce_w.at[i]), copies((expand_own, expand_sib)[i], expand_w.at[i])]
        for i in range(2)
    ]
    slope_copy = copies(slope_in, slope_l)
    early_copies = piece_copies(copies, pieces[:early], 0, quarter, expand_r, reduce_r, None)
    slope2_copy = copies(slope2_in, slope_e)
    out_copy = copies(output_weight, out_w)
    start_all([low_copy] + [copy for group in late_waits + norm_copies for copy in group])
    start_all([local_copies[0][0], slope_copy, local_copies[0][1]] + local_copies[1])
    start_all([copy for group in early_copies for copy in group] + [slope2_copy, out_copy])

    steps = piece_steps(late, early, quarter, low, expand_r, reduce_r, bias_r, slope_s, late_waits)
    steps[0] = steps[0][:3] + ([low_copy] + steps[0][3],)
    for group in norm_copies:
        wait_all(group[:1])
    feed_forward(steps, acc)

    first_gain, first_shift, reduce_bias, second_gain, second_shift = (
        ref[...].astype(f32).reshape(1, -1) for ref in vectors
    )
    hidden_copies = []
    for i in range(2):
        wait_all(norm_copies[i][1:])
        for start in range(i * block, (i + 1) * block, block // 2):
            rows = slice(start, start + block // 2)
            masked = slice(2 * i * block + start - i * block, 2 * i * block + start - i * block + block // 2)
            live = 1.0 - query_mask[masked, PAIRS : PAIRS + 1].astype(f32)
            first_norm = unit[rows, :] * first_gain + first_shift
            unit2, inverse2 = unit_norm(first_norm + (acc[rows, :] + reduce_bias))
            hidden[rows, :] = ((unit2 * second_gain + second_shift) * live).astype(bf16)
            grad_feed = norm_back(up[rows, :].astype(f32) * live * second_gain, unit2, inverse2)
            back_acc[rows, :] = grad_feed
            low[rows, :] = grad_feed.astype(bf16)
        copy = copies(hidden.at[rows_of[i]], (hidden_own.at[chip], hidden_cross)[i])
        copy.start()
        hidden_copies.append(copy)

    backs = []
    for i in range(2):
        for start in range(0, hidden_here, chunk):
            cols = slice(start, start + chunk)
            place = slice(i * hidden_here + start, i * hidden_here + start + chunk)
            backs.append(
                (
                    lambda i=i, cols=cols: reduce_w[i, cols, :],
                    lambda i=i, cols=cols: expand_w[i, :, cols],
                    1,
                    lambda place=place: slope_l[:, place],
                    ([slope_copy] if i + start == 0 else []) + (local_copies[i] if start == 0 else []),
                )
            )
    total_pieces = early + late
    for first in range(0, total_pieces, 2):
        rows = slice(first * quarter, (first + 2) * quarter)

        def slopes(first=first):
            parts = [
                slope_e[:, j * quarter : (j + 1) * quarter]
                if j < early
                else slope_s[:, (j - early) * quarter : (j - early + 1) * quarter]
                for j in (first, first + 1)
            ]
            return jnp.concatenate(parts, axis=1)

        waits = [copy for j in (first, first + 1) if j < early for copy in early_copies[j]]
        backs.append(
            (
                lambda rows=rows: reduce_r[rows, :],
                lambda rows=rows: expand_r[:, rows],
                1,
                slopes,
                ([slope2_copy] if first == 0 else []) + waits,
            )
        )

    def grads(step):
        wait_all(step[4])
        return dot(low[...], step[0](), 1, 1)

    grad = grads(backs[0])
    for i, step in enumerate(backs):
        following = grads(backs[i + 1]) if i + 1 < len(backs) else None
        back = (grad * step[3]().astype(f32)).astype(bf16)
        back_acc[...] += dot(back, step[1](), 1, step[2])
        grad = following

    grad_copies = []
    for i in range(2):
        for start in range(i * block, (i + 1) * block, block // 2):
            rows = slice(start, start + block // 2)
            grad = norm_back(back_acc[rows, :] * first_gain, unit[rows, :], inverse[rows, 0:1])
            acc[rows, :] = grad
            low[rows, :] = grad.astype(bf16)
        copy = copies(acc.at[rows_of[i]], grad_out.at[rows_of[i]])
        copy.start()
        grad_copies.append(copy)
    out_copy.wait()
    half = width // 2
    att_other[...] = dot(
        out_w[pl.ds(pl.multiple_of((1 - core) * half, half), half), :], low[...], 1, 1
    ).astype(bf16)
    att_mine[...] = dot(
        out_w[pl.ds(pl.multiple_of(core * half, half), half), :], low[...], 1, 1
    ).astype(bf16)
    wait_all(hidden_copies + grad_copies)


def middle(scalars, query_mask, vectors, saved, upstream, output_weight, weights, early, late):
    tokens, width = saved[1].shape
    block = tokens // 2
    hidden = weights[0].shape[1]
    quarter = hidden // 4
    pieces = early + late
    count = len(pieces)
    return pl.pallas_call(
        functools.partial(middle_kernel, len(early), len(late)),
        in_specs=[SM] + [VM] * 6 + [ANY] * 2 + [VM] + [ANY] * (9 + count),
        out_specs=[ANY] * 3 + [VM] * 2,
        out_shape=[
            jax.ShapeDtypeStruct(upstream.shape, bf16),
            jax.ShapeDtypeStruct((block, width), bf16),
            jax.ShapeDtypeStruct((tokens, width), f32),
            jax.ShapeDtypeStruct((width // 2, tokens), bf16),
            jax.ShapeDtypeStruct((width // 2, tokens), bf16),
        ],
        scratch_shapes=[
            pltpu.VMEM((width, width), bf16),
            pltpu.VMEM((2, width, hidden), bf16),
            pltpu.VMEM((2, hidden, width), bf16),
            pltpu.VMEM((width, count * quarter), bf16),
            pltpu.VMEM((count * quarter, width), bf16),
            pltpu.VMEM((len(late), 16, width), bf16),
            pltpu.VMEM((tokens, width), bf16),
            pltpu.VMEM((tokens, width), f32),
            pltpu.VMEM((tokens, width), f32),
            pltpu.VMEM((tokens, width), f32),
            pltpu.VMEM((tokens, 2 * hidden), bf16),
            pltpu.VMEM((tokens, len(early) * quarter), bf16),
            pltpu.VMEM((tokens, len(late) * quarter), bf16),
            pltpu.VMEM((tokens, width), bf16),
            pltpu.VMEM((tokens, width), bf16),
            pltpu.SemaphoreType.DMA((18 + count * (width // quarter + 2),)),
        ],
        compiler_params=params(48),
        cost_estimate=cost(*BRIEF),
        name="middle",
    )(
        scalars, query_mask, *vectors, *saved, upstream, output_weight, *weights,
        *pieces,
    )


def project_back_rows(core, copies, place, mine, other, grad_branch, weight, left, weight_v, grad, out):
    rows, width = out.shape
    half = other.shape[2]
    parts = 4
    step = width // parts
    here = pl.ds(place * rows, rows)
    left_copies = [
        copy
        for j in range(3)
        for copy in (
            copies(mine.at[j, here], left.at[:, columns_at((2 * j + core) * half, half)]),
            copies(other.at[j], left.at[:, columns_at((2 * j + 1 - core) * half, half)]),
        )
    ]
    weight_copies = [
        copies(weight.at[pl.ds(i * step, step)], weight_v.at[pl.ds(i * step, step)])
        for i in range(parts)
    ]
    grad_copy = copies(grad_branch.at[here], grad)
    start_all(left_copies + weight_copies[:1] + [grad_copy] + weight_copies[1:])
    wait_all(left_copies)
    for i in range(parts):
        cols = slice(i * step, (i + 1) * step)
        weight_copies[i].wait()
        total = dot(left[...], weight_v[cols, :], 1, 1)
        if i == 0:
            grad_copy.wait()
        out[:, cols] = (grad[:, cols] + total).astype(bf16)


def project_back_cross_kernel(
    scalars, mine, other, grad_branch, weight, out, left, weight_v, grad, sems
):
    project_back_rows(
        scalars[0], Copies(sems), 1, mine, other, grad_branch, weight, left, weight_v, grad, out
    )


def project_back_own_kernel(
    scalars, mine, other, grad_branch, weight, theirs, _, out, hidden_out,
    left, weight_v, grad, own, theirs_v, sems,
):
    core, chip = scalars[0], scalars[1]
    copies = Copies(sems)
    copy = copies(theirs, theirs_v)
    copy.start()
    project_back_rows(core, copies, 0, mine, other, grad_branch, weight, left, weight_v, grad, own)
    copy.wait()
    out_copies = [copies(own, out.at[chip]), copies(theirs_v, hidden_out.at[1 - chip])]
    start_all(out_copies)
    wait_all(out_copies)


def project_back_scratch(rows, weight):
    width, columns = weight.shape
    return [
        pltpu.VMEM((rows, columns), bf16),
        pltpu.VMEM((width, columns), bf16),
        pltpu.VMEM((rows, width), f32),
    ]


def project_back_cross(scalars, mine, other, grad_branch, weight):
    _, rows, _ = other.shape
    return pl.pallas_call(
        project_back_cross_kernel,
        in_specs=[SM] + [ANY] * 4,
        out_specs=VM,
        out_shape=jax.ShapeDtypeStruct((rows, weight.shape[0]), bf16),
        scratch_shapes=project_back_scratch(rows, weight) + [pltpu.SemaphoreType.DMA((11,))],
        compiler_params=params(20),
        cost_estimate=cost(*BRIEF),
        name="project_back_cross",
    )(scalars, mine, other, grad_branch, weight)


def project_back_own(scalars, mine, other, grad_branch, weight, theirs, hidden_out):
    _, rows, _ = other.shape
    width = weight.shape[0]
    block = pltpu.VMEM((rows, width), bf16)
    return pl.pallas_call(
        project_back_own_kernel,
        in_specs=[SM] + [ANY] * 6,
        out_specs=[ANY] * 2,
        out_shape=[jax.ShapeDtypeStruct(hidden_out.shape, bf16)] * 2,
        input_output_aliases={6: 1},
        scratch_shapes=project_back_scratch(rows, weight)
        + [block, block, pltpu.SemaphoreType.DMA((14,))],
        compiler_params=params(56),
        cost_estimate=cost(*BRIEF),
        name="project_back_own",
    )(scalars, mine, other, grad_branch, weight, theirs, hidden_out)


def shards(
    sizes,
    hidden_in,
    pair_lengths,
    prefix_keys,
    prefix_values,
    project_weight,
    project_bias,
    output_weight,
    output_bias,
    first_gain,
    first_shift,
    expand_weight,
    expand_bias,
    reduce_weight,
    reduce_bias,
    second_gain,
    second_shift,
    upstream,
):
    dp_size, mp_size = sizes
    rows_here, shard_len, width = hidden_in.shape
    hidden_here = expand_weight.shape[1]
    prefix = prefix_keys.shape[0]
    half = width // 2
    place = lax.axis_index("mp")
    chip, core = place // 2, place % 2
    part = lax.axis_index("dp") % 4
    scalars = jnp.stack([core, chip, part]).astype(jnp.int32)

    def across(array):
        return swap(array, "mp", 2, mp_size)

    def beside(array):
        return swap(array, "mp", 1, mp_size)

    def take(array, index):
        return lax.dynamic_index_in_dim(array, index, 0, keepdims=False)

    def row(vector):
        return vector.reshape(1, -1)

    cross = across(take(hidden_in, 1 - chip))
    hidden2 = beside(hidden_in)

    boundary = jnp.cumsum(take(pair_lengths, chip))
    blocks = jnp.stack(
        [2 * chip + core, 2 * chip + 1 - core, 2 * (1 - chip) + core, 2 * (1 - chip) + 1 - core]
    )
    position = (
        blocks[:, None] * shard_len + jnp.arange(shard_len, dtype=jnp.int32)[None, :]
    ).reshape(-1)
    segment = jnp.sum((position[:, None] >= boundary[None, :]).astype(jnp.int32), axis=1)
    column = jnp.arange(128, dtype=jnp.int32)[None, :]
    query_mask = (segment[:, None] == column).astype(bf16)
    key_mask = jnp.where(
        (segment[:, None] == column) & (column < PAIRS), 0.0, masked_score
    ).astype(bf16)
    key_mask = jnp.concatenate([jnp.zeros((prefix, 128), bf16), key_mask], 0)

    qkv, pack0, pack3 = project_first(
        scalars, hidden_in, hidden2, project_weight, project_bias, expand_weight, reduce_weight,
        expand_bias, upstream,
    )
    expand_sib, reduce_sib, bias_sib = beside(expand_weight), beside(reduce_weight), beside(expand_bias)
    cross, qkv, key_mask, query_mask, expand_sib, reduce_sib, bias_sib = lax.optimization_barrier(
        (cross, qkv, key_mask, query_mask, expand_sib, reduce_sib, bias_sib)
    )
    cross2 = beside(cross)
    piece0, piece3 = across(pack0), across(pack3)
    qkv = project_second(scalars, cross, cross2, project_weight, project_bias, qkv)
    attended_mine, attended_other, exps_mine, exps_other, recips_mine, recips_other = attend(
        scalars, qkv, prefix_keys, prefix_values, key_mask, query_mask
    )
    piece0, attended_other = lax.optimization_barrier((piece0, attended_other))
    piece1, piece2 = swap(piece0, "dp", 1, dp_size), swap(piece0, "dp", 2, dp_size)
    attended_here, piece0_sib = beside(attended_other), beside(piece0)
    attended_here, piece0_sib = lax.optimization_barrier((attended_here, piece0_sib))
    weights = (expand_weight, expand_sib, reduce_weight, reduce_sib)
    unit, inverse, total, slope, low = forward(
        scalars, attended_mine, attended_here, hidden_in, cross,
        (output_bias, first_gain, first_shift), output_weight, weights + (expand_bias, bias_sib),
    )
    piece1, piece2, piece3, low = lax.optimization_barrier((piece1, piece2, piece3, low))
    early = [piece0, piece0_sib, piece1, piece2]
    late = [beside(piece1), beside(piece2), piece3, beside(piece3)]
    total, slope2 = remote(low, total, early, hidden_here // 4)
    *late, total = lax.optimization_barrier((*late, total))
    hidden_own, hidden_cross, grad_branch, grad_mine, grad_theirs = middle(
        scalars, query_mask, (first_gain, first_shift, reduce_bias, second_gain, second_shift),
        (low, unit, inverse, total, slope, slope2), upstream, output_weight, weights, early, late,
    )
    grad_here = beside(grad_theirs)
    exps, recips = (exps_mine, exps_other), (recips_mine, recips_other)

    hidden_theirs = across(hidden_cross)
    scaled, spread, grad_prefix = prefix_back(
        scalars, qkv, prefix_values, exps, recips,
        (attended_mine, attended_other), (grad_mine, grad_here),
    )

    def both(array, bit, mp_bit):
        return lax.ppermute(
            array, ("dp", "mp"),
            [
                (d * mp_size + m, (d ^ bit) * mp_size + (m ^ mp_bit))
                for d in range(dp_size)
                for m in range(mp_size)
            ],
        )

    spread_parts = (across(grad_prefix), swap(grad_prefix, "dp", 2, dp_size), both(grad_prefix, 2, 2))
    back_mine, back_own2, back_cross2 = attend_back(
        scalars, qkv, prefix_keys, prefix_values, exps, scaled, spread
    )
    spread_parts, back_mine, back_own2, back_cross2, hidden_theirs = lax.optimization_barrier(
        (spread_parts, back_mine, back_own2, back_cross2, hidden_theirs)
    )
    grad_prefix = (grad_prefix + spread_parts[0]) + (spread_parts[1] + spread_parts[2])
    cross_there = beside(back_cross2)
    own_there = beside(back_own2)
    bit = 8
    while bit < dp_size:
        grad_prefix = grad_prefix + swap(grad_prefix, "dp", bit, dp_size)
        bit *= 2
    grad_prefix = grad_prefix.astype(bf16)
    far = swap(grad_prefix, "dp", 4, dp_size)
    in_cross = project_back_cross(scalars, back_mine, cross_there, grad_branch, project_weight)
    in_cross, far = lax.optimization_barrier((in_cross, far))
    in_cross = across(in_cross)
    grad_prefix = (grad_prefix.astype(f32) + far.astype(f32)).astype(bf16)
    grad_prefix_sib = beside(grad_prefix)
    near, near_sib = swap(grad_prefix, "dp", 1, dp_size), both(grad_prefix, 1, 1)
    grad_in, hidden_out = project_back_own(
        scalars, back_mine, own_there, grad_branch, project_weight, hidden_theirs, hidden_own
    )
    grad_in, in_cross, grad_prefix_sib, near, near_sib = lax.optimization_barrier(
        (grad_in, in_cross, grad_prefix_sib, near, near_sib)
    )
    grad_in = lax.dynamic_update_index_in_dim(grad_in, in_cross, 1 - chip, 0)
    mine = grad_prefix.astype(f32) + near.astype(f32)
    theirs = grad_prefix_sib.astype(f32) + near_sib.astype(f32)
    grad_prefix = jnp.where(
        core == 0, jnp.concatenate([mine, theirs], 2), jnp.concatenate([theirs, mine], 2)
    )
    return (hidden_out, grad_in, grad_prefix[0], grad_prefix[1])


def solution(mesh):
    placed = (
        P("dp", "mp", None),
        P("dp", None),
        P(),
        P(),
        P(),
        P(),
        P(),
        P(),
        P(),
        P(),
        P(None, "mp"),
        P("mp"),
        P("mp", None),
        P(),
        P(),
        P(),
        P("dp", "mp", None),
    )
    return jax.shard_map(
        functools.partial(shards, (mesh.shape["dp"], mesh.shape["mp"])),
        mesh=mesh,
        in_specs=placed,
        out_specs=(P("dp", "mp", None), P("dp", "mp", None), P(), P()),
        check_vma=False,
    )
```

```python
import functools

import jax
import jax.numpy as jnp
from jax import lax
from jax.experimental import pallas as pl
from jax.experimental.pallas import tpu as pltpu
from jax.sharding import PartitionSpec as P

HEADS = 16
PAIRS = 8

epsilon = 1e-05
masked_score = -1e30
root_half = 0.7071067811865476
inverse_root = 0.3989422804014327
log2_e = 1.4426950408889634
ln_2 = 0.6931471805599453

bf16 = jnp.bfloat16
f32 = jnp.float32


def dot(left, right, left_dim=1, right_dim=0):
    return lax.dot_general(
        left, right, (((left_dim,), (right_dim,)), ((), ())), preferred_element_type=f32
    )


def params(mebibytes):
    return pltpu.CompilerParams(vmem_limit_bytes=mebibytes * 2**20)


def cost(flops, bytes_accessed, transcendentals=0):
    return pl.CostEstimate(
        flops=int(flops), bytes_accessed=int(bytes_accessed), transcendentals=int(transcendentals)
    )


ANY = pl.BlockSpec(memory_space=pl.ANY)


def far_core(array):
    return pltpu.with_memory_space_constraint(array, pltpu.HBM)


def near_core(*arrays):
    return tuple(pltpu.with_memory_space_constraint(array, pltpu.VMEM) for array in arrays)


VM = pl.BlockSpec(memory_space=pltpu.VMEM)
SM = pl.BlockSpec(memory_space=pltpu.SMEM)
BRIEF = (1e6, 1e5)


def swap(array, axis, bit, size):
    return lax.ppermute(array, axis, [(i, i ^ bit) for i in range(size)])


class Copies:
    def __init__(self, sems):
        self.sems, self.used = sems, 0

    def __call__(self, source, target):
        copy = pltpu.make_async_copy(source, target, self.sems.at[self.used])
        self.used += 1
        return copy


def start_all(copies):
    for copy in copies:
        copy.start()


def wait_all(copies):
    for copy in copies:
        copy.wait()


def columns_at(start, size):
    return pl.ds(pl.multiple_of(start, size), size)


def project_tokens(core, copies, parts, weight, weight_copies, bias, out, place, tokens_v, out_v):
    block = parts[0].shape[-2]
    half = out.shape[2]
    token_copies = [
        copies(part, tokens_v.at[pl.ds(i * block, block)]) for i, part in enumerate(parts)
    ]
    start_all(token_copies)
    start_all(weight_copies)
    wait_all(token_copies)
    out_copies = []
    for j in range(3):
        wait_all(weight_copies[j : j + 1])
        shift = jnp.where(
            core == 0,
            bias[2 * j * half : (2 * j + 1) * half].astype(f32),
            bias[(2 * j + 1) * half : (2 * j + 2) * half].astype(f32),
        )
        result = dot(tokens_v[...], weight[j]) + shift.reshape(1, half)
        if j == 0:
            result = result * (log2_e * 0.125)
        out_v[j] = result.astype(bf16)
        copy = copies(out_v.at[j], out.at[j, pl.ds(place * 2 * block, 2 * block)])
        copy.start()
        out_copies.append(copy)
    return out_copies


def pack_kernel(scalars, expand, reduce, hidden_bias, upstream, pack0, pack3, packs, bias_v, sems):
    chip, part = scalars[1], scalars[2]
    copies = Copies(sems)
    width, hidden_here = expand.shape
    quarter = hidden_here // 4
    rows = 2 * quarter + 16
    bias_v[...] = jnp.broadcast_to(
        hidden_bias[...].astype(f32).reshape(1, hidden_here), (16, hidden_here)
    ).astype(bf16)
    groups = []
    for n, index in enumerate((part, 3 - part)):
        pack = packs.at[n]
        columns = columns_at(index * quarter, quarter)
        group = []
        for i in range(width // quarter):
            block = pl.ds(i * quarter, quarter)
            group.append(copies(expand.at[block, columns], pack.at[pl.ds(0, quarter), block]))
        group.append(
            copies(bias_v.at[:, columns], pack.at[pl.ds(quarter, 16), pl.ds(0, quarter)])
        )
        group.append(copies(reduce.at[columns], pack.at[pl.ds(quarter + 16, quarter)]))
        groups.append(group)
    groups[1].append(
        copies(upstream.at[1 - chip], packs.at[1, pl.ds(rows, upstream.shape[1])])
    )
    for group in groups:
        start_all(group)
    out_copies = []
    for n, (group, out) in enumerate(zip(groups, (pack0, pack3))):
        wait_all(group)
        copy = copies(packs.at[n, pl.ds(0, out.shape[0])], out)
        copy.start()
        out_copies.append(copy)
    wait_all(out_copies)


def pack(scalars, expand, reduce, hidden_bias, upstream):
    width, hidden_here = expand.shape
    quarter = hidden_here // 4
    rows = 2 * quarter + 16
    packs = [
        jax.ShapeDtypeStruct((n, width), bf16) for n in (rows, rows + upstream.shape[1])
    ]
    return pl.pallas_call(
        pack_kernel,
        in_specs=[SM, ANY, ANY, VM, ANY],
        out_specs=[ANY] * 2,
        out_shape=packs,
        scratch_shapes=[
            pltpu.VMEM((2, *packs[1].shape), bf16),
            pltpu.VMEM((16, hidden_here), bf16),
            pltpu.SemaphoreType.DMA((2 * (width // quarter + 3) + 1,)),
        ],
        compiler_params=params(56),
        cost_estimate=cost(*BRIEF),
        name="pack",
    )(scalars, expand, reduce, hidden_bias, upstream)


def project_first_kernel(
    scalars, hidden, hidden2, weight, bias, out, weight_out, tokens_v, out_v, sems
):
    core, chip = scalars[0], scalars[1]
    copies = Copies(sems)
    half = out.shape[2]
    weight_copies = [
        copies(weight.at[:, columns_at((2 * j + core) * half, half)], weight_out.at[j])
        for j in range(3)
    ]
    wait_all(
        project_tokens(
            core, copies, (hidden.at[chip], hidden2.at[chip]), weight_out, weight_copies, bias,
            out, 0, tokens_v, out_v,
        )
    )


def project_second_kernel(scalars, cross, cross2, weight, bias, _, out, tokens_v, out_v, sems):
    wait_all(
        project_tokens(
            scalars[0], Copies(sems), (cross, cross2), weight, [], bias, out, 1, tokens_v, out_v
        )
    )


def project_scratch(block, width, half):
    return [
        pltpu.VMEM((2 * block, width), bf16),
        pltpu.VMEM((3, 2 * block, half), bf16),
        pltpu.SemaphoreType.DMA((8,)),
    ]


def project_first(scalars, hidden, hidden2, weight, bias):
    _, block, width = hidden.shape
    half = width // 2
    return pl.pallas_call(
        project_first_kernel,
        in_specs=[SM, ANY, ANY, ANY, VM],
        out_specs=[ANY, VM],
        out_shape=[
            jax.ShapeDtypeStruct((3, 4 * block, half), bf16), pltpu.VMEM((3, width, half), bf16)
        ],
        scratch_shapes=project_scratch(block, width, half),
        compiler_params=params(50),
        cost_estimate=cost(*BRIEF),
        name="project_first",
    )(scalars, hidden, hidden2, weight, bias)


def project_second(scalars, cross, cross2, weight, bias, qkv):
    block, width = cross.shape
    half = width // 2
    return pl.pallas_call(
        project_second_kernel,
        in_specs=[SM, ANY, ANY, VM, VM, ANY],
        out_specs=ANY,
        out_shape=jax.ShapeDtypeStruct(qkv.shape, bf16),
        input_output_aliases={5: 0},
        scratch_shapes=project_scratch(block, width, half),
        compiler_params=params(50),
        cost_estimate=cost(*BRIEF),
        name="project_second",
    )(scalars, *near_core(cross, cross2, weight), bias, qkv)


def head_mask(shape, head, axis):
    return (lax.broadcasted_iota(jnp.int32, shape, axis) // 64) == head


def keep_head(array, head, axis):
    return jnp.where(head_mask(array.shape, head, axis), array, jnp.zeros_like(array))


def attend_kernel(
    core_ref, query, key, value, prefix_k, prefix_v, key_mask, query_mask,
    out_mine, out_other, exps_mine, exps_other, recips_mine, recips_other, keys, values_t,
):
    prefix = prefix_k.shape[0]
    tokens = query.shape[1]
    count = prefix + tokens
    chunk = tokens // 4
    keys[:prefix, :128] = prefix_k[...]
    keys[prefix:, :128] = key[0]

    @pl.when(pl.program_id(0) == 0)
    def _():
        keys[:, 128:] = key_mask[...]
        values_t[:, 64:, :] = jnp.ones((2, values_t.shape[1] - 64, count), bf16)

    prefix_t = prefix_v[...].astype(f32).T.astype(bf16)
    value_t = value[0].astype(f32).T.astype(bf16)
    for head in range(2):
        values_t[head, :64, :prefix] = prefix_t[64 * head : 64 * head + 64]
        values_t[head, :64, prefix:] = value_t[64 * head : 64 * head + 64]
    units = [(i, head) for i in (1, 3, 0, 2) for head in range(2)]

    def score(unit):
        i, head = unit
        rows = slice(i * chunk, (i + 1) * chunk)
        masked = jnp.concatenate([keep_head(query[0, rows, :], head, 1), query_mask[rows, :]], axis=1)
        return dot(keys[...], masked, 1, 1)

    ahead = 2
    pending = [score(unit) for unit in units[:ahead]]
    for n, (i, head) in enumerate(units):
        scores = pending.pop(0)
        if n + ahead < len(units):
            pending.append(score(units[n + ahead]))
        out, exps, recips = (
            (out_mine, exps_mine, recips_mine), (out_other, exps_other, recips_other)
        )[i % 2]
        cols = slice(i // 2 * chunk, (i // 2 + 1) * chunk)
        top = jnp.max(scores, axis=0, keepdims=True)
        weights = jnp.exp2(scores - top).astype(bf16)
        exps[0, head, :, cols] = weights
        summed = dot(values_t[head], weights)
        recip = 1.0 / summed[64:65, :]
        recips[0, head, :, cols] = jnp.broadcast_to(recip, (8, chunk))
        out[64 * head : 64 * head + 64, cols] = (summed[:64, :] * recip).astype(bf16)


def attend(core, qkv, prefix_keys, prefix_values, key_mask, query_mask):
    _, tokens, half = qkv.shape
    prefix = prefix_keys.shape[0]
    count = prefix + tokens
    pairs = half // 128
    prefix_spec = pl.BlockSpec((prefix, 128), lambda p, k: (0, k[0] * pairs + p))
    out_spec = pl.BlockSpec((128, tokens // 2), lambda p, k: (p, 0))
    exps_spec = pl.BlockSpec((1, 2, count, tokens // 2), lambda p, k: (p, 0, 0, 0))
    recips_spec = pl.BlockSpec((1, 2, 8, tokens // 2), lambda p, k: (p, 0, 0, 0))
    return pl.pallas_call(
        attend_kernel,
        grid_spec=pltpu.PrefetchScalarGridSpec(
            num_scalar_prefetch=1,
            grid=(pairs,),
            in_specs=[
                pl.BlockSpec((1, tokens, 128), lambda p, k, j=j: (j, 0, p)) for j in range(3)
            ]
            + [
                prefix_spec,
                prefix_spec,
                pl.BlockSpec((count, 128), lambda p, k: (0, 0)),
                pl.BlockSpec((tokens, 128), lambda p, k: (0, 0)),
            ],
            out_specs=[out_spec] * 2 + [exps_spec] * 2 + [recips_spec] * 2,
            scratch_shapes=[pltpu.VMEM((count, 256), bf16), pltpu.VMEM((2, 64 + 16, count), bf16)],
        ),
        out_shape=[jax.ShapeDtypeStruct((half, tokens // 2), bf16)] * 2
        + [jax.ShapeDtypeStruct((pairs, 2, count, tokens // 2), bf16)] * 2
        + [jax.ShapeDtypeStruct((pairs, 2, 8, tokens // 2), f32)] * 2,
        compiler_params=params(56),
        cost_estimate=cost(*BRIEF),
        name="attend",
    )(core, qkv, qkv, qkv, prefix_keys, prefix_values, key_mask, query_mask)


def ordered_rows(array):
    block = array.shape[0] // 4
    return [array[i * block : (i + 1) * block] for i in (0, 2, 1, 3)]


def prefix_back_kernel(
    core_ref, query, prefix_v, exps_mine, exps_other, recips_mine, recips_other,
    attended_mine, attended_other, grad_mine, grad_other, out_scaled, out_spread, out_prefix,
):
    pairs = exps_mine.shape[0]
    half_tokens = exps_mine.shape[3]
    sides = (
        (exps_mine, recips_mine, attended_mine, grad_mine),
        (exps_other, recips_other, attended_other, grad_other),
    )
    for pair in range(pairs):
        columns = slice(128 * pair, 128 * pair + 128)
        queries = ordered_rows(query[0, :, columns])
        units = []
        for side, (exps, recips, attended, grad) in enumerate(sides):
            tokens = slice(side * half_tokens, (side + 1) * half_tokens)
            query_side = jnp.concatenate(queries[2 * side : 2 * side + 2], axis=0)
            parts, spreads = [], []
            for head in range(2):
                rows = slice(128 * pair + 64 * head, 128 * pair + 64 * head + 64)
                scaled = grad[rows, :].astype(f32) * recips[pair, head, 0:1, :]
                parts.append(scaled.astype(bf16))
                spreads.append(
                    jnp.sum(scaled * attended[rows, :].astype(f32), axis=0, keepdims=True)
                )
            zeros = jnp.zeros_like(parts[0])
            out_scaled[pair, :, tokens] = jnp.concatenate(parts, axis=0)
            out_spread[pair, :, tokens] = jnp.concatenate(
                spreads + [jnp.zeros((6, half_tokens), f32)], axis=0
            )
            for head in range(2):
                scaled = jnp.concatenate(
                    [parts[0], zeros] if head == 0 else [zeros, parts[1]], axis=0
                )
                grad_probs = dot(prefix_v[:, columns], scaled)
                units.append((exps[pair, head], head, scaled, spreads[head], query_side, grad_probs))
        slopes = [
            (weights.astype(f32) * (grad_probs - spread)).astype(bf16)
            for weights, _, _, spread, _, grad_probs in units
        ]
        grad_keys = grad_values = None
        for (weights, head, scaled, _, query_side, _), slope in zip(units, slopes):
            key_part = dot(slope, keep_head(query_side, head, 1))
            value_part = dot(weights, scaled, 1, 1)
            grad_keys = key_part if grad_keys is None else grad_keys + key_part
            grad_values = value_part if grad_values is None else grad_values + value_part
        out_prefix[0, :, columns] = grad_keys * ln_2
        out_prefix[1, :, columns] = grad_values


def prefix_back(core, qkv, prefix_values, exps, recips, attended, grads):
    _, tokens, half = qkv.shape
    prefix = prefix_values.shape[0]
    pairs = half // 128
    heads_spec = pl.BlockSpec((half, tokens // 2), lambda i, k: (0, 0))
    exps_spec = pl.BlockSpec((pairs, 2, prefix, tokens // 2), lambda i, k: (0, 0, 0, 0))
    recips_spec = pl.BlockSpec((pairs, 2, 8, tokens // 2), lambda i, k: (0, 0, 0, 0))
    return pl.pallas_call(
        prefix_back_kernel,
        grid_spec=pltpu.PrefetchScalarGridSpec(
            num_scalar_prefetch=1,
            grid=(1,),
            in_specs=[
                pl.BlockSpec((1, tokens, half), lambda i, k: (0, 0, 0)),
                pl.BlockSpec((prefix, half), lambda i, k: (0, k[0])),
            ]
            + [exps_spec] * 2
            + [recips_spec] * 2
            + [heads_spec] * 4,
            out_specs=[
                pl.BlockSpec((pairs, 128, tokens), lambda i, k: (0, 0, 0)),
                pl.BlockSpec((pairs, 8, tokens), lambda i, k: (0, 0, 0)),
                pl.BlockSpec((2, prefix, half), lambda i, k: (0, 0, 0)),
            ],
        ),
        out_shape=[
            pltpu.VMEM((pairs, 128, tokens), bf16),
            pltpu.VMEM((pairs, 8, tokens), f32),
            jax.ShapeDtypeStruct((2, prefix, half), f32),
        ],
        compiler_params=params(56),
        cost_estimate=cost(*BRIEF),
        name="prefix_back",
    )(core, qkv, prefix_values, *exps, *recips, *attended, *grads)


def attend_back_kernel(
    core_ref, query, key, value, prefix_k, prefix_v, exps_mine, exps_other, scaled, spread,
    out_mine, out_own2, out_cross2, keys, values, keys_t, slopes, queries, queries_t,
):
    prefix = prefix_k.shape[0]
    tokens = query.shape[1]
    chunk = tokens // 4
    keys[:prefix, :] = prefix_k[...]
    keys[prefix:, :] = key[0]
    values[:prefix, :] = prefix_v[...]
    values[prefix:, :] = value[0]
    keys_t[...] = keys[...].astype(f32).T.astype(bf16)
    queries[...] = jnp.concatenate(ordered_rows(query[0]), axis=0)
    units = [(head, i) for head in range(2) for i in range(4)]

    def head_rows(array, head):
        zeros = jnp.zeros_like(array[:64])
        return jnp.concatenate([array[:64], zeros] if head == 0 else [zeros, array[64:]], axis=0)

    def grad_probs(unit):
        head, i = unit
        return dot(values[...], head_rows(scaled[0, :, i * chunk : (i + 1) * chunk], head))

    def exps_of(head, i):
        return (exps_mine, exps_other)[i // 2][0, head, :, i % 2 * chunk : (i % 2 + 1) * chunk]

    def value_part(head):
        total = None
        for side, exps in enumerate((exps_mine, exps_other)):
            cols = slice(2 * side * chunk, 2 * (side + 1) * chunk)
            part = dot(exps[0, head, prefix:, :], head_rows(scaled[0, :, cols], head), 1, 1)
            total = part if total is None else total + part
        return total

    def key_part(head):
        return dot(slopes[head, prefix:, :], keep_head(queries[...], head, 1))

    ahead = 4
    pending = [grad_probs(unit) for unit in units[:ahead]]
    for n, (head, i) in enumerate(units):
        grads = pending.pop(0)
        if n + ahead < len(units):
            pending.append(grad_probs(units[n + ahead]))
        cols = slice(i * chunk, (i + 1) * chunk)
        slopes[head, :, cols] = (
            exps_of(head, i).astype(f32) * (grads - spread[0, head : head + 1, cols])
        ).astype(bf16)
        if n == 0:
            value_first = value_part(0)
        rows = slice(64 * head, 64 * head + 64)
        queries_t[rows, cols] = dot(keys_t[rows, :], slopes[head, :, cols]) * 0.125
        if n == 4:
            key_first = key_part(0)
    value_grads = (value_first + value_part(1)).astype(bf16)
    key_grads = ((key_first + key_part(1)) * ln_2).astype(bf16)
    query_grads = queries_t[...].T.astype(bf16)
    for j, parts in enumerate(
        ([query_grads[i * chunk : (i + 1) * chunk] for i in range(4)],)
        + tuple(ordered_rows(array) for array in (key_grads, value_grads))
    ):
        out_mine[j, :chunk] = parts[0]
        out_mine[j, chunk:] = parts[1]
        out_own2[j] = parts[2]
        out_cross2[j] = parts[3]


def attend_back(core, qkv, prefix_keys, prefix_values, exps, scaled, spread):
    _, tokens, half = qkv.shape
    prefix = prefix_keys.shape[0]
    count = prefix + tokens
    pairs = half // 128
    prefix_spec = pl.BlockSpec((prefix, 128), lambda p, k: (0, k[0] * pairs + p))
    exps_spec = pl.BlockSpec((1, 2, count, tokens // 2), lambda p, k: (p, 0, 0, 0))
    rows = (tokens // 2, tokens // 4, tokens // 4)
    return pl.pallas_call(
        attend_back_kernel,
        grid_spec=pltpu.PrefetchScalarGridSpec(
            num_scalar_prefetch=1,
            grid=(pairs,),
            in_specs=[
                pl.BlockSpec((1, tokens, 128), lambda p, k, j=j: (j, 0, p)) for j in range(3)
            ]
            + [
                prefix_spec,
                prefix_spec,
                exps_spec,
                exps_spec,
                pl.BlockSpec((1, 128, tokens), lambda p, k: (p, 0, 0)),
                pl.BlockSpec((1, 8, tokens), lambda p, k: (p, 0, 0)),
            ],
            out_specs=[pl.BlockSpec((3, n, 128), lambda p, k: (0, 0, p)) for n in rows],
            scratch_shapes=[
                pltpu.VMEM((count, 128), bf16),
                pltpu.VMEM((count, 128), bf16),
                pltpu.VMEM((128, count), bf16),
                pltpu.VMEM((2, count, tokens), bf16),
                pltpu.VMEM((tokens, 128), bf16),
                pltpu.VMEM((128, tokens), f32),
            ],
        ),
        out_shape=[pltpu.VMEM((3, rows[0], half), bf16)]
        + [jax.ShapeDtypeStruct((3, n, half), bf16) for n in rows[1:]],
        compiler_params=params(46),
        cost_estimate=cost(*BRIEF),
        name="attend_back",
    )(core, qkv, qkv, qkv, prefix_keys, prefix_values, *exps, scaled, spread)


def mean_rows(array):
    return jnp.mean(array, axis=-1, keepdims=True)


def unit_norm(array):
    centered = array - mean_rows(array)
    inverse = lax.rsqrt(mean_rows(centered * centered) + epsilon)
    return centered * inverse, inverse


def norm_back(scaled, unit, inverse):
    return inverse * (scaled - mean_rows(scaled) - unit * mean_rows(scaled * unit))


def gelu_both(hidden):
    gate = 0.5 * (1.0 + lax.erf(hidden * root_half))
    slope = gate + hidden * inverse_root * jnp.exp(-0.5 * hidden * hidden)
    return (hidden * gate).astype(bf16), slope.astype(bf16)


def feed_forward(steps, total):
    hidden = None
    for i, step in enumerate(steps):
        if i == 0:
            wait_all(step[3])
            hidden = step[0]()
        following = None
        if i + 1 < len(steps):
            wait_all(steps[i + 1][3])
            following = steps[i + 1][0]()
        active, slope = gelu_both(hidden)
        step[1](slope)
        part = dot(active, step[2]())
        if total is None:
            total = part
        elif hasattr(total, "at"):
            total[...] += part
        hidden = following


def forward_kernel(
    core_ref, mine, other, own, cross, output_bias, first_gain, first_shift, output_weight,
    expand_own, expand_sib, reduce_own, reduce_sib, bias_own, bias_sib,
    unit_out, inverse_out, total_out, slope_out, low,
    out_w, expand_w, reduce_w, own_v, sems,
):
    core, chip = core_ref[0], core_ref[1]
    copies = [
        pltpu.make_async_copy(output_weight, out_w, sems.at[0]),
        pltpu.make_async_copy(expand_own, expand_w.at[0], sems.at[1]),
        pltpu.make_async_copy(reduce_own, reduce_w.at[0], sems.at[2]),
        pltpu.make_async_copy(expand_sib, expand_w.at[1], sems.at[3]),
        pltpu.make_async_copy(reduce_sib, reduce_w.at[1], sems.at[4]),
        pltpu.make_async_copy(own.at[chip], own_v, sems.at[5]),
    ]
    start_all(copies[5:] + copies[:5])
    copies[5].wait()
    copies[0].wait()
    half = mine.shape[0]
    block = own_v.shape[0]
    output_row, gain, shift = (
        ref[...].astype(f32).reshape(1, -1) for ref in (output_bias, first_gain, first_shift)
    )
    for i, ref in enumerate((own_v, cross)):
        rows = slice(i * block, (i + 1) * block)
        branch = dot(mine[:, rows], out_w[pl.ds(pl.multiple_of(core * half, half), half), :], 0, 0)
        branch += dot(
            other[:, rows], out_w[pl.ds(pl.multiple_of((1 - core) * half, half), half), :], 0, 0
        )
        unit, inverse = unit_norm(ref[...].astype(f32) + (branch + output_row))
        unit_out[rows, :] = unit
        inverse_out[rows, :] = jnp.broadcast_to(inverse, (block, 128))
        low[rows, :] = (unit * gain + shift).astype(bf16)
    chunk = 512
    hidden_here = expand_own.shape[1]

    def step(i, bias, start):
        cols = slice(start, start + chunk)

        def store(slope):
            slope_out[:, i * hidden_here + start : i * hidden_here + start + chunk] = slope

        return (
            lambda: dot(low[...], expand_w[i, :, cols]) + bias[cols].astype(f32).reshape(1, chunk),
            store,
            lambda: reduce_w[i, cols, :],
            copies[1 + 2 * i : 3 + 2 * i] if start == 0 else [],
        )

    total_out[...] = jnp.zeros(total_out.shape, f32)
    feed_forward(
        [
            step(i, bias, start)
            for i, bias in enumerate((bias_own, bias_sib))
            for start in range(0, hidden_here, chunk)
        ],
        total_out,
    )


def forward(core, mine, other, own, cross, vectors, output_weight, weights):
    tokens = mine.shape[1]
    _, block, width = own.shape
    hidden = weights[0].shape[1]
    return pl.pallas_call(
        forward_kernel,
        in_specs=[SM, VM, VM, ANY] + [VM] * 4 + [ANY] * 5 + [VM] * 2,
        out_specs=[VM] * 5,
        out_shape=[
            jax.ShapeDtypeStruct((tokens, width), f32),
            jax.ShapeDtypeStruct((tokens, 128), f32),
            jax.ShapeDtypeStruct((tokens, width), f32),
            jax.ShapeDtypeStruct((tokens, 2 * hidden), bf16),
            jax.ShapeDtypeStruct((tokens, width), bf16),
        ],
        scratch_shapes=[
            pltpu.VMEM((width, width), bf16),
            pltpu.VMEM((2, width, hidden), bf16),
            pltpu.VMEM((2, hidden, width), bf16),
            pltpu.VMEM((block, width), bf16),
            pltpu.SemaphoreType.DMA((6,)),
        ],
        compiler_params=params(36),
        cost_estimate=cost(*BRIEF),
        name="forward",
    )(core, mine, other, own, cross, *vectors, output_weight, *weights)


def piece_copies(copies, pieces, place, quarter, expand_r, reduce_r, bias_r):
    width = expand_r.shape[0]
    result = []
    for i, piece in enumerate(pieces):
        here = pl.ds((place + i) * quarter, quarter)
        group = []
        for j in range(width // quarter):
            rows = pl.ds(j * quarter, quarter)
            group.append(copies(piece.at[pl.ds(0, quarter), rows], expand_r.at[rows, here]))
        group.append(copies(piece.at[pl.ds(quarter + 16, quarter)], reduce_r.at[here]))
        if bias_r is not None:
            group.append(copies(piece.at[pl.ds(quarter, 16)], bias_r.at[i]))
        result.append(group)
    return result


def piece_steps(count, place, quarter, low, expand_r, reduce_r, bias_r, slope_out, waits):
    def step(first, n):
        rows = slice((place + first) * quarter, (place + first + n) * quarter)

        def hidden():
            bias = [bias_r[first + i, 0:1, :quarter] for i in range(n)]
            bias = bias[0] if n == 1 else jnp.concatenate(bias, axis=1)
            return dot(low[...], expand_r[:, rows]) + bias.astype(f32)

        def store(slope):
            slope_out[:, first * quarter : (first + n) * quarter] = slope

        return (
            hidden,
            store,
            lambda: reduce_r[rows, :],
            [copy for i in range(n) for copy in waits[first + i]],
        )

    return [step(first, min(2, count - first)) for first in range(0, count, 2)]


def remote_kernel(count, *refs):
    low_in, total_in = refs[:2]
    pieces = refs[2 : 2 + count]
    total_out, slope_out, low, expand_r, reduce_r, bias_r, sems = refs[2 + count :]
    quarter = reduce_r.shape[0] // count
    copies = Copies(sems)
    first = [copies(low_in, low), copies(total_in, total_out)]
    waits = piece_copies(copies, pieces, 0, quarter, expand_r, reduce_r, bias_r)
    start_all(first[:1] + waits[0] + waits[1] + first[1:])
    for group in waits[2:]:
        start_all(group)
    steps = piece_steps(count, 0, quarter, low, expand_r, reduce_r, bias_r, slope_out, waits)
    steps[0] = steps[0][:3] + (first + steps[0][3],)
    feed_forward(steps, total_out)


def remote(low, total, pieces, quarter):
    tokens, width = total.shape
    count = len(pieces)
    return pl.pallas_call(
        functools.partial(remote_kernel, count),
        in_specs=[ANY] * (2 + count),
        out_specs=[VM] * 2,
        out_shape=[
            pltpu.VMEM((tokens, width), f32),
            pltpu.VMEM((tokens, count * quarter), bf16),
        ],
        scratch_shapes=[
            pltpu.VMEM((tokens, width), bf16),
            pltpu.VMEM((width, count * quarter), bf16),
            pltpu.VMEM((count * quarter, width), bf16),
            pltpu.VMEM((count, 16, width), bf16),
            pltpu.SemaphoreType.DMA((2 + count * (width // quarter + 2),)),
        ],
        compiler_params=params(26),
        cost_estimate=cost(*BRIEF),
        name="remote",
    )(low, total, *pieces)


def middle_kernel(early, late, *refs):
    count = early + late
    scalars, query_mask = refs[:2]
    vectors = refs[2:7]
    low_in, unit_in, inverse, total_in, slope_in, slope2_in, upstream = refs[7:14]
    output_weight, expand_own, expand_sib, reduce_own, reduce_sib = refs[14:19]
    pieces = refs[19 : 19 + count]
    hidden_own, hidden_cross, grad_out, att_mine, att_other = refs[19 + count : 24 + count]
    (
        out_w, expand_w, reduce_w, expand_r, reduce_r, bias_r, low, unit, acc, back_acc,
        slope_l, slope_e, slope_s, up, hidden, sems,
    ) = refs[24 + count :]
    core, chip = scalars[0], scalars[1]
    copies = Copies(sems)
    tokens, width = unit.shape
    block = tokens // 2
    quarter = reduce_r.shape[0] // count
    chunk = 2 * quarter
    hidden_here = expand_own.shape[1]
    rows_of = [pl.ds(i * block, block) for i in range(2)]

    up_cross = pieces[early + 2].at[pl.ds(2 * quarter + 16, block)]
    low_copy = copies(low_in, low)
    late_waits = piece_copies(copies, pieces[early:], early, quarter, expand_r, reduce_r, bias_r)
    norm_copies = [
        [
            copies(total_in.at[rows_of[i]], acc.at[rows_of[i]]),
            copies(unit_in.at[rows_of[i]], unit.at[rows_of[i]]),
            copies((upstream.at[chip], up_cross)[i], up.at[rows_of[i]]),
        ]
        for i in range(2)
    ]
    local_copies = [
        [copies((reduce_own, reduce_sib)[i], reduce_w.at[i]), copies((expand_own, expand_sib)[i], expand_w.at[i])]
        for i in range(2)
    ]
    slope_copy = copies(slope_in, slope_l)
    early_copies = piece_copies(copies, pieces[:early], 0, quarter, expand_r, reduce_r, None)
    slope2_copy = copies(slope2_in, slope_e)
    out_copy = copies(output_weight, out_w)
    start_all([low_copy] + [copy for group in late_waits + norm_copies for copy in group])
    start_all([local_copies[0][0], slope_copy, local_copies[0][1]] + local_copies[1])
    start_all([copy for group in early_copies for copy in group] + [slope2_copy, out_copy])

    steps = piece_steps(late, early, quarter, low, expand_r, reduce_r, bias_r, slope_s, late_waits)
    steps[0] = steps[0][:3] + ([low_copy] + steps[0][3],)
    for group in norm_copies:
        wait_all(group[:1])
    feed_forward(steps, acc)

    first_gain, first_shift, reduce_bias, second_gain, second_shift = (
        ref[...].astype(f32).reshape(1, -1) for ref in vectors
    )
    hidden_copies = []
    for i in range(2):
        wait_all(norm_copies[i][1:])
        for start in range(i * block, (i + 1) * block, block // 2):
            rows = slice(start, start + block // 2)
            masked = slice(2 * i * block + start - i * block, 2 * i * block + start - i * block + block // 2)
            live = 1.0 - query_mask[masked, PAIRS : PAIRS + 1].astype(f32)
            first_norm = unit[rows, :] * first_gain + first_shift
            unit2, inverse2 = unit_norm(first_norm + (acc[rows, :] + reduce_bias))
            hidden[rows, :] = ((unit2 * second_gain + second_shift) * live).astype(bf16)
            grad_feed = norm_back(up[rows, :].astype(f32) * live * second_gain, unit2, inverse2)
            back_acc[rows, :] = grad_feed
            low[rows, :] = grad_feed.astype(bf16)
        copy = copies(hidden.at[rows_of[i]], (hidden_own.at[chip], hidden_cross)[i])
        copy.start()
        hidden_copies.append(copy)

    backs = []
    for i in range(2):
        for start in range(0, hidden_here, chunk):
            cols = slice(start, start + chunk)
            place = slice(i * hidden_here + start, i * hidden_here + start + chunk)
            backs.append(
                (
                    lambda i=i, cols=cols: reduce_w[i, cols, :],
                    lambda i=i, cols=cols: expand_w[i, :, cols],
                    1,
                    lambda place=place: slope_l[:, place],
                    ([slope_copy] if i + start == 0 else []) + (local_copies[i] if start == 0 else []),
                )
            )
    total_pieces = early + late
    for first in range(0, total_pieces, 2):
        rows = slice(first * quarter, (first + 2) * quarter)

        def slopes(first=first):
            parts = [
                slope_e[:, j * quarter : (j + 1) * quarter]
                if j < early
                else slope_s[:, (j - early) * quarter : (j - early + 1) * quarter]
                for j in (first, first + 1)
            ]
            return jnp.concatenate(parts, axis=1)

        waits = [copy for j in (first, first + 1) if j < early for copy in early_copies[j]]
        backs.append(
            (
                lambda rows=rows: reduce_r[rows, :],
                lambda rows=rows: expand_r[:, rows],
                1,
                slopes,
                ([slope2_copy] if first == 0 else []) + waits,
            )
        )

    def grads(step):
        wait_all(step[4])
        return dot(low[...], step[0](), 1, 1)

    grad = grads(backs[0])
    for i, step in enumerate(backs):
        following = grads(backs[i + 1]) if i + 1 < len(backs) else None
        back = (grad * step[3]().astype(f32)).astype(bf16)
        back_acc[...] += dot(back, step[1](), 1, step[2])
        grad = following

    grad_copies = []
    for i in range(2):
        for start in range(i * block, (i + 1) * block, block // 2):
            rows = slice(start, start + block // 2)
            grad = norm_back(back_acc[rows, :] * first_gain, unit[rows, :], inverse[rows, 0:1])
            acc[rows, :] = grad
            low[rows, :] = grad.astype(bf16)
        copy = copies(acc.at[rows_of[i]], grad_out.at[rows_of[i]])
        copy.start()
        grad_copies.append(copy)
    out_copy.wait()
    half = width // 2
    att_other[...] = dot(
        out_w[pl.ds(pl.multiple_of((1 - core) * half, half), half), :], low[...], 1, 1
    ).astype(bf16)
    att_mine[...] = dot(
        out_w[pl.ds(pl.multiple_of(core * half, half), half), :], low[...], 1, 1
    ).astype(bf16)
    wait_all(hidden_copies + grad_copies)


def middle(scalars, query_mask, vectors, saved, upstream, output_weight, weights, early, late):
    tokens, width = saved[1].shape
    block = tokens // 2
    hidden = weights[0].shape[1]
    quarter = hidden // 4
    pieces = early + late
    count = len(pieces)
    return pl.pallas_call(
        functools.partial(middle_kernel, len(early), len(late)),
        in_specs=[SM] + [VM] * 6 + [ANY] * 2 + [VM] + [ANY] * (9 + count),
        out_specs=[ANY] * 3 + [VM] * 2,
        out_shape=[
            jax.ShapeDtypeStruct(upstream.shape, bf16),
            jax.ShapeDtypeStruct((block, width), bf16),
            jax.ShapeDtypeStruct((tokens, width), f32),
            pltpu.VMEM((width // 2, tokens), bf16),
            pltpu.VMEM((width // 2, tokens), bf16),
        ],
        scratch_shapes=[
            pltpu.VMEM((width, width), bf16),
            pltpu.VMEM((2, width, hidden), bf16),
            pltpu.VMEM((2, hidden, width), bf16),
            pltpu.VMEM((width, count * quarter), bf16),
            pltpu.VMEM((count * quarter, width), bf16),
            pltpu.VMEM((len(late), 16, width), bf16),
            pltpu.VMEM((tokens, width), bf16),
            pltpu.VMEM((tokens, width), f32),
            pltpu.VMEM((tokens, width), f32),
            pltpu.VMEM((tokens, width), f32),
            pltpu.VMEM((tokens, 2 * hidden), bf16),
            pltpu.VMEM((tokens, len(early) * quarter), bf16),
            pltpu.VMEM((tokens, len(late) * quarter), bf16),
            pltpu.VMEM((tokens, width), bf16),
            pltpu.VMEM((tokens, width), bf16),
            pltpu.SemaphoreType.DMA((18 + count * (width // quarter + 2),)),
        ],
        compiler_params=params(48),
        cost_estimate=cost(*BRIEF),
        name="middle",
    )(
        scalars, query_mask, *vectors, *saved, upstream, output_weight, *weights,
        *pieces,
    )


def project_back_rows(core, copies, place, mine, other, grad_branch, weight, left, weight_v, grad, out):
    rows, width = out.shape
    half = other.shape[2]
    parts = 4
    step = width // parts
    here = pl.ds(place * rows, rows)
    left_copies = [
        copy
        for j in range(3)
        for copy in (
            copies(mine.at[j, here], left.at[:, columns_at((2 * j + core) * half, half)]),
            copies(other.at[j], left.at[:, columns_at((2 * j + 1 - core) * half, half)]),
        )
    ]
    weight_copies = [
        copies(weight.at[pl.ds(i * step, step)], weight_v.at[pl.ds(i * step, step)])
        for i in range(parts)
    ]
    grad_copy = copies(grad_branch.at[here], grad)
    start_all(left_copies + weight_copies[:1] + [grad_copy] + weight_copies[1:])
    wait_all(left_copies)
    for i in range(parts):
        cols = slice(i * step, (i + 1) * step)
        weight_copies[i].wait()
        total = dot(left[...], weight_v[cols, :], 1, 1)
        if i == 0:
            grad_copy.wait()
        out[:, cols] = (grad[:, cols] + total).astype(bf16)


def project_back_cross_kernel(
    scalars, mine, other, grad_branch, weight, out, left, weight_v, grad, sems
):
    project_back_rows(
        scalars[0], Copies(sems), 1, mine, other, grad_branch, weight, left, weight_v, grad, out
    )


def project_back_own_kernel(
    scalars, mine, other, grad_branch, weight, theirs, _, out, hidden_out,
    left, weight_v, grad, theirs_v, sems,
):
    core, chip = scalars[0], scalars[1]
    copies = Copies(sems)
    theirs_in = copies(theirs, theirs_v)
    theirs_out = copies(theirs_v, hidden_out.at[1 - chip])
    theirs_in.start()
    theirs_in.wait()
    theirs_out.start()
    project_back_rows(core, copies, 0, mine, other, grad_branch, weight, left, weight_v, grad, out)
    theirs_out.wait()


def project_back_scratch(rows, weight):
    width, columns = weight.shape
    return [
        pltpu.VMEM((rows, columns), bf16),
        pltpu.VMEM((width, columns), bf16),
        pltpu.VMEM((rows, width), f32),
    ]


def project_back_cross(scalars, mine, other, grad_branch, weight):
    _, rows, _ = other.shape
    return pl.pallas_call(
        project_back_cross_kernel,
        in_specs=[SM] + [ANY] * 4,
        out_specs=VM,
        out_shape=jax.ShapeDtypeStruct((rows, weight.shape[0]), bf16),
        scratch_shapes=project_back_scratch(rows, weight) + [pltpu.SemaphoreType.DMA((11,))],
        compiler_params=params(20),
        cost_estimate=cost(*BRIEF),
        name="project_back_cross",
    )(scalars, mine, other, grad_branch, weight)


def project_back_own(scalars, mine, other, grad_branch, weight, theirs, hidden_out):
    _, rows, _ = other.shape
    width = weight.shape[0]
    return pl.pallas_call(
        project_back_own_kernel,
        in_specs=[SM] + [ANY] * 6,
        out_specs=[VM, ANY],
        out_shape=[
            jax.ShapeDtypeStruct((rows, width), bf16),
            jax.ShapeDtypeStruct(hidden_out.shape, bf16),
        ],
        input_output_aliases={6: 1},
        scratch_shapes=project_back_scratch(rows, weight)
        + [pltpu.VMEM((rows, width), bf16), pltpu.SemaphoreType.DMA((13,))],
        compiler_params=params(20),
        cost_estimate=cost(*BRIEF),
        name="project_back_own",
    )(scalars, mine, other, grad_branch, weight, theirs, hidden_out)


def shards(
    sizes,
    hidden_in,
    pair_lengths,
    prefix_keys,
    prefix_values,
    project_weight,
    project_bias,
    output_weight,
    output_bias,
    first_gain,
    first_shift,
    expand_weight,
    expand_bias,
    reduce_weight,
    reduce_bias,
    second_gain,
    second_shift,
    upstream,
):
    dp_size, mp_size = sizes
    rows_here, shard_len, width = hidden_in.shape
    hidden_here = expand_weight.shape[1]
    prefix = prefix_keys.shape[0]
    half = width // 2
    place = lax.axis_index("mp")
    chip, core = place // 2, place % 2
    part = lax.axis_index("dp") % 4
    scalars = jnp.stack([core, chip, part]).astype(jnp.int32)

    def across(array):
        return swap(array, "mp", 2, mp_size)

    def beside(array):
        return swap(array, "mp", 1, mp_size)

    def take(array, index):
        return lax.dynamic_index_in_dim(array, index, 0, keepdims=False)

    def row(vector):
        return vector.reshape(1, -1)

    cross = across(take(hidden_in, 1 - chip))
    hidden2 = beside(hidden_in)

    boundary = jnp.cumsum(take(pair_lengths, chip))
    blocks = jnp.stack(
        [2 * chip + core, 2 * chip + 1 - core, 2 * (1 - chip) + core, 2 * (1 - chip) + 1 - core]
    )
    position = (
        blocks[:, None] * shard_len + jnp.arange(shard_len, dtype=jnp.int32)[None, :]
    ).reshape(-1)
    segment = jnp.sum((position[:, None] >= boundary[None, :]).astype(jnp.int32), axis=1)
    column = jnp.arange(128, dtype=jnp.int32)[None, :]
    query_mask = (segment[:, None] == column).astype(bf16)
    key_mask = jnp.where(
        (segment[:, None] == column) & (column < PAIRS), 0.0, masked_score
    ).astype(bf16)
    key_mask = jnp.concatenate([jnp.zeros((prefix, 128), bf16), key_mask], 0)

    pack0, pack3 = pack(scalars, expand_weight, reduce_weight, expand_bias, upstream)
    qkv, core_weight = project_first(scalars, hidden_in, hidden2, project_weight, project_bias)
    expand_sib, reduce_sib, bias_sib = beside(expand_weight), beside(reduce_weight), beside(expand_bias)
    cross, qkv, key_mask, query_mask, expand_sib, reduce_sib, bias_sib = lax.optimization_barrier(
        (cross, qkv, key_mask, query_mask, expand_sib, reduce_sib, bias_sib)
    )
    cross2 = beside(cross)
    piece0, piece3 = across(pack0), across(pack3)
    qkv = project_second(scalars, cross, cross2, core_weight, project_bias, qkv)
    attended_mine, attended_other, exps_mine, exps_other, recips_mine, recips_other = attend(
        scalars, qkv, prefix_keys, prefix_values, key_mask, query_mask
    )
    piece0, attended_other = lax.optimization_barrier((piece0, attended_other))
    piece1, piece2 = swap(piece0, "dp", 1, dp_size), swap(piece0, "dp", 2, dp_size)
    attended_here, piece0_sib = beside(attended_other), beside(piece0)
    attended_here, piece0_sib = lax.optimization_barrier((attended_here, piece0_sib))
    weights = tuple(
        far_core(array) for array in (expand_weight, expand_sib, reduce_weight, reduce_sib)
    )
    unit, inverse, total, slope, low = forward(
        scalars, attended_mine, attended_here, hidden_in, cross,
        (output_bias, first_gain, first_shift), output_weight, weights + (expand_bias, bias_sib),
    )
    piece1, piece2, piece3, low = lax.optimization_barrier((piece1, piece2, piece3, low))
    early = [piece0, piece0_sib, piece1, piece2]
    late = [beside(piece1), beside(piece2), piece3, beside(piece3)]
    total, slope2 = remote(low, total, early, hidden_here // 4)
    *late, total = lax.optimization_barrier((*late, total))
    total, slope2 = near_core(total, slope2)
    late = list(near_core(*late))
    hidden_own, hidden_cross, grad_branch, grad_mine, grad_theirs = middle(
        scalars, query_mask, (first_gain, first_shift, reduce_bias, second_gain, second_shift),
        (low, unit, inverse, total, slope, slope2), upstream, output_weight, weights, early, late,
    )
    grad_here = beside(grad_theirs)
    exps, recips = (exps_mine, exps_other), (recips_mine, recips_other)

    hidden_theirs = across(hidden_cross)
    scaled, spread, grad_prefix = prefix_back(
        scalars, qkv, prefix_values, exps, recips,
        (attended_mine, attended_other), near_core(grad_mine, grad_here),
    )

    def both(array, bit, mp_bit):
        return lax.ppermute(
            array, ("dp", "mp"),
            [
                (d * mp_size + m, (d ^ bit) * mp_size + (m ^ mp_bit))
                for d in range(dp_size)
                for m in range(mp_size)
            ],
        )

    spread_parts = (across(grad_prefix), swap(grad_prefix, "dp", 2, dp_size), both(grad_prefix, 2, 2))
    back_mine, back_own2, back_cross2 = attend_back(
        scalars, qkv, prefix_keys, prefix_values, exps, *near_core(scaled, spread)
    )
    spread_parts, back_mine, back_own2, back_cross2, hidden_theirs = lax.optimization_barrier(
        (spread_parts, back_mine, back_own2, back_cross2, hidden_theirs)
    )
    grad_prefix = (grad_prefix + spread_parts[0]) + (spread_parts[1] + spread_parts[2])
    cross_there = beside(back_cross2)
    own_there = beside(back_own2)
    bit = 8
    while bit < dp_size:
        grad_prefix = grad_prefix + swap(grad_prefix, "dp", bit, dp_size)
        bit *= 2
    grad_prefix = grad_prefix.astype(bf16)
    far = swap(grad_prefix, "dp", 4, dp_size)
    back_mine, cross_there = near_core(back_mine, cross_there)
    last_weight, grad_branch = far_core(project_weight), far_core(grad_branch)
    in_cross = project_back_cross(scalars, back_mine, cross_there, grad_branch, last_weight)
    in_cross, far = lax.optimization_barrier((in_cross, far))
    in_cross = across(in_cross)
    grad_prefix = (grad_prefix.astype(f32) + far.astype(f32)).astype(bf16)
    grad_prefix_sib = beside(grad_prefix)
    near, near_sib = swap(grad_prefix, "dp", 1, dp_size), both(grad_prefix, 1, 1)
    in_own, hidden_out = project_back_own(
        scalars, back_mine, own_there, grad_branch, last_weight, far_core(hidden_theirs), hidden_own
    )
    in_own, grad_prefix_sib, near, near_sib = lax.optimization_barrier(
        (in_own, grad_prefix_sib, near, near_sib)
    )
    grad_in = jnp.where(chip == 0, jnp.stack([in_own, in_cross]), jnp.stack([in_cross, in_own]))
    mine = grad_prefix.astype(f32) + near.astype(f32)
    theirs = grad_prefix_sib.astype(f32) + near_sib.astype(f32)
    grad_prefix = jnp.where(
        core == 0, jnp.concatenate([mine, theirs], 2), jnp.concatenate([theirs, mine], 2)
    )
    return (hidden_out, grad_in, grad_prefix[0], grad_prefix[1])


def solution(mesh):
    placed = (
        P("dp", "mp", None),
        P("dp", None),
        P(),
        P(),
        P(),
        P(),
        P(),
        P(),
        P(),
        P(),
        P(None, "mp"),
        P("mp"),
        P("mp", None),
        P(),
        P(),
        P(),
        P("dp", "mp", None),
    )
    return jax.shard_map(
        functools.partial(shards, (mesh.shape["dp"], mesh.shape["mp"])),
        mesh=mesh,
        in_specs=placed,
        out_specs=(P("dp", "mp", None), P("dp", "mp", None), P(), P()),
        check_vma=False,
    )
```

```python
import functools

import jax
import jax.numpy as jnp
from jax import lax
from jax.experimental import pallas as pl
from jax.experimental.pallas import tpu as pltpu
from jax.sharding import PartitionSpec as P

HEADS = 16
PAIRS = 8

epsilon = 1e-05
masked_score = -1e30
root_half = 0.7071067811865476
inverse_root = 0.3989422804014327
log2_e = 1.4426950408889634
ln_2 = 0.6931471805599453

bf16 = jnp.bfloat16
f32 = jnp.float32


def dot(left, right, left_dim=1, right_dim=0):
    return lax.dot_general(
        left, right, (((left_dim,), (right_dim,)), ((), ())), preferred_element_type=f32
    )


def params(mebibytes):
    return pltpu.CompilerParams(vmem_limit_bytes=mebibytes * 2**20)


def cost(flops, bytes_accessed, transcendentals=0):
    return pl.CostEstimate(
        flops=int(flops), bytes_accessed=int(bytes_accessed), transcendentals=int(transcendentals)
    )


ANY = pl.BlockSpec(memory_space=pl.ANY)


def far_core(array):
    return pltpu.with_memory_space_constraint(array, pltpu.HBM)


def near_core(*arrays):
    return tuple(pltpu.with_memory_space_constraint(array, pltpu.VMEM) for array in arrays)


VM = pl.BlockSpec(memory_space=pltpu.VMEM)
SM = pl.BlockSpec(memory_space=pltpu.SMEM)
BRIEF = (1e6, 1e5)


def swap(array, axis, bit, size):
    return lax.ppermute(array, axis, [(i, i ^ bit) for i in range(size)])


class Copies:
    def __init__(self, sems):
        self.sems, self.used = sems, 0

    def __call__(self, source, target):
        copy = pltpu.make_async_copy(source, target, self.sems.at[self.used])
        self.used += 1
        return copy


def start_all(copies):
    for copy in copies:
        copy.start()


def wait_all(copies):
    for copy in copies:
        copy.wait()


def columns_at(start, size):
    return pl.ds(pl.multiple_of(start, size), size)


def project_tokens(core, copies, parts, weight, weight_copies, bias, out, place, tokens_v, out_v):
    block = parts[0].shape[-2]
    half = out.shape[2]
    token_copies = [
        copies(part, tokens_v.at[pl.ds(i * block, block)]) for i, part in enumerate(parts)
    ]
    start_all(token_copies)
    start_all(weight_copies)
    wait_all(token_copies)
    out_copies = []
    for j in range(3):
        wait_all(weight_copies[j : j + 1])
        shift = jnp.where(
            core == 0,
            bias[2 * j * half : (2 * j + 1) * half].astype(f32),
            bias[(2 * j + 1) * half : (2 * j + 2) * half].astype(f32),
        )
        result = dot(tokens_v[...], weight[j]) + shift.reshape(1, half)
        if j == 0:
            result = result * (log2_e * 0.125)
        out_v[j] = result.astype(bf16)
        copy = copies(out_v.at[j], out.at[j, pl.ds(place * 2 * block, 2 * block)])
        copy.start()
        out_copies.append(copy)
    return out_copies


def pack_kernel(scalars, expand, reduce, hidden_bias, upstream, pack0, pack3, packs, bias_v, sems):
    chip, part = scalars[1], scalars[2]
    copies = Copies(sems)
    width, hidden_here = expand.shape
    quarter = hidden_here // 4
    rows = 2 * quarter + 16
    bias_v[...] = jnp.broadcast_to(
        hidden_bias[...].astype(f32).reshape(1, hidden_here), (16, hidden_here)
    ).astype(bf16)
    groups = []
    for n, index in enumerate((part, 3 - part)):
        pack = packs.at[n]
        columns = columns_at(index * quarter, quarter)
        group = []
        for i in range(width // quarter):
            block = pl.ds(i * quarter, quarter)
            group.append(copies(expand.at[block, columns], pack.at[pl.ds(0, quarter), block]))
        group.append(
            copies(bias_v.at[:, columns], pack.at[pl.ds(quarter, 16), pl.ds(0, quarter)])
        )
        group.append(copies(reduce.at[columns], pack.at[pl.ds(quarter + 16, quarter)]))
        groups.append(group)
    groups[1].append(
        copies(upstream.at[1 - chip], packs.at[1, pl.ds(rows, upstream.shape[1])])
    )
    for group in groups:
        start_all(group)
    out_copies = []
    for n, (group, out) in enumerate(zip(groups, (pack0, pack3))):
        wait_all(group)
        copy = copies(packs.at[n, pl.ds(0, out.shape[0])], out)
        copy.start()
        out_copies.append(copy)
    wait_all(out_copies)


def pack(scalars, expand, reduce, hidden_bias, upstream):
    width, hidden_here = expand.shape
    quarter = hidden_here // 4
    rows = 2 * quarter + 16
    packs = [
        jax.ShapeDtypeStruct((n, width), bf16) for n in (rows, rows + upstream.shape[1])
    ]
    return pl.pallas_call(
        pack_kernel,
        in_specs=[SM, ANY, ANY, VM, ANY],
        out_specs=[ANY] * 2,
        out_shape=packs,
        scratch_shapes=[
            pltpu.VMEM((2, *packs[1].shape), bf16),
            pltpu.VMEM((16, hidden_here), bf16),
            pltpu.SemaphoreType.DMA((2 * (width // quarter + 3) + 1,)),
        ],
        compiler_params=params(56),
        cost_estimate=cost(*BRIEF),
        name="pack",
    )(scalars, expand, reduce, hidden_bias, upstream)


def project_first_kernel(
    scalars, hidden, hidden2, weight, bias, out, weight_out, tokens_v, out_v, sems
):
    core, chip = scalars[0], scalars[1]
    copies = Copies(sems)
    half = out.shape[2]
    weight_copies = [
        copies(weight.at[:, columns_at((2 * j + core) * half, half)], weight_out.at[j])
        for j in range(3)
    ]
    wait_all(
        project_tokens(
            core, copies, (hidden.at[chip], hidden2.at[chip]), weight_out, weight_copies, bias,
            out, 0, tokens_v, out_v,
        )
    )


def project_second_kernel(scalars, cross, cross2, weight, bias, _, out, tokens_v, out_v, sems):
    wait_all(
        project_tokens(
            scalars[0], Copies(sems), (cross, cross2), weight, [], bias, out, 1, tokens_v, out_v
        )
    )


def project_scratch(block, width, half):
    return [
        pltpu.VMEM((2 * block, width), bf16),
        pltpu.VMEM((3, 2 * block, half), bf16),
        pltpu.SemaphoreType.DMA((8,)),
    ]


def project_first(scalars, hidden, hidden2, weight, bias):
    _, block, width = hidden.shape
    half = width // 2
    return pl.pallas_call(
        project_first_kernel,
        in_specs=[SM, ANY, ANY, ANY, VM],
        out_specs=[ANY, VM],
        out_shape=[
            jax.ShapeDtypeStruct((3, 4 * block, half), bf16), pltpu.VMEM((3, width, half), bf16)
        ],
        scratch_shapes=project_scratch(block, width, half),
        compiler_params=params(50),
        cost_estimate=cost(*BRIEF),
        name="project_first",
    )(scalars, hidden, hidden2, weight, bias)


def project_second(scalars, cross, cross2, weight, bias, qkv):
    block, width = cross.shape
    half = width // 2
    return pl.pallas_call(
        project_second_kernel,
        in_specs=[SM, ANY, ANY, VM, VM, ANY],
        out_specs=ANY,
        out_shape=jax.ShapeDtypeStruct(qkv.shape, bf16),
        input_output_aliases={5: 0},
        scratch_shapes=project_scratch(block, width, half),
        compiler_params=params(50),
        cost_estimate=cost(*BRIEF),
        name="project_second",
    )(scalars, *near_core(cross, cross2, weight), bias, qkv)


def head_mask(shape, head, axis):
    return (lax.broadcasted_iota(jnp.int32, shape, axis) // 64) == head


def keep_head(array, head, axis):
    return jnp.where(head_mask(array.shape, head, axis), array, jnp.zeros_like(array))


def attend_kernel(
    core_ref, query, key, value, prefix_k, prefix_v, key_mask, query_mask,
    out_mine, out_other, exps_mine, exps_other, recips_mine, recips_other, keys, values_t,
):
    prefix = prefix_k.shape[0]
    tokens = query.shape[1]
    count = prefix + tokens
    chunk = tokens // 4
    keys[:prefix, :128] = prefix_k[...]
    keys[prefix:, :128] = key[0]

    @pl.when(pl.program_id(0) == 0)
    def _():
        keys[:, 128:] = key_mask[...]
        values_t[:, 64:, :] = jnp.ones((2, values_t.shape[1] - 64, count), bf16)

    prefix_t = prefix_v[...].astype(f32).T.astype(bf16)
    value_t = value[0].astype(f32).T.astype(bf16)
    for head in range(2):
        values_t[head, :64, :prefix] = prefix_t[64 * head : 64 * head + 64]
        values_t[head, :64, prefix:] = value_t[64 * head : 64 * head + 64]
    units = [(i, head) for i in (1, 3, 0, 2) for head in range(2)]

    def score(unit):
        i, head = unit
        rows = slice(i * chunk, (i + 1) * chunk)
        masked = jnp.concatenate([keep_head(query[0, rows, :], head, 1), query_mask[rows, :]], axis=1)
        return dot(keys[...], masked, 1, 1)

    ahead = 2
    pending = [score(unit) for unit in units[:ahead]]
    for n, (i, head) in enumerate(units):
        scores = pending.pop(0)
        if n + ahead < len(units):
            pending.append(score(units[n + ahead]))
        out, exps, recips = (
            (out_mine, exps_mine, recips_mine), (out_other, exps_other, recips_other)
        )[i % 2]
        cols = slice(i // 2 * chunk, (i // 2 + 1) * chunk)
        top = jnp.max(scores, axis=0, keepdims=True)
        weights = jnp.exp2(scores - top).astype(bf16)
        exps[0, head, :, cols] = weights
        summed = dot(values_t[head], weights)
        recip = 1.0 / summed[64:65, :]
        recips[0, head, :, cols] = jnp.broadcast_to(recip, (8, chunk))
        out[64 * head : 64 * head + 64, cols] = (summed[:64, :] * recip).astype(bf16)


def attend(core, qkv, prefix_keys, prefix_values, key_mask, query_mask):
    _, tokens, half = qkv.shape
    prefix = prefix_keys.shape[0]
    count = prefix + tokens
    pairs = half // 128
    prefix_spec = pl.BlockSpec((prefix, 128), lambda p, k: (0, k[0] * pairs + p))
    out_spec = pl.BlockSpec((128, tokens // 2), lambda p, k: (p, 0))
    exps_spec = pl.BlockSpec((1, 2, count, tokens // 2), lambda p, k: (p, 0, 0, 0))
    recips_spec = pl.BlockSpec((1, 2, 8, tokens // 2), lambda p, k: (p, 0, 0, 0))
    return pl.pallas_call(
        attend_kernel,
        grid_spec=pltpu.PrefetchScalarGridSpec(
            num_scalar_prefetch=1,
            grid=(pairs,),
            in_specs=[
                pl.BlockSpec((1, tokens, 128), lambda p, k, j=j: (j, 0, p)) for j in range(3)
            ]
            + [
                prefix_spec,
                prefix_spec,
                pl.BlockSpec((count, 128), lambda p, k: (0, 0)),
                pl.BlockSpec((tokens, 128), lambda p, k: (0, 0)),
            ],
            out_specs=[out_spec] * 2 + [exps_spec] * 2 + [recips_spec] * 2,
            scratch_shapes=[pltpu.VMEM((count, 256), bf16), pltpu.VMEM((2, 64 + 16, count), bf16)],
        ),
        out_shape=[jax.ShapeDtypeStruct((half, tokens // 2), bf16)] * 2
        + [jax.ShapeDtypeStruct((pairs, 2, count, tokens // 2), bf16)] * 2
        + [jax.ShapeDtypeStruct((pairs, 2, 8, tokens // 2), f32)] * 2,
        compiler_params=params(56),
        cost_estimate=cost(*BRIEF),
        name="attend",
    )(core, qkv, qkv, qkv, prefix_keys, prefix_values, key_mask, query_mask)


def ordered_rows(array):
    block = array.shape[0] // 4
    return [array[i * block : (i + 1) * block] for i in (0, 2, 1, 3)]


def attend_back_kernel(
    core_ref, query, key, value, prefix_k, prefix_v, exps_mine, exps_other, recips_mine, recips_other,
    attended_mine, attended_other, grad_mine, grad_other,
    out_mine, out_own2, out_cross2, out_prefix,
    keys, values, keys_t, slopes, queries, queries_t, scaled,
):
    prefix = prefix_k.shape[0]
    tokens = query.shape[1]
    chunk = tokens // 4
    half = tokens // 2
    keys[:prefix, :] = prefix_k[...]
    keys[prefix:, :] = key[0]
    values[:prefix, :] = prefix_v[...]
    values[prefix:, :] = value[0]
    keys_t[...] = keys[...].astype(f32).T.astype(bf16)
    queries[...] = jnp.concatenate(ordered_rows(query[0]), axis=0)
    spreads = []
    for head in range(2):
        rows = slice(64 * head, 64 * head + 64)
        parts = []
        for side, (recips, attended, grad) in enumerate(
            ((recips_mine, attended_mine, grad_mine), (recips_other, attended_other, grad_other))
        ):
            part = grad[rows, :].astype(f32) * recips[0, head, 0:1, :]
            scaled[rows, side * half : (side + 1) * half] = part.astype(bf16)
            parts.append(jnp.sum(part * attended[rows, :].astype(f32), axis=0, keepdims=True))
        spreads.append(jnp.concatenate(parts, axis=1))
    units = [(head, i) for head in range(2) for i in range(4)]

    def head_rows(array, head):
        zeros = jnp.zeros_like(array[:64])
        return jnp.concatenate([array[:64], zeros] if head == 0 else [zeros, array[64:]], axis=0)

    def grad_probs(unit):
        head, i = unit
        return dot(values[...], head_rows(scaled[:, i * chunk : (i + 1) * chunk], head))

    def exps_of(head, i):
        return (exps_mine, exps_other)[i // 2][0, head, :, i % 2 * chunk : (i % 2 + 1) * chunk]

    def value_part(head):
        total = None
        for side, exps in enumerate((exps_mine, exps_other)):
            cols = slice(side * half, (side + 1) * half)
            part = dot(exps[0, head], head_rows(scaled[:, cols], head), 1, 1)
            total = part if total is None else total + part
        return total

    def key_part(head):
        return dot(slopes[head], keep_head(queries[...], head, 1))

    ahead = 4
    pending = [grad_probs(unit) for unit in units[:ahead]]
    for n, (head, i) in enumerate(units):
        grads = pending.pop(0)
        if n + ahead < len(units):
            pending.append(grad_probs(units[n + ahead]))
        cols = slice(i * chunk, (i + 1) * chunk)
        slopes[head, :, cols] = (
            exps_of(head, i).astype(f32) * (grads - spreads[head][:, cols])
        ).astype(bf16)
        if n == 0:
            value_first = value_part(0)
        rows = slice(64 * head, 64 * head + 64)
        queries_t[rows, cols] = dot(keys_t[rows, :], slopes[head, :, cols]) * 0.125
        if n == 4:
            key_first = key_part(0)
    value_grads = value_first + value_part(1)
    key_grads = (key_first + key_part(1)) * ln_2
    out_prefix[0] = key_grads[:prefix]
    out_prefix[1] = value_grads[:prefix]
    query_grads = queries_t[...].T.astype(bf16)
    for j, parts in enumerate(
        ([query_grads[i * chunk : (i + 1) * chunk] for i in range(4)],)
        + tuple(ordered_rows(array[prefix:].astype(bf16)) for array in (key_grads, value_grads))
    ):
        out_mine[j, :chunk] = parts[0]
        out_mine[j, chunk:] = parts[1]
        out_own2[j] = parts[2]
        out_cross2[j] = parts[3]


def attend_back(core, qkv, prefix_keys, prefix_values, exps, recips, attended, grads):
    _, tokens, half = qkv.shape
    prefix = prefix_keys.shape[0]
    count = prefix + tokens
    pairs = half // 128
    prefix_spec = pl.BlockSpec((prefix, 128), lambda p, k: (0, k[0] * pairs + p))
    exps_spec = pl.BlockSpec((1, 2, count, tokens // 2), lambda p, k: (p, 0, 0, 0))
    recips_spec = pl.BlockSpec((1, 2, 8, tokens // 2), lambda p, k: (p, 0, 0, 0))
    heads_spec = pl.BlockSpec((128, tokens // 2), lambda p, k: (p, 0))
    rows = (tokens // 2, tokens // 4, tokens // 4)
    return pl.pallas_call(
        attend_back_kernel,
        grid_spec=pltpu.PrefetchScalarGridSpec(
            num_scalar_prefetch=1,
            grid=(pairs,),
            in_specs=[
                pl.BlockSpec((1, tokens, 128), lambda p, k, j=j: (j, 0, p)) for j in range(3)
            ]
            + [prefix_spec] * 2
            + [exps_spec] * 2
            + [recips_spec] * 2
            + [heads_spec] * 4,
            out_specs=[pl.BlockSpec((3, n, 128), lambda p, k: (0, 0, p)) for n in rows]
            + [pl.BlockSpec((2, prefix, 128), lambda p, k: (0, 0, p))],
            scratch_shapes=[
                pltpu.VMEM((count, 128), bf16),
                pltpu.VMEM((count, 128), bf16),
                pltpu.VMEM((128, count), bf16),
                pltpu.VMEM((2, count, tokens), bf16),
                pltpu.VMEM((tokens, 128), bf16),
                pltpu.VMEM((128, tokens), f32),
                pltpu.VMEM((128, tokens), bf16),
            ],
        ),
        out_shape=[pltpu.VMEM((3, rows[0], half), bf16)]
        + [jax.ShapeDtypeStruct((3, n, half), bf16) for n in rows[1:]]
        + [jax.ShapeDtypeStruct((2, prefix, half), f32)],
        compiler_params=params(46),
        cost_estimate=cost(*BRIEF),
        name="attend_back",
    )(core, qkv, qkv, qkv, prefix_keys, prefix_values, *exps, *recips, *attended, *grads)


def mean_rows(array):
    return jnp.mean(array, axis=-1, keepdims=True)


def unit_norm(array):
    centered = array - mean_rows(array)
    inverse = lax.rsqrt(mean_rows(centered * centered) + epsilon)
    return centered * inverse, inverse


def norm_back(scaled, unit, inverse):
    return inverse * (scaled - mean_rows(scaled) - unit * mean_rows(scaled * unit))


def gelu_both(hidden):
    gate = 0.5 * (1.0 + lax.erf(hidden * root_half))
    slope = gate + hidden * inverse_root * jnp.exp(-0.5 * hidden * hidden)
    return (hidden * gate).astype(bf16), slope.astype(bf16)


def feed_forward(steps, total):
    hidden = None
    for i, step in enumerate(steps):
        if i == 0:
            wait_all(step[3])
            hidden = step[0]()
        following = None
        if i + 1 < len(steps):
            wait_all(steps[i + 1][3])
            following = steps[i + 1][0]()
        active, slope = gelu_both(hidden)
        step[1](slope)
        part = dot(active, step[2]())
        if total is None:
            total = part
        elif hasattr(total, "at"):
            total[...] += part
        hidden = following


def forward_kernel(
    core_ref, mine, other, own, cross, output_bias, first_gain, first_shift, output_weight,
    expand_own, expand_sib, reduce_own, reduce_sib, bias_own, bias_sib,
    unit_out, inverse_out, total_out, slope_out, low,
    out_w, expand_w, reduce_w, own_v, sems,
):
    core, chip = core_ref[0], core_ref[1]
    copies = [
        pltpu.make_async_copy(output_weight, out_w, sems.at[0]),
        pltpu.make_async_copy(expand_own, expand_w.at[0], sems.at[1]),
        pltpu.make_async_copy(reduce_own, reduce_w.at[0], sems.at[2]),
        pltpu.make_async_copy(expand_sib, expand_w.at[1], sems.at[3]),
        pltpu.make_async_copy(reduce_sib, reduce_w.at[1], sems.at[4]),
        pltpu.make_async_copy(own.at[chip], own_v, sems.at[5]),
    ]
    start_all(copies[5:] + copies[:5])
    copies[5].wait()
    copies[0].wait()
    half = mine.shape[0]
    block = own_v.shape[0]
    output_row, gain, shift = (
        ref[...].astype(f32).reshape(1, -1) for ref in (output_bias, first_gain, first_shift)
    )
    for i, ref in enumerate((own_v, cross)):
        rows = slice(i * block, (i + 1) * block)
        branch = dot(mine[:, rows], out_w[pl.ds(pl.multiple_of(core * half, half), half), :], 0, 0)
        branch += dot(
            other[:, rows], out_w[pl.ds(pl.multiple_of((1 - core) * half, half), half), :], 0, 0
        )
        unit, inverse = unit_norm(ref[...].astype(f32) + (branch + output_row))
        unit_out[rows, :] = unit
        inverse_out[rows, :] = jnp.broadcast_to(inverse, (block, 128))
        low[rows, :] = (unit * gain + shift).astype(bf16)
    chunk = 512
    hidden_here = expand_own.shape[1]

    def step(i, bias, start):
        cols = slice(start, start + chunk)

        def store(slope):
            slope_out[:, i * hidden_here + start : i * hidden_here + start + chunk] = slope

        return (
            lambda: dot(low[...], expand_w[i, :, cols]) + bias[cols].astype(f32).reshape(1, chunk),
            store,
            lambda: reduce_w[i, cols, :],
            copies[1 + 2 * i : 3 + 2 * i] if start == 0 else [],
        )

    total_out[...] = jnp.zeros(total_out.shape, f32)
    feed_forward(
        [
            step(i, bias, start)
            for i, bias in enumerate((bias_own, bias_sib))
            for start in range(0, hidden_here, chunk)
        ],
        total_out,
    )


def forward(core, mine, other, own, cross, vectors, output_weight, weights):
    tokens = mine.shape[1]
    _, block, width = own.shape
    hidden = weights[0].shape[1]
    return pl.pallas_call(
        forward_kernel,
        in_specs=[SM, VM, VM, ANY] + [VM] * 4 + [ANY] * 5 + [VM] * 2,
        out_specs=[VM] * 5,
        out_shape=[
            jax.ShapeDtypeStruct((tokens, width), f32),
            jax.ShapeDtypeStruct((tokens, 128), f32),
            jax.ShapeDtypeStruct((tokens, width), f32),
            jax.ShapeDtypeStruct((tokens, 2 * hidden), bf16),
            jax.ShapeDtypeStruct((tokens, width), bf16),
        ],
        scratch_shapes=[
            pltpu.VMEM((width, width), bf16),
            pltpu.VMEM((2, width, hidden), bf16),
            pltpu.VMEM((2, hidden, width), bf16),
            pltpu.VMEM((block, width), bf16),
            pltpu.SemaphoreType.DMA((6,)),
        ],
        compiler_params=params(36),
        cost_estimate=cost(*BRIEF),
        name="forward",
    )(core, mine, other, own, cross, *vectors, output_weight, *weights)


def piece_copies(copies, pieces, place, quarter, expand_r, reduce_r, bias_r):
    width = expand_r.shape[0]
    result = []
    for i, piece in enumerate(pieces):
        here = pl.ds((place + i) * quarter, quarter)
        group = []
        for j in range(width // quarter):
            rows = pl.ds(j * quarter, quarter)
            group.append(copies(piece.at[pl.ds(0, quarter), rows], expand_r.at[rows, here]))
        group.append(copies(piece.at[pl.ds(quarter + 16, quarter)], reduce_r.at[here]))
        if bias_r is not None:
            group.append(copies(piece.at[pl.ds(quarter, 16)], bias_r.at[i]))
        result.append(group)
    return result


def piece_steps(count, place, quarter, low, expand_r, reduce_r, bias_r, slope_out, waits):
    def step(first, n):
        rows = slice((place + first) * quarter, (place + first + n) * quarter)

        def hidden():
            bias = [bias_r[first + i, 0:1, :quarter] for i in range(n)]
            bias = bias[0] if n == 1 else jnp.concatenate(bias, axis=1)
            return dot(low[...], expand_r[:, rows]) + bias.astype(f32)

        def store(slope):
            slope_out[:, first * quarter : (first + n) * quarter] = slope

        return (
            hidden,
            store,
            lambda: reduce_r[rows, :],
            [copy for i in range(n) for copy in waits[first + i]],
        )

    return [step(first, min(2, count - first)) for first in range(0, count, 2)]


def remote_kernel(count, *refs):
    low_in, total_in = refs[:2]
    pieces = refs[2 : 2 + count]
    total_out, slope_out, low, expand_r, reduce_r, bias_r, sems = refs[2 + count :]
    quarter = reduce_r.shape[0] // count
    copies = Copies(sems)
    first = [copies(low_in, low), copies(total_in, total_out)]
    waits = piece_copies(copies, pieces, 0, quarter, expand_r, reduce_r, bias_r)
    start_all(first[:1] + waits[0] + waits[1] + first[1:])
    for group in waits[2:]:
        start_all(group)
    steps = piece_steps(count, 0, quarter, low, expand_r, reduce_r, bias_r, slope_out, waits)
    steps[0] = steps[0][:3] + (first + steps[0][3],)
    feed_forward(steps, total_out)


def remote(low, total, pieces, quarter):
    tokens, width = total.shape
    count = len(pieces)
    return pl.pallas_call(
        functools.partial(remote_kernel, count),
        in_specs=[ANY] * (2 + count),
        out_specs=[VM] * 2,
        out_shape=[
            pltpu.VMEM((tokens, width), f32),
            pltpu.VMEM((tokens, count * quarter), bf16),
        ],
        scratch_shapes=[
            pltpu.VMEM((tokens, width), bf16),
            pltpu.VMEM((width, count * quarter), bf16),
            pltpu.VMEM((count * quarter, width), bf16),
            pltpu.VMEM((count, 16, width), bf16),
            pltpu.SemaphoreType.DMA((2 + count * (width // quarter + 2),)),
        ],
        compiler_params=params(26),
        cost_estimate=cost(*BRIEF),
        name="remote",
    )(low, total, *pieces)


def middle_kernel(early, late, *refs):
    count = early + late
    scalars, query_mask = refs[:2]
    vectors = refs[2:7]
    low_in, unit_in, inverse, total_in, slope_in, slope2_in, upstream = refs[7:14]
    output_weight, expand_own, expand_sib, reduce_own, reduce_sib = refs[14:19]
    pieces = refs[19 : 19 + count]
    hidden_own, hidden_cross, grad_out, att_mine, att_other = refs[19 + count : 24 + count]
    (
        out_w, expand_w, reduce_w, expand_r, reduce_r, bias_r, low, unit, acc, back_acc,
        slope_l, slope_e, slope_s, up, hidden, sems,
    ) = refs[24 + count :]
    core, chip = scalars[0], scalars[1]
    copies = Copies(sems)
    tokens, width = unit.shape
    block = tokens // 2
    quarter = reduce_r.shape[0] // count
    chunk = 2 * quarter
    hidden_here = expand_own.shape[1]
    rows_of = [pl.ds(i * block, block) for i in range(2)]

    up_cross = pieces[early + 2].at[pl.ds(2 * quarter + 16, block)]
    low_copy = copies(low_in, low)
    late_waits = piece_copies(copies, pieces[early:], early, quarter, expand_r, reduce_r, bias_r)
    norm_copies = [
        [
            copies(total_in.at[rows_of[i]], acc.at[rows_of[i]]),
            copies(unit_in.at[rows_of[i]], unit.at[rows_of[i]]),
            copies((upstream.at[chip], up_cross)[i], up.at[rows_of[i]]),
        ]
        for i in range(2)
    ]
    local_copies = [
        [copies((reduce_own, reduce_sib)[i], reduce_w.at[i]), copies((expand_own, expand_sib)[i], expand_w.at[i])]
        for i in range(2)
    ]
    slope_copy = copies(slope_in, slope_l)
    early_copies = piece_copies(copies, pieces[:early], 0, quarter, expand_r, reduce_r, None)
    slope2_copy = copies(slope2_in, slope_e)
    out_copy = copies(output_weight, out_w)
    start_all([low_copy] + [copy for group in late_waits + norm_copies for copy in group])
    start_all([local_copies[0][0], slope_copy, local_copies[0][1]] + local_copies[1])
    start_all([copy for group in early_copies for copy in group] + [slope2_copy, out_copy])

    steps = piece_steps(late, early, quarter, low, expand_r, reduce_r, bias_r, slope_s, late_waits)
    steps[0] = steps[0][:3] + ([low_copy] + steps[0][3],)
    for group in norm_copies:
        wait_all(group[:1])
    feed_forward(steps, acc)

    first_gain, first_shift, reduce_bias, second_gain, second_shift = (
        ref[...].astype(f32).reshape(1, -1) for ref in vectors
    )
    hidden_copies = []
    for i in range(2):
        wait_all(norm_copies[i][1:])
        for start in range(i * block, (i + 1) * block, block // 2):
            rows = slice(start, start + block // 2)
            masked = slice(2 * i * block + start - i * block, 2 * i * block + start - i * block + block // 2)
            live = 1.0 - query_mask[masked, PAIRS : PAIRS + 1].astype(f32)
            first_norm = unit[rows, :] * first_gain + first_shift
            unit2, inverse2 = unit_norm(first_norm + (acc[rows, :] + reduce_bias))
            hidden[rows, :] = ((unit2 * second_gain + second_shift) * live).astype(bf16)
            grad_feed = norm_back(up[rows, :].astype(f32) * live * second_gain, unit2, inverse2)
            back_acc[rows, :] = grad_feed
            low[rows, :] = grad_feed.astype(bf16)
        copy = copies(hidden.at[rows_of[i]], (hidden_own.at[chip], hidden_cross)[i])
        copy.start()
        hidden_copies.append(copy)

    backs = []
    for i in range(2):
        for start in range(0, hidden_here, chunk):
            cols = slice(start, start + chunk)
            place = slice(i * hidden_here + start, i * hidden_here + start + chunk)
            backs.append(
                (
                    lambda i=i, cols=cols: reduce_w[i, cols, :],
                    lambda i=i, cols=cols: expand_w[i, :, cols],
                    1,
                    lambda place=place: slope_l[:, place],
                    ([slope_copy] if i + start == 0 else []) + (local_copies[i] if start == 0 else []),
                )
            )
    total_pieces = early + late
    for first in range(0, total_pieces, 2):
        rows = slice(first * quarter, (first + 2) * quarter)

        def slopes(first=first):
            parts = [
                slope_e[:, j * quarter : (j + 1) * quarter]
                if j < early
                else slope_s[:, (j - early) * quarter : (j - early + 1) * quarter]
                for j in (first, first + 1)
            ]
            return jnp.concatenate(parts, axis=1)

        waits = [copy for j in (first, first + 1) if j < early for copy in early_copies[j]]
        backs.append(
            (
                lambda rows=rows: reduce_r[rows, :],
                lambda rows=rows: expand_r[:, rows],
                1,
                slopes,
                ([slope2_copy] if first == 0 else []) + waits,
            )
        )

    def grads(step):
        wait_all(step[4])
        return dot(low[...], step[0](), 1, 1)

    grad = grads(backs[0])
    for i, step in enumerate(backs):
        following = grads(backs[i + 1]) if i + 1 < len(backs) else None
        back = (grad * step[3]().astype(f32)).astype(bf16)
        back_acc[...] += dot(back, step[1](), 1, step[2])
        grad = following

    grad_copies = []
    for i in range(2):
        for start in range(i * block, (i + 1) * block, block // 2):
            rows = slice(start, start + block // 2)
            grad = norm_back(back_acc[rows, :] * first_gain, unit[rows, :], inverse[rows, 0:1])
            acc[rows, :] = grad
            low[rows, :] = grad.astype(bf16)
        copy = copies(acc.at[rows_of[i]], grad_out.at[rows_of[i]])
        copy.start()
        grad_copies.append(copy)
    out_copy.wait()
    half = width // 2
    att_other[...] = dot(
        out_w[pl.ds(pl.multiple_of((1 - core) * half, half), half), :], low[...], 1, 1
    ).astype(bf16)
    att_mine[...] = dot(
        out_w[pl.ds(pl.multiple_of(core * half, half), half), :], low[...], 1, 1
    ).astype(bf16)
    wait_all(hidden_copies + grad_copies)


def middle(scalars, query_mask, vectors, saved, upstream, output_weight, weights, early, late):
    tokens, width = saved[1].shape
    block = tokens // 2
    hidden = weights[0].shape[1]
    quarter = hidden // 4
    pieces = early + late
    count = len(pieces)
    return pl.pallas_call(
        functools.partial(middle_kernel, len(early), len(late)),
        in_specs=[SM] + [VM] * 6 + [ANY] * 2 + [VM] + [ANY] * (9 + count),
        out_specs=[ANY] * 3 + [VM] * 2,
        out_shape=[
            jax.ShapeDtypeStruct(upstream.shape, bf16),
            jax.ShapeDtypeStruct((block, width), bf16),
            jax.ShapeDtypeStruct((tokens, width), f32),
            pltpu.VMEM((width // 2, tokens), bf16),
            pltpu.VMEM((width // 2, tokens), bf16),
        ],
        scratch_shapes=[
            pltpu.VMEM((width, width), bf16),
            pltpu.VMEM((2, width, hidden), bf16),
            pltpu.VMEM((2, hidden, width), bf16),
            pltpu.VMEM((width, count * quarter), bf16),
            pltpu.VMEM((count * quarter, width), bf16),
            pltpu.VMEM((len(late), 16, width), bf16),
            pltpu.VMEM((tokens, width), bf16),
            pltpu.VMEM((tokens, width), f32),
            pltpu.VMEM((tokens, width), f32),
            pltpu.VMEM((tokens, width), f32),
            pltpu.VMEM((tokens, 2 * hidden), bf16),
            pltpu.VMEM((tokens, len(early) * quarter), bf16),
            pltpu.VMEM((tokens, len(late) * quarter), bf16),
            pltpu.VMEM((tokens, width), bf16),
            pltpu.VMEM((tokens, width), bf16),
            pltpu.SemaphoreType.DMA((18 + count * (width // quarter + 2),)),
        ],
        compiler_params=params(42),
        cost_estimate=cost(*BRIEF),
        name="middle",
    )(
        scalars, query_mask, *vectors, *saved, upstream, output_weight, *weights,
        *pieces,
    )


def project_back_rows(core, copies, place, mine, other, grad_branch, weight, left, weight_v, grad, out):
    rows, width = out.shape
    half = other.shape[2]
    parts = 4
    step = width // parts
    here = pl.ds(place * rows, rows)
    left_copies = [
        copy
        for j in range(3)
        for copy in (
            copies(mine.at[j, here], left.at[:, columns_at((2 * j + core) * half, half)]),
            copies(other.at[j], left.at[:, columns_at((2 * j + 1 - core) * half, half)]),
        )
    ]
    weight_copies = [
        copies(weight.at[pl.ds(i * step, step)], weight_v.at[pl.ds(i * step, step)])
        for i in range(parts)
    ]
    grad_copy = copies(grad_branch.at[here], grad)
    start_all(left_copies + weight_copies[:1] + [grad_copy] + weight_copies[1:])
    wait_all(left_copies)
    for i in range(parts):
        cols = slice(i * step, (i + 1) * step)
        weight_copies[i].wait()
        total = dot(left[...], weight_v[cols, :], 1, 1)
        if i == 0:
            grad_copy.wait()
        out[:, cols] = (grad[:, cols] + total).astype(bf16)


def project_back_cross_kernel(
    scalars, mine, other, grad_branch, weight, out, left, weight_v, grad, sems
):
    project_back_rows(
        scalars[0], Copies(sems), 1, mine, other, grad_branch, weight, left, weight_v, grad, out
    )


def project_back_own_kernel(
    scalars, mine, other, grad_branch, weight, theirs, _, out, hidden_out,
    left, weight_v, grad, theirs_v, sems,
):
    core, chip = scalars[0], scalars[1]
    copies = Copies(sems)
    theirs_in = copies(theirs, theirs_v)
    theirs_out = copies(theirs_v, hidden_out.at[1 - chip])
    theirs_in.start()
    theirs_in.wait()
    theirs_out.start()
    project_back_rows(core, copies, 0, mine, other, grad_branch, weight, left, weight_v, grad, out)
    theirs_out.wait()


def project_back_scratch(rows, weight):
    width, columns = weight.shape
    return [
        pltpu.VMEM((rows, columns), bf16),
        pltpu.VMEM((width, columns), bf16),
        pltpu.VMEM((rows, width), f32),
    ]


def project_back_cross(scalars, mine, other, grad_branch, weight):
    _, rows, _ = other.shape
    return pl.pallas_call(
        project_back_cross_kernel,
        in_specs=[SM] + [ANY] * 4,
        out_specs=VM,
        out_shape=jax.ShapeDtypeStruct((rows, weight.shape[0]), bf16),
        scratch_shapes=project_back_scratch(rows, weight) + [pltpu.SemaphoreType.DMA((11,))],
        compiler_params=params(20),
        cost_estimate=cost(*BRIEF),
        name="project_back_cross",
    )(scalars, mine, other, grad_branch, weight)


def project_back_own(scalars, mine, other, grad_branch, weight, theirs, hidden_out):
    _, rows, _ = other.shape
    width = weight.shape[0]
    return pl.pallas_call(
        project_back_own_kernel,
        in_specs=[SM] + [ANY] * 6,
        out_specs=[VM, ANY],
        out_shape=[
            jax.ShapeDtypeStruct((rows, width), bf16),
            jax.ShapeDtypeStruct(hidden_out.shape, bf16),
        ],
        input_output_aliases={6: 1},
        scratch_shapes=project_back_scratch(rows, weight)
        + [pltpu.VMEM((rows, width), bf16), pltpu.SemaphoreType.DMA((13,))],
        compiler_params=params(20),
        cost_estimate=cost(*BRIEF),
        name="project_back_own",
    )(scalars, mine, other, grad_branch, weight, theirs, hidden_out)


def shards(
    sizes,
    hidden_in,
    pair_lengths,
    prefix_keys,
    prefix_values,
    project_weight,
    project_bias,
    output_weight,
    output_bias,
    first_gain,
    first_shift,
    expand_weight,
    expand_bias,
    reduce_weight,
    reduce_bias,
    second_gain,
    second_shift,
    upstream,
):
    dp_size, mp_size = sizes
    rows_here, shard_len, width = hidden_in.shape
    hidden_here = expand_weight.shape[1]
    prefix = prefix_keys.shape[0]
    half = width // 2
    place = lax.axis_index("mp")
    chip, core = place // 2, place % 2
    part = lax.axis_index("dp") % 4
    scalars = jnp.stack([core, chip, part]).astype(jnp.int32)

    def across(array):
        return swap(array, "mp", 2, mp_size)

    def beside(array):
        return swap(array, "mp", 1, mp_size)

    def take(array, index):
        return lax.dynamic_index_in_dim(array, index, 0, keepdims=False)

    def row(vector):
        return vector.reshape(1, -1)

    cross = across(take(hidden_in, 1 - chip))
    hidden2 = beside(hidden_in)

    boundary = jnp.cumsum(take(pair_lengths, chip))
    blocks = jnp.stack(
        [2 * chip + core, 2 * chip + 1 - core, 2 * (1 - chip) + core, 2 * (1 - chip) + 1 - core]
    )
    position = (
        blocks[:, None] * shard_len + jnp.arange(shard_len, dtype=jnp.int32)[None, :]
    ).reshape(-1)
    segment = jnp.sum((position[:, None] >= boundary[None, :]).astype(jnp.int32), axis=1)
    column = jnp.arange(128, dtype=jnp.int32)[None, :]
    query_mask = (segment[:, None] == column).astype(bf16)
    key_mask = jnp.where(
        (segment[:, None] == column) & (column < PAIRS), 0.0, masked_score
    ).astype(bf16)
    key_mask = jnp.concatenate([jnp.zeros((prefix, 128), bf16), key_mask], 0)

    pack0, pack3 = pack(scalars, expand_weight, reduce_weight, expand_bias, upstream)
    qkv, core_weight = project_first(scalars, hidden_in, hidden2, project_weight, project_bias)
    expand_sib, reduce_sib, bias_sib = beside(expand_weight), beside(reduce_weight), beside(expand_bias)
    cross, qkv, key_mask, query_mask, expand_sib, reduce_sib, bias_sib = lax.optimization_barrier(
        (cross, qkv, key_mask, query_mask, expand_sib, reduce_sib, bias_sib)
    )
    cross2 = beside(cross)
    piece0, piece3 = across(pack0), across(pack3)
    qkv = project_second(scalars, cross, cross2, core_weight, project_bias, qkv)
    attended_mine, attended_other, exps_mine, exps_other, recips_mine, recips_other = attend(
        scalars, qkv, prefix_keys, prefix_values, key_mask, query_mask
    )
    piece0, attended_other = lax.optimization_barrier((piece0, attended_other))
    piece1, piece2 = swap(piece0, "dp", 1, dp_size), swap(piece0, "dp", 2, dp_size)
    attended_here, piece0_sib = beside(attended_other), beside(piece0)
    attended_here, piece0_sib = lax.optimization_barrier((attended_here, piece0_sib))
    weights = tuple(
        far_core(array) for array in (expand_weight, expand_sib, reduce_weight, reduce_sib)
    )
    unit, inverse, total, slope, low = forward(
        scalars, attended_mine, attended_here, hidden_in, cross,
        (output_bias, first_gain, first_shift), output_weight, weights + (expand_bias, bias_sib),
    )
    piece1, piece2, piece3, low = lax.optimization_barrier((piece1, piece2, piece3, low))
    early = [piece0, piece0_sib, piece1, piece2]
    late = [beside(piece1), beside(piece2), piece3, beside(piece3)]
    total, slope2 = remote(low, total, early, hidden_here // 4)
    *late, total = lax.optimization_barrier((*late, total))
    total, slope2 = near_core(total, slope2)
    late = list(near_core(*late))
    hidden_own, hidden_cross, grad_branch, grad_mine, grad_theirs = middle(
        scalars, query_mask, (first_gain, first_shift, reduce_bias, second_gain, second_shift),
        (low, unit, inverse, total, slope, slope2), upstream, output_weight, weights, early, late,
    )
    grad_here = beside(grad_theirs)
    exps, recips = (exps_mine, exps_other), (recips_mine, recips_other)

    hidden_theirs = across(hidden_cross)
    back_mine, back_own2, back_cross2, grad_prefix = attend_back(
        scalars, qkv, prefix_keys, prefix_values, exps, recips, (attended_mine, attended_other),
        near_core(grad_mine, grad_here),
    )
    back_mine, back_own2, back_cross2, grad_prefix, hidden_theirs = lax.optimization_barrier(
        (back_mine, back_own2, back_cross2, grad_prefix, hidden_theirs)
    )

    def step(array, dp_bit, mp_bit):
        return lax.ppermute(
            array, ("dp", "mp"),
            [
                (d * mp_size + m, (d ^ dp_bit) * mp_size + (m ^ mp_bit))
                for d in range(dp_size)
                for m in range(mp_size)
            ],
        )

    def four_sum(parts):
        own_part, first, second, both = (part.astype(f32) for part in parts)
        return (own_part + first) + (second + both)

    cross_there = beside(back_cross2)
    own_there = beside(back_own2)
    low_prefix = grad_prefix.astype(bf16)
    group = (low_prefix, step(low_prefix, 0, 2), step(low_prefix, 2, 0), step(low_prefix, 2, 2))
    back_mine, cross_there = near_core(back_mine, cross_there)
    last_weight, grad_branch = far_core(project_weight), far_core(grad_branch)
    in_cross = project_back_cross(scalars, back_mine, cross_there, grad_branch, last_weight)
    in_cross, group = lax.optimization_barrier((in_cross, group))
    in_cross = across(in_cross)
    grad_prefix = four_sum(group)
    bit = 8
    while bit < dp_size:
        grad_prefix = grad_prefix + swap(grad_prefix, "dp", bit, dp_size)
        bit *= 2
    low_prefix = grad_prefix.astype(bf16)
    group = (low_prefix, step(low_prefix, 1, 0), step(low_prefix, 4, 0), step(low_prefix, 5, 0))
    in_own, hidden_out = project_back_own(
        scalars, back_mine, own_there, grad_branch, last_weight, far_core(hidden_theirs), hidden_own
    )
    in_own, in_cross, group = lax.optimization_barrier((in_own, in_cross, group))
    grad_in = jnp.where(chip == 0, jnp.stack([in_own, in_cross]), jnp.stack([in_cross, in_own]))
    grad_prefix = four_sum(group)
    grad_prefix_sib = beside(grad_prefix)
    grad_prefix = jnp.where(
        core == 0,
        jnp.concatenate([grad_prefix, grad_prefix_sib], 2),
        jnp.concatenate([grad_prefix_sib, grad_prefix], 2),
    )
    return (hidden_out, grad_in, grad_prefix[0], grad_prefix[1])


def solution(mesh):
    placed = (
        P("dp", "mp", None),
        P("dp", None),
        P(),
        P(),
        P(),
        P(),
        P(),
        P(),
        P(),
        P(),
        P(None, "mp"),
        P("mp"),
        P("mp", None),
        P(),
        P(),
        P(),
        P("dp", "mp", None),
    )
    return jax.shard_map(
        functools.partial(shards, (mesh.shape["dp"], mesh.shape["mp"])),
        mesh=mesh,
        in_specs=placed,
        out_specs=(P("dp", "mp", None), P("dp", "mp", None), P(), P()),
        check_vma=False,
    )
```

```python
import functools

import jax
import jax.numpy as jnp
from jax import lax
from jax.experimental import pallas as pl
from jax.experimental.pallas import tpu as pltpu
from jax.sharding import PartitionSpec as P

HEADS = 16
PAIRS = 8

epsilon = 1e-05
masked_score = -1e30
root_half = 0.7071067811865476
inverse_root = 0.3989422804014327
log2_e = 1.4426950408889634
ln_2 = 0.6931471805599453

bf16 = jnp.bfloat16
f32 = jnp.float32


def dot(left, right, left_dim=1, right_dim=0):
    return lax.dot_general(
        left, right, (((left_dim,), (right_dim,)), ((), ())), preferred_element_type=f32
    )


def params(mebibytes):
    return pltpu.CompilerParams(vmem_limit_bytes=mebibytes * 2**20)


def cost(flops, bytes_accessed, transcendentals=0):
    return pl.CostEstimate(
        flops=int(flops), bytes_accessed=int(bytes_accessed), transcendentals=int(transcendentals)
    )


ANY = pl.BlockSpec(memory_space=pl.ANY)


def far_core(array):
    return pltpu.with_memory_space_constraint(array, pltpu.HBM)


def near_core(*arrays):
    return tuple(pltpu.with_memory_space_constraint(array, pltpu.VMEM) for array in arrays)


VM = pl.BlockSpec(memory_space=pltpu.VMEM)
SM = pl.BlockSpec(memory_space=pltpu.SMEM)
BRIEF = (1e6, 1e5)


def swap(array, axis, bit, size):
    return lax.ppermute(array, axis, [(i, i ^ bit) for i in range(size)])


class Copies:
    def __init__(self, sems):
        self.sems, self.used = sems, 0

    def __call__(self, source, target):
        copy = pltpu.make_async_copy(source, target, self.sems.at[self.used])
        self.used += 1
        return copy


def start_all(copies):
    for copy in copies:
        copy.start()


def wait_all(copies):
    for copy in copies:
        copy.wait()


def columns_at(start, size):
    return pl.ds(pl.multiple_of(start, size), size)


def project_tokens(core, copies, parts, weight, weight_copies, bias, out, place, tokens_v, out_v):
    block = parts[0].shape[-2]
    half = out.shape[2]
    token_copies = [
        copies(part, tokens_v.at[pl.ds(i * block, block)]) for i, part in enumerate(parts)
    ]
    start_all(token_copies)
    start_all(weight_copies)
    wait_all(token_copies)
    out_copies = []
    for j in range(3):
        wait_all(weight_copies[j : j + 1])
        shift = jnp.where(
            core == 0,
            bias[2 * j * half : (2 * j + 1) * half].astype(f32),
            bias[(2 * j + 1) * half : (2 * j + 2) * half].astype(f32),
        )
        result = dot(tokens_v[...], weight[j]) + shift.reshape(1, half)
        if j == 0:
            result = result * (log2_e * 0.125)
        out_v[j] = result.astype(bf16)
        copy = copies(out_v.at[j], out.at[j, pl.ds(place * 2 * block, 2 * block)])
        copy.start()
        out_copies.append(copy)
    return out_copies


def pack_kernel(scalars, expand, reduce, hidden_bias, upstream, pack0, pack3, packs, bias_v, sems):
    chip, part = scalars[1], scalars[2]
    copies = Copies(sems)
    width, hidden_here = expand.shape
    quarter = hidden_here // 4
    bias_v[...] = jnp.broadcast_to(
        hidden_bias[...].astype(f32).reshape(1, hidden_here), (16, hidden_here)
    ).astype(bf16)
    groups = []
    for n, index in enumerate((part, 3 - part)):
        pack = packs.at[n]
        columns = columns_at(index * quarter, quarter)
        group = []
        for i in range(width // quarter):
            block = pl.ds(i * quarter, quarter)
            group.append(copies(expand.at[block, columns], pack.at[pl.ds(0, quarter), block]))
        group.append(copies(reduce.at[columns], pack.at[pl.ds(quarter, quarter)]))
        groups.append(group)
    groups[0].append(copies(bias_v, packs.at[0, pl.ds(2 * quarter, 16), pl.ds(0, hidden_here)]))
    groups[1].append(
        copies(upstream.at[1 - chip], packs.at[1, pl.ds(2 * quarter, upstream.shape[1])])
    )
    for group in groups:
        start_all(group)
    out_copies = []
    for n, (group, out) in enumerate(zip(groups, (pack0, pack3))):
        wait_all(group)
        copy = copies(packs.at[n, pl.ds(0, out.shape[0])], out)
        copy.start()
        out_copies.append(copy)
    wait_all(out_copies)


def pack(scalars, expand, reduce, hidden_bias, upstream):
    width, hidden_here = expand.shape
    quarter = hidden_here // 4
    packs = [
        jax.ShapeDtypeStruct((2 * quarter + n, width), bf16) for n in (16, upstream.shape[1])
    ]
    return pl.pallas_call(
        pack_kernel,
        in_specs=[SM, ANY, ANY, VM, ANY],
        out_specs=[ANY] * 2,
        out_shape=packs,
        scratch_shapes=[
            pltpu.VMEM((2, *packs[1].shape), bf16),
            pltpu.VMEM((16, hidden_here), bf16),
            pltpu.SemaphoreType.DMA((2 * (width // quarter + 2) + 2,)),
        ],
        compiler_params=params(56),
        cost_estimate=cost(*BRIEF),
        name="pack",
    )(scalars, expand, reduce, hidden_bias, upstream)


def project_first_kernel(
    scalars, hidden, hidden2, weight, bias, out, weight_out, tokens_v, out_v, sems
):
    core, chip = scalars[0], scalars[1]
    copies = Copies(sems)
    half = out.shape[2]
    weight_copies = [
        copies(weight.at[:, columns_at((2 * j + core) * half, half)], weight_out.at[j])
        for j in range(3)
    ]
    wait_all(
        project_tokens(
            core, copies, (hidden.at[chip], hidden2.at[chip]), weight_out, weight_copies, bias,
            out, 0, tokens_v, out_v,
        )
    )


def project_second_kernel(scalars, cross, cross2, weight, bias, _, out, tokens_v, out_v, sems):
    wait_all(
        project_tokens(
            scalars[0], Copies(sems), (cross, cross2), weight, [], bias, out, 1, tokens_v, out_v
        )
    )


def project_scratch(block, width, half):
    return [
        pltpu.VMEM((2 * block, width), bf16),
        pltpu.VMEM((3, 2 * block, half), bf16),
        pltpu.SemaphoreType.DMA((8,)),
    ]


def project_first(scalars, hidden, hidden2, weight, bias):
    _, block, width = hidden.shape
    half = width // 2
    return pl.pallas_call(
        project_first_kernel,
        in_specs=[SM, ANY, ANY, ANY, VM],
        out_specs=[ANY, VM],
        out_shape=[
            jax.ShapeDtypeStruct((3, 4 * block, half), bf16), pltpu.VMEM((3, width, half), bf16)
        ],
        scratch_shapes=project_scratch(block, width, half),
        compiler_params=params(50),
        cost_estimate=cost(*BRIEF),
        name="project_first",
    )(scalars, hidden, hidden2, weight, bias)


def project_second(scalars, cross, cross2, weight, bias, qkv):
    block, width = cross.shape
    half = width // 2
    return pl.pallas_call(
        project_second_kernel,
        in_specs=[SM, ANY, ANY, VM, VM, ANY],
        out_specs=ANY,
        out_shape=jax.ShapeDtypeStruct(qkv.shape, bf16),
        input_output_aliases={5: 0},
        scratch_shapes=project_scratch(block, width, half),
        compiler_params=params(50),
        cost_estimate=cost(*BRIEF),
        name="project_second",
    )(scalars, *near_core(cross, cross2, weight), bias, qkv)


def head_mask(shape, head, axis):
    return (lax.broadcasted_iota(jnp.int32, shape, axis) // 64) == head


def keep_head(array, head, axis):
    return jnp.where(head_mask(array.shape, head, axis), array, jnp.zeros_like(array))


def attend_kernel(
    core_ref, query, key, value, prefix_k, prefix_v, key_mask, query_mask,
    out_mine, out_other, exps_mine, exps_other, recips_mine, recips_other, keys, values_t,
):
    prefix = prefix_k.shape[0]
    tokens = query.shape[1]
    count = prefix + tokens
    chunk = tokens // 4
    keys[:prefix, :128] = prefix_k[...]
    keys[prefix:, :128] = key[0]

    @pl.when(pl.program_id(0) == 0)
    def _():
        keys[:, 128:] = key_mask[...]
        values_t[:, 64:, :] = jnp.ones((2, values_t.shape[1] - 64, count), bf16)

    prefix_t = prefix_v[...].astype(f32).T.astype(bf16)
    value_t = value[0].astype(f32).T.astype(bf16)
    for head in range(2):
        values_t[head, :64, :prefix] = prefix_t[64 * head : 64 * head + 64]
        values_t[head, :64, prefix:] = value_t[64 * head : 64 * head + 64]
    units = [(i, head) for i in (1, 3, 0, 2) for head in range(2)]

    def score(unit):
        i, head = unit
        rows = slice(i * chunk, (i + 1) * chunk)
        masked = jnp.concatenate([keep_head(query[0, rows, :], head, 1), query_mask[rows, :]], axis=1)
        return dot(keys[...], masked, 1, 1)

    ahead = 2
    pending = [score(unit) for unit in units[:ahead]]
    for n, (i, head) in enumerate(units):
        scores = pending.pop(0)
        if n + ahead < len(units):
            pending.append(score(units[n + ahead]))
        out, exps, recips = (
            (out_mine, exps_mine, recips_mine), (out_other, exps_other, recips_other)
        )[i % 2]
        cols = slice(i // 2 * chunk, (i // 2 + 1) * chunk)
        top = jnp.max(scores, axis=0, keepdims=True)
        weights = jnp.exp2(scores - top).astype(bf16)
        exps[0, head, :, cols] = weights
        summed = dot(values_t[head], weights)
        recip = 1.0 / summed[64:65, :]
        recips[0, head, :, cols] = jnp.broadcast_to(recip, (8, chunk))
        out[64 * head : 64 * head + 64, cols] = (summed[:64, :] * recip).astype(bf16)


def attend(core, qkv, prefix_keys, prefix_values, key_mask, query_mask):
    _, tokens, half = qkv.shape
    prefix = prefix_keys.shape[0]
    count = prefix + tokens
    pairs = half // 128
    prefix_spec = pl.BlockSpec((prefix, 128), lambda p, k: (0, k[0] * pairs + p))
    out_spec = pl.BlockSpec((128, tokens // 2), lambda p, k: (p, 0))
    exps_spec = pl.BlockSpec((1, 2, count, tokens // 2), lambda p, k: (p, 0, 0, 0))
    recips_spec = pl.BlockSpec((1, 2, 8, tokens // 2), lambda p, k: (p, 0, 0, 0))
    return pl.pallas_call(
        attend_kernel,
        grid_spec=pltpu.PrefetchScalarGridSpec(
            num_scalar_prefetch=1,
            grid=(pairs,),
            in_specs=[
                pl.BlockSpec((1, tokens, 128), lambda p, k, j=j: (j, 0, p)) for j in range(3)
            ]
            + [
                prefix_spec,
                prefix_spec,
                pl.BlockSpec((count, 128), lambda p, k: (0, 0)),
                pl.BlockSpec((tokens, 128), lambda p, k: (0, 0)),
            ],
            out_specs=[out_spec] * 2 + [exps_spec] * 2 + [recips_spec] * 2,
            scratch_shapes=[pltpu.VMEM((count, 256), bf16), pltpu.VMEM((2, 64 + 16, count), bf16)],
        ),
        out_shape=[jax.ShapeDtypeStruct((half, tokens // 2), bf16)] * 2
        + [jax.ShapeDtypeStruct((pairs, 2, count, tokens // 2), bf16)] * 2
        + [jax.ShapeDtypeStruct((pairs, 2, 8, tokens // 2), f32)] * 2,
        compiler_params=params(56),
        cost_estimate=cost(*BRIEF),
        name="attend",
    )(core, qkv, qkv, qkv, prefix_keys, prefix_values, key_mask, query_mask)


def ordered_rows(array):
    block = array.shape[0] // 4
    return [array[i * block : (i + 1) * block] for i in (0, 2, 1, 3)]


def attend_back_kernel(
    core_ref, query, key, value, prefix_k, prefix_v, exps_mine, exps_other, recips_mine, recips_other,
    attended_mine, attended_other, grad_mine, grad_other, weight,
    out_mine, out_own2, out_cross2, out_prefix, weight_out,
    keys, values, keys_t, slopes, queries, queries_t, scaled, weight_sem,
):
    prefix = prefix_k.shape[0]
    tokens = query.shape[1]
    chunk = tokens // 4
    half = tokens // 2
    pair = pl.program_id(0)
    weight_copy = pltpu.make_async_copy(weight, weight_out, weight_sem.at[0])

    @pl.when(pair == 1)
    def _():
        weight_copy.start()

    keys[:prefix, :] = prefix_k[...]
    keys[prefix:, :] = key[0]
    values[:prefix, :] = prefix_v[...]
    values[prefix:, :] = value[0]
    keys_t[...] = keys[...].astype(f32).T.astype(bf16)
    queries[...] = jnp.concatenate(ordered_rows(query[0]), axis=0)
    spreads = []
    for head in range(2):
        rows = slice(64 * head, 64 * head + 64)
        parts = []
        for side, (recips, attended, grad) in enumerate(
            ((recips_mine, attended_mine, grad_mine), (recips_other, attended_other, grad_other))
        ):
            part = grad[rows, :].astype(f32) * recips[0, head, 0:1, :]
            scaled[rows, side * half : (side + 1) * half] = part.astype(bf16)
            parts.append(jnp.sum(part * attended[rows, :].astype(f32), axis=0, keepdims=True))
        spreads.append(jnp.concatenate(parts, axis=1))
    units = [(head, i) for head in range(2) for i in range(4)]

    def head_rows(array, head):
        zeros = jnp.zeros_like(array[:64])
        return jnp.concatenate([array[:64], zeros] if head == 0 else [zeros, array[64:]], axis=0)

    def grad_probs(unit):
        head, i = unit
        return dot(values[...], head_rows(scaled[:, i * chunk : (i + 1) * chunk], head))

    def exps_of(head, i):
        return (exps_mine, exps_other)[i // 2][0, head, :, i % 2 * chunk : (i % 2 + 1) * chunk]

    def value_part(head):
        total = None
        for side, exps in enumerate((exps_mine, exps_other)):
            cols = slice(side * half, (side + 1) * half)
            part = dot(exps[0, head], head_rows(scaled[:, cols], head), 1, 1)
            total = part if total is None else total + part
        return total

    def key_part(head):
        return dot(slopes[head], keep_head(queries[...], head, 1))

    ahead = 4
    pending = [grad_probs(unit) for unit in units[:ahead]]
    for n, (head, i) in enumerate(units):
        grads = pending.pop(0)
        if n + ahead < len(units):
            pending.append(grad_probs(units[n + ahead]))
        cols = slice(i * chunk, (i + 1) * chunk)
        slopes[head, :, cols] = (
            exps_of(head, i).astype(f32) * (grads - spreads[head][:, cols])
        ).astype(bf16)
        if n == 0:
            value_first = value_part(0)
        rows = slice(64 * head, 64 * head + 64)
        queries_t[rows, cols] = dot(keys_t[rows, :], slopes[head, :, cols]) * 0.125
        if n == 4:
            key_first = key_part(0)
    value_grads = value_first + value_part(1)
    key_grads = (key_first + key_part(1)) * ln_2
    out_prefix[0] = key_grads[:prefix]
    out_prefix[1] = value_grads[:prefix]
    query_grads = queries_t[...].T.astype(bf16)
    for j, parts in enumerate(
        ([query_grads[i * chunk : (i + 1) * chunk] for i in range(4)],)
        + tuple(ordered_rows(array[prefix:].astype(bf16)) for array in (key_grads, value_grads))
    ):
        out_mine[j, :chunk] = parts[0]
        out_mine[j, chunk:] = parts[1]
        out_own2[j] = parts[2]
        out_cross2[j] = parts[3]

    @pl.when(pair == pl.num_programs(0) - 1)
    def _():
        weight_copy.wait()


def attend_back(core, qkv, prefix_keys, prefix_values, exps, recips, attended, grads, weight):
    _, tokens, half = qkv.shape
    prefix = prefix_keys.shape[0]
    count = prefix + tokens
    pairs = half // 128
    prefix_spec = pl.BlockSpec((prefix, 128), lambda p, k: (0, k[0] * pairs + p))
    exps_spec = pl.BlockSpec((1, 2, count, tokens // 2), lambda p, k: (p, 0, 0, 0))
    recips_spec = pl.BlockSpec((1, 2, 8, tokens // 2), lambda p, k: (p, 0, 0, 0))
    heads_spec = pl.BlockSpec((128, tokens // 2), lambda p, k: (p, 0))
    rows = (tokens // 2, tokens // 4, tokens // 4)
    return pl.pallas_call(
        attend_back_kernel,
        grid_spec=pltpu.PrefetchScalarGridSpec(
            num_scalar_prefetch=1,
            grid=(pairs,),
            in_specs=[
                pl.BlockSpec((1, tokens, 128), lambda p, k, j=j: (j, 0, p)) for j in range(3)
            ]
            + [prefix_spec] * 2
            + [exps_spec] * 2
            + [recips_spec] * 2
            + [heads_spec] * 4
            + [ANY],
            out_specs=[pl.BlockSpec((3, n, 128), lambda p, k: (0, 0, p)) for n in rows]
            + [pl.BlockSpec((2, prefix, 128), lambda p, k: (0, 0, p)), ANY],
            scratch_shapes=[
                pltpu.VMEM((count, 128), bf16),
                pltpu.VMEM((count, 128), bf16),
                pltpu.VMEM((128, count), bf16),
                pltpu.VMEM((2, count, tokens), bf16),
                pltpu.VMEM((tokens, 128), bf16),
                pltpu.VMEM((128, tokens), f32),
                pltpu.VMEM((128, tokens), bf16),
                pltpu.SemaphoreType.DMA((1,)),
            ],
        ),
        out_shape=[pltpu.VMEM((3, rows[0], half), bf16)]
        + [jax.ShapeDtypeStruct((3, n, half), bf16) for n in rows[1:]]
        + [jax.ShapeDtypeStruct((2, prefix, half), f32), pltpu.VMEM(weight.shape, bf16)],
        compiler_params=params(40),
        cost_estimate=cost(*BRIEF),
        name="attend_back",
    )(core, qkv, qkv, qkv, prefix_keys, prefix_values, *exps, *recips, *attended, *grads, weight)


def mean_rows(array):
    return jnp.mean(array, axis=-1, keepdims=True)


def unit_norm(array):
    centered = array - mean_rows(array)
    inverse = lax.rsqrt(mean_rows(centered * centered) + epsilon)
    return centered * inverse, inverse


def norm_back(scaled, unit, inverse):
    return inverse * (scaled - mean_rows(scaled) - unit * mean_rows(scaled * unit))


def gelu_both(hidden):
    gate = 0.5 * (1.0 + lax.erf(hidden * root_half))
    slope = gate + hidden * inverse_root * jnp.exp(-0.5 * hidden * hidden)
    return (hidden * gate).astype(bf16), slope.astype(bf16)


def feed_forward(steps, total):
    hidden = None
    for i, step in enumerate(steps):
        if i == 0:
            wait_all(step[3])
            hidden = step[0]()
        following = None
        if i + 1 < len(steps):
            wait_all(steps[i + 1][3])
            following = steps[i + 1][0]()
        active, slope = gelu_both(hidden)
        step[1](slope)
        part = dot(active, step[2]())
        if total is None:
            total = part
        elif hasattr(total, "at"):
            total[...] += part
        hidden = following


def forward_kernel(
    core_ref, mine, other, own, cross, output_bias, first_gain, first_shift, output_weight,
    expand_own, expand_sib, reduce_own, reduce_sib, bias_own, bias_sib, piece0, piece1,
    unit_out, inverse_out, total_out, slope_out, low,
    out_w, expand_w, reduce_w, expand_r, reduce_r, bias_r, own_v, sems,
):
    core, chip = core_ref[0], core_ref[1]
    copies = [
        pltpu.make_async_copy(output_weight, out_w, sems.at[0]),
        pltpu.make_async_copy(expand_own, expand_w.at[0], sems.at[1]),
        pltpu.make_async_copy(reduce_own, reduce_w.at[0], sems.at[2]),
        pltpu.make_async_copy(expand_sib, expand_w.at[1], sems.at[3]),
        pltpu.make_async_copy(reduce_sib, reduce_w.at[1], sems.at[4]),
        pltpu.make_async_copy(own.at[chip], own_v, sems.at[5]),
    ]
    start_all(copies[5:] + copies[:5])
    piece_sems = Copies(sems)
    piece_sems.used = 6
    quarter = reduce_r.shape[0] // 2
    waits = piece_copies(piece_sems, (piece0, piece1), 0, quarter, expand_r, reduce_r)
    waits[0] = waits[0] + bias_copies(piece_sems, (piece0, piece1), quarter, bias_r)
    for group in waits:
        start_all(group)
    biases = bias_rows(core_ref[2], (0, 0), quarter, bias_r)
    copies[5].wait()
    copies[0].wait()
    half = mine.shape[0]
    block = own_v.shape[0]
    output_row, gain, shift = (
        ref[...].astype(f32).reshape(1, -1) for ref in (output_bias, first_gain, first_shift)
    )
    for i, ref in enumerate((own_v, cross)):
        rows = slice(i * block, (i + 1) * block)
        branch = dot(mine[:, rows], out_w[pl.ds(pl.multiple_of(core * half, half), half), :], 0, 0)
        branch += dot(
            other[:, rows], out_w[pl.ds(pl.multiple_of((1 - core) * half, half), half), :], 0, 0
        )
        unit, inverse = unit_norm(ref[...].astype(f32) + (branch + output_row))
        unit_out[rows, :] = unit
        inverse_out[rows, :] = jnp.broadcast_to(inverse, (block, 128))
        low[rows, :] = (unit * gain + shift).astype(bf16)
    chunk = 512
    hidden_here = expand_own.shape[1]

    def step(i, bias, start):
        cols = slice(start, start + chunk)

        def store(slope):
            slope_out[:, i * hidden_here + start : i * hidden_here + start + chunk] = slope

        return (
            lambda: dot(low[...], expand_w[i, :, cols]) + bias[cols].astype(f32).reshape(1, chunk),
            store,
            lambda: reduce_w[i, cols, :],
            copies[1 + 2 * i : 3 + 2 * i] if start == 0 else [],
        )

    total_out[...] = jnp.zeros(total_out.shape, f32)
    feed_forward(
        [
            step(i, bias, start)
            for i, bias in enumerate((bias_own, bias_sib))
            for start in range(0, hidden_here, chunk)
        ]
        + piece_steps(
            2, 0, quarter, low, expand_r, reduce_r, biases, slope_out, waits, 2 * hidden_here
        ),
        total_out,
    )


def forward(core, mine, other, own, cross, vectors, output_weight, weights, pieces):
    tokens = mine.shape[1]
    _, block, width = own.shape
    hidden = weights[0].shape[1]
    quarter = hidden // 4
    return pl.pallas_call(
        forward_kernel,
        in_specs=[SM, VM, VM, ANY] + [VM] * 4 + [ANY] * 5 + [VM] * 2 + [ANY] * 2,
        out_specs=[VM] * 5,
        out_shape=[
            jax.ShapeDtypeStruct((tokens, width), f32),
            jax.ShapeDtypeStruct((tokens, 128), f32),
            jax.ShapeDtypeStruct((tokens, width), f32),
            jax.ShapeDtypeStruct((tokens, 2 * hidden + 2 * quarter), bf16),
            jax.ShapeDtypeStruct((tokens, width), bf16),
        ],
        scratch_shapes=[
            pltpu.VMEM((width, width), bf16),
            pltpu.VMEM((2, width, hidden), bf16),
            pltpu.VMEM((2, hidden, width), bf16),
            pltpu.VMEM((width, 2 * quarter), bf16),
            pltpu.VMEM((2 * quarter, width), bf16),
            pltpu.VMEM((2, 16, width), bf16),
            pltpu.VMEM((block, width), bf16),
            pltpu.SemaphoreType.DMA((6 + 2 * (width // quarter + 2),)),
        ],
        compiler_params=params(40),
        cost_estimate=cost(*BRIEF),
        name="forward",
    )(core, mine, other, own, cross, *vectors, output_weight, *weights, *pieces)


def piece_copies(copies, pieces, place, quarter, expand_r, reduce_r):
    width = expand_r.shape[0]
    result = []
    for i, piece in enumerate(pieces):
        here = pl.ds((place + i) * quarter, quarter)
        group = []
        for j in range(width // quarter):
            rows = pl.ds(j * quarter, quarter)
            group.append(copies(piece.at[pl.ds(0, quarter), rows], expand_r.at[rows, here]))
        group.append(copies(piece.at[pl.ds(quarter, quarter)], reduce_r.at[here]))
        result.append(group)
    return result


def bias_copies(copies, pieces, quarter, bias_r):
    return [
        copies(piece.at[pl.ds(2 * quarter, 16)], bias_r.at[i]) for i, piece in enumerate(pieces)
    ]


def bias_rows(part, bits, quarter, bias_r):
    return [
        lambda i=i, bit=bit: bias_r[
            i, 0:1, pl.ds(pl.multiple_of(lax.bitwise_xor(part, bit) * quarter, quarter), quarter)
        ]
        for i, bit in enumerate(bits)
    ]


def piece_steps(
    count, place, quarter, low, expand_r, reduce_r, biases, slope_out, waits, slope_place=0
):
    def step(first):
        rows = slice((place + first) * quarter, (place + first + 2) * quarter)

        def hidden():
            bias = [biases[first + i]() for i in range(2)]
            return dot(low[...], expand_r[:, rows]) + jnp.concatenate(bias, axis=1).astype(f32)

        def store(slope):
            start = slope_place + first * quarter
            slope_out[:, start : start + 2 * quarter] = slope

        return (
            hidden,
            store,
            lambda: reduce_r[rows, :],
            waits[first] + waits[first + 1],
        )

    return [step(first) for first in range(0, count, 2)]


def remote_kernel(bits, *refs):
    count = len(bits)
    scalars, low_in, total_in = refs[:3]
    pieces = refs[3 : 3 + count]
    total_out, slope_out, low, expand_r, reduce_r, bias_r, sems = refs[3 + count :]
    quarter = reduce_r.shape[0] // count
    copies = Copies(sems)
    first = [copies(low_in, low), copies(total_in, total_out)]
    waits = piece_copies(copies, pieces, 0, quarter, expand_r, reduce_r)
    waits[0] = waits[0] + bias_copies(copies, pieces, quarter, bias_r)
    start_all(first[:1] + waits[0] + waits[1] + first[1:])
    for group in waits[2:]:
        start_all(group)
    biases = bias_rows(scalars[2], bits, quarter, bias_r)
    steps = piece_steps(count, 0, quarter, low, expand_r, reduce_r, biases, slope_out, waits)
    steps[0] = steps[0][:3] + (first + steps[0][3],)
    feed_forward(steps, total_out)


def remote(scalars, low, total, bits, pieces, quarter):
    tokens, width = total.shape
    count = len(pieces)
    return pl.pallas_call(
        functools.partial(remote_kernel, bits),
        in_specs=[SM] + [ANY] * (2 + count),
        out_specs=[VM] * 2,
        out_shape=[
            pltpu.VMEM((tokens, width), f32),
            pltpu.VMEM((tokens, count * quarter), bf16),
        ],
        scratch_shapes=[
            pltpu.VMEM((tokens, width), bf16),
            pltpu.VMEM((width, count * quarter), bf16),
            pltpu.VMEM((count * quarter, width), bf16),
            pltpu.VMEM((count, 16, width), bf16),
            pltpu.SemaphoreType.DMA((2 + count * (width // quarter + 2),)),
        ],
        compiler_params=params(26),
        cost_estimate=cost(*BRIEF),
        name="remote",
    )(scalars, low, total, *pieces)


def middle_kernel(early, late, *refs):
    count = early + late
    scalars, query_mask = refs[:2]
    vectors = refs[2:7]
    low_in, unit_in, inverse, total_in, slope_in, slope2_in, upstream = refs[7:14]
    output_weight, expand_own, expand_sib, reduce_own, reduce_sib = refs[14:19]
    pieces = refs[19 : 19 + count]
    up_cross = refs[19 + count]
    hidden_own, hidden_cross, grad_out, att_mine, att_other = refs[20 + count : 25 + count]
    (
        out_w, expand_w, reduce_w, expand_r, reduce_r, bias_r, low, unit, acc, back_acc,
        slope_l, slope_e, slope_s, up, hidden, sems,
    ) = refs[25 + count :]
    core, chip = scalars[0], scalars[1]
    copies = Copies(sems)
    tokens, width = unit.shape
    block = tokens // 2
    quarter = reduce_r.shape[0] // count
    chunk = 2 * quarter
    hidden_here = expand_own.shape[1]
    rows_of = [pl.ds(i * block, block) for i in range(2)]

    up_cross = up_cross.at[pl.ds(2 * quarter, block)]
    low_copy = copies(low_in, low)
    late_waits = piece_copies(copies, pieces[early:], early, quarter, expand_r, reduce_r)
    late_waits[0] = late_waits[0] + bias_copies(
        copies, (*pieces[early : early + 2], *pieces[:2]), quarter, bias_r
    )
    biases = bias_rows(scalars[2], (1, 2, 3, 3), quarter, bias_r)
    norm_copies = [
        [
            copies(total_in.at[rows_of[i]], acc.at[rows_of[i]]),
            copies(unit_in.at[rows_of[i]], unit.at[rows_of[i]]),
            copies((upstream.at[chip], up_cross)[i], up.at[rows_of[i]]),
        ]
        for i in range(2)
    ]
    local_copies = [
        [copies((reduce_own, reduce_sib)[i], reduce_w.at[i]), copies((expand_own, expand_sib)[i], expand_w.at[i])]
        for i in range(2)
    ]
    slope_copy = copies(slope_in, slope_l)
    early_copies = piece_copies(copies, pieces[:early], 0, quarter, expand_r, reduce_r)
    slope2_copy = copies(slope2_in, slope_e)
    out_copy = copies(output_weight, out_w)
    start_all([low_copy] + [copy for group in late_waits + norm_copies for copy in group])
    start_all([local_copies[0][0], slope_copy, local_copies[0][1]] + local_copies[1])
    start_all([copy for group in early_copies for copy in group] + [slope2_copy, out_copy])

    steps = piece_steps(late, early, quarter, low, expand_r, reduce_r, biases, slope_s, late_waits)
    steps[0] = steps[0][:3] + ([low_copy] + steps[0][3],)
    for group in norm_copies:
        wait_all(group[:1])
    feed_forward(steps, acc)

    first_gain, first_shift, reduce_bias, second_gain, second_shift = (
        ref[...].astype(f32).reshape(1, -1) for ref in vectors
    )
    hidden_copies = []
    for i in range(2):
        wait_all(norm_copies[i][1:])
        for start in range(i * block, (i + 1) * block, block // 2):
            rows = slice(start, start + block // 2)
            masked = slice(2 * i * block + start - i * block, 2 * i * block + start - i * block + block // 2)
            live = 1.0 - query_mask[masked, PAIRS : PAIRS + 1].astype(f32)
            first_norm = unit[rows, :] * first_gain + first_shift
            unit2, inverse2 = unit_norm(first_norm + (acc[rows, :] + reduce_bias))
            hidden[rows, :] = ((unit2 * second_gain + second_shift) * live).astype(bf16)
            grad_feed = norm_back(up[rows, :].astype(f32) * live * second_gain, unit2, inverse2)
            back_acc[rows, :] = grad_feed
            low[rows, :] = grad_feed.astype(bf16)
        copy = copies(hidden.at[rows_of[i]], (hidden_own.at[chip], hidden_cross)[i])
        copy.start()
        hidden_copies.append(copy)

    backs = []
    for i in range(2):
        for start in range(0, hidden_here, chunk):
            cols = slice(start, start + chunk)
            place = slice(i * hidden_here + start, i * hidden_here + start + chunk)
            backs.append(
                (
                    lambda i=i, cols=cols: reduce_w[i, cols, :],
                    lambda i=i, cols=cols: expand_w[i, :, cols],
                    1,
                    lambda place=place: slope_l[:, place],
                    ([slope_copy] if i + start == 0 else []) + (local_copies[i] if start == 0 else []),
                )
            )
    total_pieces = early + late
    for first in range(0, total_pieces, 2):
        rows = slice(first * quarter, (first + 2) * quarter)

        def slopes(first=first):
            parts = [
                slope_l[:, 2 * hidden_here + j * quarter : 2 * hidden_here + (j + 1) * quarter]
                if j < 2
                else slope_e[:, (j - 2) * quarter : (j - 1) * quarter]
                if j < early
                else slope_s[:, (j - early) * quarter : (j - early + 1) * quarter]
                for j in (first, first + 1)
            ]
            return jnp.concatenate(parts, axis=1)

        waits = [copy for j in (first, first + 1) if j < early for copy in early_copies[j]]
        backs.append(
            (
                lambda rows=rows: reduce_r[rows, :],
                lambda rows=rows: expand_r[:, rows],
                1,
                slopes,
                ([slope2_copy] if first == 0 else []) + waits,
            )
        )

    def grads(step):
        wait_all(step[4])
        return dot(low[...], step[0](), 1, 1)

    grad = grads(backs[0])
    for i, step in enumerate(backs):
        following = grads(backs[i + 1]) if i + 1 < len(backs) else None
        back = (grad * step[3]().astype(f32)).astype(bf16)
        back_acc[...] += dot(back, step[1](), 1, step[2])
        grad = following

    grad_copies = []
    for i in range(2):
        for start in range(i * block, (i + 1) * block, block // 2):
            rows = slice(start, start + block // 2)
            grad = norm_back(back_acc[rows, :] * first_gain, unit[rows, :], inverse[rows, 0:1])
            acc[rows, :] = grad
            low[rows, :] = grad.astype(bf16)
        copy = copies(acc.at[rows_of[i]], grad_out.at[rows_of[i]])
        copy.start()
        grad_copies.append(copy)
    out_copy.wait()
    half = width // 2
    att_other[...] = dot(
        out_w[pl.ds(pl.multiple_of((1 - core) * half, half), half), :], low[...], 1, 1
    ).astype(bf16)
    att_mine[...] = dot(
        out_w[pl.ds(pl.multiple_of(core * half, half), half), :], low[...], 1, 1
    ).astype(bf16)
    wait_all(hidden_copies + grad_copies)


def middle(scalars, query_mask, vectors, saved, upstream, output_weight, weights, early, late, last):
    tokens, width = saved[1].shape
    block = tokens // 2
    hidden = weights[0].shape[1]
    quarter = hidden // 4
    pieces = early + late
    count = len(pieces)
    return pl.pallas_call(
        functools.partial(middle_kernel, len(early), len(late)),
        in_specs=[SM] + [VM] * 6 + [ANY] * 2 + [VM] + [ANY] * (10 + count),
        out_specs=[ANY] * 3 + [VM] * 2,
        out_shape=[
            jax.ShapeDtypeStruct(upstream.shape, bf16),
            jax.ShapeDtypeStruct((block, width), bf16),
            jax.ShapeDtypeStruct((tokens, width), f32),
            pltpu.VMEM((width // 2, tokens), bf16),
            pltpu.VMEM((width // 2, tokens), bf16),
        ],
        scratch_shapes=[
            pltpu.VMEM((width, width), bf16),
            pltpu.VMEM((2, width, hidden), bf16),
            pltpu.VMEM((2, hidden, width), bf16),
            pltpu.VMEM((width, count * quarter), bf16),
            pltpu.VMEM((count * quarter, width), bf16),
            pltpu.VMEM((len(late), 16, width), bf16),
            pltpu.VMEM((tokens, width), bf16),
            pltpu.VMEM((tokens, width), f32),
            pltpu.VMEM((tokens, width), f32),
            pltpu.VMEM((tokens, width), f32),
            pltpu.VMEM((tokens, 2 * hidden + 2 * quarter), bf16),
            pltpu.VMEM((tokens, (len(early) - 2) * quarter), bf16),
            pltpu.VMEM((tokens, len(late) * quarter), bf16),
            pltpu.VMEM((tokens, width), bf16),
            pltpu.VMEM((tokens, width), bf16),
            pltpu.SemaphoreType.DMA((18 + len(late) + count * (width // quarter + 1),)),
        ],
        compiler_params=params(42),
        cost_estimate=cost(*BRIEF),
        name="middle",
    )(
        scalars, query_mask, *vectors, *saved, upstream, output_weight, *weights,
        *pieces, last,
    )


def project_back_rows(core, copies, place, mine, other, grad_branch, weight, left, grad, out):
    rows, width = out.shape
    half = other.shape[2]
    step = width // 4
    here = pl.ds(place * rows, rows)
    left_copies = [
        copy
        for j in range(3)
        for copy in (
            copies(mine.at[j, here], left.at[:, columns_at((2 * j + core) * half, half)]),
            copies(other.at[j], left.at[:, columns_at((2 * j + 1 - core) * half, half)]),
        )
    ]
    grad_copy = copies(grad_branch.at[here], grad)
    start_all(left_copies + [grad_copy])
    wait_all(left_copies)
    for start in range(0, width, step):
        cols = slice(start, start + step)
        total = dot(left[...], weight[cols, :], 1, 1)
        if start == 0:
            grad_copy.wait()
        out[:, cols] = (grad[:, cols] + total).astype(bf16)


def project_back_cross_kernel(scalars, mine, other, grad_branch, weight, out, left, grad, sems):
    project_back_rows(
        scalars[0], Copies(sems), 1, mine, other, grad_branch, weight, left, grad, out
    )


def project_back_own_kernel(
    scalars, mine, other, grad_branch, weight, theirs, _, out, hidden_out, left, grad, theirs_v, sems
):
    core, chip = scalars[0], scalars[1]
    copies = Copies(sems)
    theirs_in = copies(theirs, theirs_v)
    theirs_out = copies(theirs_v, hidden_out.at[1 - chip])
    theirs_in.start()
    theirs_in.wait()
    theirs_out.start()
    project_back_rows(core, copies, 0, mine, other, grad_branch, weight, left, grad, out)
    theirs_out.wait()


def project_back_scratch(rows, weight):
    width, columns = weight.shape
    return [pltpu.VMEM((rows, columns), bf16), pltpu.VMEM((rows, width), f32)]


def project_back_cross(scalars, mine, other, grad_branch, weight):
    _, rows, _ = other.shape
    return pl.pallas_call(
        project_back_cross_kernel,
        in_specs=[SM] + [ANY] * 3 + [VM],
        out_specs=VM,
        out_shape=jax.ShapeDtypeStruct((rows, weight.shape[0]), bf16),
        scratch_shapes=project_back_scratch(rows, weight) + [pltpu.SemaphoreType.DMA((7,))],
        compiler_params=params(40),
        cost_estimate=cost(*BRIEF),
        name="project_back_cross",
    )(scalars, *near_core(mine, other), grad_branch, *near_core(weight))


def project_back_own(scalars, mine, other, grad_branch, weight, theirs, hidden_out):
    _, rows, _ = other.shape
    width = weight.shape[0]
    return pl.pallas_call(
        project_back_own_kernel,
        in_specs=[SM] + [ANY] * 3 + [VM] + [ANY] * 2,
        out_specs=[VM, ANY],
        out_shape=[
            jax.ShapeDtypeStruct((rows, width), bf16),
            jax.ShapeDtypeStruct(hidden_out.shape, bf16),
        ],
        input_output_aliases={6: 1},
        scratch_shapes=project_back_scratch(rows, weight)
        + [pltpu.VMEM((rows, width), bf16), pltpu.SemaphoreType.DMA((9,))],
        compiler_params=params(40),
        cost_estimate=cost(*BRIEF),
        name="project_back_own",
    )(scalars, *near_core(mine, other), grad_branch, *near_core(weight), theirs, hidden_out)


def shards(
    sizes,
    hidden_in,
    pair_lengths,
    prefix_keys,
    prefix_values,
    project_weight,
    project_bias,
    output_weight,
    output_bias,
    first_gain,
    first_shift,
    expand_weight,
    expand_bias,
    reduce_weight,
    reduce_bias,
    second_gain,
    second_shift,
    upstream,
):
    dp_size, mp_size = sizes
    rows_here, shard_len, width = hidden_in.shape
    hidden_here = expand_weight.shape[1]
    prefix = prefix_keys.shape[0]
    half = width // 2
    place = lax.axis_index("mp")
    chip, core = place // 2, place % 2
    part = lax.axis_index("dp") % 4
    scalars = jnp.stack([core, chip, part]).astype(jnp.int32)

    def across(array):
        return swap(array, "mp", 2, mp_size)

    def beside(array):
        return swap(array, "mp", 1, mp_size)

    def take(array, index):
        return lax.dynamic_index_in_dim(array, index, 0, keepdims=False)

    def row(vector):
        return vector.reshape(1, -1)

    cross = across(take(hidden_in, 1 - chip))
    hidden2 = beside(hidden_in)

    boundary = jnp.cumsum(take(pair_lengths, chip))
    blocks = jnp.stack(
        [2 * chip + core, 2 * chip + 1 - core, 2 * (1 - chip) + core, 2 * (1 - chip) + 1 - core]
    )
    position = (
        blocks[:, None] * shard_len + jnp.arange(shard_len, dtype=jnp.int32)[None, :]
    ).reshape(-1)
    segment = jnp.sum((position[:, None] >= boundary[None, :]).astype(jnp.int32), axis=1)
    column = jnp.arange(128, dtype=jnp.int32)[None, :]
    query_mask = (segment[:, None] == column).astype(bf16)
    key_mask = jnp.where(
        (segment[:, None] == column) & (column < PAIRS), 0.0, masked_score
    ).astype(bf16)
    key_mask = jnp.concatenate([jnp.zeros((prefix, 128), bf16), key_mask], 0)

    pack0, pack3 = pack(scalars, expand_weight, reduce_weight, expand_bias, upstream)
    qkv, core_weight = project_first(scalars, hidden_in, hidden2, project_weight, project_bias)
    expand_sib, reduce_sib, bias_sib = beside(expand_weight), beside(reduce_weight), beside(expand_bias)
    cross, qkv, key_mask, query_mask, expand_sib, reduce_sib, bias_sib = lax.optimization_barrier(
        (cross, qkv, key_mask, query_mask, expand_sib, reduce_sib, bias_sib)
    )
    cross2 = beside(cross)
    piece0, piece3 = across(pack0), across(pack3)
    qkv = project_second(scalars, cross, cross2, core_weight, project_bias, qkv)
    attended_mine, attended_other, exps_mine, exps_other, recips_mine, recips_other = attend(
        scalars, qkv, prefix_keys, prefix_values, key_mask, query_mask
    )
    piece0, attended_other = lax.optimization_barrier((piece0, attended_other))
    piece1, piece2 = swap(piece0, "dp", 1, dp_size), swap(piece0, "dp", 2, dp_size)
    attended_here, piece0_sib = beside(attended_other), beside(piece0)
    attended_here, piece0_sib = lax.optimization_barrier((attended_here, piece0_sib))
    weights = tuple(
        far_core(array) for array in (expand_weight, expand_sib, reduce_weight, reduce_sib)
    )

    unit, inverse, total, slope, low = forward(
        scalars, attended_mine, attended_here, hidden_in, cross,
        (output_bias, first_gain, first_shift), output_weight, weights + (expand_bias, bias_sib),
        (piece0, piece0_sib),
    )
    piece1, piece2, low = lax.optimization_barrier((piece1, piece2, low))
    late = [beside(piece1), beside(piece2)]
    piece3, low = lax.optimization_barrier((piece3, low))
    quarter = hidden_here // 4
    quarter3 = piece3[: 2 * quarter]
    late += [quarter3, beside(quarter3)]
    total, slope2 = remote(scalars, low, total, (1, 2), [piece1, piece2], quarter)
    *late, total = lax.optimization_barrier((*late, total))
    total, slope2 = near_core(total, slope2)
    late = list(near_core(*late))
    early = [piece0, piece0_sib, piece1, piece2]
    hidden_own, hidden_cross, grad_branch, grad_mine, grad_theirs = middle(
        scalars, query_mask,
        (first_gain, first_shift, reduce_bias, second_gain, second_shift),
        (low, unit, inverse, total, slope, slope2), upstream, output_weight, weights, early, late,
        piece3,
    )
    grad_here = beside(grad_theirs)
    exps, recips = (exps_mine, exps_other), (recips_mine, recips_other)

    hidden_theirs = across(hidden_cross)
    back_mine, back_own2, back_cross2, grad_prefix, last_weight = attend_back(
        scalars, qkv, prefix_keys, prefix_values, exps, recips, (attended_mine, attended_other),
        near_core(grad_mine, grad_here), far_core(project_weight),
    )
    back_mine, back_own2, back_cross2, grad_prefix, hidden_theirs = lax.optimization_barrier(
        (back_mine, back_own2, back_cross2, grad_prefix, hidden_theirs)
    )

    def step(array, dp_bit, mp_bit):
        return lax.ppermute(
            array, ("dp", "mp"),
            [
                (d * mp_size + m, (d ^ dp_bit) * mp_size + (m ^ mp_bit))
                for d in range(dp_size)
                for m in range(mp_size)
            ],
        )

    def four_sum(parts):
        own_part, first, second, both = (part.astype(f32) for part in parts)
        return (own_part + first) + (second + both)

    cross_there = beside(back_cross2)
    own_there = beside(back_own2)
    low_prefix = grad_prefix.astype(bf16)
    group = (low_prefix, step(low_prefix, 0, 2), step(low_prefix, 2, 0), step(low_prefix, 2, 2))
    grad_branch = far_core(grad_branch)
    in_cross = project_back_cross(scalars, back_mine, cross_there, grad_branch, last_weight)
    in_cross, group = lax.optimization_barrier((in_cross, group))
    in_cross = across(in_cross)
    grad_prefix = four_sum(group)
    bit = 8
    while bit < dp_size:
        grad_prefix = grad_prefix + swap(grad_prefix, "dp", bit, dp_size)
        bit *= 2
    low_prefix = grad_prefix.astype(bf16)
    group = (low_prefix, step(low_prefix, 1, 0), step(low_prefix, 4, 0), step(low_prefix, 5, 0))
    in_own, hidden_out = project_back_own(
        scalars, back_mine, own_there, grad_branch, last_weight, far_core(hidden_theirs), hidden_own
    )
    in_own, in_cross, group = lax.optimization_barrier((in_own, in_cross, group))
    grad_in = jnp.where(chip == 0, jnp.stack([in_own, in_cross]), jnp.stack([in_cross, in_own]))
    grad_prefix = four_sum(group)
    grad_prefix_sib = beside(grad_prefix)
    grad_prefix = jnp.where(
        core == 0,
        jnp.concatenate([grad_prefix, grad_prefix_sib], 2),
        jnp.concatenate([grad_prefix_sib, grad_prefix], 2),
    )
    return (hidden_out, grad_in, grad_prefix[0], grad_prefix[1])


def solution(mesh):
    placed = (
        P("dp", "mp", None),
        P("dp", None),
        P(),
        P(),
        P(),
        P(),
        P(),
        P(),
        P(),
        P(),
        P(None, "mp"),
        P("mp"),
        P("mp", None),
        P(),
        P(),
        P(),
        P("dp", "mp", None),
    )
    return jax.shard_map(
        functools.partial(shards, (mesh.shape["dp"], mesh.shape["mp"])),
        mesh=mesh,
        in_specs=placed,
        out_specs=(P("dp", "mp", None), P("dp", "mp", None), P(), P()),
        check_vma=False,
    )
```

```python
import functools

import jax
import jax.numpy as jnp
from jax import lax
from jax.experimental import pallas as pl
from jax.experimental.pallas import tpu as pltpu
from jax.sharding import PartitionSpec as P

HEADS = 16
PAIRS = 8

epsilon = 1e-05
masked_score = -1e30
root_half = 0.7071067811865476
inverse_root = 0.3989422804014327
log2_e = 1.4426950408889634
ln_2 = 0.6931471805599453

bf16 = jnp.bfloat16
f32 = jnp.float32


def dot(left, right, left_dim=1, right_dim=0):
    return lax.dot_general(
        left, right, (((left_dim,), (right_dim,)), ((), ())), preferred_element_type=f32
    )


def params(mebibytes):
    return pltpu.CompilerParams(vmem_limit_bytes=mebibytes * 2**20)


def cost(flops, bytes_accessed, transcendentals=0):
    return pl.CostEstimate(
        flops=int(flops), bytes_accessed=int(bytes_accessed), transcendentals=int(transcendentals)
    )


ANY = pl.BlockSpec(memory_space=pl.ANY)


def far_core(array):
    return pltpu.with_memory_space_constraint(array, pltpu.HBM)


def near_core(*arrays):
    return tuple(pltpu.with_memory_space_constraint(array, pltpu.VMEM) for array in arrays)


VM = pl.BlockSpec(memory_space=pltpu.VMEM)
SM = pl.BlockSpec(memory_space=pltpu.SMEM)
BRIEF = (1e6, 1e5)


def swap(array, axis, bit, size):
    return lax.ppermute(array, axis, [(i, i ^ bit) for i in range(size)])


class Copies:
    def __init__(self, sems):
        self.sems, self.used = sems, 0

    def __call__(self, source, target):
        copy = pltpu.make_async_copy(source, target, self.sems.at[self.used])
        self.used += 1
        return copy


def start_all(copies):
    for copy in copies:
        copy.start()


def wait_all(copies):
    for copy in copies:
        copy.wait()


def columns_at(start, size):
    return pl.ds(pl.multiple_of(start, size), size)


def project_tokens(core, copies, parts, weight, weight_copies, bias, out, place, tokens_v, out_v):
    block = parts[0].shape[-2]
    half = out.shape[2]
    token_copies = [
        copies(part, tokens_v.at[pl.ds(i * block, block)]) for i, part in enumerate(parts)
    ]
    start_all(token_copies)
    start_all(weight_copies)
    wait_all(token_copies)
    out_copies = []
    for j in range(3):
        wait_all(weight_copies[j : j + 1])
        shift = jnp.where(
            core == 0,
            bias[2 * j * half : (2 * j + 1) * half].astype(f32),
            bias[(2 * j + 1) * half : (2 * j + 2) * half].astype(f32),
        )
        result = dot(tokens_v[...], weight[j]) + shift.reshape(1, half)
        if j == 0:
            result = result * (log2_e * 0.125)
        out_v[j] = result.astype(bf16)
        copy = copies(out_v.at[j], out.at[j, pl.ds(place * 2 * block, 2 * block)])
        copy.start()
        out_copies.append(copy)
    return out_copies


def pack_kernel(scalars, expand, reduce, hidden_bias, upstream, pack0, pack3, packs, bias_v, sems):
    chip, part = scalars[1], scalars[2]
    copies = Copies(sems)
    width, hidden_here = expand.shape
    quarter = hidden_here // 4
    bias_v[...] = jnp.broadcast_to(
        hidden_bias[...].astype(f32).reshape(1, hidden_here), (16, hidden_here)
    ).astype(bf16)
    groups = []
    for n, index in enumerate((part, 3 - part)):
        pack = packs.at[n]
        columns = columns_at(index * quarter, quarter)
        group = []
        for i in range(width // quarter):
            block = pl.ds(i * quarter, quarter)
            group.append(copies(expand.at[block, columns], pack.at[pl.ds(0, quarter), block]))
        group.append(copies(reduce.at[columns], pack.at[pl.ds(quarter, quarter)]))
        groups.append(group)
    groups[0].append(copies(bias_v, packs.at[0, pl.ds(2 * quarter, 16), pl.ds(0, hidden_here)]))
    groups[1].append(
        copies(upstream.at[1 - chip], packs.at[1, pl.ds(2 * quarter, upstream.shape[1])])
    )
    for group in groups:
        start_all(group)
    out_copies = []
    for n, (group, out) in enumerate(zip(groups, (pack0, pack3))):
        wait_all(group)
        copy = copies(packs.at[n, pl.ds(0, out.shape[0])], out)
        copy.start()
        out_copies.append(copy)
    wait_all(out_copies)


def pack(scalars, expand, reduce, hidden_bias, upstream):
    width, hidden_here = expand.shape
    quarter = hidden_here // 4
    packs = [
        jax.ShapeDtypeStruct((2 * quarter + n, width), bf16) for n in (16, upstream.shape[1])
    ]
    return pl.pallas_call(
        pack_kernel,
        in_specs=[SM, ANY, ANY, VM, ANY],
        out_specs=[ANY] * 2,
        out_shape=packs,
        scratch_shapes=[
            pltpu.VMEM((2, *packs[1].shape), bf16),
            pltpu.VMEM((16, hidden_here), bf16),
            pltpu.SemaphoreType.DMA((2 * (width // quarter + 2) + 2,)),
        ],
        compiler_params=params(56),
        cost_estimate=cost(*BRIEF),
        name="pack",
    )(scalars, expand, reduce, hidden_bias, upstream)


def project_first_kernel(
    scalars, hidden, hidden2, weight, bias, out, weight_out, tokens_v, out_v, sems
):
    core, chip = scalars[0], scalars[1]
    copies = Copies(sems)
    half = out.shape[2]
    weight_copies = [
        copies(weight.at[:, columns_at((2 * j + core) * half, half)], weight_out.at[j])
        for j in range(3)
    ]
    wait_all(
        project_tokens(
            core, copies, (hidden.at[chip], hidden2.at[chip]), weight_out, weight_copies, bias,
            out, 0, tokens_v, out_v,
        )
    )


def project_second_kernel(scalars, cross, cross2, weight, bias, _, out, tokens_v, out_v, sems):
    wait_all(
        project_tokens(
            scalars[0], Copies(sems), (cross, cross2), weight, [], bias, out, 1, tokens_v, out_v
        )
    )


def project_scratch(block, width, half):
    return [
        pltpu.VMEM((2 * block, width), bf16),
        pltpu.VMEM((3, 2 * block, half), bf16),
        pltpu.SemaphoreType.DMA((8,)),
    ]


def project_first(scalars, hidden, hidden2, weight, bias):
    _, block, width = hidden.shape
    half = width // 2
    return pl.pallas_call(
        project_first_kernel,
        in_specs=[SM, ANY, ANY, ANY, VM],
        out_specs=[ANY, VM],
        out_shape=[
            jax.ShapeDtypeStruct((3, 4 * block, half), bf16), pltpu.VMEM((3, width, half), bf16)
        ],
        scratch_shapes=project_scratch(block, width, half),
        compiler_params=params(50),
        cost_estimate=cost(*BRIEF),
        name="project_first",
    )(scalars, hidden, hidden2, weight, bias)


def project_second(scalars, cross, cross2, weight, bias, qkv):
    block, width = cross.shape
    half = width // 2
    return pl.pallas_call(
        project_second_kernel,
        in_specs=[SM, ANY, ANY, VM, VM, ANY],
        out_specs=ANY,
        out_shape=jax.ShapeDtypeStruct(qkv.shape, bf16),
        input_output_aliases={5: 0},
        scratch_shapes=project_scratch(block, width, half),
        compiler_params=params(50),
        cost_estimate=cost(*BRIEF),
        name="project_second",
    )(scalars, *near_core(cross, cross2, weight), bias, qkv)


def head_mask(shape, head, axis):
    return (lax.broadcasted_iota(jnp.int32, shape, axis) // 64) == head


def keep_head(array, head, axis):
    return jnp.where(head_mask(array.shape, head, axis), array, jnp.zeros_like(array))


def attend_kernel(
    core_ref, query, key, value, prefix_k, prefix_v, key_mask, query_mask,
    out_mine, out_other, exps_mine, exps_other, recips_mine, recips_other, keys, values_t,
):
    prefix = prefix_k.shape[0]
    tokens = query.shape[1]
    count = prefix + tokens
    chunk = tokens // 4
    keys[:prefix, :128] = prefix_k[...]
    keys[prefix:, :128] = key[0]

    @pl.when(pl.program_id(0) == 0)
    def _():
        keys[:, 128:] = key_mask[...]
        values_t[:, 64:, :] = jnp.ones((2, values_t.shape[1] - 64, count), bf16)

    prefix_t = prefix_v[...].astype(f32).T.astype(bf16)
    value_t = value[0].astype(f32).T.astype(bf16)
    for head in range(2):
        values_t[head, :64, :prefix] = prefix_t[64 * head : 64 * head + 64]
        values_t[head, :64, prefix:] = value_t[64 * head : 64 * head + 64]
    units = [(i, head) for i in (1, 3, 0, 2) for head in range(2)]

    def score(unit):
        i, head = unit
        rows = slice(i * chunk, (i + 1) * chunk)
        masked = jnp.concatenate([keep_head(query[0, rows, :], head, 1), query_mask[rows, :]], axis=1)
        return dot(keys[...], masked, 1, 1)

    ahead = 2
    pending = [score(unit) for unit in units[:ahead]]
    for n, (i, head) in enumerate(units):
        scores = pending.pop(0)
        if n + ahead < len(units):
            pending.append(score(units[n + ahead]))
        out, exps, recips = (
            (out_mine, exps_mine, recips_mine), (out_other, exps_other, recips_other)
        )[i % 2]
        cols = slice(i // 2 * chunk, (i // 2 + 1) * chunk)
        top = jnp.max(scores, axis=0, keepdims=True)
        weights = jnp.exp2(scores - top).astype(bf16)
        exps[0, head, :, cols] = weights
        summed = dot(values_t[head], weights)
        recip = 1.0 / summed[64:65, :]
        recips[0, head, :, cols] = jnp.broadcast_to(recip, (8, chunk))
        out[64 * head : 64 * head + 64, cols] = (summed[:64, :] * recip).astype(bf16)


def attend(core, qkv, prefix_keys, prefix_values, key_mask, query_mask):
    _, tokens, half = qkv.shape
    prefix = prefix_keys.shape[0]
    count = prefix + tokens
    pairs = half // 128
    prefix_spec = pl.BlockSpec((prefix, 128), lambda p, k: (0, k[0] * pairs + p))
    out_spec = pl.BlockSpec((128, tokens // 2), lambda p, k: (p, 0))
    exps_spec = pl.BlockSpec((1, 2, count, tokens // 2), lambda p, k: (p, 0, 0, 0))
    recips_spec = pl.BlockSpec((1, 2, 8, tokens // 2), lambda p, k: (p, 0, 0, 0))
    return pl.pallas_call(
        attend_kernel,
        grid_spec=pltpu.PrefetchScalarGridSpec(
            num_scalar_prefetch=1,
            grid=(pairs,),
            in_specs=[
                pl.BlockSpec((1, tokens, 128), lambda p, k, j=j: (j, 0, p)) for j in range(3)
            ]
            + [
                prefix_spec,
                prefix_spec,
                pl.BlockSpec((count, 128), lambda p, k: (0, 0)),
                pl.BlockSpec((tokens, 128), lambda p, k: (0, 0)),
            ],
            out_specs=[out_spec] * 2 + [exps_spec] * 2 + [recips_spec] * 2,
            scratch_shapes=[pltpu.VMEM((count, 256), bf16), pltpu.VMEM((2, 64 + 16, count), bf16)],
        ),
        out_shape=[jax.ShapeDtypeStruct((half, tokens // 2), bf16)] * 2
        + [jax.ShapeDtypeStruct((pairs, 2, count, tokens // 2), bf16)] * 2
        + [jax.ShapeDtypeStruct((pairs, 2, 8, tokens // 2), f32)] * 2,
        compiler_params=params(56),
        cost_estimate=cost(*BRIEF),
        name="attend",
    )(core, qkv, qkv, qkv, prefix_keys, prefix_values, key_mask, query_mask)


def ordered_rows(array):
    block = array.shape[0] // 4
    return [array[i * block : (i + 1) * block] for i in (0, 2, 1, 3)]


def attend_back_kernel(
    core_ref, query, key, value, prefix_k, prefix_v, exps_mine, exps_other, recips_mine, recips_other,
    attended_mine, attended_other, grad_mine, grad_other, weight,
    out_mine, out_own2, out_cross2, out_prefix, weight_out,
    keys, values, keys_t, slopes, queries, queries_t, scaled, weight_sem,
):
    prefix = prefix_k.shape[0]
    tokens = query.shape[1]
    chunk = tokens // 4
    half = tokens // 2
    pair = pl.program_id(0)
    weight_copy = pltpu.make_async_copy(weight, weight_out, weight_sem.at[0])

    @pl.when(pair == 1)
    def _():
        weight_copy.start()

    keys[:prefix, :] = prefix_k[...]
    keys[prefix:, :] = key[0]
    values[:prefix, :] = prefix_v[...]
    values[prefix:, :] = value[0]
    keys_t[...] = keys[...].astype(f32).T.astype(bf16)
    queries[...] = jnp.concatenate(ordered_rows(query[0]), axis=0)
    spreads = []
    for head in range(2):
        rows = slice(64 * head, 64 * head + 64)
        parts = []
        for side, (recips, attended, grad) in enumerate(
            ((recips_mine, attended_mine, grad_mine), (recips_other, attended_other, grad_other))
        ):
            part = grad[rows, :].astype(f32) * recips[0, head, 0:1, :]
            scaled[rows, side * half : (side + 1) * half] = part.astype(bf16)
            parts.append(jnp.sum(part * attended[rows, :].astype(f32), axis=0, keepdims=True))
        spreads.append(jnp.concatenate(parts, axis=1))
    units = [(head, i) for head in range(2) for i in range(4)]

    def head_rows(array, head):
        zeros = jnp.zeros_like(array[:64])
        return jnp.concatenate([array[:64], zeros] if head == 0 else [zeros, array[64:]], axis=0)

    def grad_probs(unit):
        head, i = unit
        return dot(values[...], head_rows(scaled[:, i * chunk : (i + 1) * chunk], head))

    def exps_of(head, i):
        return (exps_mine, exps_other)[i // 2][0, head, :, i % 2 * chunk : (i % 2 + 1) * chunk]

    def value_part(head):
        total = None
        for side, exps in enumerate((exps_mine, exps_other)):
            cols = slice(side * half, (side + 1) * half)
            part = dot(exps[0, head], head_rows(scaled[:, cols], head), 1, 1)
            total = part if total is None else total + part
        return total

    def key_part(head):
        return dot(slopes[head], keep_head(queries[...], head, 1))

    ahead = 4
    pending = [grad_probs(unit) for unit in units[:ahead]]
    for n, (head, i) in enumerate(units):
        grads = pending.pop(0)
        if n + ahead < len(units):
            pending.append(grad_probs(units[n + ahead]))
        cols = slice(i * chunk, (i + 1) * chunk)
        slopes[head, :, cols] = (
            exps_of(head, i).astype(f32) * (grads - spreads[head][:, cols])
        ).astype(bf16)
        if n == 0:
            value_first = value_part(0)
        rows = slice(64 * head, 64 * head + 64)
        queries_t[rows, cols] = dot(keys_t[rows, :], slopes[head, :, cols]) * 0.125
        if n == 4:
            key_first = key_part(0)
    value_grads = value_first + value_part(1)
    key_grads = (key_first + key_part(1)) * ln_2
    out_prefix[0] = key_grads[:prefix]
    out_prefix[1] = value_grads[:prefix]
    query_grads = queries_t[...].T.astype(bf16)
    for j, parts in enumerate(
        ([query_grads[i * chunk : (i + 1) * chunk] for i in range(4)],)
        + tuple(ordered_rows(array[prefix:].astype(bf16)) for array in (key_grads, value_grads))
    ):
        out_mine[j, :chunk] = parts[0]
        out_mine[j, chunk:] = parts[1]
        out_own2[j] = parts[2]
        out_cross2[j] = parts[3]

    @pl.when(pair == pl.num_programs(0) - 1)
    def _():
        weight_copy.wait()


def attend_back(core, qkv, prefix_keys, prefix_values, exps, recips, attended, grads, weight):
    _, tokens, half = qkv.shape
    prefix = prefix_keys.shape[0]
    count = prefix + tokens
    pairs = half // 128
    prefix_spec = pl.BlockSpec((prefix, 128), lambda p, k: (0, k[0] * pairs + p))
    exps_spec = pl.BlockSpec((1, 2, count, tokens // 2), lambda p, k: (p, 0, 0, 0))
    recips_spec = pl.BlockSpec((1, 2, 8, tokens // 2), lambda p, k: (p, 0, 0, 0))
    heads_spec = pl.BlockSpec((128, tokens // 2), lambda p, k: (p, 0))
    rows = (tokens // 2, tokens // 4, tokens // 4)
    return pl.pallas_call(
        attend_back_kernel,
        grid_spec=pltpu.PrefetchScalarGridSpec(
            num_scalar_prefetch=1,
            grid=(pairs,),
            in_specs=[
                pl.BlockSpec((1, tokens, 128), lambda p, k, j=j: (j, 0, p)) for j in range(3)
            ]
            + [prefix_spec] * 2
            + [exps_spec] * 2
            + [recips_spec] * 2
            + [heads_spec] * 4
            + [ANY],
            out_specs=[pl.BlockSpec((3, n, 128), lambda p, k: (0, 0, p)) for n in rows]
            + [pl.BlockSpec((2, prefix, 128), lambda p, k: (0, 0, p)), ANY],
            scratch_shapes=[
                pltpu.VMEM((count, 128), bf16),
                pltpu.VMEM((count, 128), bf16),
                pltpu.VMEM((128, count), bf16),
                pltpu.VMEM((2, count, tokens), bf16),
                pltpu.VMEM((tokens, 128), bf16),
                pltpu.VMEM((128, tokens), f32),
                pltpu.VMEM((128, tokens), bf16),
                pltpu.SemaphoreType.DMA((1,)),
            ],
        ),
        out_shape=[pltpu.VMEM((3, rows[0], half), bf16)]
        + [jax.ShapeDtypeStruct((3, n, half), bf16) for n in rows[1:]]
        + [jax.ShapeDtypeStruct((2, prefix, half), f32), pltpu.VMEM(weight.shape, bf16)],
        compiler_params=params(40),
        cost_estimate=cost(*BRIEF),
        name="attend_back",
    )(core, qkv, qkv, qkv, prefix_keys, prefix_values, *exps, *recips, *attended, *grads, weight)


def mean_rows(array):
    return jnp.mean(array, axis=-1, keepdims=True)


def unit_norm(array):
    centered = array - mean_rows(array)
    inverse = lax.rsqrt(mean_rows(centered * centered) + epsilon)
    return centered * inverse, inverse


def norm_back(scaled, unit, inverse):
    return inverse * (scaled - mean_rows(scaled) - unit * mean_rows(scaled * unit))


def gelu_both(hidden):
    gate = 0.5 * (1.0 + lax.erf(hidden * root_half))
    slope = gate + hidden * inverse_root * jnp.exp(-0.5 * hidden * hidden)
    return (hidden * gate).astype(bf16), slope.astype(bf16)


def feed_forward(steps, total):
    hidden = None
    for i, step in enumerate(steps):
        if i == 0:
            wait_all(step[3])
            hidden = step[0]()
        following = None
        if i + 1 < len(steps):
            wait_all(steps[i + 1][3])
            following = steps[i + 1][0]()
        active, slope = gelu_both(hidden)
        step[1](slope)
        part = dot(active, step[2]())
        if total is None:
            total = part
        elif hasattr(total, "at"):
            total[...] += part
        hidden = following


def forward_kernel(
    core_ref, mine, other, own, cross, output_bias, first_gain, first_shift, output_weight,
    expand_own, expand_sib, reduce_own, reduce_sib, bias_own, bias_sib, piece0, piece1,
    unit_out, inverse_out, total_out, slope_out, low,
    out_w, expand_w, reduce_w, expand_r, reduce_r, bias_r, own_v, sems,
):
    core, chip = core_ref[0], core_ref[1]
    copies = [
        pltpu.make_async_copy(output_weight, out_w, sems.at[0]),
        pltpu.make_async_copy(expand_own, expand_w.at[0], sems.at[1]),
        pltpu.make_async_copy(reduce_own, reduce_w.at[0], sems.at[2]),
        pltpu.make_async_copy(expand_sib, expand_w.at[1], sems.at[3]),
        pltpu.make_async_copy(reduce_sib, reduce_w.at[1], sems.at[4]),
        pltpu.make_async_copy(own.at[chip], own_v, sems.at[5]),
    ]
    start_all(copies[5:] + copies[:5])
    piece_sems = Copies(sems)
    piece_sems.used = 6
    quarter = reduce_r.shape[0] // 2
    waits = piece_copies(piece_sems, (piece0, piece1), 0, quarter, expand_r, reduce_r)
    waits[0] = waits[0] + bias_copies(piece_sems, (piece0, piece1), quarter, bias_r)
    for group in waits:
        start_all(group)
    biases = bias_rows(core_ref[2], (0, 0), quarter, bias_r)
    copies[5].wait()
    copies[0].wait()
    half = mine.shape[0]
    block = own_v.shape[0]
    output_row, gain, shift = (
        ref[...].astype(f32).reshape(1, -1) for ref in (output_bias, first_gain, first_shift)
    )
    for i, ref in enumerate((own_v, cross)):
        rows = slice(i * block, (i + 1) * block)
        branch = dot(mine[:, rows], out_w[pl.ds(pl.multiple_of(core * half, half), half), :], 0, 0)
        branch += dot(
            other[:, rows], out_w[pl.ds(pl.multiple_of((1 - core) * half, half), half), :], 0, 0
        )
        unit, inverse = unit_norm(ref[...].astype(f32) + (branch + output_row))
        unit_out[rows, :] = unit
        inverse_out[rows, :] = jnp.broadcast_to(inverse, (block, 128))
        low[rows, :] = (unit * gain + shift).astype(bf16)
    chunk = 512
    hidden_here = expand_own.shape[1]

    def step(i, bias, start):
        cols = slice(start, start + chunk)

        def store(slope):
            slope_out[:, i * hidden_here + start : i * hidden_here + start + chunk] = slope

        return (
            lambda: dot(low[...], expand_w[i, :, cols]) + bias[cols].astype(f32).reshape(1, chunk),
            store,
            lambda: reduce_w[i, cols, :],
            copies[1 + 2 * i : 3 + 2 * i] if start == 0 else [],
        )

    total_out[...] = jnp.zeros(total_out.shape, f32)
    feed_forward(
        [
            step(i, bias, start)
            for i, bias in enumerate((bias_own, bias_sib))
            for start in range(0, hidden_here, chunk)
        ]
        + piece_steps(
            2, 0, quarter, low, expand_r, reduce_r, biases, slope_out, waits, 2 * hidden_here
        ),
        total_out,
    )


def forward(core, mine, other, own, cross, vectors, output_weight, weights, pieces):
    tokens = mine.shape[1]
    _, block, width = own.shape
    hidden = weights[0].shape[1]
    quarter = hidden // 4
    return pl.pallas_call(
        forward_kernel,
        in_specs=[SM, VM, VM, ANY] + [VM] * 4 + [ANY] * 5 + [VM] * 2 + [ANY] * 2,
        out_specs=[VM] * 5,
        out_shape=[
            jax.ShapeDtypeStruct((tokens, width), f32),
            jax.ShapeDtypeStruct((tokens, 128), f32),
            jax.ShapeDtypeStruct((tokens, width), f32),
            jax.ShapeDtypeStruct((tokens, 2 * hidden + 2 * quarter), bf16),
            jax.ShapeDtypeStruct((tokens, width), bf16),
        ],
        scratch_shapes=[
            pltpu.VMEM((width, width), bf16),
            pltpu.VMEM((2, width, hidden), bf16),
            pltpu.VMEM((2, hidden, width), bf16),
            pltpu.VMEM((width, 2 * quarter), bf16),
            pltpu.VMEM((2 * quarter, width), bf16),
            pltpu.VMEM((2, 16, width), bf16),
            pltpu.VMEM((block, width), bf16),
            pltpu.SemaphoreType.DMA((6 + 2 * (width // quarter + 2),)),
        ],
        compiler_params=params(40),
        cost_estimate=cost(*BRIEF),
        name="forward",
    )(core, mine, other, own, cross, *vectors, output_weight, *weights, *pieces)


def piece_copies(copies, pieces, place, quarter, expand_r, reduce_r):
    width = expand_r.shape[0]
    result = []
    for i, piece in enumerate(pieces):
        here = pl.ds((place + i) * quarter, quarter)
        group = []
        for j in range(width // quarter):
            rows = pl.ds(j * quarter, quarter)
            group.append(copies(piece.at[pl.ds(0, quarter), rows], expand_r.at[rows, here]))
        group.append(copies(piece.at[pl.ds(quarter, quarter)], reduce_r.at[here]))
        result.append(group)
    return result


def bias_copies(copies, pieces, quarter, bias_r):
    return [
        copies(piece.at[pl.ds(2 * quarter, 16)], bias_r.at[i]) for i, piece in enumerate(pieces)
    ]


def bias_rows(part, bits, quarter, bias_r):
    return [
        lambda i=i, bit=bit: bias_r[
            i, 0:1, pl.ds(pl.multiple_of(lax.bitwise_xor(part, bit) * quarter, quarter), quarter)
        ]
        for i, bit in enumerate(bits)
    ]


def piece_steps(
    count, place, quarter, low, expand_r, reduce_r, biases, slope_out, waits, slope_place=0
):
    def step(first):
        rows = slice((place + first) * quarter, (place + first + 2) * quarter)

        def hidden():
            bias = [biases[first + i]() for i in range(2)]
            return dot(low[...], expand_r[:, rows]) + jnp.concatenate(bias, axis=1).astype(f32)

        def store(slope):
            start = slope_place + first * quarter
            slope_out[:, start : start + 2 * quarter] = slope

        return (
            hidden,
            store,
            lambda: reduce_r[rows, :],
            waits[first] + waits[first + 1],
        )

    return [step(first) for first in range(0, count, 2)]


def remote_kernel(bits, *refs):
    count = len(bits)
    scalars, low_in, total_in = refs[:3]
    pieces = refs[3 : 3 + count]
    total_out, slope_out, low, expand_r, reduce_r, bias_r, sems = refs[3 + count :]
    quarter = reduce_r.shape[0] // count
    copies = Copies(sems)
    first = [copies(low_in, low), copies(total_in, total_out)]
    waits = piece_copies(copies, pieces, 0, quarter, expand_r, reduce_r)
    waits[0] = waits[0] + bias_copies(copies, pieces, quarter, bias_r)
    start_all(first[:1] + waits[0] + waits[1] + first[1:])
    for group in waits[2:]:
        start_all(group)
    biases = bias_rows(scalars[2], bits, quarter, bias_r)
    steps = piece_steps(count, 0, quarter, low, expand_r, reduce_r, biases, slope_out, waits)
    steps[0] = steps[0][:3] + (first + steps[0][3],)
    feed_forward(steps, total_out)


def remote(scalars, low, total, bits, pieces, quarter):
    tokens, width = total.shape
    count = len(pieces)
    return pl.pallas_call(
        functools.partial(remote_kernel, bits),
        in_specs=[SM] + [ANY] * (2 + count),
        out_specs=[VM] * 2,
        out_shape=[
            pltpu.VMEM((tokens, width), f32),
            pltpu.VMEM((tokens, count * quarter), bf16),
        ],
        scratch_shapes=[
            pltpu.VMEM((tokens, width), bf16),
            pltpu.VMEM((width, count * quarter), bf16),
            pltpu.VMEM((count * quarter, width), bf16),
            pltpu.VMEM((count, 16, width), bf16),
            pltpu.SemaphoreType.DMA((2 + count * (width // quarter + 2),)),
        ],
        compiler_params=params(26),
        cost_estimate=cost(*BRIEF),
        name="remote",
    )(scalars, low, total, *pieces)


def middle_kernel(early, late, *refs):
    count = early + late
    scalars, query_mask = refs[:2]
    vectors = refs[2:7]
    low_in, unit_in, inverse, total_in, slope_in, slope2_in, slope3_in, upstream = refs[7:15]
    output_weight, expand_own, expand_sib, reduce_own, reduce_sib = refs[15:20]
    pieces = refs[20 : 20 + count]
    up_cross = refs[20 + count]
    hidden_own, hidden_cross, grad_out, att_mine, att_other = refs[21 + count : 26 + count]
    (
        out_w, expand_w, reduce_w, expand_r, reduce_r, bias_r, low, unit, acc, back_acc,
        slope_l, slope_e, slope_s, up, hidden, sems,
    ) = refs[26 + count :]
    core, chip = scalars[0], scalars[1]
    copies = Copies(sems)
    tokens, width = unit.shape
    block = tokens // 2
    quarter = reduce_r.shape[0] // count
    chunk = 2 * quarter
    hidden_here = expand_own.shape[1]
    rows_of = [pl.ds(i * block, block) for i in range(2)]

    up_cross = up_cross.at[pl.ds(2 * quarter, block)]
    low_copy = copies(low_in, low)
    late_waits = piece_copies(copies, pieces[early:], early, quarter, expand_r, reduce_r)
    late_waits[0] = late_waits[0] + bias_copies(copies, pieces[:2], quarter, bias_r)
    biases = bias_rows(scalars[2], (3, 3), quarter, bias_r)
    norm_copies = [
        [
            copies(total_in.at[rows_of[i]], acc.at[rows_of[i]]),
            copies(unit_in.at[rows_of[i]], unit.at[rows_of[i]]),
            copies((upstream.at[chip], up_cross)[i], up.at[rows_of[i]]),
        ]
        for i in range(2)
    ]
    local_copies = [
        [copies((reduce_own, reduce_sib)[i], reduce_w.at[i]), copies((expand_own, expand_sib)[i], expand_w.at[i])]
        for i in range(2)
    ]
    slope_copy = copies(slope_in, slope_l)
    early_copies = piece_copies(copies, pieces[:early], 0, quarter, expand_r, reduce_r)
    slope2_copies = [
        copies(array, slope_e.at[:, pl.ds(2 * i * quarter, 2 * quarter)])
        for i, array in enumerate((slope2_in, slope3_in))
    ]
    out_copy = copies(output_weight, out_w)
    start_all([low_copy] + [copy for group in late_waits + norm_copies for copy in group])
    start_all([local_copies[0][0], slope_copy, local_copies[0][1]] + local_copies[1])
    start_all([copy for group in early_copies for copy in group] + slope2_copies + [out_copy])

    steps = piece_steps(late, early, quarter, low, expand_r, reduce_r, biases, slope_s, late_waits)
    steps[0] = steps[0][:3] + ([low_copy] + steps[0][3],)
    for group in norm_copies:
        wait_all(group[:1])
    feed_forward(steps, acc)

    first_gain, first_shift, reduce_bias, second_gain, second_shift = (
        ref[...].astype(f32).reshape(1, -1) for ref in vectors
    )
    hidden_copies = []
    for i in range(2):
        wait_all(norm_copies[i][1:])
        for start in range(i * block, (i + 1) * block, block // 2):
            rows = slice(start, start + block // 2)
            masked = slice(2 * i * block + start - i * block, 2 * i * block + start - i * block + block // 2)
            live = 1.0 - query_mask[masked, PAIRS : PAIRS + 1].astype(f32)
            first_norm = unit[rows, :] * first_gain + first_shift
            unit2, inverse2 = unit_norm(first_norm + (acc[rows, :] + reduce_bias))
            hidden[rows, :] = ((unit2 * second_gain + second_shift) * live).astype(bf16)
            grad_feed = norm_back(up[rows, :].astype(f32) * live * second_gain, unit2, inverse2)
            back_acc[rows, :] = grad_feed
            low[rows, :] = grad_feed.astype(bf16)
        copy = copies(hidden.at[rows_of[i]], (hidden_own.at[chip], hidden_cross)[i])
        copy.start()
        hidden_copies.append(copy)

    backs = []
    for i in range(2):
        for start in range(0, hidden_here, chunk):
            cols = slice(start, start + chunk)
            place = slice(i * hidden_here + start, i * hidden_here + start + chunk)
            backs.append(
                (
                    lambda i=i, cols=cols: reduce_w[i, cols, :],
                    lambda i=i, cols=cols: expand_w[i, :, cols],
                    1,
                    lambda place=place: slope_l[:, place],
                    ([slope_copy] if i + start == 0 else []) + (local_copies[i] if start == 0 else []),
                )
            )
    total_pieces = early + late
    for first in range(0, total_pieces, 2):
        rows = slice(first * quarter, (first + 2) * quarter)

        def slopes(first=first):
            parts = [
                slope_l[:, 2 * hidden_here + j * quarter : 2 * hidden_here + (j + 1) * quarter]
                if j < 2
                else slope_e[:, (j - 2) * quarter : (j - 1) * quarter]
                if j < early
                else slope_s[:, (j - early) * quarter : (j - early + 1) * quarter]
                for j in (first, first + 1)
            ]
            return jnp.concatenate(parts, axis=1)

        waits = [copy for j in (first, first + 1) if j < early for copy in early_copies[j]]
        backs.append(
            (
                lambda rows=rows: reduce_r[rows, :],
                lambda rows=rows: expand_r[:, rows],
                1,
                slopes,
                (slope2_copies if first == 0 else []) + waits,
            )
        )

    def grads(step):
        wait_all(step[4])
        return dot(low[...], step[0](), 1, 1)

    grad = grads(backs[0])
    for i, step in enumerate(backs):
        following = grads(backs[i + 1]) if i + 1 < len(backs) else None
        back = (grad * step[3]().astype(f32)).astype(bf16)
        back_acc[...] += dot(back, step[1](), 1, step[2])
        grad = following

    grad_copies = []
    for i in range(2):
        for start in range(i * block, (i + 1) * block, block // 2):
            rows = slice(start, start + block // 2)
            grad = norm_back(back_acc[rows, :] * first_gain, unit[rows, :], inverse[rows, 0:1])
            acc[rows, :] = grad
            low[rows, :] = grad.astype(bf16)
        copy = copies(acc.at[rows_of[i]], grad_out.at[rows_of[i]])
        copy.start()
        grad_copies.append(copy)
    out_copy.wait()
    half = width // 2
    att_other[...] = dot(
        out_w[pl.ds(pl.multiple_of((1 - core) * half, half), half), :], low[...], 1, 1
    ).astype(bf16)
    att_mine[...] = dot(
        out_w[pl.ds(pl.multiple_of(core * half, half), half), :], low[...], 1, 1
    ).astype(bf16)
    wait_all(hidden_copies + grad_copies)


def middle(scalars, query_mask, vectors, saved, upstream, output_weight, weights, early, late, last):
    tokens, width = saved[1].shape
    block = tokens // 2
    hidden = weights[0].shape[1]
    quarter = hidden // 4
    pieces = early + late
    count = len(pieces)
    return pl.pallas_call(
        functools.partial(middle_kernel, len(early), len(late)),
        in_specs=[SM] + [VM] * 6 + [ANY] * 2 + [VM] + [ANY] * (11 + count),
        out_specs=[ANY] * 3 + [VM] * 2,
        out_shape=[
            jax.ShapeDtypeStruct(upstream.shape, bf16),
            jax.ShapeDtypeStruct((block, width), bf16),
            jax.ShapeDtypeStruct((tokens, width), f32),
            pltpu.VMEM((width // 2, tokens), bf16),
            pltpu.VMEM((width // 2, tokens), bf16),
        ],
        scratch_shapes=[
            pltpu.VMEM((width, width), bf16),
            pltpu.VMEM((2, width, hidden), bf16),
            pltpu.VMEM((2, hidden, width), bf16),
            pltpu.VMEM((width, count * quarter), bf16),
            pltpu.VMEM((count * quarter, width), bf16),
            pltpu.VMEM((len(late), 16, width), bf16),
            pltpu.VMEM((tokens, width), bf16),
            pltpu.VMEM((tokens, width), f32),
            pltpu.VMEM((tokens, width), f32),
            pltpu.VMEM((tokens, width), f32),
            pltpu.VMEM((tokens, 2 * hidden + 2 * quarter), bf16),
            pltpu.VMEM((tokens, (len(early) - 2) * quarter), bf16),
            pltpu.VMEM((tokens, len(late) * quarter), bf16),
            pltpu.VMEM((tokens, width), bf16),
            pltpu.VMEM((tokens, width), bf16),
            pltpu.SemaphoreType.DMA((19 + len(late) + count * (width // quarter + 1),)),
        ],
        compiler_params=params(42),
        cost_estimate=cost(*BRIEF),
        name="middle",
    )(
        scalars, query_mask, *vectors, *saved, upstream, output_weight, *weights,
        *pieces, last,
    )


def project_back_rows(core, copies, place, mine, other, grad_branch, weight, left, grad, out):
    rows, width = out.shape
    half = other.shape[2]
    step = width // 4
    here = pl.ds(place * rows, rows)
    left_copies = [
        copy
        for j in range(3)
        for copy in (
            copies(mine.at[j, here], left.at[:, columns_at((2 * j + core) * half, half)]),
            copies(other.at[j], left.at[:, columns_at((2 * j + 1 - core) * half, half)]),
        )
    ]
    grad_copy = copies(grad_branch.at[here], grad)
    start_all(left_copies + [grad_copy])
    wait_all(left_copies)
    for start in range(0, width, step):
        cols = slice(start, start + step)
        total = dot(left[...], weight[cols, :], 1, 1)
        if start == 0:
            grad_copy.wait()
        out[:, cols] = (grad[:, cols] + total).astype(bf16)


def project_back_cross_kernel(scalars, mine, other, grad_branch, weight, out, left, grad, sems):
    project_back_rows(
        scalars[0], Copies(sems), 1, mine, other, grad_branch, weight, left, grad, out
    )


def project_back_own_kernel(
    scalars, mine, other, grad_branch, weight, theirs, _, out, hidden_out, left, grad, theirs_v, sems
):
    core, chip = scalars[0], scalars[1]
    copies = Copies(sems)
    theirs_in = copies(theirs, theirs_v)
    theirs_out = copies(theirs_v, hidden_out.at[1 - chip])
    theirs_in.start()
    theirs_in.wait()
    theirs_out.start()
    project_back_rows(core, copies, 0, mine, other, grad_branch, weight, left, grad, out)
    theirs_out.wait()


def project_back_scratch(rows, weight):
    width, columns = weight.shape
    return [pltpu.VMEM((rows, columns), bf16), pltpu.VMEM((rows, width), f32)]


def project_back_cross(scalars, mine, other, grad_branch, weight):
    _, rows, _ = other.shape
    return pl.pallas_call(
        project_back_cross_kernel,
        in_specs=[SM] + [ANY] * 3 + [VM],
        out_specs=VM,
        out_shape=jax.ShapeDtypeStruct((rows, weight.shape[0]), bf16),
        scratch_shapes=project_back_scratch(rows, weight) + [pltpu.SemaphoreType.DMA((7,))],
        compiler_params=params(40),
        cost_estimate=cost(*BRIEF),
        name="project_back_cross",
    )(scalars, *near_core(mine, other), grad_branch, *near_core(weight))


def project_back_own(scalars, mine, other, grad_branch, weight, theirs, hidden_out):
    _, rows, _ = other.shape
    width = weight.shape[0]
    return pl.pallas_call(
        project_back_own_kernel,
        in_specs=[SM] + [ANY] * 3 + [VM] + [ANY] * 2,
        out_specs=[VM, ANY],
        out_shape=[
            jax.ShapeDtypeStruct((rows, width), bf16),
            jax.ShapeDtypeStruct(hidden_out.shape, bf16),
        ],
        input_output_aliases={6: 1},
        scratch_shapes=project_back_scratch(rows, weight)
        + [pltpu.VMEM((rows, width), bf16), pltpu.SemaphoreType.DMA((9,))],
        compiler_params=params(40),
        cost_estimate=cost(*BRIEF),
        name="project_back_own",
    )(scalars, *near_core(mine, other), grad_branch, *near_core(weight), theirs, hidden_out)


def shards(
    sizes,
    hidden_in,
    pair_lengths,
    prefix_keys,
    prefix_values,
    project_weight,
    project_bias,
    output_weight,
    output_bias,
    first_gain,
    first_shift,
    expand_weight,
    expand_bias,
    reduce_weight,
    reduce_bias,
    second_gain,
    second_shift,
    upstream,
):
    dp_size, mp_size = sizes
    rows_here, shard_len, width = hidden_in.shape
    hidden_here = expand_weight.shape[1]
    prefix = prefix_keys.shape[0]
    half = width // 2
    place = lax.axis_index("mp")
    chip, core = place // 2, place % 2
    part = lax.axis_index("dp") % 4
    scalars = jnp.stack([core, chip, part]).astype(jnp.int32)

    def across(array):
        return swap(array, "mp", 2, mp_size)

    def beside(array):
        return swap(array, "mp", 1, mp_size)

    def take(array, index):
        return lax.dynamic_index_in_dim(array, index, 0, keepdims=False)

    def row(vector):
        return vector.reshape(1, -1)

    cross = across(take(hidden_in, 1 - chip))
    hidden2 = beside(hidden_in)

    boundary = jnp.cumsum(take(pair_lengths, chip))
    blocks = jnp.stack(
        [2 * chip + core, 2 * chip + 1 - core, 2 * (1 - chip) + core, 2 * (1 - chip) + 1 - core]
    )
    position = (
        blocks[:, None] * shard_len + jnp.arange(shard_len, dtype=jnp.int32)[None, :]
    ).reshape(-1)
    segment = jnp.sum((position[:, None] >= boundary[None, :]).astype(jnp.int32), axis=1)
    column = jnp.arange(128, dtype=jnp.int32)[None, :]
    query_mask = (segment[:, None] == column).astype(bf16)
    key_mask = jnp.where(
        (segment[:, None] == column) & (column < PAIRS), 0.0, masked_score
    ).astype(bf16)
    key_mask = jnp.concatenate([jnp.zeros((prefix, 128), bf16), key_mask], 0)

    pack0, pack3 = pack(scalars, expand_weight, reduce_weight, expand_bias, upstream)
    qkv, core_weight = project_first(scalars, hidden_in, hidden2, project_weight, project_bias)
    expand_sib, reduce_sib, bias_sib = beside(expand_weight), beside(reduce_weight), beside(expand_bias)
    cross, qkv, key_mask, query_mask, expand_sib, reduce_sib, bias_sib = lax.optimization_barrier(
        (cross, qkv, key_mask, query_mask, expand_sib, reduce_sib, bias_sib)
    )
    cross2 = beside(cross)
    piece0, piece3 = across(pack0), across(pack3)
    qkv = project_second(scalars, cross, cross2, core_weight, project_bias, qkv)
    attended_mine, attended_other, exps_mine, exps_other, recips_mine, recips_other = attend(
        scalars, qkv, prefix_keys, prefix_values, key_mask, query_mask
    )
    piece0, attended_other = lax.optimization_barrier((piece0, attended_other))
    piece1, piece2 = swap(piece0, "dp", 1, dp_size), swap(piece0, "dp", 2, dp_size)
    attended_here, piece0_sib = beside(attended_other), beside(piece0)
    attended_here, piece0_sib = lax.optimization_barrier((attended_here, piece0_sib))
    weights = tuple(
        far_core(array) for array in (expand_weight, expand_sib, reduce_weight, reduce_sib)
    )

    unit, inverse, total, slope, low = forward(
        scalars, attended_mine, attended_here, hidden_in, cross,
        (output_bias, first_gain, first_shift), output_weight, weights + (expand_bias, bias_sib),
        (piece0, piece0_sib),
    )
    quarter = hidden_here // 4
    piece1, piece2, low = lax.optimization_barrier((piece1, piece2, low))
    piece1_sib, piece2_sib = beside(piece1), beside(piece2)
    total, slope2 = remote(scalars, low, total, (1, 2), [piece1, piece2], quarter)
    piece3, total, slope2 = lax.optimization_barrier((piece3, total, slope2))
    quarter3 = piece3[: 2 * quarter]
    late = [quarter3, beside(quarter3)]
    total, slope2 = near_core(total, slope2)
    total, slope3 = remote(scalars, low, total, (1, 2), [piece1_sib, piece2_sib], quarter)
    *late, total, slope2, slope3 = lax.optimization_barrier((*late, total, slope2, slope3))
    *late, piece3, total, slope2, slope3 = near_core(*late, piece3, total, slope2, slope3)
    early = [piece0, piece0_sib, piece1, piece2, piece1_sib, piece2_sib]
    hidden_own, hidden_cross, grad_branch, grad_mine, grad_theirs = middle(
        scalars, query_mask,
        (first_gain, first_shift, reduce_bias, second_gain, second_shift),
        (low, unit, inverse, total, slope, slope2, slope3), upstream, output_weight, weights, early, late,
        piece3,
    )
    grad_here = beside(grad_theirs)
    exps, recips = (exps_mine, exps_other), (recips_mine, recips_other)

    hidden_theirs = across(hidden_cross)
    back_mine, back_own2, back_cross2, grad_prefix, last_weight = attend_back(
        scalars, qkv, prefix_keys, prefix_values, exps, recips, (attended_mine, attended_other),
        near_core(grad_mine, grad_here), far_core(project_weight),
    )
    back_mine, back_own2, back_cross2, grad_prefix, hidden_theirs = lax.optimization_barrier(
        (back_mine, back_own2, back_cross2, grad_prefix, hidden_theirs)
    )

    def step(array, dp_bit, mp_bit):
        return lax.ppermute(
            array, ("dp", "mp"),
            [
                (d * mp_size + m, (d ^ dp_bit) * mp_size + (m ^ mp_bit))
                for d in range(dp_size)
                for m in range(mp_size)
            ],
        )

    def four_sum(parts):
        own_part, first, second, both = (part.astype(f32) for part in parts)
        return (own_part + first) + (second + both)

    cross_there = beside(back_cross2)
    own_there = beside(back_own2)
    low_prefix = grad_prefix.astype(bf16)
    group = (low_prefix, step(low_prefix, 0, 2), step(low_prefix, 1, 0), step(low_prefix, 1, 2))
    grad_branch = far_core(grad_branch)
    in_cross = project_back_cross(scalars, back_mine, cross_there, grad_branch, last_weight)
    in_cross, group = lax.optimization_barrier((in_cross, group))
    in_cross = across(in_cross)
    grad_prefix = four_sum(group)
    bit = 8
    while bit < dp_size:
        grad_prefix = grad_prefix + swap(grad_prefix, "dp", bit, dp_size)
        bit *= 2
    low_prefix = grad_prefix.astype(bf16)
    group = (low_prefix, step(low_prefix, 2, 0), step(low_prefix, 4, 0), step(low_prefix, 6, 0))
    in_own, hidden_out = project_back_own(
        scalars, back_mine, own_there, grad_branch, last_weight, far_core(hidden_theirs), hidden_own
    )
    in_own, in_cross, group = lax.optimization_barrier((in_own, in_cross, group))
    grad_in = jnp.where(chip == 0, jnp.stack([in_own, in_cross]), jnp.stack([in_cross, in_own]))
    grad_prefix = four_sum(group)
    grad_prefix_sib = beside(grad_prefix)
    grad_prefix = jnp.where(
        core == 0,
        jnp.concatenate([grad_prefix, grad_prefix_sib], 2),
        jnp.concatenate([grad_prefix_sib, grad_prefix], 2),
    )
    return (hidden_out, grad_in, grad_prefix[0], grad_prefix[1])


def solution(mesh):
    placed = (
        P("dp", "mp", None),
        P("dp", None),
        P(),
        P(),
        P(),
        P(),
        P(),
        P(),
        P(),
        P(),
        P(None, "mp"),
        P("mp"),
        P("mp", None),
        P(),
        P(),
        P(),
        P("dp", "mp", None),
    )
    return jax.shard_map(
        functools.partial(shards, (mesh.shape["dp"], mesh.shape["mp"])),
        mesh=mesh,
        in_specs=placed,
        out_specs=(P("dp", "mp", None), P("dp", "mp", None), P(), P()),
        check_vma=False,
    )
```

```python
import functools

import jax
import jax.numpy as jnp
from jax import lax
from jax.experimental import pallas as pl
from jax.experimental.pallas import tpu as pltpu
from jax.sharding import PartitionSpec as P

HEADS = 16
PAIRS = 8

epsilon = 1e-05
masked_score = -1e30
root_half = 0.7071067811865476
inverse_root = 0.3989422804014327
log2_e = 1.4426950408889634
ln_2 = 0.6931471805599453

bf16 = jnp.bfloat16
f32 = jnp.float32


def dot(left, right, left_dim=1, right_dim=0):
    return lax.dot_general(
        left, right, (((left_dim,), (right_dim,)), ((), ())), preferred_element_type=f32
    )


def params(mebibytes):
    return pltpu.CompilerParams(vmem_limit_bytes=mebibytes * 2**20)


def cost(flops, bytes_accessed, transcendentals=0):
    return pl.CostEstimate(
        flops=int(flops), bytes_accessed=int(bytes_accessed), transcendentals=int(transcendentals)
    )


ANY = pl.BlockSpec(memory_space=pl.ANY)


def far_core(array):
    return pltpu.with_memory_space_constraint(array, pltpu.HBM)


def near_core(*arrays):
    return tuple(pltpu.with_memory_space_constraint(array, pltpu.VMEM) for array in arrays)


VM = pl.BlockSpec(memory_space=pltpu.VMEM)
SM = pl.BlockSpec(memory_space=pltpu.SMEM)
BRIEF = (1e6, 1e5)


def swap(array, axis, bit, size):
    return lax.ppermute(array, axis, [(i, i ^ bit) for i in range(size)])


class Copies:
    def __init__(self, sems):
        self.sems, self.used = sems, 0

    def __call__(self, source, target):
        copy = pltpu.make_async_copy(source, target, self.sems.at[self.used])
        self.used += 1
        return copy


def start_all(copies):
    for copy in copies:
        copy.start()


def wait_all(copies):
    for copy in copies:
        copy.wait()


def columns_at(start, size):
    return pl.ds(pl.multiple_of(start, size), size)


def project_tokens(core, copies, parts, weight, weight_copies, bias, out, place, tokens_v, out_v):
    block = parts[0].shape[-2]
    half = out.shape[2]
    token_copies = [
        copies(part, tokens_v.at[pl.ds(i * block, block)]) for i, part in enumerate(parts)
    ]
    start_all(token_copies)
    start_all(weight_copies)
    wait_all(token_copies)
    out_copies = []
    for j in range(3):
        wait_all(weight_copies[j : j + 1])
        shift = jnp.where(
            core == 0,
            bias[2 * j * half : (2 * j + 1) * half].astype(f32),
            bias[(2 * j + 1) * half : (2 * j + 2) * half].astype(f32),
        )
        result = dot(tokens_v[...], weight[j]) + shift.reshape(1, half)
        if j == 0:
            result = result * (log2_e * 0.125)
        out_v[j] = result.astype(bf16)
        copy = copies(out_v.at[j], out.at[j, pl.ds(place * 2 * block, 2 * block)])
        copy.start()
        out_copies.append(copy)
    return out_copies


def pack_kernel(scalars, expand, reduce, hidden_bias, upstream, pack0, pack3, packs, bias_v, sems):
    chip, part = scalars[1], scalars[2]
    copies = Copies(sems)
    width, hidden_here = expand.shape
    quarter = hidden_here // 4
    bias_v[...] = jnp.broadcast_to(
        hidden_bias[...].astype(f32).reshape(1, hidden_here), (16, hidden_here)
    ).astype(bf16)
    groups = []
    for n, index in enumerate((part, 3 - part)):
        pack = packs.at[n]
        columns = columns_at(index * quarter, quarter)
        group = []
        for i in range(width // quarter):
            block = pl.ds(i * quarter, quarter)
            group.append(copies(expand.at[block, columns], pack.at[pl.ds(0, quarter), block]))
        group.append(copies(reduce.at[columns], pack.at[pl.ds(quarter, quarter)]))
        groups.append(group)
    groups[0].append(copies(bias_v, packs.at[0, pl.ds(2 * quarter, 16), pl.ds(0, hidden_here)]))
    groups[1].append(
        copies(upstream.at[1 - chip], packs.at[1, pl.ds(2 * quarter, upstream.shape[1])])
    )
    for group in groups:
        start_all(group)
    out_copies = []
    for n, (group, out) in enumerate(zip(groups, (pack0, pack3))):
        wait_all(group)
        copy = copies(packs.at[n, pl.ds(0, out.shape[0])], out)
        copy.start()
        out_copies.append(copy)
    wait_all(out_copies)


def pack(scalars, expand, reduce, hidden_bias, upstream):
    width, hidden_here = expand.shape
    quarter = hidden_here // 4
    packs = [
        jax.ShapeDtypeStruct((2 * quarter + n, width), bf16) for n in (16, upstream.shape[1])
    ]
    return pl.pallas_call(
        pack_kernel,
        in_specs=[SM, ANY, ANY, VM, ANY],
        out_specs=[ANY] * 2,
        out_shape=packs,
        scratch_shapes=[
            pltpu.VMEM((2, *packs[1].shape), bf16),
            pltpu.VMEM((16, hidden_here), bf16),
            pltpu.SemaphoreType.DMA((2 * (width // quarter + 2) + 2,)),
        ],
        compiler_params=params(56),
        cost_estimate=cost(*BRIEF),
        name="pack",
    )(scalars, expand, reduce, hidden_bias, upstream)


def project_first_kernel(
    scalars, hidden, hidden2, weight, bias, out, weight_out, tokens_v, out_v, sems
):
    core, chip = scalars[0], scalars[1]
    copies = Copies(sems)
    half = out.shape[2]
    weight_copies = [
        copies(weight.at[:, columns_at((2 * j + core) * half, half)], weight_out.at[j])
        for j in range(3)
    ]
    wait_all(
        project_tokens(
            core, copies, (hidden.at[chip], hidden2.at[chip]), weight_out, weight_copies, bias,
            out, 0, tokens_v, out_v,
        )
    )


def project_second_kernel(scalars, cross, cross2, weight, bias, _, out, tokens_v, out_v, sems):
    wait_all(
        project_tokens(
            scalars[0], Copies(sems), (cross, cross2), weight, [], bias, out, 1, tokens_v, out_v
        )
    )


def project_scratch(block, width, half):
    return [
        pltpu.VMEM((2 * block, width), bf16),
        pltpu.VMEM((3, 2 * block, half), bf16),
        pltpu.SemaphoreType.DMA((8,)),
    ]


def project_first(scalars, hidden, hidden2, weight, bias):
    _, block, width = hidden.shape
    half = width // 2
    return pl.pallas_call(
        project_first_kernel,
        in_specs=[SM, ANY, ANY, ANY, VM],
        out_specs=[ANY, VM],
        out_shape=[
            jax.ShapeDtypeStruct((3, 4 * block, half), bf16), pltpu.VMEM((3, width, half), bf16)
        ],
        scratch_shapes=project_scratch(block, width, half),
        compiler_params=params(50),
        cost_estimate=cost(*BRIEF),
        name="project_first",
    )(scalars, hidden, hidden2, weight, bias)


def project_second(scalars, cross, cross2, weight, bias, qkv):
    block, width = cross.shape
    half = width // 2
    return pl.pallas_call(
        project_second_kernel,
        in_specs=[SM, ANY, ANY, VM, VM, ANY],
        out_specs=ANY,
        out_shape=jax.ShapeDtypeStruct(qkv.shape, bf16),
        input_output_aliases={5: 0},
        scratch_shapes=project_scratch(block, width, half),
        compiler_params=params(50),
        cost_estimate=cost(*BRIEF),
        name="project_second",
    )(scalars, *near_core(cross, cross2, weight), bias, qkv)


def head_mask(shape, head, axis):
    return (lax.broadcasted_iota(jnp.int32, shape, axis) // 64) == head


def keep_head(array, head, axis):
    return jnp.where(head_mask(array.shape, head, axis), array, jnp.zeros_like(array))


def attend_kernel(
    core_ref, query, key, value, prefix_k, prefix_v, key_mask, query_mask,
    out_mine, out_other, exps_mine, exps_other, recips_mine, recips_other, keys, values_t,
):
    prefix = prefix_k.shape[0]
    tokens = query.shape[1]
    count = prefix + tokens
    chunk = tokens // 4
    keys[:prefix, :128] = prefix_k[...]
    keys[prefix:, :128] = key[0]

    @pl.when(pl.program_id(0) == 0)
    def _():
        keys[:, 128:] = key_mask[...]
        values_t[:, 64:, :] = jnp.ones((2, values_t.shape[1] - 64, count), bf16)

    prefix_t = prefix_v[...].astype(f32).T.astype(bf16)
    value_t = value[0].astype(f32).T.astype(bf16)
    for head in range(2):
        values_t[head, :64, :prefix] = prefix_t[64 * head : 64 * head + 64]
        values_t[head, :64, prefix:] = value_t[64 * head : 64 * head + 64]
    units = [(i, head) for i in (1, 3, 0, 2) for head in range(2)]

    def score(unit):
        i, head = unit
        rows = slice(i * chunk, (i + 1) * chunk)
        masked = jnp.concatenate([keep_head(query[0, rows, :], head, 1), query_mask[rows, :]], axis=1)
        return dot(keys[...], masked, 1, 1)

    ahead = 2
    pending = [score(unit) for unit in units[:ahead]]
    for n, (i, head) in enumerate(units):
        scores = pending.pop(0)
        if n + ahead < len(units):
            pending.append(score(units[n + ahead]))
        out, exps, recips = (
            (out_mine, exps_mine, recips_mine), (out_other, exps_other, recips_other)
        )[i % 2]
        cols = slice(i // 2 * chunk, (i // 2 + 1) * chunk)
        top = jnp.max(scores, axis=0, keepdims=True)
        weights = jnp.exp2(scores - top).astype(bf16)
        exps[0, head, :, cols] = weights
        summed = dot(values_t[head], weights)
        recip = 1.0 / summed[64:65, :]
        recips[0, head, :, cols] = jnp.broadcast_to(recip, (8, chunk))
        out[64 * head : 64 * head + 64, cols] = (summed[:64, :] * recip).astype(bf16)


def attend(core, qkv, prefix_keys, prefix_values, key_mask, query_mask):
    _, tokens, half = qkv.shape
    prefix = prefix_keys.shape[0]
    count = prefix + tokens
    pairs = half // 128
    prefix_spec = pl.BlockSpec((prefix, 128), lambda p, k: (0, k[0] * pairs + p))
    out_spec = pl.BlockSpec((128, tokens // 2), lambda p, k: (p, 0))
    exps_spec = pl.BlockSpec((1, 2, count, tokens // 2), lambda p, k: (p, 0, 0, 0))
    recips_spec = pl.BlockSpec((1, 2, 8, tokens // 2), lambda p, k: (p, 0, 0, 0))
    return pl.pallas_call(
        attend_kernel,
        grid_spec=pltpu.PrefetchScalarGridSpec(
            num_scalar_prefetch=1,
            grid=(pairs,),
            in_specs=[
                pl.BlockSpec((1, tokens, 128), lambda p, k, j=j: (j, 0, p)) for j in range(3)
            ]
            + [
                prefix_spec,
                prefix_spec,
                pl.BlockSpec((count, 128), lambda p, k: (0, 0)),
                pl.BlockSpec((tokens, 128), lambda p, k: (0, 0)),
            ],
            out_specs=[out_spec] * 2 + [exps_spec] * 2 + [recips_spec] * 2,
            scratch_shapes=[pltpu.VMEM((count, 256), bf16), pltpu.VMEM((2, 64 + 16, count), bf16)],
        ),
        out_shape=[jax.ShapeDtypeStruct((half, tokens // 2), bf16)] * 2
        + [jax.ShapeDtypeStruct((pairs, 2, count, tokens // 2), bf16)] * 2
        + [jax.ShapeDtypeStruct((pairs, 2, 8, tokens // 2), f32)] * 2,
        compiler_params=params(56),
        cost_estimate=cost(*BRIEF),
        name="attend",
    )(core, qkv, qkv, qkv, prefix_keys, prefix_values, key_mask, query_mask)


def ordered_rows(array):
    block = array.shape[0] // 4
    return [array[i * block : (i + 1) * block] for i in (0, 2, 1, 3)]


def attend_back_kernel(
    core_ref, query, key, value, prefix_k, prefix_v, exps_mine, exps_other, recips_mine, recips_other,
    attended_mine, attended_other, grad_mine, grad_other, weight,
    out_mine, out_own2, out_cross2, out_prefix, weight_out,
    keys, values, keys_t, slopes, queries, queries_t, scaled, weight_sem,
):
    prefix = prefix_k.shape[0]
    tokens = query.shape[1]
    chunk = tokens // 4
    half = tokens // 2
    pair = pl.program_id(0)
    weight_copy = pltpu.make_async_copy(weight, weight_out, weight_sem.at[0])

    @pl.when(pair == 1)
    def _():
        weight_copy.start()

    keys[:prefix, :] = prefix_k[...]
    keys[prefix:, :] = key[0]
    values[:prefix, :] = prefix_v[...]
    values[prefix:, :] = value[0]
    keys_t[...] = keys[...].astype(f32).T.astype(bf16)
    queries[...] = jnp.concatenate(ordered_rows(query[0]), axis=0)
    spreads = []
    for head in range(2):
        rows = slice(64 * head, 64 * head + 64)
        parts = []
        for side, (recips, attended, grad) in enumerate(
            ((recips_mine, attended_mine, grad_mine), (recips_other, attended_other, grad_other))
        ):
            part = grad[rows, :].astype(f32) * recips[0, head, 0:1, :]
            scaled[rows, side * half : (side + 1) * half] = part.astype(bf16)
            parts.append(jnp.sum(part * attended[rows, :].astype(f32), axis=0, keepdims=True))
        spreads.append(jnp.concatenate(parts, axis=1))
    units = [(head, i) for head in range(2) for i in range(4)]

    def head_rows(array, head):
        zeros = jnp.zeros_like(array[:64])
        return jnp.concatenate([array[:64], zeros] if head == 0 else [zeros, array[64:]], axis=0)

    def grad_probs(unit):
        head, i = unit
        return dot(values[...], head_rows(scaled[:, i * chunk : (i + 1) * chunk], head))

    def exps_of(head, i):
        return (exps_mine, exps_other)[i // 2][0, head, :, i % 2 * chunk : (i % 2 + 1) * chunk]

    def value_part(head):
        total = None
        for side, exps in enumerate((exps_mine, exps_other)):
            cols = slice(side * half, (side + 1) * half)
            part = dot(exps[0, head], head_rows(scaled[:, cols], head), 1, 1)
            total = part if total is None else total + part
        return total

    def key_part(head):
        return dot(slopes[head], keep_head(queries[...], head, 1))

    ahead = 4
    pending = [grad_probs(unit) for unit in units[:ahead]]
    for n, (head, i) in enumerate(units):
        grads = pending.pop(0)
        if n + ahead < len(units):
            pending.append(grad_probs(units[n + ahead]))
        cols = slice(i * chunk, (i + 1) * chunk)
        slopes[head, :, cols] = (
            exps_of(head, i).astype(f32) * (grads - spreads[head][:, cols])
        ).astype(bf16)
        if n == 0:
            value_first = value_part(0)
        rows = slice(64 * head, 64 * head + 64)
        queries_t[rows, cols] = dot(keys_t[rows, :], slopes[head, :, cols]) * 0.125
        if n == 4:
            key_first = key_part(0)
    value_grads = value_first + value_part(1)
    key_grads = (key_first + key_part(1)) * ln_2
    out_prefix[0] = key_grads[:prefix]
    out_prefix[1] = value_grads[:prefix]
    query_grads = queries_t[...].T.astype(bf16)
    for j, parts in enumerate(
        ([query_grads[i * chunk : (i + 1) * chunk] for i in range(4)],)
        + tuple(ordered_rows(array[prefix:].astype(bf16)) for array in (key_grads, value_grads))
    ):
        out_mine[j, :chunk] = parts[0]
        out_mine[j, chunk:] = parts[1]
        out_own2[j] = parts[2]
        out_cross2[j] = parts[3]

    @pl.when(pair == pl.num_programs(0) - 1)
    def _():
        weight_copy.wait()


def attend_back(core, qkv, prefix_keys, prefix_values, exps, recips, attended, grads, weight):
    _, tokens, half = qkv.shape
    prefix = prefix_keys.shape[0]
    count = prefix + tokens
    pairs = half // 128
    prefix_spec = pl.BlockSpec((prefix, 128), lambda p, k: (0, k[0] * pairs + p))
    exps_spec = pl.BlockSpec((1, 2, count, tokens // 2), lambda p, k: (p, 0, 0, 0))
    recips_spec = pl.BlockSpec((1, 2, 8, tokens // 2), lambda p, k: (p, 0, 0, 0))
    heads_spec = pl.BlockSpec((128, tokens // 2), lambda p, k: (p, 0))
    rows = (tokens // 2, tokens // 4, tokens // 4)
    return pl.pallas_call(
        attend_back_kernel,
        grid_spec=pltpu.PrefetchScalarGridSpec(
            num_scalar_prefetch=1,
            grid=(pairs,),
            in_specs=[
                pl.BlockSpec((1, tokens, 128), lambda p, k, j=j: (j, 0, p)) for j in range(3)
            ]
            + [prefix_spec] * 2
            + [exps_spec] * 2
            + [recips_spec] * 2
            + [heads_spec] * 4
            + [ANY],
            out_specs=[pl.BlockSpec((3, n, 128), lambda p, k: (0, 0, p)) for n in rows]
            + [pl.BlockSpec((2, prefix, 128), lambda p, k: (0, 0, p)), ANY],
            scratch_shapes=[
                pltpu.VMEM((count, 128), bf16),
                pltpu.VMEM((count, 128), bf16),
                pltpu.VMEM((128, count), bf16),
                pltpu.VMEM((2, count, tokens), bf16),
                pltpu.VMEM((tokens, 128), bf16),
                pltpu.VMEM((128, tokens), f32),
                pltpu.VMEM((128, tokens), bf16),
                pltpu.SemaphoreType.DMA((1,)),
            ],
        ),
        out_shape=[pltpu.VMEM((3, rows[0], half), bf16)]
        + [jax.ShapeDtypeStruct((3, n, half), bf16) for n in rows[1:]]
        + [jax.ShapeDtypeStruct((2, prefix, half), f32), pltpu.VMEM(weight.shape, bf16)],
        compiler_params=params(40),
        cost_estimate=cost(*BRIEF),
        name="attend_back",
    )(core, qkv, qkv, qkv, prefix_keys, prefix_values, *exps, *recips, *attended, *grads, weight)


def mean_rows(array):
    return jnp.mean(array, axis=-1, keepdims=True)


def unit_norm(array):
    centered = array - mean_rows(array)
    inverse = lax.rsqrt(mean_rows(centered * centered) + epsilon)
    return centered * inverse, inverse


def norm_back(scaled, unit, inverse):
    return inverse * (scaled - mean_rows(scaled) - unit * mean_rows(scaled * unit))


def gelu_both(hidden):
    gate = 0.5 * (1.0 + lax.erf(hidden * root_half))
    slope = gate + hidden * inverse_root * jnp.exp(-0.5 * hidden * hidden)
    return (hidden * gate).astype(bf16), slope.astype(bf16)


def feed_forward(steps, total):
    hidden = None
    for i, step in enumerate(steps):
        if i == 0:
            wait_all(step[3])
            hidden = step[0]()
        following = None
        if i + 1 < len(steps):
            wait_all(steps[i + 1][3])
            following = steps[i + 1][0]()
        active, slope = gelu_both(hidden)
        step[1](slope)
        part = dot(active, step[2]())
        if total is None:
            total = part
        elif hasattr(total, "at"):
            total[...] += part
        hidden = following


def forward_kernel(
    core_ref, mine, other, own, cross, output_bias, first_gain, first_shift, output_weight,
    expand_own, expand_sib, reduce_own, reduce_sib, bias_own, bias_sib, piece0, piece1,
    unit_out, inverse_out, total_out, slope_out, low,
    out_w, expand_w, reduce_w, expand_r, reduce_r, bias_r, own_v, sems,
):
    core, chip = core_ref[0], core_ref[1]
    copies = [
        pltpu.make_async_copy(output_weight, out_w, sems.at[0]),
        pltpu.make_async_copy(expand_own, expand_w.at[0], sems.at[1]),
        pltpu.make_async_copy(reduce_own, reduce_w.at[0], sems.at[2]),
        pltpu.make_async_copy(expand_sib, expand_w.at[1], sems.at[3]),
        pltpu.make_async_copy(reduce_sib, reduce_w.at[1], sems.at[4]),
        pltpu.make_async_copy(own.at[chip], own_v, sems.at[5]),
    ]
    start_all(copies[5:] + copies[:5])
    piece_sems = Copies(sems)
    piece_sems.used = 6
    quarter = reduce_r.shape[0] // 2
    waits = piece_copies(piece_sems, (piece0, piece1), 0, quarter, expand_r, reduce_r)
    waits[0] = waits[0] + bias_copies(piece_sems, (piece0, piece1), quarter, bias_r)
    for group in waits:
        start_all(group)
    biases = bias_rows(core_ref[2], (0, 0), quarter, bias_r)
    copies[5].wait()
    copies[0].wait()
    half = mine.shape[0]
    block = own_v.shape[0]
    output_row, gain, shift = (
        ref[...].astype(f32).reshape(1, -1) for ref in (output_bias, first_gain, first_shift)
    )
    for i, ref in enumerate((own_v, cross)):
        rows = slice(i * block, (i + 1) * block)
        branch = dot(mine[:, rows], out_w[pl.ds(pl.multiple_of(core * half, half), half), :], 0, 0)
        branch += dot(
            other[:, rows], out_w[pl.ds(pl.multiple_of((1 - core) * half, half), half), :], 0, 0
        )
        unit, inverse = unit_norm(ref[...].astype(f32) + (branch + output_row))
        unit_out[rows, :] = unit
        inverse_out[rows, :] = jnp.broadcast_to(inverse, (block, 128))
        low[rows, :] = (unit * gain + shift).astype(bf16)
    chunk = 512
    hidden_here = expand_own.shape[1]

    def step(i, bias, start):
        cols = slice(start, start + chunk)

        def store(slope):
            slope_out[:, i * hidden_here + start : i * hidden_here + start + chunk] = slope

        return (
            lambda: dot(low[...], expand_w[i, :, cols]) + bias[cols].astype(f32).reshape(1, chunk),
            store,
            lambda: reduce_w[i, cols, :],
            copies[1 + 2 * i : 3 + 2 * i] if start == 0 else [],
        )

    total_out[...] = jnp.zeros(total_out.shape, f32)
    feed_forward(
        [
            step(i, bias, start)
            for i, bias in enumerate((bias_own, bias_sib))
            for start in range(0, hidden_here, chunk)
        ]
        + piece_steps(
            2, 0, quarter, low, expand_r, reduce_r, biases, slope_out, waits, 2 * hidden_here
        ),
        total_out,
    )


def forward(core, mine, other, own, cross, vectors, output_weight, weights, pieces):
    tokens = mine.shape[1]
    _, block, width = own.shape
    hidden = weights[0].shape[1]
    quarter = hidden // 4
    return pl.pallas_call(
        forward_kernel,
        in_specs=[SM, VM, VM, ANY] + [VM] * 4 + [ANY] * 5 + [VM] * 2 + [ANY] * 2,
        out_specs=[VM] * 5,
        out_shape=[
            jax.ShapeDtypeStruct((tokens, width), f32),
            jax.ShapeDtypeStruct((tokens, 128), f32),
            jax.ShapeDtypeStruct((tokens, width), f32),
            jax.ShapeDtypeStruct((tokens, 2 * hidden + 2 * quarter), bf16),
            jax.ShapeDtypeStruct((tokens, width), bf16),
        ],
        scratch_shapes=[
            pltpu.VMEM((width, width), bf16),
            pltpu.VMEM((2, width, hidden), bf16),
            pltpu.VMEM((2, hidden, width), bf16),
            pltpu.VMEM((width, 2 * quarter), bf16),
            pltpu.VMEM((2 * quarter, width), bf16),
            pltpu.VMEM((2, 16, width), bf16),
            pltpu.VMEM((block, width), bf16),
            pltpu.SemaphoreType.DMA((6 + 2 * (width // quarter + 2),)),
        ],
        compiler_params=params(40),
        cost_estimate=cost(*BRIEF),
        name="forward",
    )(core, mine, other, own, cross, *vectors, output_weight, *weights, *pieces)


def piece_copies(copies, pieces, place, quarter, expand_r, reduce_r):
    width = expand_r.shape[0]
    result = []
    for i, piece in enumerate(pieces):
        here = pl.ds((place + i) * quarter, quarter)
        group = []
        for j in range(width // quarter):
            rows = pl.ds(j * quarter, quarter)
            group.append(copies(piece.at[pl.ds(0, quarter), rows], expand_r.at[rows, here]))
        group.append(copies(piece.at[pl.ds(quarter, quarter)], reduce_r.at[here]))
        result.append(group)
    return result


def bias_copies(copies, pieces, quarter, bias_r):
    return [
        copies(piece.at[pl.ds(2 * quarter, 16)], bias_r.at[i]) for i, piece in enumerate(pieces)
    ]


def bias_rows(part, bits, quarter, bias_r):
    return [
        lambda i=i, bit=bit: bias_r[
            i, 0:1, pl.ds(pl.multiple_of(lax.bitwise_xor(part, bit) * quarter, quarter), quarter)
        ]
        for i, bit in enumerate(bits)
    ]


def piece_steps(
    count, place, quarter, low, expand_r, reduce_r, biases, slope_out, waits, slope_place=0
):
    def step(first):
        rows = slice((place + first) * quarter, (place + first + 2) * quarter)

        def hidden():
            bias = [biases[first + i]() for i in range(2)]
            return dot(low[...], expand_r[:, rows]) + jnp.concatenate(bias, axis=1).astype(f32)

        def store(slope):
            start = slope_place + first * quarter
            slope_out[:, start : start + 2 * quarter] = slope

        return (
            hidden,
            store,
            lambda: reduce_r[rows, :],
            waits[first] + waits[first + 1],
        )

    return [step(first) for first in range(0, count, 2)]


def remote_kernel(bits, *refs):
    count = len(bits)
    scalars, low_in, total_in = refs[:3]
    pieces = refs[3 : 3 + count]
    total_out, slope_out, low, expand_r, reduce_r, bias_r, sems = refs[3 + count :]
    quarter = reduce_r.shape[0] // count
    copies = Copies(sems)
    first = [copies(low_in, low), copies(total_in, total_out)]
    waits = piece_copies(copies, pieces, 0, quarter, expand_r, reduce_r)
    waits[0] = waits[0] + bias_copies(copies, pieces, quarter, bias_r)
    start_all(first[:1] + waits[0] + waits[1] + first[1:])
    for group in waits[2:]:
        start_all(group)
    biases = bias_rows(scalars[2], bits, quarter, bias_r)
    steps = piece_steps(count, 0, quarter, low, expand_r, reduce_r, biases, slope_out, waits)
    steps[0] = steps[0][:3] + (first + steps[0][3],)
    feed_forward(steps, total_out)


def remote(scalars, low, total, bits, pieces, quarter):
    tokens, width = total.shape
    count = len(pieces)
    return pl.pallas_call(
        functools.partial(remote_kernel, bits),
        in_specs=[SM] + [ANY] * (2 + count),
        out_specs=[VM] * 2,
        out_shape=[
            pltpu.VMEM((tokens, width), f32),
            pltpu.VMEM((tokens, count * quarter), bf16),
        ],
        scratch_shapes=[
            pltpu.VMEM((tokens, width), bf16),
            pltpu.VMEM((width, count * quarter), bf16),
            pltpu.VMEM((count * quarter, width), bf16),
            pltpu.VMEM((count, 16, width), bf16),
            pltpu.SemaphoreType.DMA((2 + count * (width // quarter + 2),)),
        ],
        compiler_params=params(26),
        cost_estimate=cost(*BRIEF),
        name="remote",
    )(scalars, low, total, *pieces)


def middle_kernel(early, late, *refs):
    count = early + late
    scalars, query_mask = refs[:2]
    vectors = refs[2:7]
    low_in, unit_in, inverse, total_in, slope_in, slope2_in, slope3_in, upstream = refs[7:15]
    output_weight, expand_own, expand_sib, reduce_own, reduce_sib = refs[15:20]
    pieces = refs[20 : 20 + count]
    up_cross = refs[20 + count]
    hidden_own, hidden_cross, grad_out, att_mine, att_other = refs[21 + count : 26 + count]
    (
        out_w, expand_w, reduce_w, expand_r, reduce_r, bias_r, low, unit, acc, back_acc,
        slope_l, slope_e, slope_s, up, hidden, sems,
    ) = refs[26 + count :]
    core, chip = scalars[0], scalars[1]
    copies = Copies(sems)
    tokens, width = unit.shape
    block = tokens // 2
    quarter = reduce_r.shape[0] // count
    chunk = 2 * quarter
    hidden_here = expand_own.shape[1]
    rows_of = [pl.ds(i * block, block) for i in range(2)]

    up_cross = up_cross.at[pl.ds(2 * quarter, block)]
    low_copy = copies(low_in, low)
    late_waits = piece_copies(copies, pieces[early:], early, quarter, expand_r, reduce_r)
    late_waits[0] = late_waits[0] + bias_copies(copies, pieces[:2], quarter, bias_r)
    biases = bias_rows(scalars[2], (3, 3), quarter, bias_r)
    norm_copies = [
        [
            copies(total_in.at[rows_of[i]], acc.at[rows_of[i]]),
            copies(unit_in.at[rows_of[i]], unit.at[rows_of[i]]),
            copies((upstream.at[chip], up_cross)[i], up.at[rows_of[i]]),
        ]
        for i in range(2)
    ]
    local_copies = [
        [copies((reduce_own, reduce_sib)[i], reduce_w.at[i]), copies((expand_own, expand_sib)[i], expand_w.at[i])]
        for i in range(2)
    ]
    slope_copy = copies(slope_in, slope_l)
    early_copies = piece_copies(copies, pieces[:early], 0, quarter, expand_r, reduce_r)
    slope2_copies = [
        copies(array, slope_e.at[:, pl.ds(2 * i * quarter, 2 * quarter)])
        for i, array in enumerate((slope2_in, slope3_in))
    ]
    out_copy = copies(output_weight, out_w)
    start_all([low_copy] + [copy for group in late_waits + norm_copies for copy in group])
    start_all([local_copies[0][0], slope_copy, local_copies[0][1]] + local_copies[1])
    start_all([copy for group in early_copies for copy in group] + slope2_copies + [out_copy])

    steps = piece_steps(late, early, quarter, low, expand_r, reduce_r, biases, slope_s, late_waits)
    steps[0] = steps[0][:3] + ([low_copy] + steps[0][3],)
    for group in norm_copies:
        wait_all(group[:1])
    feed_forward(steps, acc)

    first_gain, first_shift, reduce_bias, second_gain, second_shift = (
        ref[...].astype(f32).reshape(1, -1) for ref in vectors
    )
    hidden_copies = []
    for i in range(2):
        wait_all(norm_copies[i][1:])
        for start in range(i * block, (i + 1) * block, block // 2):
            rows = slice(start, start + block // 2)
            masked = slice(2 * i * block + start - i * block, 2 * i * block + start - i * block + block // 2)
            live = 1.0 - query_mask[masked, PAIRS : PAIRS + 1].astype(f32)
            first_norm = unit[rows, :] * first_gain + first_shift
            unit2, inverse2 = unit_norm(first_norm + (acc[rows, :] + reduce_bias))
            hidden[rows, :] = ((unit2 * second_gain + second_shift) * live).astype(bf16)
            grad_feed = norm_back(up[rows, :].astype(f32) * live * second_gain, unit2, inverse2)
            back_acc[rows, :] = grad_feed
            low[rows, :] = grad_feed.astype(bf16)
        copy = copies(hidden.at[rows_of[i]], (hidden_own.at[chip], hidden_cross)[i])
        copy.start()
        hidden_copies.append(copy)

    backs = []
    for i in range(2):
        for start in range(0, hidden_here, chunk):
            cols = slice(start, start + chunk)
            place = slice(i * hidden_here + start, i * hidden_here + start + chunk)
            backs.append(
                (
                    lambda i=i, cols=cols: reduce_w[i, cols, :],
                    lambda i=i, cols=cols: expand_w[i, :, cols],
                    1,
                    lambda place=place: slope_l[:, place],
                    ([slope_copy] if i + start == 0 else []) + (local_copies[i] if start == 0 else []),
                )
            )
    total_pieces = early + late
    for first in range(0, total_pieces, 2):
        rows = slice(first * quarter, (first + 2) * quarter)

        def slopes(first=first):
            parts = [
                slope_l[:, 2 * hidden_here + j * quarter : 2 * hidden_here + (j + 1) * quarter]
                if j < 2
                else slope_e[:, (j - 2) * quarter : (j - 1) * quarter]
                if j < early
                else slope_s[:, (j - early) * quarter : (j - early + 1) * quarter]
                for j in (first, first + 1)
            ]
            return jnp.concatenate(parts, axis=1)

        waits = [copy for j in (first, first + 1) if j < early for copy in early_copies[j]]
        backs.append(
            (
                lambda rows=rows: reduce_r[rows, :],
                lambda rows=rows: expand_r[:, rows],
                1,
                slopes,
                (slope2_copies if first == 0 else []) + waits,
            )
        )

    def grads(step):
        wait_all(step[4])
        return dot(low[...], step[0](), 1, 1)

    grad = grads(backs[0])
    for i, step in enumerate(backs):
        following = grads(backs[i + 1]) if i + 1 < len(backs) else None
        back = (grad * step[3]().astype(f32)).astype(bf16)
        back_acc[...] += dot(back, step[1](), 1, step[2])
        grad = following

    grad_copies = []
    for i in range(2):
        for start in range(i * block, (i + 1) * block, block // 2):
            rows = slice(start, start + block // 2)
            grad = norm_back(back_acc[rows, :] * first_gain, unit[rows, :], inverse[rows, 0:1])
            acc[rows, :] = grad
            low[rows, :] = grad.astype(bf16)
        copy = copies(acc.at[rows_of[i]], grad_out.at[rows_of[i]])
        copy.start()
        grad_copies.append(copy)
    out_copy.wait()
    half = width // 2
    att_other[...] = dot(
        out_w[pl.ds(pl.multiple_of((1 - core) * half, half), half), :], low[...], 1, 1
    ).astype(bf16)
    att_mine[...] = dot(
        out_w[pl.ds(pl.multiple_of(core * half, half), half), :], low[...], 1, 1
    ).astype(bf16)
    wait_all(hidden_copies + grad_copies)


def middle(scalars, query_mask, vectors, saved, upstream, output_weight, weights, early, late, last):
    tokens, width = saved[1].shape
    block = tokens // 2
    hidden = weights[0].shape[1]
    quarter = hidden // 4
    pieces = early + late
    count = len(pieces)
    return pl.pallas_call(
        functools.partial(middle_kernel, len(early), len(late)),
        in_specs=[SM] + [VM] * 6 + [ANY] * 2 + [VM] + [ANY] * (11 + count),
        out_specs=[ANY] * 3 + [VM] * 2,
        out_shape=[
            jax.ShapeDtypeStruct(upstream.shape, bf16),
            jax.ShapeDtypeStruct((block, width), bf16),
            jax.ShapeDtypeStruct((tokens, width), f32),
            pltpu.VMEM((width // 2, tokens), bf16),
            pltpu.VMEM((width // 2, tokens), bf16),
        ],
        scratch_shapes=[
            pltpu.VMEM((width, width), bf16),
            pltpu.VMEM((2, width, hidden), bf16),
            pltpu.VMEM((2, hidden, width), bf16),
            pltpu.VMEM((width, count * quarter), bf16),
            pltpu.VMEM((count * quarter, width), bf16),
            pltpu.VMEM((len(late), 16, width), bf16),
            pltpu.VMEM((tokens, width), bf16),
            pltpu.VMEM((tokens, width), f32),
            pltpu.VMEM((tokens, width), f32),
            pltpu.VMEM((tokens, width), f32),
            pltpu.VMEM((tokens, 2 * hidden + 2 * quarter), bf16),
            pltpu.VMEM((tokens, (len(early) - 2) * quarter), bf16),
            pltpu.VMEM((tokens, len(late) * quarter), bf16),
            pltpu.VMEM((tokens, width), bf16),
            pltpu.VMEM((tokens, width), bf16),
            pltpu.SemaphoreType.DMA((19 + len(late) + count * (width // quarter + 1),)),
        ],
        compiler_params=params(42),
        cost_estimate=cost(*BRIEF),
        name="middle",
    )(
        scalars, query_mask, *vectors, *saved, upstream, output_weight, *weights,
        *pieces, last,
    )


def project_back_rows(core, copies, place, mine, other, grad_branch, weight, left, grad, out):
    rows, width = out.shape
    half = other.shape[2]
    step = width // 4
    here = pl.ds(place * rows, rows)
    left_copies = [
        copy
        for j in range(3)
        for copy in (
            copies(mine.at[j, here], left.at[:, columns_at((2 * j + core) * half, half)]),
            copies(other.at[j], left.at[:, columns_at((2 * j + 1 - core) * half, half)]),
        )
    ]
    grad_copy = copies(grad_branch.at[here], grad)
    start_all(left_copies + [grad_copy])
    wait_all(left_copies)
    for start in range(0, width, step):
        cols = slice(start, start + step)
        total = dot(left[...], weight[cols, :], 1, 1)
        if start == 0:
            grad_copy.wait()
        out[:, cols] = (grad[:, cols] + total).astype(bf16)


def project_back_cross_kernel(
    scalars, mine, other, grad_branch, weight, first, second, left, grad, out, sems
):
    project_back_rows(
        scalars[0], Copies(sems), 1, mine, other, grad_branch, weight, left, grad, out
    )
    half = first.shape[0]
    first[...] = out[:half, :]
    second[...] = out[half:, :]


def project_back_own_kernel(
    scalars, mine, other, grad_branch, weight, theirs, _, out, hidden_out, left, grad, theirs_v, sems
):
    core, chip = scalars[0], scalars[1]
    copies = Copies(sems)
    theirs_in = copies(theirs, theirs_v)
    theirs_out = copies(theirs_v, hidden_out.at[1 - chip])
    theirs_in.start()
    theirs_in.wait()
    theirs_out.start()
    project_back_rows(core, copies, 0, mine, other, grad_branch, weight, left, grad, out)
    theirs_out.wait()


def project_back_scratch(rows, weight):
    width, columns = weight.shape
    return [pltpu.VMEM((rows, columns), bf16), pltpu.VMEM((rows, width), f32)]


def project_back_cross(scalars, mine, other, grad_branch, weight):
    _, rows, _ = other.shape
    out = jax.ShapeDtypeStruct((rows // 2, weight.shape[0]), bf16)
    return pl.pallas_call(
        project_back_cross_kernel,
        in_specs=[SM] + [ANY] * 3 + [VM],
        out_specs=[VM, VM],
        out_shape=[out, out],
        scratch_shapes=project_back_scratch(rows, weight)
        + [pltpu.VMEM((rows, weight.shape[0]), bf16), pltpu.SemaphoreType.DMA((7,))],
        compiler_params=params(16),
        cost_estimate=cost(*BRIEF),
        name="project_back_cross",
    )(scalars, *near_core(mine, other), grad_branch, *near_core(weight))


def project_back_own(scalars, mine, other, grad_branch, weight, theirs, hidden_out):
    _, rows, _ = other.shape
    width = weight.shape[0]
    return pl.pallas_call(
        project_back_own_kernel,
        in_specs=[SM] + [ANY] * 3 + [VM] + [ANY] * 2,
        out_specs=[VM, ANY],
        out_shape=[
            jax.ShapeDtypeStruct((rows, width), bf16),
            jax.ShapeDtypeStruct(hidden_out.shape, bf16),
        ],
        input_output_aliases={6: 1},
        scratch_shapes=project_back_scratch(rows, weight)
        + [pltpu.VMEM((rows, width), bf16), pltpu.SemaphoreType.DMA((9,))],
        compiler_params=params(16),
        cost_estimate=cost(*BRIEF),
        name="project_back_own",
    )(scalars, *near_core(mine, other), grad_branch, *near_core(weight), theirs, hidden_out)


def shards(
    sizes,
    hidden_in,
    pair_lengths,
    prefix_keys,
    prefix_values,
    project_weight,
    project_bias,
    output_weight,
    output_bias,
    first_gain,
    first_shift,
    expand_weight,
    expand_bias,
    reduce_weight,
    reduce_bias,
    second_gain,
    second_shift,
    upstream,
):
    dp_size, mp_size = sizes
    rows_here, shard_len, width = hidden_in.shape
    hidden_here = expand_weight.shape[1]
    prefix = prefix_keys.shape[0]
    half = width // 2
    place = lax.axis_index("mp")
    chip, core = place // 2, place % 2
    part = lax.axis_index("dp") % 4
    scalars = jnp.stack([core, chip, part]).astype(jnp.int32)

    def across(array):
        return swap(array, "mp", 2, mp_size)

    def beside(array):
        return swap(array, "mp", 1, mp_size)

    def take(array, index):
        return lax.dynamic_index_in_dim(array, index, 0, keepdims=False)

    def row(vector):
        return vector.reshape(1, -1)

    cross = across(take(hidden_in, 1 - chip))
    hidden2 = beside(hidden_in)

    boundary = jnp.cumsum(take(pair_lengths, chip))
    blocks = jnp.stack(
        [2 * chip + core, 2 * chip + 1 - core, 2 * (1 - chip) + core, 2 * (1 - chip) + 1 - core]
    )
    position = (
        blocks[:, None] * shard_len + jnp.arange(shard_len, dtype=jnp.int32)[None, :]
    ).reshape(-1)
    segment = jnp.sum((position[:, None] >= boundary[None, :]).astype(jnp.int32), axis=1)
    column = jnp.arange(128, dtype=jnp.int32)[None, :]
    query_mask = (segment[:, None] == column).astype(bf16)
    key_mask = jnp.where(
        (segment[:, None] == column) & (column < PAIRS), 0.0, masked_score
    ).astype(bf16)
    key_mask = jnp.concatenate([jnp.zeros((prefix, 128), bf16), key_mask], 0)

    pack0, pack3 = pack(scalars, expand_weight, reduce_weight, expand_bias, upstream)
    qkv, core_weight = project_first(scalars, hidden_in, hidden2, project_weight, project_bias)
    expand_sib, reduce_sib, bias_sib = beside(expand_weight), beside(reduce_weight), beside(expand_bias)
    cross, qkv, key_mask, query_mask, expand_sib, reduce_sib, bias_sib = lax.optimization_barrier(
        (cross, qkv, key_mask, query_mask, expand_sib, reduce_sib, bias_sib)
    )
    cross2 = beside(cross)
    piece0, piece3 = across(pack0), across(pack3)
    qkv = project_second(scalars, cross, cross2, core_weight, project_bias, qkv)
    attended_mine, attended_other, exps_mine, exps_other, recips_mine, recips_other = attend(
        scalars, qkv, prefix_keys, prefix_values, key_mask, query_mask
    )
    piece0, attended_other = lax.optimization_barrier((piece0, attended_other))
    piece1, piece2 = swap(piece0, "dp", 1, dp_size), swap(piece0, "dp", 2, dp_size)
    attended_here, piece0_sib = beside(attended_other), beside(piece0)
    attended_here, piece0_sib = lax.optimization_barrier((attended_here, piece0_sib))
    weights = tuple(
        far_core(array) for array in (expand_weight, expand_sib, reduce_weight, reduce_sib)
    )

    unit, inverse, total, slope, low = forward(
        scalars, attended_mine, attended_here, hidden_in, cross,
        (output_bias, first_gain, first_shift), output_weight, weights + (expand_bias, bias_sib),
        (piece0, piece0_sib),
    )
    quarter = hidden_here // 4
    piece1, piece2, low = lax.optimization_barrier((piece1, piece2, low))
    piece1_sib, piece2_sib = beside(piece1), beside(piece2)
    total, slope2 = remote(scalars, low, total, (1, 2), [piece1, piece2], quarter)
    piece3, total, slope2 = lax.optimization_barrier((piece3, total, slope2))
    quarter3 = piece3[: 2 * quarter]
    late = [quarter3, beside(quarter3)]
    total, slope2 = near_core(total, slope2)
    total, slope3 = remote(scalars, low, total, (1, 2), [piece1_sib, piece2_sib], quarter)
    *late, total, slope2, slope3 = lax.optimization_barrier((*late, total, slope2, slope3))
    *late, piece3, total, slope2, slope3 = near_core(*late, piece3, total, slope2, slope3)
    early = [piece0, piece0_sib, piece1, piece2, piece1_sib, piece2_sib]
    hidden_own, hidden_cross, grad_branch, grad_mine, grad_theirs = middle(
        scalars, query_mask,
        (first_gain, first_shift, reduce_bias, second_gain, second_shift),
        (low, unit, inverse, total, slope, slope2, slope3), upstream, output_weight, weights, early, late,
        piece3,
    )
    grad_here = beside(grad_theirs)
    exps, recips = (exps_mine, exps_other), (recips_mine, recips_other)

    hidden_theirs = across(hidden_cross)
    back_mine, back_own2, back_cross2, grad_prefix, last_weight = attend_back(
        scalars, qkv, prefix_keys, prefix_values, exps, recips, (attended_mine, attended_other),
        near_core(grad_mine, grad_here), far_core(project_weight),
    )
    back_mine, back_own2, back_cross2, grad_prefix, hidden_theirs = lax.optimization_barrier(
        (back_mine, back_own2, back_cross2, grad_prefix, hidden_theirs)
    )

    def step(array, dp_bit, mp_bit):
        return lax.ppermute(
            array, ("dp", "mp"),
            [
                (d * mp_size + m, (d ^ dp_bit) * mp_size + (m ^ mp_bit))
                for d in range(dp_size)
                for m in range(mp_size)
            ],
        )

    def four_sum(parts):
        own_part, first, second, both = (part.astype(f32) for part in parts)
        return (own_part + first) + (second + both)

    cross_there = beside(back_cross2)
    own_there = beside(back_own2)
    low_prefix = grad_prefix.astype(bf16)
    group = (low_prefix, step(low_prefix, 0, 2), step(low_prefix, 1, 0), step(low_prefix, 1, 2))
    grad_branch = far_core(grad_branch)
    in_cross = project_back_cross(scalars, back_mine, cross_there, grad_branch, last_weight)
    _, group = lax.optimization_barrier((in_cross, group))
    in_cross = [across(part) for part in in_cross]
    grad_prefix = four_sum(group)
    bit = 8
    while bit < dp_size:
        grad_prefix = grad_prefix + swap(grad_prefix, "dp", bit, dp_size)
        bit *= 2
    low_prefix = grad_prefix.astype(bf16)
    group = (low_prefix, step(low_prefix, 2, 0), step(low_prefix, 4, 0), step(low_prefix, 6, 0))
    in_own, hidden_out = project_back_own(
        scalars, back_mine, own_there, grad_branch, last_weight, far_core(hidden_theirs), hidden_own
    )
    in_own, in_cross, group = lax.optimization_barrier((in_own, in_cross, group))
    in_cross = jnp.concatenate(in_cross, 0)
    grad_in = jnp.where(chip == 0, jnp.stack([in_own, in_cross]), jnp.stack([in_cross, in_own]))
    grad_prefix = four_sum(group)
    grad_prefix_sib = beside(grad_prefix)
    grad_prefix = jnp.where(
        core == 0,
        jnp.concatenate([grad_prefix, grad_prefix_sib], 2),
        jnp.concatenate([grad_prefix_sib, grad_prefix], 2),
    )
    return (hidden_out, grad_in, grad_prefix[0], grad_prefix[1])


def solution(mesh):
    placed = (
        P("dp", "mp", None),
        P("dp", None),
        P(),
        P(),
        P(),
        P(),
        P(),
        P(),
        P(),
        P(),
        P(None, "mp"),
        P("mp"),
        P("mp", None),
        P(),
        P(),
        P(),
        P("dp", "mp", None),
    )
    return jax.shard_map(
        functools.partial(shards, (mesh.shape["dp"], mesh.shape["mp"])),
        mesh=mesh,
        in_specs=placed,
        out_specs=(P("dp", "mp", None), P("dp", "mp", None), P(), P()),
        check_vma=False,
    )
```

```python
import functools

import jax
import jax.numpy as jnp
from jax import lax
from jax.experimental import pallas as pl
from jax.experimental.pallas import tpu as pltpu
from jax.sharding import PartitionSpec as P

HEADS = 16
PAIRS = 8

epsilon = 1e-05
masked_score = -1e30
root_half = 0.7071067811865476
inverse_root = 0.3989422804014327
log2_e = 1.4426950408889634
ln_2 = 0.6931471805599453

bf16 = jnp.bfloat16
f32 = jnp.float32


def dot(left, right, left_dim=1, right_dim=0):
    return lax.dot_general(
        left, right, (((left_dim,), (right_dim,)), ((), ())), preferred_element_type=f32
    )


def params(mebibytes):
    return pltpu.CompilerParams(vmem_limit_bytes=mebibytes * 2**20)


def cost(flops, bytes_accessed, transcendentals=0):
    return pl.CostEstimate(
        flops=int(flops), bytes_accessed=int(bytes_accessed), transcendentals=int(transcendentals)
    )


ANY = pl.BlockSpec(memory_space=pl.ANY)


def far_core(array):
    return pltpu.with_memory_space_constraint(array, pltpu.HBM)


def near_core(*arrays):
    return tuple(pltpu.with_memory_space_constraint(array, pltpu.VMEM) for array in arrays)


VM = pl.BlockSpec(memory_space=pltpu.VMEM)
SM = pl.BlockSpec(memory_space=pltpu.SMEM)
BRIEF = (1e6, 1e5)


def swap(array, axis, bit, size):
    return lax.ppermute(array, axis, [(i, i ^ bit) for i in range(size)])


class Copies:
    def __init__(self, sems):
        self.sems, self.used = sems, 0

    def __call__(self, source, target):
        copy = pltpu.make_async_copy(source, target, self.sems.at[self.used])
        self.used += 1
        return copy


def start_all(copies):
    for copy in copies:
        copy.start()


def wait_all(copies):
    for copy in copies:
        copy.wait()


def columns_at(start, size):
    return pl.ds(pl.multiple_of(start, size), size)


def project_tokens(core, copies, parts, weight, weight_copies, bias, out, place, tokens_v, out_v):
    block = parts[0].shape[-2]
    half = out.shape[2]
    token_copies = [
        copies(part, tokens_v.at[pl.ds(i * block, block)]) for i, part in enumerate(parts)
    ]
    start_all(token_copies)
    start_all(weight_copies)
    wait_all(token_copies)
    out_copies = []
    for j in range(3):
        wait_all(weight_copies[j : j + 1])
        shift = jnp.where(
            core == 0,
            bias[2 * j * half : (2 * j + 1) * half].astype(f32),
            bias[(2 * j + 1) * half : (2 * j + 2) * half].astype(f32),
        )
        result = dot(tokens_v[...], weight[j]) + shift.reshape(1, half)
        if j == 0:
            result = result * (log2_e * 0.125)
        out_v[j] = result.astype(bf16)
        copy = copies(out_v.at[j], out.at[j, pl.ds(place * 2 * block, 2 * block)])
        copy.start()
        out_copies.append(copy)
    return out_copies


def pack_kernel(scalars, expand, reduce, hidden_bias, upstream, pack0, pack3, packs, bias_v, sems):
    chip, part = scalars[1], scalars[2]
    copies = Copies(sems)
    width, hidden_here = expand.shape
    quarter = hidden_here // 4
    bias_v[...] = jnp.broadcast_to(
        hidden_bias[...].astype(f32).reshape(1, hidden_here), (16, hidden_here)
    ).astype(bf16)
    groups = []
    for n, index in enumerate((part, 3 - part)):
        pack = packs.at[n]
        columns = columns_at(index * quarter, quarter)
        group = []
        for i in range(width // quarter):
            block = pl.ds(i * quarter, quarter)
            group.append(copies(expand.at[block, columns], pack.at[pl.ds(0, quarter), block]))
        group.append(copies(reduce.at[columns], pack.at[pl.ds(quarter, quarter)]))
        groups.append(group)
    groups[0].append(copies(bias_v, packs.at[0, pl.ds(2 * quarter, 16), pl.ds(0, hidden_here)]))
    groups[1].append(
        copies(upstream.at[1 - chip], packs.at[1, pl.ds(2 * quarter, upstream.shape[1])])
    )
    for group in groups:
        start_all(group)
    out_copies = []
    for n, (group, out) in enumerate(zip(groups, (pack0, pack3))):
        wait_all(group)
        copy = copies(packs.at[n, pl.ds(0, out.shape[0])], out)
        copy.start()
        out_copies.append(copy)
    wait_all(out_copies)


def pack(scalars, expand, reduce, hidden_bias, upstream):
    width, hidden_here = expand.shape
    quarter = hidden_here // 4
    packs = [
        jax.ShapeDtypeStruct((2 * quarter + n, width), bf16) for n in (16, upstream.shape[1])
    ]
    return pl.pallas_call(
        pack_kernel,
        in_specs=[SM, ANY, ANY, VM, ANY],
        out_specs=[ANY] * 2,
        out_shape=packs,
        scratch_shapes=[
            pltpu.VMEM((2, *packs[1].shape), bf16),
            pltpu.VMEM((16, hidden_here), bf16),
            pltpu.SemaphoreType.DMA((2 * (width // quarter + 2) + 2,)),
        ],
        compiler_params=params(56),
        cost_estimate=cost(*BRIEF),
        name="pack",
    )(scalars, expand, reduce, hidden_bias, upstream)


def project_first_kernel(
    scalars, hidden, hidden2, weight, bias, out, weight_out, tokens_v, out_v, sems
):
    core, chip = scalars[0], scalars[1]
    copies = Copies(sems)
    half = out.shape[2]
    weight_copies = [
        copies(weight.at[:, columns_at((2 * j + core) * half, half)], weight_out.at[j])
        for j in range(3)
    ]
    wait_all(
        project_tokens(
            core, copies, (hidden.at[chip], hidden2.at[chip]), weight_out, weight_copies, bias,
            out, 0, tokens_v, out_v,
        )
    )


def project_second_kernel(scalars, cross, cross2, weight, bias, _, out, tokens_v, out_v, sems):
    wait_all(
        project_tokens(
            scalars[0], Copies(sems), (cross, cross2), weight, [], bias, out, 1, tokens_v, out_v
        )
    )


def project_scratch(block, width, half):
    return [
        pltpu.VMEM((2 * block, width), bf16),
        pltpu.VMEM((3, 2 * block, half), bf16),
        pltpu.SemaphoreType.DMA((8,)),
    ]


def project_first(scalars, hidden, hidden2, weight, bias):
    _, block, width = hidden.shape
    half = width // 2
    return pl.pallas_call(
        project_first_kernel,
        in_specs=[SM, ANY, ANY, ANY, VM],
        out_specs=[ANY, VM],
        out_shape=[
            jax.ShapeDtypeStruct((3, 4 * block, half), bf16), pltpu.VMEM((3, width, half), bf16)
        ],
        scratch_shapes=project_scratch(block, width, half),
        compiler_params=params(50),
        cost_estimate=cost(*BRIEF),
        name="project_first",
    )(scalars, hidden, hidden2, weight, bias)


def project_second(scalars, cross, cross2, weight, bias, qkv):
    block, width = cross.shape
    half = width // 2
    return pl.pallas_call(
        project_second_kernel,
        in_specs=[SM, ANY, ANY, VM, VM, ANY],
        out_specs=ANY,
        out_shape=jax.ShapeDtypeStruct(qkv.shape, bf16),
        input_output_aliases={5: 0},
        scratch_shapes=project_scratch(block, width, half),
        compiler_params=params(50),
        cost_estimate=cost(*BRIEF),
        name="project_second",
    )(scalars, *near_core(cross, cross2, weight), bias, qkv)


def head_mask(shape, head, axis):
    return (lax.broadcasted_iota(jnp.int32, shape, axis) // 64) == head


def keep_head(array, head, axis):
    return jnp.where(head_mask(array.shape, head, axis), array, jnp.zeros_like(array))


def attend_kernel(
    core_ref, query, key, value, prefix_k, prefix_v, key_mask, query_mask,
    out_mine, out_other, exps_mine, exps_other, recips_mine, recips_other, keys, values_t,
):
    prefix = prefix_k.shape[0]
    tokens = query.shape[1]
    count = prefix + tokens
    chunk = tokens // 4
    keys[:prefix, :128] = prefix_k[...]
    keys[prefix:, :128] = key[0]

    @pl.when(pl.program_id(0) == 0)
    def _():
        keys[:, 128:] = key_mask[...]
        values_t[:, 64:, :] = jnp.ones((2, values_t.shape[1] - 64, count), bf16)

    prefix_t = prefix_v[...].astype(f32).T.astype(bf16)
    value_t = value[0].astype(f32).T.astype(bf16)
    for head in range(2):
        values_t[head, :64, :prefix] = prefix_t[64 * head : 64 * head + 64]
        values_t[head, :64, prefix:] = value_t[64 * head : 64 * head + 64]
    units = [(i, head) for i in (1, 3, 0, 2) for head in range(2)]

    def score(unit):
        i, head = unit
        rows = slice(i * chunk, (i + 1) * chunk)
        masked = jnp.concatenate([keep_head(query[0, rows, :], head, 1), query_mask[rows, :]], axis=1)
        return dot(keys[...], masked, 1, 1)

    ahead = 2
    pending = [score(unit) for unit in units[:ahead]]
    for n, (i, head) in enumerate(units):
        scores = pending.pop(0)
        if n + ahead < len(units):
            pending.append(score(units[n + ahead]))
        out, exps, recips = (
            (out_mine, exps_mine, recips_mine), (out_other, exps_other, recips_other)
        )[i % 2]
        cols = slice(i // 2 * chunk, (i // 2 + 1) * chunk)
        top = jnp.max(scores, axis=0, keepdims=True)
        weights = jnp.exp2(scores - top).astype(bf16)
        exps[0, head, :, cols] = weights
        summed = dot(values_t[head], weights)
        recip = 1.0 / summed[64:65, :]
        recips[0, head, :, cols] = jnp.broadcast_to(recip, (8, chunk))
        out[64 * head : 64 * head + 64, cols] = (summed[:64, :] * recip).astype(bf16)


def attend(core, qkv, prefix_keys, prefix_values, key_mask, query_mask):
    _, tokens, half = qkv.shape
    prefix = prefix_keys.shape[0]
    count = prefix + tokens
    pairs = half // 128
    prefix_spec = pl.BlockSpec((prefix, 128), lambda p, k: (0, k[0] * pairs + p))
    out_spec = pl.BlockSpec((128, tokens // 2), lambda p, k: (p, 0))
    exps_spec = pl.BlockSpec((1, 2, count, tokens // 2), lambda p, k: (p, 0, 0, 0))
    recips_spec = pl.BlockSpec((1, 2, 8, tokens // 2), lambda p, k: (p, 0, 0, 0))
    return pl.pallas_call(
        attend_kernel,
        grid_spec=pltpu.PrefetchScalarGridSpec(
            num_scalar_prefetch=1,
            grid=(pairs,),
            in_specs=[
                pl.BlockSpec((1, tokens, 128), lambda p, k, j=j: (j, 0, p)) for j in range(3)
            ]
            + [
                prefix_spec,
                prefix_spec,
                pl.BlockSpec((count, 128), lambda p, k: (0, 0)),
                pl.BlockSpec((tokens, 128), lambda p, k: (0, 0)),
            ],
            out_specs=[out_spec] * 2 + [exps_spec] * 2 + [recips_spec] * 2,
            scratch_shapes=[pltpu.VMEM((count, 256), bf16), pltpu.VMEM((2, 64 + 16, count), bf16)],
        ),
        out_shape=[jax.ShapeDtypeStruct((half, tokens // 2), bf16)] * 2
        + [jax.ShapeDtypeStruct((pairs, 2, count, tokens // 2), bf16)] * 2
        + [jax.ShapeDtypeStruct((pairs, 2, 8, tokens // 2), f32)] * 2,
        compiler_params=params(56),
        cost_estimate=cost(*BRIEF),
        name="attend",
    )(core, qkv, qkv, qkv, prefix_keys, prefix_values, key_mask, query_mask)


def ordered_rows(array):
    block = array.shape[0] // 4
    return [array[i * block : (i + 1) * block] for i in (0, 2, 1, 3)]


def attend_back_kernel(
    core_ref, query, key, value, prefix_k, prefix_v, exps_mine, exps_other, recips_mine, recips_other,
    attended_mine, attended_other, grad_mine, grad_other, weight,
    out_mine, out_own2, out_cross2, out_prefix, weight_out,
    keys, values, keys_t, slopes, queries, queries_t, scaled, weight_sem,
):
    prefix = prefix_k.shape[0]
    tokens = query.shape[1]
    chunk = tokens // 4
    half = tokens // 2
    pair = pl.program_id(0)
    weight_copy = pltpu.make_async_copy(weight, weight_out, weight_sem.at[0])

    @pl.when(pair == 1)
    def _():
        weight_copy.start()

    keys[:prefix, :] = prefix_k[...]
    keys[prefix:, :] = key[0]
    values[:prefix, :] = prefix_v[...]
    values[prefix:, :] = value[0]
    keys_t[...] = keys[...].astype(f32).T.astype(bf16)
    queries[...] = jnp.concatenate(ordered_rows(query[0]), axis=0)
    spreads = []
    for head in range(2):
        rows = slice(64 * head, 64 * head + 64)
        parts = []
        for side, (recips, attended, grad) in enumerate(
            ((recips_mine, attended_mine, grad_mine), (recips_other, attended_other, grad_other))
        ):
            part = grad[rows, :].astype(f32) * recips[0, head, 0:1, :]
            scaled[rows, side * half : (side + 1) * half] = part.astype(bf16)
            parts.append(jnp.sum(part * attended[rows, :].astype(f32), axis=0, keepdims=True))
        spreads.append(jnp.concatenate(parts, axis=1))
    units = [(head, i) for head in range(2) for i in range(4)]

    def head_rows(array, head):
        zeros = jnp.zeros_like(array[:64])
        return jnp.concatenate([array[:64], zeros] if head == 0 else [zeros, array[64:]], axis=0)

    def grad_probs(unit):
        head, i = unit
        return dot(values[...], head_rows(scaled[:, i * chunk : (i + 1) * chunk], head))

    def exps_of(head, i):
        return (exps_mine, exps_other)[i // 2][0, head, :, i % 2 * chunk : (i % 2 + 1) * chunk]

    def value_part(head):
        total = None
        for side, exps in enumerate((exps_mine, exps_other)):
            cols = slice(side * half, (side + 1) * half)
            part = dot(exps[0, head], head_rows(scaled[:, cols], head), 1, 1)
            total = part if total is None else total + part
        return total

    def key_part(head):
        return dot(slopes[head], keep_head(queries[...], head, 1))

    ahead = 4
    pending = [grad_probs(unit) for unit in units[:ahead]]
    for n, (head, i) in enumerate(units):
        grads = pending.pop(0)
        if n + ahead < len(units):
            pending.append(grad_probs(units[n + ahead]))
        cols = slice(i * chunk, (i + 1) * chunk)
        slopes[head, :, cols] = (
            exps_of(head, i).astype(f32) * (grads - spreads[head][:, cols])
        ).astype(bf16)
        if n == 0:
            value_first = value_part(0)
        rows = slice(64 * head, 64 * head + 64)
        queries_t[rows, cols] = dot(keys_t[rows, :], slopes[head, :, cols]) * 0.125
        if n == 4:
            key_first = key_part(0)
    value_grads = value_first + value_part(1)
    key_grads = (key_first + key_part(1)) * ln_2
    out_prefix[0] = key_grads[:prefix]
    out_prefix[1] = value_grads[:prefix]
    query_grads = queries_t[...].T.astype(bf16)
    for j, parts in enumerate(
        ([query_grads[i * chunk : (i + 1) * chunk] for i in range(4)],)
        + tuple(ordered_rows(array[prefix:].astype(bf16)) for array in (key_grads, value_grads))
    ):
        out_mine[j, :chunk] = parts[0]
        out_mine[j, chunk:] = parts[1]
        out_own2[j] = parts[2]
        out_cross2[j] = parts[3]

    @pl.when(pair == pl.num_programs(0) - 1)
    def _():
        weight_copy.wait()


def attend_back(core, qkv, prefix_keys, prefix_values, exps, recips, attended, grads, weight):
    _, tokens, half = qkv.shape
    prefix = prefix_keys.shape[0]
    count = prefix + tokens
    pairs = half // 128
    prefix_spec = pl.BlockSpec((prefix, 128), lambda p, k: (0, k[0] * pairs + p))
    exps_spec = pl.BlockSpec((1, 2, count, tokens // 2), lambda p, k: (p, 0, 0, 0))
    recips_spec = pl.BlockSpec((1, 2, 8, tokens // 2), lambda p, k: (p, 0, 0, 0))
    heads_spec = pl.BlockSpec((128, tokens // 2), lambda p, k: (p, 0))
    rows = (tokens // 2, tokens // 4, tokens // 4)
    return pl.pallas_call(
        attend_back_kernel,
        grid_spec=pltpu.PrefetchScalarGridSpec(
            num_scalar_prefetch=1,
            grid=(pairs,),
            in_specs=[
                pl.BlockSpec((1, tokens, 128), lambda p, k, j=j: (j, 0, p)) for j in range(3)
            ]
            + [prefix_spec] * 2
            + [exps_spec] * 2
            + [recips_spec] * 2
            + [heads_spec] * 4
            + [ANY],
            out_specs=[pl.BlockSpec((3, n, 128), lambda p, k: (0, 0, p)) for n in rows]
            + [pl.BlockSpec((2, prefix, 128), lambda p, k: (0, 0, p)), ANY],
            scratch_shapes=[
                pltpu.VMEM((count, 128), bf16),
                pltpu.VMEM((count, 128), bf16),
                pltpu.VMEM((128, count), bf16),
                pltpu.VMEM((2, count, tokens), bf16),
                pltpu.VMEM((tokens, 128), bf16),
                pltpu.VMEM((128, tokens), f32),
                pltpu.VMEM((128, tokens), bf16),
                pltpu.SemaphoreType.DMA((1,)),
            ],
        ),
        out_shape=[pltpu.VMEM((3, rows[0], half), bf16)]
        + [jax.ShapeDtypeStruct((3, n, half), bf16) for n in rows[1:]]
        + [jax.ShapeDtypeStruct((2, prefix, half), f32), pltpu.VMEM(weight.shape, bf16)],
        compiler_params=params(40),
        cost_estimate=cost(*BRIEF),
        name="attend_back",
    )(core, qkv, qkv, qkv, prefix_keys, prefix_values, *exps, *recips, *attended, *grads, weight)


def mean_rows(array):
    return jnp.mean(array, axis=-1, keepdims=True)


def unit_norm(array):
    centered = array - mean_rows(array)
    inverse = lax.rsqrt(mean_rows(centered * centered) + epsilon)
    return centered * inverse, inverse


def norm_back(scaled, unit, inverse):
    return inverse * (scaled - mean_rows(scaled) - unit * mean_rows(scaled * unit))


def gelu_both(hidden):
    gate = 0.5 * (1.0 + lax.erf(hidden * root_half))
    slope = gate + hidden * inverse_root * jnp.exp(-0.5 * hidden * hidden)
    return (hidden * gate).astype(bf16), slope.astype(bf16)


def feed_forward(steps, total):
    hidden = None
    for i, step in enumerate(steps):
        if i == 0:
            wait_all(step[3])
            hidden = step[0]()
        following = None
        if i + 1 < len(steps):
            wait_all(steps[i + 1][3])
            following = steps[i + 1][0]()
        active, slope = gelu_both(hidden)
        step[1](slope)
        part = dot(active, step[2]())
        if total is None:
            total = part
        elif hasattr(total, "at"):
            total[...] += part
        hidden = following


def forward_kernel(
    core_ref, mine, other, own, cross, output_bias, first_gain, first_shift, output_weight,
    expand_own, expand_sib, reduce_own, reduce_sib, bias_own, bias_sib, piece0, piece1,
    unit_out, inverse_out, total_out, slope_out, low,
    out_w, expand_w, reduce_w, expand_r, reduce_r, bias_r, own_v, sems,
):
    core, chip = core_ref[0], core_ref[1]
    copies = [
        pltpu.make_async_copy(output_weight, out_w, sems.at[0]),
        pltpu.make_async_copy(expand_own, expand_w.at[0], sems.at[1]),
        pltpu.make_async_copy(reduce_own, reduce_w.at[0], sems.at[2]),
        pltpu.make_async_copy(expand_sib, expand_w.at[1], sems.at[3]),
        pltpu.make_async_copy(reduce_sib, reduce_w.at[1], sems.at[4]),
        pltpu.make_async_copy(own.at[chip], own_v, sems.at[5]),
    ]
    start_all(copies[5:] + copies[:5])
    piece_sems = Copies(sems)
    piece_sems.used = 6
    quarter = reduce_r.shape[0] // 2
    waits = piece_copies(piece_sems, (piece0, piece1), 0, quarter, expand_r, reduce_r)
    waits[0] = waits[0] + bias_copies(piece_sems, (piece0, piece1), quarter, bias_r)
    for group in waits:
        start_all(group)
    biases = bias_rows(core_ref[2], (0, 0), quarter, bias_r)
    copies[5].wait()
    copies[0].wait()
    half = mine.shape[0]
    block = own_v.shape[0]
    output_row, gain, shift = (
        ref[...].astype(f32).reshape(1, -1) for ref in (output_bias, first_gain, first_shift)
    )
    for i, ref in enumerate((own_v, cross)):
        rows = slice(i * block, (i + 1) * block)
        branch = dot(mine[:, rows], out_w[pl.ds(pl.multiple_of(core * half, half), half), :], 0, 0)
        branch += dot(
            other[:, rows], out_w[pl.ds(pl.multiple_of((1 - core) * half, half), half), :], 0, 0
        )
        unit, inverse = unit_norm(ref[...].astype(f32) + (branch + output_row))
        unit_out[rows, :] = unit
        inverse_out[rows, :] = jnp.broadcast_to(inverse, (block, 128))
        low[rows, :] = (unit * gain + shift).astype(bf16)
    chunk = 512
    hidden_here = expand_own.shape[1]

    def step(i, bias, start):
        cols = slice(start, start + chunk)

        def store(slope):
            slope_out[:, i * hidden_here + start : i * hidden_here + start + chunk] = slope

        return (
            lambda: dot(low[...], expand_w[i, :, cols]) + bias[cols].astype(f32).reshape(1, chunk),
            store,
            lambda: reduce_w[i, cols, :],
            copies[1 + 2 * i : 3 + 2 * i] if start == 0 else [],
        )

    total_out[...] = jnp.zeros(total_out.shape, f32)
    feed_forward(
        [
            step(i, bias, start)
            for i, bias in enumerate((bias_own, bias_sib))
            for start in range(0, hidden_here, chunk)
        ]
        + piece_steps(
            2, 0, quarter, low, expand_r, reduce_r, biases, slope_out, waits, 2 * hidden_here
        ),
        total_out,
    )


def forward(core, mine, other, own, cross, vectors, output_weight, weights, pieces):
    tokens = mine.shape[1]
    _, block, width = own.shape
    hidden = weights[0].shape[1]
    quarter = hidden // 4
    return pl.pallas_call(
        forward_kernel,
        in_specs=[SM, VM, VM, ANY] + [VM] * 4 + [ANY] * 5 + [VM] * 2 + [ANY] * 2,
        out_specs=[VM] * 5,
        out_shape=[
            jax.ShapeDtypeStruct((tokens, width), f32),
            jax.ShapeDtypeStruct((tokens, 128), f32),
            jax.ShapeDtypeStruct((tokens, width), f32),
            jax.ShapeDtypeStruct((tokens, 2 * hidden + 2 * quarter), bf16),
            jax.ShapeDtypeStruct((tokens, width), bf16),
        ],
        scratch_shapes=[
            pltpu.VMEM((width, width), bf16),
            pltpu.VMEM((2, width, hidden), bf16),
            pltpu.VMEM((2, hidden, width), bf16),
            pltpu.VMEM((width, 2 * quarter), bf16),
            pltpu.VMEM((2 * quarter, width), bf16),
            pltpu.VMEM((2, 16, width), bf16),
            pltpu.VMEM((block, width), bf16),
            pltpu.SemaphoreType.DMA((6 + 2 * (width // quarter + 2),)),
        ],
        compiler_params=params(40),
        cost_estimate=cost(*BRIEF),
        name="forward",
    )(core, mine, other, own, cross, *vectors, output_weight, *weights, *pieces)


def piece_copies(copies, pieces, place, quarter, expand_r, reduce_r):
    width = expand_r.shape[0]
    result = []
    for i, piece in enumerate(pieces):
        here = pl.ds((place + i) * quarter, quarter)
        group = []
        for j in range(width // quarter):
            rows = pl.ds(j * quarter, quarter)
            group.append(copies(piece.at[pl.ds(0, quarter), rows], expand_r.at[rows, here]))
        group.append(copies(piece.at[pl.ds(quarter, quarter)], reduce_r.at[here]))
        result.append(group)
    return result


def bias_copies(copies, pieces, quarter, bias_r):
    return [
        copies(piece.at[pl.ds(2 * quarter, 16)], bias_r.at[i]) for i, piece in enumerate(pieces)
    ]


def bias_rows(part, bits, quarter, bias_r):
    return [
        lambda i=i, bit=bit: bias_r[
            i, 0:1, pl.ds(pl.multiple_of(lax.bitwise_xor(part, bit) * quarter, quarter), quarter)
        ]
        for i, bit in enumerate(bits)
    ]


def piece_steps(
    count, place, quarter, low, expand_r, reduce_r, biases, slope_out, waits, slope_place=0
):
    def step(first):
        rows = slice((place + first) * quarter, (place + first + 2) * quarter)

        def hidden():
            bias = [biases[first + i]() for i in range(2)]
            return dot(low[...], expand_r[:, rows]) + jnp.concatenate(bias, axis=1).astype(f32)

        def store(slope):
            start = slope_place + first * quarter
            slope_out[:, start : start + 2 * quarter] = slope

        return (
            hidden,
            store,
            lambda: reduce_r[rows, :],
            waits[first] + waits[first + 1],
        )

    return [step(first) for first in range(0, count, 2)]


def remote_kernel(bits, *refs):
    count = len(bits)
    scalars, low_in, total_in = refs[:3]
    pieces = refs[3 : 3 + count]
    total_out, slope_out, low, expand_r, reduce_r, bias_r, sems = refs[3 + count :]
    quarter = reduce_r.shape[0] // count
    copies = Copies(sems)
    first = [copies(low_in, low), copies(total_in, total_out)]
    waits = piece_copies(copies, pieces, 0, quarter, expand_r, reduce_r)
    waits[0] = waits[0] + bias_copies(copies, pieces, quarter, bias_r)
    start_all(first[:1] + waits[0] + waits[1] + first[1:])
    for group in waits[2:]:
        start_all(group)
    biases = bias_rows(scalars[2], bits, quarter, bias_r)
    steps = piece_steps(count, 0, quarter, low, expand_r, reduce_r, biases, slope_out, waits)
    steps[0] = steps[0][:3] + (first + steps[0][3],)
    feed_forward(steps, total_out)


def remote(scalars, low, total, bits, pieces, quarter):
    tokens, width = total.shape
    count = len(pieces)
    return pl.pallas_call(
        functools.partial(remote_kernel, bits),
        in_specs=[SM] + [ANY] * (2 + count),
        out_specs=[VM] * 2,
        out_shape=[
            pltpu.VMEM((tokens, width), f32),
            pltpu.VMEM((tokens, count * quarter), bf16),
        ],
        scratch_shapes=[
            pltpu.VMEM((tokens, width), bf16),
            pltpu.VMEM((width, count * quarter), bf16),
            pltpu.VMEM((count * quarter, width), bf16),
            pltpu.VMEM((count, 16, width), bf16),
            pltpu.SemaphoreType.DMA((2 + count * (width // quarter + 2),)),
        ],
        compiler_params=params(26),
        cost_estimate=cost(*BRIEF),
        name="remote",
    )(scalars, low, total, *pieces)


def middle_kernel(early, late, *refs):
    count = early + late
    scalars, query_mask = refs[:2]
    vectors = refs[2:7]
    low_in, unit_in, inverse, total_in, slope_in, slope2_in, slope3_in, upstream = refs[7:15]
    output_weight, expand_own, expand_sib, reduce_own, reduce_sib = refs[15:20]
    pieces = refs[20 : 20 + count]
    up_cross = refs[20 + count]
    hidden_own, hidden_cross, grad_out, att_mine, att_other = refs[21 + count : 26 + count]
    (
        out_w, expand_w, reduce_w, expand_r, reduce_r, bias_r, low, unit, acc, back_acc,
        slope_l, slope_e, slope_s, up, hidden, sems,
    ) = refs[26 + count :]
    core, chip = scalars[0], scalars[1]
    copies = Copies(sems)
    tokens, width = unit.shape
    block = tokens // 2
    quarter = reduce_r.shape[0] // count
    chunk = 2 * quarter
    hidden_here = expand_own.shape[1]
    rows_of = [pl.ds(i * block, block) for i in range(2)]

    up_cross = up_cross.at[pl.ds(2 * quarter, block)]
    low_copy = copies(low_in, low)
    late_waits = piece_copies(copies, pieces[early:], early, quarter, expand_r, reduce_r)
    late_waits[0] = late_waits[0] + bias_copies(copies, pieces[:2], quarter, bias_r)
    biases = bias_rows(scalars[2], (3, 3), quarter, bias_r)
    norm_copies = [
        [
            copies(total_in.at[rows_of[i]], acc.at[rows_of[i]]),
            copies(unit_in.at[rows_of[i]], unit.at[rows_of[i]]),
            copies((upstream.at[chip], up_cross)[i], up.at[rows_of[i]]),
        ]
        for i in range(2)
    ]
    local_copies = [
        [copies((reduce_own, reduce_sib)[i], reduce_w.at[i]), copies((expand_own, expand_sib)[i], expand_w.at[i])]
        for i in range(2)
    ]
    slope_copy = copies(slope_in, slope_l)
    early_copies = piece_copies(copies, pieces[:early], 0, quarter, expand_r, reduce_r)
    slope2_copies = [
        copies(array, slope_e.at[:, pl.ds(2 * i * quarter, 2 * quarter)])
        for i, array in enumerate((slope2_in, slope3_in))
    ]
    out_copy = copies(output_weight, out_w)
    start_all([low_copy] + [copy for group in late_waits + norm_copies for copy in group])
    start_all([local_copies[0][0], slope_copy, local_copies[0][1]] + local_copies[1])
    start_all([copy for group in early_copies for copy in group] + slope2_copies + [out_copy])

    steps = piece_steps(late, early, quarter, low, expand_r, reduce_r, biases, slope_s, late_waits)
    steps[0] = steps[0][:3] + ([low_copy] + steps[0][3],)
    for group in norm_copies:
        wait_all(group[:1])
    feed_forward(steps, acc)

    first_gain, first_shift, reduce_bias, second_gain, second_shift = (
        ref[...].astype(f32).reshape(1, -1) for ref in vectors
    )
    hidden_copies = []
    for i in range(2):
        wait_all(norm_copies[i][1:])
        for start in range(i * block, (i + 1) * block, block // 2):
            rows = slice(start, start + block // 2)
            masked = slice(2 * i * block + start - i * block, 2 * i * block + start - i * block + block // 2)
            live = 1.0 - query_mask[masked, PAIRS : PAIRS + 1].astype(f32)
            first_norm = unit[rows, :] * first_gain + first_shift
            unit2, inverse2 = unit_norm(first_norm + (acc[rows, :] + reduce_bias))
            hidden[rows, :] = ((unit2 * second_gain + second_shift) * live).astype(bf16)
            grad_feed = norm_back(up[rows, :].astype(f32) * live * second_gain, unit2, inverse2)
            back_acc[rows, :] = grad_feed
            low[rows, :] = grad_feed.astype(bf16)
        copy = copies(hidden.at[rows_of[i]], (hidden_own.at[chip], hidden_cross)[i])
        copy.start()
        hidden_copies.append(copy)

    backs = []
    for i in range(2):
        for start in range(0, hidden_here, chunk):
            cols = slice(start, start + chunk)
            place = slice(i * hidden_here + start, i * hidden_here + start + chunk)
            backs.append(
                (
                    lambda i=i, cols=cols: reduce_w[i, cols, :],
                    lambda i=i, cols=cols: expand_w[i, :, cols],
                    1,
                    lambda place=place: slope_l[:, place],
                    ([slope_copy] if i + start == 0 else []) + (local_copies[i] if start == 0 else []),
                )
            )
    total_pieces = early + late
    for first in range(0, total_pieces, 2):
        rows = slice(first * quarter, (first + 2) * quarter)

        def slopes(first=first):
            parts = [
                slope_l[:, 2 * hidden_here + j * quarter : 2 * hidden_here + (j + 1) * quarter]
                if j < 2
                else slope_e[:, (j - 2) * quarter : (j - 1) * quarter]
                if j < early
                else slope_s[:, (j - early) * quarter : (j - early + 1) * quarter]
                for j in (first, first + 1)
            ]
            return jnp.concatenate(parts, axis=1)

        waits = [copy for j in (first, first + 1) if j < early for copy in early_copies[j]]
        backs.append(
            (
                lambda rows=rows: reduce_r[rows, :],
                lambda rows=rows: expand_r[:, rows],
                1,
                slopes,
                (slope2_copies if first == 0 else []) + waits,
            )
        )

    def grads(step):
        wait_all(step[4])
        return dot(low[...], step[0](), 1, 1)

    grad = grads(backs[0])
    for i, step in enumerate(backs):
        following = grads(backs[i + 1]) if i + 1 < len(backs) else None
        back = (grad * step[3]().astype(f32)).astype(bf16)
        back_acc[...] += dot(back, step[1](), 1, step[2])
        grad = following

    grad_copies = []
    for i in range(2):
        for start in range(i * block, (i + 1) * block, block // 2):
            rows = slice(start, start + block // 2)
            grad = norm_back(back_acc[rows, :] * first_gain, unit[rows, :], inverse[rows, 0:1])
            acc[rows, :] = grad
            low[rows, :] = grad.astype(bf16)
        copy = copies(acc.at[rows_of[i]], grad_out.at[rows_of[i]])
        copy.start()
        grad_copies.append(copy)
    out_copy.wait()
    half = width // 2
    att_other[...] = dot(
        out_w[pl.ds(pl.multiple_of((1 - core) * half, half), half), :], low[...], 1, 1
    ).astype(bf16)
    att_mine[...] = dot(
        out_w[pl.ds(pl.multiple_of(core * half, half), half), :], low[...], 1, 1
    ).astype(bf16)
    wait_all(hidden_copies + grad_copies)


def middle(scalars, query_mask, vectors, saved, upstream, output_weight, weights, early, late, last):
    tokens, width = saved[1].shape
    block = tokens // 2
    hidden = weights[0].shape[1]
    quarter = hidden // 4
    pieces = early + late
    count = len(pieces)
    return pl.pallas_call(
        functools.partial(middle_kernel, len(early), len(late)),
        in_specs=[SM] + [VM] * 6 + [ANY] * 2 + [VM] + [ANY] * (11 + count),
        out_specs=[ANY] * 3 + [VM] * 2,
        out_shape=[
            jax.ShapeDtypeStruct(upstream.shape, bf16),
            jax.ShapeDtypeStruct((block, width), bf16),
            jax.ShapeDtypeStruct((tokens, width), f32),
            pltpu.VMEM((width // 2, tokens), bf16),
            pltpu.VMEM((width // 2, tokens), bf16),
        ],
        scratch_shapes=[
            pltpu.VMEM((width, width), bf16),
            pltpu.VMEM((2, width, hidden), bf16),
            pltpu.VMEM((2, hidden, width), bf16),
            pltpu.VMEM((width, count * quarter), bf16),
            pltpu.VMEM((count * quarter, width), bf16),
            pltpu.VMEM((len(late), 16, width), bf16),
            pltpu.VMEM((tokens, width), bf16),
            pltpu.VMEM((tokens, width), f32),
            pltpu.VMEM((tokens, width), f32),
            pltpu.VMEM((tokens, width), f32),
            pltpu.VMEM((tokens, 2 * hidden + 2 * quarter), bf16),
            pltpu.VMEM((tokens, (len(early) - 2) * quarter), bf16),
            pltpu.VMEM((tokens, len(late) * quarter), bf16),
            pltpu.VMEM((tokens, width), bf16),
            pltpu.VMEM((tokens, width), bf16),
            pltpu.SemaphoreType.DMA((19 + len(late) + count * (width // quarter + 1),)),
        ],
        compiler_params=params(42),
        cost_estimate=cost(*BRIEF),
        name="middle",
    )(
        scalars, query_mask, *vectors, *saved, upstream, output_weight, *weights,
        *pieces, last,
    )


def project_back_rows(core, copies, place, mine, other, grad_branch, weight, left, grad, out):
    rows, width = out.shape
    half = other.shape[2]
    step = width // 4
    here = pl.ds(place * rows, rows)
    left_copies = [
        copy
        for j in range(3)
        for copy in (
            copies(mine.at[j, here], left.at[:, columns_at((2 * j + core) * half, half)]),
            copies(other.at[j], left.at[:, columns_at((2 * j + 1 - core) * half, half)]),
        )
    ]
    grad_copy = copies(grad_branch.at[here], grad)
    start_all(left_copies + [grad_copy])
    wait_all(left_copies)
    for start in range(0, width, step):
        cols = slice(start, start + step)
        total = dot(left[...], weight[cols, :], 1, 1)
        if start == 0:
            grad_copy.wait()
        out[:, cols] = (grad[:, cols] + total).astype(bf16)


def project_back_cross_kernel(scalars, mine, other, grad_branch, weight, out, left, grad, sems):
    project_back_rows(
        scalars[0], Copies(sems), 1, mine, other, grad_branch, weight, left, grad, out
    )


def project_back_own_kernel(
    scalars, mine, other, grad_branch, weight, theirs, _, out, hidden_out, left, grad, theirs_v, sems
):
    core, chip = scalars[0], scalars[1]
    copies = Copies(sems)
    theirs_in = copies(theirs, theirs_v)
    theirs_out = copies(theirs_v, hidden_out.at[1 - chip])
    theirs_in.start()
    theirs_in.wait()
    theirs_out.start()
    project_back_rows(core, copies, 0, mine, other, grad_branch, weight, left, grad, out)
    theirs_out.wait()


def project_back_scratch(rows, weight):
    width, columns = weight.shape
    return [pltpu.VMEM((rows, columns), bf16), pltpu.VMEM((rows, width), f32)]


def project_back_cross(scalars, mine, other, grad_branch, weight):
    _, rows, _ = other.shape
    return pl.pallas_call(
        project_back_cross_kernel,
        in_specs=[SM] + [ANY] * 3 + [VM],
        out_specs=VM,
        out_shape=jax.ShapeDtypeStruct((rows, weight.shape[0]), bf16),
        scratch_shapes=project_back_scratch(rows, weight) + [pltpu.SemaphoreType.DMA((7,))],
        compiler_params=params(40),
        cost_estimate=cost(*BRIEF),
        name="project_back_cross",
    )(scalars, *near_core(mine, other), grad_branch, *near_core(weight))


def project_back_own(scalars, mine, other, grad_branch, weight, theirs, hidden_out):
    _, rows, _ = other.shape
    width = weight.shape[0]
    return pl.pallas_call(
        project_back_own_kernel,
        in_specs=[SM] + [ANY] * 3 + [VM] + [ANY] * 2,
        out_specs=[VM, ANY],
        out_shape=[
            jax.ShapeDtypeStruct((rows, width), bf16),
            jax.ShapeDtypeStruct(hidden_out.shape, bf16),
        ],
        input_output_aliases={6: 1},
        scratch_shapes=project_back_scratch(rows, weight)
        + [pltpu.VMEM((rows, width), bf16), pltpu.SemaphoreType.DMA((9,))],
        compiler_params=params(40),
        cost_estimate=cost(*BRIEF),
        name="project_back_own",
    )(scalars, *near_core(mine, other), grad_branch, *near_core(weight), theirs, hidden_out)


def shards(
    sizes,
    hidden_in,
    pair_lengths,
    prefix_keys,
    prefix_values,
    project_weight,
    project_bias,
    output_weight,
    output_bias,
    first_gain,
    first_shift,
    expand_weight,
    expand_bias,
    reduce_weight,
    reduce_bias,
    second_gain,
    second_shift,
    upstream,
):
    dp_size, mp_size = sizes
    rows_here, shard_len, width = hidden_in.shape
    hidden_here = expand_weight.shape[1]
    prefix = prefix_keys.shape[0]
    half = width // 2
    place = lax.axis_index("mp")
    chip, core = place // 2, place % 2
    part = lax.axis_index("dp") % 4
    scalars = jnp.stack([core, chip, part]).astype(jnp.int32)

    def across(array):
        return swap(array, "mp", 2, mp_size)

    def beside(array):
        return swap(array, "mp", 1, mp_size)

    def take(array, index):
        return lax.dynamic_index_in_dim(array, index, 0, keepdims=False)

    def row(vector):
        return vector.reshape(1, -1)

    theirs = take(hidden_in, 1 - chip)
    theirs, expand_out, reduce_out = lax.optimization_barrier((theirs, expand_weight, reduce_weight))
    cross = across(theirs)
    hidden2 = beside(hidden_in)

    boundary = jnp.cumsum(take(pair_lengths, chip))
    blocks = jnp.stack(
        [2 * chip + core, 2 * chip + 1 - core, 2 * (1 - chip) + core, 2 * (1 - chip) + 1 - core]
    )
    position = (
        blocks[:, None] * shard_len + jnp.arange(shard_len, dtype=jnp.int32)[None, :]
    ).reshape(-1)
    segment = jnp.sum((position[:, None] >= boundary[None, :]).astype(jnp.int32), axis=1)
    column = jnp.arange(128, dtype=jnp.int32)[None, :]
    query_mask = (segment[:, None] == column).astype(bf16)
    key_mask = jnp.where(
        (segment[:, None] == column) & (column < PAIRS), 0.0, masked_score
    ).astype(bf16)
    key_mask = jnp.concatenate([jnp.zeros((prefix, 128), bf16), key_mask], 0)

    pack0, pack3 = pack(scalars, expand_weight, reduce_weight, expand_bias, upstream)
    qkv, core_weight = project_first(scalars, hidden_in, hidden2, project_weight, project_bias)
    expand_sib, reduce_sib, bias_sib = beside(expand_out), beside(reduce_out), beside(expand_bias)
    cross, qkv, key_mask, query_mask, expand_sib, reduce_sib, bias_sib = lax.optimization_barrier(
        (cross, qkv, key_mask, query_mask, expand_sib, reduce_sib, bias_sib)
    )
    cross2 = beside(cross)
    piece0, piece3 = across(pack0), across(pack3)
    qkv = project_second(scalars, cross, cross2, core_weight, project_bias, qkv)
    attended_mine, attended_other, exps_mine, exps_other, recips_mine, recips_other = attend(
        scalars, qkv, prefix_keys, prefix_values, key_mask, query_mask
    )
    piece0, attended_other = lax.optimization_barrier((piece0, attended_other))
    piece1, piece2 = swap(piece0, "dp", 1, dp_size), swap(piece0, "dp", 2, dp_size)
    attended_here, piece0_sib = beside(attended_other), beside(piece0)
    attended_here, piece0_sib = lax.optimization_barrier((attended_here, piece0_sib))
    weights = tuple(
        far_core(array) for array in (expand_weight, expand_sib, reduce_weight, reduce_sib)
    )

    unit, inverse, total, slope, low = forward(
        scalars, attended_mine, attended_here, hidden_in, cross,
        (output_bias, first_gain, first_shift), output_weight, weights + (expand_bias, bias_sib),
        (piece0, piece0_sib),
    )
    quarter = hidden_here // 4
    piece1, piece2, low = lax.optimization_barrier((piece1, piece2, low))
    piece1_sib, piece2_sib = beside(piece1), beside(piece2)
    total, slope2 = remote(scalars, low, total, (1, 2), [piece1, piece2], quarter)
    piece3, total, slope2 = lax.optimization_barrier((piece3, total, slope2))
    quarter3 = piece3[: 2 * quarter]
    late = [quarter3, beside(quarter3)]
    total, slope2 = near_core(total, slope2)
    total, slope3 = remote(scalars, low, total, (1, 2), [piece1_sib, piece2_sib], quarter)
    *late, total, slope2, slope3 = lax.optimization_barrier((*late, total, slope2, slope3))
    *late, piece3, total, slope2, slope3 = near_core(*late, piece3, total, slope2, slope3)
    early = [piece0, piece0_sib, piece1, piece2, piece1_sib, piece2_sib]
    hidden_own, hidden_cross, grad_branch, grad_mine, grad_theirs = middle(
        scalars, query_mask,
        (first_gain, first_shift, reduce_bias, second_gain, second_shift),
        (low, unit, inverse, total, slope, slope2, slope3), upstream, output_weight, weights, early, late,
        piece3,
    )
    grad_here = beside(grad_theirs)
    exps, recips = (exps_mine, exps_other), (recips_mine, recips_other)

    hidden_theirs = across(hidden_cross)
    back_mine, back_own2, back_cross2, grad_prefix, last_weight = attend_back(
        scalars, qkv, prefix_keys, prefix_values, exps, recips, (attended_mine, attended_other),
        near_core(grad_mine, grad_here), far_core(project_weight),
    )
    back_mine, back_own2, back_cross2, grad_prefix, hidden_theirs = lax.optimization_barrier(
        (back_mine, back_own2, back_cross2, grad_prefix, hidden_theirs)
    )

    def step(array, dp_bit, mp_bit):
        return lax.ppermute(
            array, ("dp", "mp"),
            [
                (d * mp_size + m, (d ^ dp_bit) * mp_size + (m ^ mp_bit))
                for d in range(dp_size)
                for m in range(mp_size)
            ],
        )

    def four_sum(parts):
        own_part, first, second, both = (part.astype(f32) for part in parts)
        return (own_part + first) + (second + both)

    cross_there = beside(back_cross2)
    own_there = beside(back_own2)
    low_prefix = grad_prefix.astype(bf16)
    group = (low_prefix, step(low_prefix, 0, 2), step(low_prefix, 1, 0), step(low_prefix, 1, 2))
    grad_branch = far_core(grad_branch)
    in_cross = project_back_cross(scalars, back_mine, cross_there, grad_branch, last_weight)
    in_cross, group = lax.optimization_barrier((in_cross, group))
    in_cross = across(in_cross)
    grad_prefix = four_sum(group)
    bit = 8
    while bit < dp_size:
        grad_prefix = grad_prefix + swap(grad_prefix, "dp", bit, dp_size)
        bit *= 2
    low_prefix = grad_prefix.astype(bf16)
    group = (low_prefix, step(low_prefix, 2, 0), step(low_prefix, 4, 0), step(low_prefix, 6, 0))
    in_own, hidden_out = project_back_own(
        scalars, back_mine, own_there, grad_branch, last_weight, far_core(hidden_theirs), hidden_own
    )
    in_own, in_cross, group = lax.optimization_barrier((in_own, in_cross, group))
    grad_in = jnp.where(chip == 0, jnp.stack([in_own, in_cross]), jnp.stack([in_cross, in_own]))
    grad_prefix = four_sum(group)
    grad_prefix_sib = beside(grad_prefix)
    grad_prefix = jnp.where(
        core == 0,
        jnp.concatenate([grad_prefix, grad_prefix_sib], 2),
        jnp.concatenate([grad_prefix_sib, grad_prefix], 2),
    )
    return (hidden_out, grad_in, grad_prefix[0], grad_prefix[1])


def solution(mesh):
    placed = (
        P("dp", "mp", None),
        P("dp", None),
        P(),
        P(),
        P(),
        P(),
        P(),
        P(),
        P(),
        P(),
        P(None, "mp"),
        P("mp"),
        P("mp", None),
        P(),
        P(),
        P(),
        P("dp", "mp", None),
    )
    return jax.shard_map(
        functools.partial(shards, (mesh.shape["dp"], mesh.shape["mp"])),
        mesh=mesh,
        in_specs=placed,
        out_specs=(P("dp", "mp", None), P("dp", "mp", None), P(), P()),
        check_vma=False,
    )
```
